32 devices in a mesh: dp: 8 (over z, x), tensor: 4 (over y, core).
Axes of the slice: x: 2, y: 2, z: 4, core: 2. Of those that a mesh axis runs over, the one named last changes fastest.
Arguments:
- inputs: float32 [8, 1024, 768], P('dp', 'tensor'), may hold values from -6 to 6
- cotangent: float32 [8, 1024, 768], P('dp', 'tensor'), may hold values from -6 to 6
- lengths: int32 [8], P('dp'), may hold values from 256 to 1024, as said below
- routes: int32 [8, 1024, 1], P('dp', 'tensor'), may hold values from 0 to 7; in each aligned block of 256 rows (0 to 255, 256 to 511, ..., all dimensions but the last counted through in order) at most 40 rows name the same one
- attention_weight: float32 [4, 768, 768], P(None, 'dp', 'tensor')
- attention_mean: float32 [4, 768, 768], P(None, 'dp', 'tensor')
- attention_square: float32 [4, 768, 768], P(None, 'dp', 'tensor')
- expert_weight: float32 [8, 2, 768, 3072], P('dp', None, None, 'tensor')
- expert_mean: float32 [8, 2, 768, 3072], P('dp', None, None, 'tensor')
- expert_square: float32 [8, 2, 768, 3072], P('dp', None, None, 'tensor')
- router_matrix: float32 [768, 8], P(('dp', 'tensor'))
- router_mean: float32 [768, 8], P(('dp', 'tensor'))
- router_square: float32 [768, 8], P(('dp', 'tensor'))
- norm_gains: float32 [2, 768], P(None, ('dp', 'tensor')), may hold values from 0.9 to 3.3
- gains_mean: float32 [2, 768], P(None, ('dp', 'tensor'))
- gains_square: float32 [2, 768], P(None, ('dp', 'tensor'))
Outputs:
- block_output: float32 [8, 1024, 768], P('dp', 'tensor')
- input_grad: float32 [8, 1024, 768], P('dp', 'tensor')
- grad_norm: float32 [], replicated
- attention_updated: float32 [4, 768, 768], P(None, 'dp', 'tensor')
- attention_mean_updated: float32 [4, 768, 768], P(None, 'dp', 'tensor')
- attention_square_updated: float32 [4, 768, 768], P(None, 'dp', 'tensor')
- expert_updated: float32 [8, 2, 768, 3072], P('dp', None, None, 'tensor')
- expert_mean_updated: float32 [8, 2, 768, 3072], P('dp', None, None, 'tensor')
- expert_square_updated: float32 [8, 2, 768, 3072], P('dp', None, None, 'tensor')
- router_updated: float32 [768, 8], P(('dp', 'tensor'))
- router_mean_updated: float32 [768, 8], P(('dp', 'tensor'))
- router_square_updated: float32 [768, 8], P(('dp', 'tensor'))
- gains_updated: float32 [2, 768], P(None, ('dp', 'tensor'))
- gains_mean_updated: float32 [2, 768], P(None, ('dp', 'tensor'))
- gains_square_updated: float32 [2, 768], P(None, ('dp', 'tensor'))
- expert_branch: float32 [8, 1024, 768], P('dp', 'tensor')
The draws below stay inside these ranges and needn't reach their ends.
Inputs may be any that keep to these rules, and one draw needn't show every extreme that they name: `lengths`: in every group of 8 consecutive sequences one has length exactly 1024. `routes`: within each aligned block of 256 positions of one sequence no expert is named more than 40 times, and in some block one is named exactly 40 times.
All inputs are finite; a program needn't handle non-finite values.
Results may differ from the reference program's by a relative error of at most 0.015.
Values may be sent and summed in bfloat16 or wider, within the bound.
No kernel may reach another device: no remote copies, remote signals or barrier semaphores. Data moves between devices by JAX's collectives and lax.ppermute only.
A program may use at most 128 MiB of HBM per device.

```python
import math
from functools import partial
import jax
import jax.numpy as jnp
import numpy as np
from jax import lax

D = 768
H = 12
DH = 64
FF = 3072
LEN = 1024
SEQ_DP = 1
STEP = 10
EXPERTS = 8
SEQS = 8
LQ = 256
CAPQ = 40
N_TENSOR = 4


def gradient_unit():
    return 1.0 / math.sqrt(14.0 * D * H * DH + 1.84 * D * FF / EXPERTS + 1600.0 * D)


def first_moment(key, shape, scale):
    return 0.111 * scale * jax.random.normal(key, shape, jnp.float32)


def second_moment(key, shape, scale):
    spread = jnp.exp(jax.random.uniform(key, shape, jnp.float32, math.log(0.5), math.log(8.0)))
    return 0.001 * scale * scale * spread


def attention_scale():
    return jnp.array([2.2, 2.2, 1.1, 1.1], jnp.float32).reshape(4, 1, 1) * gradient_unit()


def expert_scale():
    return jnp.array([1.15 / EXPERTS, 0.72 / EXPERTS], jnp.float32).reshape(1, 2, 1, 1) * gradient_unit()


def router_scale():
    return 40.0 / math.sqrt(EXPERTS) * gradient_unit()


def gains_scale():
    return jnp.array([1.4, 0.6], jnp.float32).reshape(2, 1) * gradient_unit()


def draw_lengths(key, part):
    key = jax.random.fold_in(key, 11)
    first_key, second_key = jax.random.split(key)
    drawn = jax.random.randint(first_key, (SEQS,), LEN // 4, LEN + 1)
    chosen = jax.random.randint(second_key, (SEQS // 8,), 0, 8)
    longest = jnp.arange(SEQS) % 8 == jnp.repeat(chosen, 8)
    return jnp.where(longest, LEN, drawn).astype(jnp.int32)


def draw_attention_weight(key, part):
    key = jax.random.fold_in(key, 21)
    scales = jnp.array([0.71 / math.sqrt(D), 0.71 / math.sqrt(D), 0.83 / math.sqrt(D), 0.79 / math.sqrt(H * DH)], jnp.float32).reshape(4, 1, 1)
    return jax.random.normal(key, (4, D, H * DH), jnp.float32) * scales


def draw_attention_mean(key, part):
    key = jax.random.fold_in(key, 22)
    return first_moment(key, (4, D, H * DH), attention_scale())


def draw_attention_square(key, part):
    key = jax.random.fold_in(key, 23)
    return second_moment(key, (4, D, H * DH), attention_scale())


def draw_expert_weight(key, part):
    key = jax.random.fold_in(key, 31)
    first_key, second_key = jax.random.split(key)
    columns = (0.5 + jnp.arange(FF, dtype=jnp.float32) / (FF - 1)) * (0.4 * math.sqrt(EXPERTS / D))
    inward = jax.random.normal(first_key, (EXPERTS, 1, D, FF), jnp.float32) * columns
    outward = jax.random.normal(second_key, (EXPERTS, 1, D, FF), jnp.float32) * (1.38 * math.sqrt(EXPERTS / FF))
    return jnp.concatenate([inward, outward], axis=1)


def draw_expert_mean(key, part):
    key = jax.random.fold_in(key, 32)
    return first_moment(key, (EXPERTS, 2, D, FF), expert_scale())


def draw_expert_square(key, part):
    key = jax.random.fold_in(key, 33)
    return second_moment(key, (EXPERTS, 2, D, FF), expert_scale())


def draw_router_matrix(key, part):
    key = jax.random.fold_in(key, 41)
    return jax.random.normal(key, (D, EXPERTS), jnp.float32) * (0.24 / math.sqrt(D))


def draw_router_mean(key, part):
    key = jax.random.fold_in(key, 42)
    return first_moment(key, (D, EXPERTS), router_scale())


def draw_router_square(key, part):
    key = jax.random.fold_in(key, 43)
    return second_moment(key, (D, EXPERTS), router_scale())


def draw_norm_gains(key, part):
    key = jax.random.fold_in(key, 51)
    rising = 1.0 + 2.0 * jnp.arange(D, dtype=jnp.float32) / (D - 1)
    jitter = jax.random.uniform(key, (2, D), jnp.float32, 0.9, 1.1)
    return rising[None, :] * jitter


def draw_gains_mean(key, part):
    key = jax.random.fold_in(key, 52)
    return first_moment(key, (2, D), gains_scale())


def draw_gains_square(key, part):
    key = jax.random.fold_in(key, 53)
    return second_moment(key, (2, D), gains_scale())


def block_levels(stream_key, extent, cuts, smallest, high):
    level, own = 1.0, jax.random.fold_in(stream_key, 6)
    for dim, parts in cuts:
        steps = jnp.exp(jax.random.uniform(jax.random.fold_in(own, dim), (parts,), jnp.float32, smallest / len(cuts), high / len(cuts)))
        level = level * jnp.repeat(steps, extent[dim] // parts).reshape([-1 if axis == dim else 1 for axis in range(len(extent))])
    return level


def shared_out(own_key, own, number, rows, count, top, limit, skew):
    order = jax.random.permutation(own_key, count)
    crowded, common = portions_of(count, rows * top, limit, skew, True), portions_of(count, rows * top, limit, skew, False)
    places = jnp.arange(count)

    def named(sizes, offset_by):
        used = int((sizes > 0).sum())
        fixed = max(1, used // 4)
        passed = fixed + (places - fixed + offset_by * (used - fixed)) % max(1, count - fixed)
        return jnp.zeros((count,), jnp.int32).at[order[jnp.where(places < fixed, places, passed)]].set(jnp.asarray(sizes, jnp.int32))

    sizes = jnp.where(number % 4 == 0, named(crowded, number // 4), named(common, number - number // 4 - 1))
    mixed = jax.random.permutation(jax.random.fold_in(own, 3), count)
    source_of, taker = mixed[0:count // 2 * 2:2], mixed[1:count // 2 * 2:2]
    margin = jnp.minimum(sizes[source_of] - 1, limit - sizes[taker]) // 2
    margin = jnp.where((source_of == order[0]) | (taker == order[0]) | (sizes[taker] == 0), 0, jnp.maximum(margin, 0))
    passed = jax.random.randint(jax.random.fold_in(own, 4), (count // 2,), 0, 1 << 20) % (margin + 1)
    sizes = sizes.at[source_of].add(-passed).at[taker].add(passed)
    labels = jnp.searchsorted(jnp.cumsum(sizes), jnp.arange(rows * top), side="right").astype(jnp.int32)
    listing = labels.reshape(top, rows).T
    listing = listing[jax.random.permutation(jax.random.fold_in(own, 1), rows)]
    offset_by = jax.random.randint(jax.random.fold_in(own, 2), (rows, 1), 0, top)
    return jnp.take_along_axis(listing, (jnp.arange(top)[None, :] + offset_by) % top, axis=1)


def portions_of(count, total, most, skew, full):
    portions = [(1 << 20) // math.isqrt(grade ** skew) + 1 for grade in range(1, count + 1)]
    largest = most if full else min(most, max(-(-total // count), total * portions[0] // sum(portions)))
    least = 1 if total - largest >= count - 1 else 0
    given, spare = [largest] + [least] * (count - 1), total - largest - least * (count - 1)
    while spare > 0:
        candidates = [i for i in range(1, count) if given[i] < largest] or [i for i in range(1, count) if given[i] < most]
        mass, left = sum([portions[i] for i in candidates]), spare
        for i in candidates:
            extra = min(most - given[i], max(1, left * portions[i] // mass), spare)
            given[i] = given[i] + extra
            spare = spare - extra
    return np.array(given)


def gaussian(stream_key, dims, scale, limit, cuts=(), held_as=jnp.bfloat16):
    values = scale * jax.random.normal(stream_key, dims, jnp.float32)
    if cuts:
        values = values * block_levels(stream_key, dims, cuts, -0.22, 0.18)
    return jnp.clip(values, -limit, limit).astype(held_as)


def setup_inputs(seed: int = 0) -> dict:
    key_list = jax.random.split(jax.random.key(seed), 17)
    inputs = gaussian(key_list[0], (SEQS, LEN, D), 1.0, 6.0, ((0, 8), (1, 4)), jnp.float32)
    cotangent = gaussian(key_list[1], (SEQS, LEN, D), 1.0, 6.0, ((0, 8), (1, 4)), jnp.float32)
    lengths = draw_lengths(jax.random.fold_in(key_list[16], 71), 0)
    routes_keys = jax.random.split(jax.random.fold_in(key_list[3], 1), SEQS * LEN // LQ)
    routes_turns = jax.random.permutation(jax.random.fold_in(key_list[3], 3), SEQS * LEN // LQ)
    routes = jax.vmap(lambda own, number: shared_out(jax.random.fold_in(key_list[3], 2), own, number, LQ, EXPERTS, 1, CAPQ, 2))(routes_keys, routes_turns).reshape((SEQS, LEN, 1))
    attention_weight = draw_attention_weight(jax.random.fold_in(key_list[16], 71), 0)
    attention_mean = draw_attention_mean(jax.random.fold_in(key_list[16], 71), 0)
    attention_square = draw_attention_square(jax.random.fold_in(key_list[16], 71), 0)
    expert_weight = draw_expert_weight(jax.random.fold_in(key_list[16], 71), 0)
    expert_mean = draw_expert_mean(jax.random.fold_in(key_list[16], 71), 0)
    expert_square = draw_expert_square(jax.random.fold_in(key_list[16], 71), 0)
    router_matrix = draw_router_matrix(jax.random.fold_in(key_list[16], 71), 0)
    router_mean = draw_router_mean(jax.random.fold_in(key_list[16], 71), 0)
    router_square = draw_router_square(jax.random.fold_in(key_list[16], 71), 0)
    norm_gains = draw_norm_gains(jax.random.fold_in(key_list[16], 71), 0)
    gains_mean = draw_gains_mean(jax.random.fold_in(key_list[16], 71), 0)
    gains_square = draw_gains_square(jax.random.fold_in(key_list[16], 71), 0)
    return dict(inputs=inputs, cotangent=cotangent, lengths=lengths, routes=routes, attention_weight=attention_weight, attention_mean=attention_mean, attention_square=attention_square, expert_weight=expert_weight, expert_mean=expert_mean, expert_square=expert_square, router_matrix=router_matrix, router_mean=router_mean, router_square=router_square, norm_gains=norm_gains, gains_mean=gains_mean, gains_square=gains_square)


highest_precision = lax.Precision.HIGHEST
norm_epsilon = 1e-06
beta_first = 0.9
beta_second = 0.999
adam_epsilon = 1e-08
decay_factor = 0.01
clip_limit = 1.0
masked_score = -1e+30

@jax.custom_vjp
def low(v):
    return lax.optimization_barrier(v.astype(jnp.bfloat16)).astype(jnp.float32)

@jax.custom_vjp
def low_back(v):
    return v

def low_keep(v):
    return (low(v), None)

def low_pass(kept, grad):
    return (grad,)

def back_keep(v):
    return (v, None)

def back_low(kept, grad):
    return (low(grad),)
low.defvjp(low_keep, low_pass)
low_back.defvjp(back_keep, back_low)

def rms_scale(values, gain_row):
    mean_square = lax.optimization_barrier(jnp.mean(values * values, axis=-1, keepdims=True))
    return values * lax.rsqrt(mean_square + norm_epsilon) * gain_row

def attend_group(packed):
    query_rows, key_matrix, value_matrix, group_lengths = packed
    scores = jnp.einsum('sqhe,skhe->shqk', query_rows, key_matrix, precision=highest_precision) * (1.0 / math.sqrt(DH))
    visible = jnp.arange(LEN)[None, :] < group_lengths[:, None]
    scores = jnp.where(visible[:, None, None, :], scores, masked_score)
    scores = low_back(scores)
    probabilities = jax.nn.softmax(scores, axis=-1)
    return jnp.einsum('shqk,skhe->sqhe', low(probabilities), value_matrix, precision=highest_precision)

def expert_apply(packed):
    slot_rows, weight_pair = packed
    inner_rows = low_back(jnp.dot(slot_rows, weight_pair[0], precision=highest_precision))
    active = low(jax.nn.gelu(inner_rows))
    return jnp.einsum('rf,df->rd', active, weight_pair[1], precision=highest_precision)

def token_slots(routes, lengths):
    seq_count = routes.shape[0]
    quarter = LEN // N_TENSOR
    valid = jnp.arange(LEN)[None, :] < lengths[:, None]
    chosen_expert = routes[..., 0]
    match = chosen_expert[..., None] == jnp.arange(EXPERTS)[None, None, :]
    onehot = (match & valid[..., None]).astype(jnp.int32).reshape(seq_count, N_TENSOR, quarter, EXPERTS)
    rank_all = jnp.cumsum(onehot, axis=2) - 1
    rank_own = lax.optimization_barrier(jnp.sum(rank_all * match.astype(jnp.int32).reshape(onehot.shape), axis=3))
    block_index = (jnp.arange(seq_count)[:, None] * N_TENSOR + jnp.arange(N_TENSOR)[None, :])[..., None]
    total_slots = seq_count * N_TENSOR * CAPQ
    slot_flat = chosen_expert.reshape(seq_count, N_TENSOR, quarter) * total_slots + block_index * CAPQ + rank_own
    slot_flat = jnp.where(valid.reshape(seq_count, N_TENSOR, quarter), slot_flat, EXPERTS * total_slots)
    return slot_flat.reshape(seq_count, LEN).astype(jnp.int32)

def forward(inputs, attention_weight, expert_weight, router_matrix, norm_gains, lengths, routes):
    seq_count = inputs.shape[0]
    width = inputs.shape[2]
    hidden_one = rms_scale(inputs, norm_gains[0])
    attention_input = low(hidden_one)
    attention_reduced = low(attention_weight)
    query_rows = low_back(low(jnp.einsum('ikn,ny->iky', attention_input, attention_reduced[0], precision=highest_precision)))
    key_matrix = low_back(low(jnp.einsum('ikn,ny->iky', attention_input, attention_reduced[1], precision=highest_precision)))
    value_matrix = low_back(low(jnp.einsum('ikn,ny->iky', attention_input, attention_reduced[2], precision=highest_precision)))
    group_shape = (seq_count // SEQ_DP, SEQ_DP, LEN, H, DH)
    context_rows = lax.map(jax.checkpoint(attend_group), (query_rows.reshape(group_shape), key_matrix.reshape(group_shape), value_matrix.reshape(group_shape), lengths.reshape(seq_count // SEQ_DP, SEQ_DP)))
    context_rows = low_back(low(context_rows.reshape(seq_count, LEN, H * DH)))
    attention_output = low_back(jnp.einsum('coz,uz->cou', context_rows, attention_reduced[3], precision=highest_precision))
    middle = inputs + attention_output
    hidden_second = rms_scale(middle, norm_gains[1])
    router_scores = jnp.einsum('ftb,bx->ftx', hidden_second, router_matrix, precision=highest_precision)
    gate_value = jnp.take_along_axis(jax.nn.softmax(router_scores, axis=-1), routes, axis=-1)
    valid_scale = (jnp.arange(LEN)[None, :] < lengths[:, None]).astype(jnp.float32)[..., None]
    expert_in = low_back(low(hidden_second))
    slot_flat = token_slots(routes, lengths).reshape(-1)
    total_slots = seq_count * N_TENSOR * CAPQ
    buffer_rows = jnp.zeros((EXPERTS * total_slots, width), jnp.float32).at[slot_flat].set(expert_in.reshape(-1, width), mode='drop')
    expert_out = lax.map(jax.checkpoint(expert_apply), (buffer_rows.reshape(EXPERTS, total_slots, width), low(expert_weight)))
    expert_out = low_back(low(expert_out)).reshape(EXPERTS * total_slots, width)
    picked = jnp.take(expert_out, slot_flat, axis=0, mode='fill', fill_value=0.0).reshape(inputs.shape)
    expert_branch = gate_value * valid_scale * picked
    return (middle + expert_branch, expert_branch)

def learning_rates():
    attention_rate = jnp.array([0.71 / math.sqrt(D), 0.71 / math.sqrt(D), 0.83 / math.sqrt(D), 0.79 / math.sqrt(H * DH)], jnp.float32).reshape(4, 1, 1)
    expert_rate = jnp.array([0.4 * math.sqrt(EXPERTS / D), 1.38 * math.sqrt(EXPERTS / FF)], jnp.float32).reshape(1, 2, 1, 1)
    router_rate = 0.24 / math.sqrt(D)
    gains_rate = 0.5
    return (attention_rate, expert_rate, router_rate, gains_rate)

def adam_update(weight, moment_one, moment_two, gradient, step_rate):
    moment_one_next = beta_first * moment_one + (1.0 - beta_first) * gradient
    moment_two_next = beta_second * moment_two + (1.0 - beta_second) * gradient * gradient
    corrected_one = moment_one_next / (1.0 - beta_first ** STEP)
    corrected_two = moment_two_next / (1.0 - beta_second ** STEP)
    weight_next = weight - step_rate * (corrected_one / (jnp.sqrt(corrected_two) + adam_epsilon) + decay_factor * weight)
    return (weight_next, moment_one_next, moment_two_next)

def reference(inputs, cotangent, lengths, routes, attention_weight, attention_mean, attention_square, expert_weight, expert_mean, expert_square, router_matrix, router_mean, router_square, norm_gains, gains_mean, gains_square):
    block_output, pullback, expert_branch = jax.vjp(partial(forward, lengths=lengths, routes=routes), inputs, attention_weight, expert_weight, router_matrix, norm_gains, has_aux=True)
    input_grad, attention_grad, expert_grad, router_grad, gains_grad = pullback(cotangent)
    square_total = jnp.sum(attention_grad * attention_grad) + jnp.sum(expert_grad * expert_grad) + jnp.sum(router_grad * router_grad) + jnp.sum(gains_grad * gains_grad)
    grad_norm = jnp.sqrt(square_total)
    factor = jnp.minimum(1.0, clip_limit / (grad_norm + norm_epsilon))
    attention_rate, expert_rate, router_rate, gains_rate = learning_rates()
    attention_new = adam_update(attention_weight, attention_mean, attention_square, attention_grad * factor, attention_rate)
    expert_new = adam_update(expert_weight, expert_mean, expert_square, expert_grad * factor, expert_rate)
    router_new = adam_update(router_matrix, router_mean, router_square, router_grad * factor, router_rate)
    gains_new = adam_update(norm_gains, gains_mean, gains_square, gains_grad * factor, gains_rate)
    return (block_output, input_grad, grad_norm, attention_new[0], attention_new[1], attention_new[2], expert_new[0], expert_new[1], expert_new[2], router_new[0], router_new[1], router_new[2], gains_new[0], gains_new[1], gains_new[2], expert_branch)
```

```python
from functools import partial
import math

import jax
import jax.numpy as jnp
from jax import lax
from jax.sharding import PartitionSpec as P

D = 768
H = 12
DH = 64
FF = 3072
STEP = 10

HIGHEST = lax.Precision.HIGHEST
norm_epsilon = 1e-06
beta_first = 0.9
beta_second = 0.999
adam_epsilon = 1e-08
decay_factor = 0.01
clip_limit = 1.0
masked_score = -1e30
bf16 = jnp.bfloat16
f32 = jnp.float32


def swap(values, axis, mask):
    count = lax.axis_size(axis)
    return lax.ppermute(values, axis, [(i, i ^ mask) for i in range(count)])


def bits_of(count):
    return [1 << b for b in range(count.bit_length() - 1)]


def gather_relative(block, axis, order):
    held = {0: block}
    for mask in order:
        for j in list(held):
            held[j ^ mask] = swap(held[j], axis, mask)
    return [held[j] for j in range(len(held))]


def fold_relative(blocks, axis, order):
    held = dict(enumerate(blocks))
    for mask in order:
        for j in [j for j in held if j & mask]:
            came = swap(held.pop(j), axis, mask)
            held[j ^ mask] = (held[j ^ mask].astype(f32) + came.astype(f32)).astype(bf16)
    return held[0]


def exchange_relative(blocks, axis):
    return [blocks[0]] + [swap(blocks[j], axis, j) for j in range(1, len(blocks))]


def xor_order(stack, index):
    count = stack.shape[0]
    return jnp.stack(
        [lax.dynamic_index_in_dim(stack, index ^ j, 0, keepdims=False) for j in range(count)]
    )


def mm(a, b):
    return jnp.dot(a, b, preferred_element_type=f32)


def mm_nt(a, b):
    return lax.dot_general(a, b, (((1,), (1,)), ((), ())), preferred_element_type=f32)


def mm_tn(a, b):
    return lax.dot_general(a, b, (((0,), (0,)), ((), ())), preferred_element_type=f32)


def norm_root(values):
    return lax.rsqrt(jnp.mean(values * values, axis=-1, keepdims=True) + norm_epsilon)


def norm_backward(values, root, gain_row, grad):
    scaled = values * root
    gain_grad = jnp.sum(grad * scaled, axis=0)
    inner = grad * gain_row
    centre = jnp.mean(inner * scaled, axis=-1, keepdims=True)
    return root * (inner - scaled * centre), gain_grad


def attention_forward(query_rows, key_matrix, value_matrix, visible):
    full_len, inner_width = query_rows.shape
    head_count = inner_width // DH
    score_scale = 1.0 / math.sqrt(DH)
    split = lambda rows: rows.reshape(full_len, head_count, DH)
    queries, keys, values = split(query_rows), split(key_matrix), split(value_matrix)
    scores = jnp.einsum("qhe,khe->hqk", queries, keys, preferred_element_type=f32) * score_scale
    scores = jnp.where(visible[None, None, :], scores, masked_score)
    row_max = jnp.max(scores, axis=-1, keepdims=True)
    exponent_rows = jnp.exp(scores - row_max)
    row_total = jnp.sum(exponent_rows, axis=-1, keepdims=True)
    probabilities = (exponent_rows / row_total).astype(bf16)
    context = jnp.einsum("hqk,khe->qhe", probabilities, values, preferred_element_type=f32)
    return (
        context.astype(bf16).reshape(full_len, inner_width),
        (row_max + jnp.log(row_total))[..., 0],
    )


def attention_backward(query_rows, key_matrix, value_matrix, visible, log_total, context_grad):
    full_len, inner_width = query_rows.shape
    head_count = inner_width // DH
    score_scale = 1.0 / math.sqrt(DH)
    split = lambda rows: rows.reshape(full_len, head_count, DH)
    queries, keys, values = split(query_rows), split(key_matrix), split(value_matrix)
    grads = split(context_grad)
    scores = jnp.einsum("qhe,khe->hqk", queries, keys, preferred_element_type=f32) * score_scale
    scores = jnp.where(visible[None, None, :], scores, masked_score)
    probabilities = jnp.exp(scores - log_total[..., None])
    prob_low = probabilities.astype(bf16)
    value_grad = jnp.einsum("hqk,qhe->khe", prob_low, grads, preferred_element_type=f32)
    prob_grad = jnp.einsum("qhe,khe->hqk", grads, values, preferred_element_type=f32)
    centre = jnp.sum(prob_grad * probabilities, axis=-1, keepdims=True)
    score_grad = (probabilities * (prob_grad - centre)).astype(bf16)
    query_grad = jnp.einsum("hqk,khe->qhe", score_grad, keys, preferred_element_type=f32)
    key_grad = jnp.einsum("hqk,qhe->khe", score_grad, queries, preferred_element_type=f32)
    join = lambda grad, scale: (grad * scale).astype(bf16).reshape(full_len, inner_width)
    return join(query_grad, score_scale), join(key_grad, score_scale), join(value_grad, 1.0)


def gelu_pair(values):
    c = math.sqrt(2.0 / math.pi)
    square = values * values
    th = jnp.tanh(c * values * (1.0 + 0.044715 * square))
    half = 0.5 * (1.0 + th)
    slope = half + 0.5 * values * (1.0 - th * th) * c * (1.0 + 3.0 * 0.044715 * square)
    return values * half, slope


def adam_update(weight, moment_one, moment_two, gradient, step_rate):
    moment_one_next = beta_first * moment_one + (1.0 - beta_first) * gradient
    moment_two_next = beta_second * moment_two + (1.0 - beta_second) * gradient * gradient
    corrected_one = moment_one_next / (1.0 - beta_first**STEP)
    corrected_two = moment_two_next / (1.0 - beta_second**STEP)
    weight_next = weight - step_rate * (
        corrected_one / (jnp.sqrt(corrected_two) + adam_epsilon) + decay_factor * weight
    )
    return (weight_next, moment_one_next, moment_two_next)


def on_device(
    inputs,
    cotangent,
    lengths,
    routes,
    attention_weight,
    attention_mean,
    attention_square,
    expert_weight,
    expert_mean,
    expert_square,
    router_matrix,
    router_mean,
    router_square,
    norm_gains,
    gains_mean,
    gains_square,
):
    quarter, width = inputs.shape[1:]
    dp_count, tensor_count = lax.axis_size("dp"), lax.axis_size("tensor")
    device_count = dp_count * tensor_count
    expert_count = router_matrix.shape[1]
    capacity = max(2, (5 * quarter + 4 * expert_count - 1) // (4 * expert_count))
    own_dp, own_tensor = lax.axis_index("dp"), lax.axis_index("tensor")
    dp_near, dp_far = bits_of(dp_count), bits_of(dp_count)[::-1]
    near, far = bits_of(tensor_count), bits_of(tensor_count)[::-1]
    near_mask, far_mask = near[0], far[0]
    share = router_matrix.shape[0]
    few = dp_count <= 8

    rows = inputs[0]
    root_one = norm_root(rows)
    scaled_one = rows * root_one
    row_blocks = gather_relative(scaled_one.astype(bf16), "tensor", far)
    scaled_rows = jnp.concatenate(row_blocks, axis=0)
    weight_own = attention_weight.astype(bf16)
    weight_blocks = gather_relative(weight_own, "dp", dp_far)
    small = jnp.concatenate([norm_gains, router_matrix.T], axis=0)
    small_all = lax.all_to_all(
        jnp.broadcast_to(small[None], (device_count,) + small.shape), ("dp", "tensor"), 0, 0, tiled=True
    )
    small_full = small_all.transpose(1, 0, 2).reshape(small.shape[0], width)
    gains_full, router_rows = small_full[:2], small_full[2:]
    weights = xor_order(jnp.stack(weight_blocks), own_dp).transpose(1, 0, 2, 3)
    weights = weights.reshape(4, width, -1)

    length = lengths[0]
    blocks_at = own_tensor ^ jnp.arange(tensor_count)
    positions = (blocks_at[:, None] * quarter + jnp.arange(quarter)[None, :]).reshape(-1)
    visible = positions < length
    local_valid = own_tensor * quarter + jnp.arange(quarter) < length
    valid_scale = local_valid.astype(f32)[:, None]
    chosen = routes[0, :, 0]
    match = chosen[:, None] == jnp.arange(expert_count)[None, :]
    onehot = (match & local_valid[:, None]).astype(f32)
    lower = (jnp.arange(quarter)[:, None] >= jnp.arange(quarter)[None, :]).astype(f32)
    rank = jnp.sum((mm(lower, onehot) - 1.0) * match.astype(f32), axis=1).astype(jnp.int32)
    slot_expert = chosen ^ own_dp if few else chosen
    slot = jnp.where(local_valid, slot_expert * capacity + rank, -1)
    slot_count = expert_count * capacity
    place = (jnp.arange(slot_count)[:, None] == slot[None, :]).astype(bf16)

    def trade(values):
        blocks = values.reshape(expert_count, capacity, width)
        if few:
            return jnp.concatenate(exchange_relative([blocks[j] for j in range(expert_count)], "dp"), axis=0)
        return lax.all_to_all(blocks, "dp", 0, 0, tiled=True).reshape(slot_count, width)

    def send_out(values):
        own = trade(mm(place, values).astype(bf16))
        return jnp.concatenate([own, swap(own, "tensor", far_mask)], axis=0)

    def bring_back(parts):
        other = swap(parts[slot_count:].astype(bf16), "tensor", far_mask)
        total = (parts[:slot_count] + other.astype(f32)).astype(bf16)
        return mm_tn(place, trade(total))

    expert_own = expert_weight[0].astype(bf16)
    expert_pair = swap(expert_own, "tensor", near_mask)
    expert_in = jnp.concatenate([expert_own[0], expert_pair[0]], axis=1)
    expert_out = jnp.concatenate([expert_own[1], expert_pair[1]], axis=1)

    attention_input = (scaled_rows.astype(f32) * gains_full[0]).astype(bf16)
    query_rows = mm(attention_input, weights[0]).astype(bf16)
    key_matrix = mm(attention_input, weights[1]).astype(bf16)
    value_matrix = mm(attention_input, weights[2]).astype(bf16)
    context, log_total = attention_forward(query_rows, key_matrix, value_matrix, visible)
    out_weight = jnp.concatenate(gather_relative(weights[3], "tensor", far), axis=1)

    def row_blocks_of(values):
        return [values[j * quarter : (j + 1) * quarter] for j in range(tensor_count)]

    context_own = jnp.concatenate(exchange_relative(row_blocks_of(context), "tensor"), axis=1)
    middle = rows + mm_nt(context_own, out_weight)

    root_two = norm_root(middle)
    hidden_second = middle * root_two * gains_full[1]
    scores = lax.dot_general(
        hidden_second, router_rows, (((1,), (1,)), ((), ())), precision=HIGHEST
    )
    chances = jax.nn.softmax(scores, axis=-1)
    picked_one = match.astype(f32)
    gate = jnp.sum(chances * picked_one, axis=-1, keepdims=True)
    gate_valid = gate * valid_scale
    grad_rows = cotangent[0]

    expert_rows = send_out(hidden_second.astype(bf16))
    expert_grads = send_out((gate_valid * grad_rows).astype(bf16))
    active, slope = gelu_pair(mm(expert_rows, expert_in))
    active = active.astype(bf16)
    picked = bring_back(mm_nt(active, expert_out))
    inner_grad = (mm(expert_grads, expert_out) * slope).astype(bf16)
    hidden_grad = bring_back(mm_nt(inner_grad, expert_in))
    half = expert_own.shape[2]
    expert_sums = jnp.stack([mm_tn(expert_rows, inner_grad), mm_tn(expert_grads, active)])
    expert_came = swap(expert_sums[..., half:].astype(bf16), "tensor", near_mask)
    expert_grad = expert_sums[..., :half] + expert_came.astype(f32)

    branch = gate_valid * picked
    block_output = middle + branch

    gate_grad = valid_scale * jnp.sum(grad_rows * picked, axis=-1, keepdims=True)
    score_grad = gate * (picked_one - chances) * gate_grad
    router_grad = lax.dot_general(
        score_grad, hidden_second, (((0,), (0,)), ((), ())), precision=HIGHEST
    )
    second_grad = hidden_grad + jnp.dot(score_grad, router_rows, precision=HIGHEST)
    middle_part, gain_two_grad = norm_backward(middle, root_two, gains_full[1], second_grad)
    middle_grad = grad_rows + middle_part

    middle_low = middle_grad.astype(bf16)
    context_parts = mm(middle_low, out_weight).astype(bf16)
    heads_width = out_weight.shape[1] // tensor_count
    context_grad = jnp.concatenate(
        exchange_relative(
            [context_parts[:, j * heads_width : (j + 1) * heads_width] for j in range(tensor_count)],
            "tensor",
        ),
        axis=0,
    )
    middle_all = jnp.concatenate(gather_relative(middle_low, "tensor", far), axis=0)
    query_grad, key_grad, value_grad = attention_backward(
        query_rows, key_matrix, value_matrix, visible, log_total, context_grad
    )
    input_parts = (
        mm_nt(query_grad, weights[0]) + mm_nt(key_grad, weights[1]) + mm_nt(value_grad, weights[2])
    ).astype(bf16)
    first_grad = fold_relative(row_blocks_of(input_parts), "tensor", near).astype(f32)
    input_part, gain_one_grad = norm_backward(rows, root_one, gains_full[0], first_grad)
    input_grad = middle_grad + input_part

    def owners_sum(gradient):
        stack = xor_order(gradient.astype(bf16).reshape(dp_count, -1, gradient.shape[1]), own_dp)
        return fold_relative([stack[j] for j in range(dp_count)], "dp", dp_near)

    attention_grad = jnp.stack(
        [
            owners_sum(mm_tn(attention_input, query_grad)),
            owners_sum(mm_tn(attention_input, key_grad)),
            owners_sum(mm_tn(attention_input, value_grad)),
            owners_sum(mm_tn(middle_all, context)),
        ]
    ).astype(f32)

    small_grad = jnp.concatenate([gain_one_grad[None], gain_two_grad[None], router_grad], axis=0)
    small_cut = small_grad.reshape(-1, device_count, share).transpose(1, 0, 2)
    small_own = jnp.sum(lax.all_to_all(small_cut, ("dp", "tensor"), 0, 0, tiled=True), axis=0)
    gains_grad, router_own = small_own[:2], small_own[2:].T

    square_sum = (
        jnp.sum(attention_grad * attention_grad)
        + jnp.sum(expert_grad * expert_grad)
        + jnp.sum(small_own * small_own)
    )
    square_sum = jnp.full((8, 128), square_sum)
    for mask in near:
        square_sum = square_sum + swap(square_sum, "tensor", mask)
    for mask in dp_near:
        square_sum = square_sum + swap(square_sum, "dp", mask)
    grad_norm = jnp.sqrt(square_sum[0, 0])
    factor = jnp.minimum(1.0, clip_limit / (grad_norm + norm_epsilon))
    attention_rate = jnp.array(
        [0.71 / math.sqrt(D), 0.71 / math.sqrt(D), 0.83 / math.sqrt(D), 0.79 / math.sqrt(H * DH)],
        f32,
    ).reshape(4, 1, 1)
    expert_rate = jnp.array(
        [0.4 * math.sqrt(expert_count / D), 1.38 * math.sqrt(expert_count / FF)], f32
    ).reshape(1, 2, 1, 1)
    attention_new = adam_update(
        attention_weight, attention_mean, attention_square, attention_grad * factor, attention_rate
    )
    expert_new = adam_update(
        expert_weight, expert_mean, expert_square, expert_grad[None] * factor, expert_rate
    )
    router_new = adam_update(
        router_matrix, router_mean, router_square, router_own * factor, 0.24 / math.sqrt(D)
    )
    gains_new = adam_update(norm_gains, gains_mean, gains_square, gains_grad * factor, 0.5)
    return (
        block_output[None],
        input_grad[None],
        grad_norm,
        *attention_new,
        *expert_new,
        *router_new,
        *gains_new,
        branch[None],
    )


def solution(mesh):
    rows = P("dp", "tensor", None)
    attention = P(None, "dp", "tensor")
    expert = P("dp", None, None, "tensor")
    router = P(("dp", "tensor"), None)
    gains = P(None, ("dp", "tensor"))
    weights = (attention,) * 3 + (expert,) * 3 + (router,) * 3 + (gains,) * 3
    return jax.shard_map(
        on_device,
        mesh=mesh,
        in_specs=(rows, rows, P("dp"), rows) + weights,
        out_specs=(rows, rows, P()) + weights + (rows,),
        check_vma=False,
    )
```

```python
import math

import jax
import jax.numpy as jnp
from jax import lax
from jax.experimental import pallas as pl
from jax.experimental.pallas import tpu as pltpu
from jax.sharding import PartitionSpec as P

D = 768
H = 12
DH = 64
FF = 3072
STEP = 10

HIGHEST = lax.Precision.HIGHEST
norm_epsilon = 1e-06
beta_first = 0.9
beta_second = 0.999
adam_epsilon = 1e-08
decay_factor = 0.01
clip_limit = 1.0
masked_score = -1e30
score_scale = 1.0 / math.sqrt(DH)
bf16 = jnp.bfloat16
f32 = jnp.float32
MIB = 1 << 20
LANES = 128


def swap(values, axis, mask):
    count = lax.axis_size(axis)
    return lax.ppermute(values, axis, [(i, i ^ mask) for i in range(count)])


def bits_of(count):
    return [1 << b for b in range(count.bit_length() - 1)]


def gather_relative(block, axis, order):
    held = {0: block}
    for mask in order:
        for j in list(held):
            held[j ^ mask] = swap(held[j], axis, mask)
    return [held[j] for j in range(len(held))]


def xor_order(stack, index):
    count = stack.shape[0]
    return jnp.stack(
        [lax.dynamic_index_in_dim(stack, index ^ j, 0, keepdims=False) for j in range(count)]
    )


def mm(a, b):
    return jnp.dot(a, b, preferred_element_type=f32)


def mm_nt(a, b, precision=None):
    return lax.dot_general(
        a, b, (((1,), (1,)), ((), ())), preferred_element_type=f32, precision=precision
    )


def mm_tn(a, b, precision=None):
    return lax.dot_general(
        a, b, (((0,), (0,)), ((), ())), preferred_element_type=f32, precision=precision
    )


def norm_root(values):
    return lax.rsqrt(jnp.mean(values * values, axis=-1, keepdims=True) + norm_epsilon)


def norm_backward(values, root, gain_row, grad):
    scaled = values * root
    inner = grad * gain_row
    centre = jnp.mean(inner * scaled, axis=-1, keepdims=True)
    return root * (inner - scaled * centre)


def gelu_pair(values):
    c = math.sqrt(2.0 / math.pi)
    square = values * values
    th = jnp.tanh(c * values * (1.0 + 0.044715 * square))
    half = 0.5 * (1.0 + th)
    slope = half + 0.5 * values * (1.0 - th * th) * c * (1.0 + 3.0 * 0.044715 * square)
    return values * half, slope


def adam_update(weight, moment_one, moment_two, gradient, step_rate):
    moment_one_next = beta_first * moment_one + (1.0 - beta_first) * gradient
    moment_two_next = beta_second * moment_two + (1.0 - beta_second) * gradient * gradient
    corrected_one = moment_one_next / (1.0 - beta_first**STEP)
    corrected_two = moment_two_next / (1.0 - beta_second**STEP)
    weight_next = weight - step_rate * (
        corrected_one / (jnp.sqrt(corrected_two) + adam_epsilon) + decay_factor * weight
    )
    return (weight_next, moment_one_next, moment_two_next)


def shape_of(shape, dtype):
    return jax.ShapeDtypeStruct(shape, dtype)


def whole(shape):
    return pl.BlockSpec(shape, lambda *_: (0,) * len(shape))


def scalars():
    return pl.BlockSpec(memory_space=pltpu.SMEM)


def params(limit):
    return pltpu.CompilerParams(vmem_limit_bytes=limit * MIB)


def pack_columns(q, k, v, o):
    wide = LANES
    return jnp.concatenate(
        [q[:, :wide], k[:, :wide], v[:, :wide], o[:, :wide], q[:, wide:], k[:, wide:], v[:, wide:], o[:, wide:]],
        axis=1,
    )


def unpack_columns(packed):
    wide, rest = LANES, DH
    end = 4 * wide
    return jnp.stack(
        [
            jnp.concatenate(
                [packed[:, i * wide : (i + 1) * wide], packed[:, end + i * rest : end + (i + 1) * rest]], axis=1
            )
            for i in range(4)
        ]
    )


def attention_kernel(quarter, blocks, info, x0, x1, x2, x3, gain, weight, context, chances, qkv, a, kaug, vt):
    step = pl.program_id(0)
    full_len = quarter * blocks

    @pl.when(step == 0)
    def _():
        for j, ref in enumerate((x0, x1, x2, x3)):
            start = pl.multiple_of((info[0] ^ j) * quarter, quarter)
            a[pl.ds(start, quarter), :] = (ref[...].astype(f32) * gain[...]).astype(bf16)
        for j in range(blocks):
            rows = slice(j * quarter, (j + 1) * quarter)
            first = mm(a[rows, :], weight[:, : 3 * LANES]).astype(bf16)
            second = mm(a[rows, :], weight[:, 4 * LANES :]).astype(bf16)
            qkv[rows, : 3 * LANES] = first
            qkv[rows, 3 * LANES :] = second
            kaug[rows, :LANES] = first[:, LANES : 2 * LANES]
            lane = lax.broadcasted_iota(jnp.int32, (quarter, LANES), 1)
            row = lax.broadcasted_iota(jnp.int32, (quarter, LANES), 0) + j * quarter
            hidden = jnp.where((lane == 0) & (row >= info[1]), masked_score, 0.0)
            kaug[rows, LANES:] = jnp.where(lane < DH, hidden, second[:, :LANES].astype(f32)).astype(bf16)
            vt[:LANES, rows] = first[:, 2 * LANES :].T
            vt[LANES:, rows] = second[:, LANES:].T[:DH]

    rows = pl.ds(pl.multiple_of(step * quarter, quarter), quarter)
    q01 = (qkv[rows, :LANES].astype(f32) * score_scale).T.astype(bf16)
    q2 = (qkv[rows, 3 * LANES : 4 * LANES].astype(f32) * score_scale).T.astype(bf16)[:DH]
    ones = (lax.broadcasted_iota(jnp.int32, (DH, quarter), 0) == 0).astype(f32).astype(bf16)
    zeros = jnp.zeros((DH, quarter), bf16)
    queries = (
        jnp.concatenate([q01[:DH], zeros, ones, zeros], axis=0),
        jnp.concatenate([zeros, q01[DH:], ones, zeros], axis=0),
        jnp.concatenate([zeros, zeros, ones, q2], axis=0),
    )
    for h in range(3):
        scores = mm(kaug[...], queries[h])
        top = jnp.max(scores, axis=0, keepdims=True)
        powers = jnp.exp(scores - top)
        total = jnp.sum(powers, axis=0, keepdims=True)
        low = (powers * (1.0 / total)).astype(bf16)
        chances[h] = low
        context[0, h * DH : (h + 1) * DH, :] = mm(vt[h * DH : (h + 1) * DH, :], low).astype(bf16)


def attention_forward(info, rows, gain, weight):
    quarter, width = rows[0].shape
    blocks = len(rows)
    full_len = quarter * blocks
    inner = 3 * DH
    return pl.pallas_call(
        lambda *refs: attention_kernel(quarter, blocks, *refs),
        grid=(blocks,),
        in_specs=[scalars()] + [whole((quarter, width))] * 4 + [whole((1, width)), whole(weight.shape)],
        out_specs=[
            pl.BlockSpec((1, inner, quarter), lambda i: (i, 0, 0)),
            pl.BlockSpec((3, full_len, quarter), lambda i: (0, 0, i)),
            whole((full_len, 5 * LANES)),
        ],
        out_shape=[
            shape_of((blocks, inner, quarter), bf16),
            shape_of((3, full_len, full_len), bf16),
            shape_of((full_len, 5 * LANES), bf16),
        ],
        scratch_shapes=[
            pltpu.VMEM((full_len, width), bf16),
            pltpu.VMEM((full_len, 2 * LANES), bf16),
            pltpu.VMEM((inner, full_len), bf16),
        ],
        compiler_params=params(40),
        cost_estimate=pl.CostEstimate(
            flops=2 * full_len * (width * 5 * LANES + 2 * full_len * inner),
            bytes_accessed=12 * MIB,
            transcendentals=3 * full_len * full_len,
        ),
        name="attend",
    )(info, *rows, gain, weight)


def turn_kernel(quarter, blocks, info, x0, x1, x2, x3, qkv, context, xt, kt, q2, cn):
    for j, ref in enumerate((x0, x1, x2, x3)):
        xt[info[0] ^ j] = ref[...].T
    for j in range(blocks):
        rows = slice(j * quarter, (j + 1) * quarter)
        third = qkv[rows, 3 * LANES : 4 * LANES].T
        kt[:LANES, rows] = qkv[rows, LANES : 2 * LANES].T
        kt[LANES:, rows] = third[DH:]
        zeros = jnp.zeros((DH, quarter), bf16)
        q2[rows, :] = jnp.concatenate([zeros, third[:DH]], axis=0).T
        cn[rows, :LANES] = context[j, :LANES, :].T
        cn[rows, LANES:] = jnp.concatenate([zeros, context[j, LANES:, :]], axis=0).T


def turn(info, rows, qkv, context):
    quarter, width = rows[0].shape
    blocks = len(rows)
    full_len = quarter * blocks
    shapes = [
        shape_of((blocks, width, quarter), bf16),
        shape_of((3 * DH, full_len), bf16),
        shape_of((full_len, LANES), bf16),
        shape_of((full_len, 2 * LANES), bf16),
    ]
    return pl.pallas_call(
        lambda *refs: turn_kernel(quarter, blocks, *refs),
        in_specs=[scalars()] + [whole((quarter, width))] * 4 + [whole(qkv.shape), whole(context.shape)],
        out_specs=[whole(s.shape) for s in shapes],
        out_shape=shapes,
        compiler_params=params(32),
        cost_estimate=pl.CostEstimate(flops=0, bytes_accessed=8 * MIB, transcendentals=0),
        name="turn",
    )(info, *rows, qkv, context)


def middle_kernel(
    blocks, info, rows, context, w0, w1, w2, w3, gain, router, place, match, rankhot, valid,
    middle, root, chances, gate, slots, gates,
):
    inner = context.shape[1]
    total = rows[...]
    for j, ref in enumerate((w0, w1, w2, w3)):
        total = total + mm_tn(context[info[0] ^ j], ref[...])
    middle[...] = total
    scale = norm_root(total)
    root[...] = scale
    hidden = total * scale * gain[...]
    slots[...] = mm(place[...], hidden.astype(bf16)).astype(bf16)
    scores = mm_nt(hidden, router[...], HIGHEST)
    powers = jnp.exp(scores - jnp.max(scores, axis=-1, keepdims=True))
    share = powers / jnp.sum(powers, axis=-1, keepdims=True)
    chances[...] = share
    own = jnp.sum(share * match[...], axis=-1, keepdims=True)
    gate[...] = own
    table = mm_tn(match[...] * (own * valid[...]), rankhot[...], HIGHEST)
    for e in range(table.shape[0]):
        for j in range(blocks):
            gates[e * blocks + j] = jnp.broadcast_to(table[e : e + 1, :], (8, LANES))


def middle_part(info, rows, context, out_weights, gain, router, place, match, rankhot, valid):
    quarter, width = rows.shape
    blocks = len(out_weights)
    experts = router.shape[0]
    shapes = [
        shape_of((quarter, width), f32),
        shape_of((quarter, 1), f32),
        shape_of((quarter, experts), f32),
        shape_of((quarter, 1), f32),
        shape_of((place.shape[0], width), bf16),
        shape_of((experts * blocks, 8, LANES), f32),
    ]
    arrays = (rows, context, *out_weights, gain, router, place, match, rankhot, valid)
    return pl.pallas_call(
        lambda *refs: middle_kernel(blocks, *refs),
        in_specs=[scalars()] + [whole(a.shape) for a in arrays],
        out_specs=[whole(s.shape) for s in shapes],
        out_shape=shapes,
        compiler_params=params(32),
        cost_estimate=pl.CostEstimate(
            flops=4 * quarter * width * width, bytes_accessed=6 * MIB, transcendentals=0
        ),
        name="middle",
    )(info, *arrays)


def expert_kernel(count, rows, grads, weight, out, back, out_sum, back_sum):
    step = pl.program_id(0)
    inward, outward = weight[0, 0], weight[0, 1]
    active, slope = gelu_pair(mm(rows[...], inward))
    part = mm_nt(active.astype(bf16), outward)
    inner = (mm(grads[...], outward) * slope).astype(bf16)
    back_part = mm_nt(inner, inward)

    @pl.when(step == 0)
    def _():
        out_sum[...] = part
        back_sum[...] = back_part

    @pl.when(step > 0)
    def _():
        out_sum[...] += part
        back_sum[...] += back_part

    @pl.when(step == count - 1)
    def _():
        result = out_sum[...].astype(bf16)
        out[...] = result
        width = result.shape[1]
        back[:, :width] = back_sum[...].astype(bf16)
        match = jnp.sum(grads[...].astype(f32) * result.astype(f32), axis=-1, keepdims=True)
        high = match.astype(bf16).astype(f32)
        lane = lax.broadcasted_iota(jnp.int32, (result.shape[0], LANES), 1)
        tail = jnp.where(lane == 0, high, jnp.where(lane == 1, match - high, 0.0))
        back[:, width:] = tail.astype(bf16)


def expert_part(rows, grads, weights):
    slots, width = rows.shape
    count, _, _, hidden = weights.shape
    return pl.pallas_call(
        lambda *refs: expert_kernel(count, *refs),
        grid=(count,),
        in_specs=[
            whole((slots, width)),
            whole((slots, width)),
            pl.BlockSpec((1, 2, width, hidden), lambda i: (i, 0, 0, 0)),
        ],
        out_specs=[whole((slots, width)), whole((slots, width + LANES))],
        out_shape=[shape_of((slots, width), bf16), shape_of((slots, width + LANES), bf16)],
        scratch_shapes=[pltpu.VMEM((slots, width), f32), pltpu.VMEM((slots, width), f32)],
        compiler_params=params(40),
        cost_estimate=pl.CostEstimate(
            flops=8 * slots * width * hidden * count,
            bytes_accessed=12 * MIB,
            transcendentals=slots * hidden * count,
        ),
        name="experts",
    )(rows, grads, weights)


def expert_grad_kernel(count, rows, grads, gates, weight, out, square):
    step = pl.program_id(0)
    slots, width = rows.shape[1:]
    active, slope = gelu_pair(mm(rows[0], weight[0]))
    inner = (mm(grads[0], weight[1]) * slope * gates[0]).astype(bf16)
    scaled = (grads[0].astype(f32) * gates[0]).astype(bf16)
    first = mm_tn(rows[0], inner)
    second = mm_tn(scaled, active.astype(bf16))

    @pl.when(step == 0)
    def _():
        out[0] = first
        out[1] = second

    @pl.when(step > 0)
    def _():
        out[0] += first
        out[1] += second

    @pl.when(step == count - 1)
    def _():
        square[...] = jnp.sum(out[0] * out[0] + out[1] * out[1], axis=0, keepdims=True)


def expert_gradient(rows, grads, gates, weight):
    count, slots, width = rows.shape
    hidden = weight.shape[2]
    block = pl.BlockSpec((1, slots, width), lambda i: (i, 0, 0))
    return pl.pallas_call(
        lambda *refs: expert_grad_kernel(count, *refs),
        grid=(count,),
        in_specs=[block, block, pl.BlockSpec((1, slots, 1), lambda i: (i, 0, 0)), whole(weight.shape)],
        out_specs=[whole((2, width, hidden)), whole((1, hidden))],
        out_shape=[shape_of((2, width, hidden), f32), shape_of((1, hidden), f32)],
        compiler_params=params(48),
        cost_estimate=pl.CostEstimate(
            flops=8 * slots * width * hidden * count,
            bytes_accessed=12 * MIB,
            transcendentals=slots * hidden * count,
        ),
        name="expert_gradient",
    )(rows, grads, gates, weight)


def return_kernel(
    info, back, place, middle, root, chances, gate, match, cotangent, gain, router, w0, w1, w2, w3,
    grad, turned, parts, gain_grad, router_grad,
):
    width = middle.shape[1]
    came = mm_tn(place[...], back[...])
    gate_grad = came[:, width : width + 1] + came[:, width + 1 : width + 2]
    own = gate[...]
    score_grad = own * (match[...] - chances[...]) * gate_grad
    scaled = middle[...] * root[...]
    hidden = scaled * gain[...]
    router_grad[...] = mm_tn(score_grad, hidden, HIGHEST)
    second = own * came[:, :width] + jnp.dot(
        score_grad, router[...], precision=HIGHEST, preferred_element_type=f32
    )
    gain_grad[...] = jnp.sum(second * scaled, axis=0, keepdims=True)
    inner = second * gain[...]
    centre = jnp.mean(inner * scaled, axis=-1, keepdims=True)
    total = cotangent[...] + root[...] * (inner - scaled * centre)
    grad[...] = total
    low = total.astype(bf16)
    turned[...] = low.T
    for j, ref in enumerate((w0, w1, w2, w3)):
        parts[info[0] ^ j] = mm_nt(ref[...], low).astype(bf16)


def return_part(info, back, place, middle, root, chances, gate, match, cotangent, gain, router, out_weights):
    quarter, width = middle.shape
    experts = router.shape[0]
    inner = out_weights[0].shape[0]
    shapes = [
        shape_of((quarter, width), f32),
        shape_of((width, quarter), bf16),
        shape_of((len(out_weights), inner, quarter), bf16),
        shape_of((1, width), f32),
        shape_of((experts, width), f32),
    ]
    arrays = (back, place, middle, root, chances, gate, match, cotangent, gain, router, *out_weights)
    return pl.pallas_call(
        return_kernel,
        in_specs=[scalars()] + [whole(a.shape) for a in arrays],
        out_specs=[whole(s.shape) for s in shapes],
        out_shape=shapes,
        compiler_params=params(32),
        cost_estimate=pl.CostEstimate(
            flops=4 * quarter * width * width, bytes_accessed=7 * MIB, transcendentals=0
        ),
        name="returned",
    )(info, *arrays)


def attention_back_kernel(blocks, grads, context, chances, qkv, kt, q2, packed, vaug, k01, k2, v01, v2):
    step = pl.program_id(0)
    quarter = grads.shape[2]

    @pl.when(step == 0)
    def _():
        vaug[:, :LANES] = qkv[:, 2 * LANES : 3 * LANES]
        vaug[:, LANES:] = qkv[:, 4 * LANES :]
        for ref in (k01, k2, v01, v2):
            ref[...] = jnp.zeros(ref.shape, f32)

    rows = pl.ds(pl.multiple_of(step * quarter, quarter), quarter)
    heads = grads[0]
    lane = lax.broadcasted_iota(jnp.int32, (quarter, LANES), 1)
    zeros = jnp.zeros((DH, quarter), bf16)
    q01 = qkv[rows, :LANES].astype(f32)
    g01 = heads[:LANES].T.astype(f32)
    g2 = jnp.concatenate([heads[LANES:], zeros], axis=0).T
    query_parts = []
    for h in range(3):
        part = heads[h * DH : (h + 1) * DH]
        centre = jnp.sum(
            part.astype(f32) * context[0, h * DH : (h + 1) * DH, :].astype(f32), axis=0, keepdims=True
        )
        pieces = [zeros] * 4
        pieces[h] = part
        chance_grad = mm(vaug[...], jnp.concatenate(pieces, axis=0))
        low = chances[h]
        score_grad = (low.astype(f32) * (chance_grad - centre)).astype(bf16)
        query_parts.append(mm(kt[h * DH : (h + 1) * DH, :], score_grad) * score_scale)
        if h < 2:
            inside = (lane >= h * DH) & (lane < (h + 1) * DH)
            k01[...] += mm(score_grad, jnp.where(inside, q01, 0.0).astype(bf16))
            v01[...] += mm(low, jnp.where(inside, g01, 0.0).astype(bf16))
        else:
            k2[...] += mm(score_grad, q2[rows, :])
            v2[...] += mm(low, g2)
    packed[rows, :LANES] = jnp.concatenate(query_parts[:2], axis=0).T.astype(bf16)
    packed[rows, 4 * LANES : 5 * LANES] = (
        jnp.concatenate([query_parts[2], jnp.zeros((DH, quarter), f32)], axis=0).T.astype(bf16)
    )

    @pl.when(step == blocks - 1)
    def _():
        packed[:, LANES : 2 * LANES] = (k01[...] * score_scale).astype(bf16)
        packed[:, 2 * LANES : 3 * LANES] = v01[...].astype(bf16)
        packed[:, 3 * LANES : 4 * LANES] = jnp.zeros(k01.shape, bf16)
        packed[:, 4 * LANES : 5 * LANES] = packed[:, 4 * LANES : 5 * LANES] + (k2[...] * score_scale).astype(bf16)
        packed[:, 5 * LANES :] = v2[...].astype(bf16)


def attention_backward(grads, context, chances, qkv, kt, q2):
    blocks, inner, quarter = grads.shape
    full_len = quarter * blocks
    block = pl.BlockSpec((1, inner, quarter), lambda i: (i, 0, 0))
    return pl.pallas_call(
        lambda *refs: attention_back_kernel(blocks, *refs),
        grid=(blocks,),
        in_specs=[
            block,
            block,
            pl.BlockSpec((3, full_len, quarter), lambda i: (0, 0, i)),
            whole(qkv.shape),
            whole(kt.shape),
            whole(q2.shape),
        ],
        out_specs=whole((full_len, 6 * LANES)),
        out_shape=shape_of((full_len, 6 * LANES), bf16),
        scratch_shapes=[pltpu.VMEM((full_len, 2 * LANES), bf16)] + [pltpu.VMEM((full_len, LANES), f32)] * 4,
        compiler_params=params(40),
        cost_estimate=pl.CostEstimate(
            flops=8 * full_len * full_len * inner, bytes_accessed=12 * MIB, transcendentals=0
        ),
        name="attend_back",
    )(grads, context, chances, qkv, kt, q2)


def weight_grad_kernel(blocks, xt, packed, grads, cn, weight, gain, out, gain_grad):
    quarter = xt.shape[2]
    total, outer = None, None
    for j in range(blocks):
        rows = slice(j * quarter, (j + 1) * quarter)
        part = mm(xt[j], packed[rows, :])
        own = mm(grads[j], cn[rows, :])
        total = part if total is None else total + part
        outer = own if outer is None else outer + own
    gain_grad[...] = jnp.sum(total * weight[...].astype(f32), axis=1, keepdims=True)
    total = total * gain[...]
    out[:, : 3 * LANES] = total[:, : 3 * LANES].astype(bf16)
    out[:, 3 * LANES : 4 * LANES] = outer[:, :LANES].astype(bf16)
    out[:, 4 * LANES : 5 * LANES] = total[:, 4 * LANES : 5 * LANES].astype(bf16)
    out[:, 5 * LANES :] = (total[:, 5 * LANES :] + outer[:, LANES:]).astype(bf16)


def weight_gradient(xt, packed, grads, cn, weight, gain):
    blocks, width, quarter = xt.shape
    tall = 256
    full_len = quarter * blocks
    cut = pl.BlockSpec((blocks, tall, quarter), lambda i: (0, i, 0))
    return pl.pallas_call(
        lambda *refs: weight_grad_kernel(blocks, *refs),
        grid=(width // tall,),
        in_specs=[
            cut,
            whole(packed.shape),
            cut,
            whole(cn.shape),
            pl.BlockSpec((tall, 6 * LANES), lambda i: (i, 0)),
            pl.BlockSpec((tall, 1), lambda i: (i, 0)),
        ],
        out_specs=[pl.BlockSpec((tall, 6 * LANES), lambda i: (i, 0)), pl.BlockSpec((tall, 1), lambda i: (i, 0))],
        out_shape=[shape_of((width, 6 * LANES), bf16), shape_of((width, 1), f32)],
        compiler_params=params(32),
        cost_estimate=pl.CostEstimate(
            flops=2 * full_len * width * 8 * LANES, bytes_accessed=8 * MIB, transcendentals=0
        ),
        name="weight_gradient",
    )(xt, packed, grads, cn, weight, gain)


def on_device(
    inputs,
    cotangent,
    lengths,
    routes,
    attention_weight,
    attention_mean,
    attention_square,
    expert_weight,
    expert_mean,
    expert_square,
    router_matrix,
    router_mean,
    router_square,
    norm_gains,
    gains_mean,
    gains_square,
):
    quarter, width = inputs.shape[1:]
    dp_count, tensor_count = lax.axis_size("dp"), lax.axis_size("tensor")
    device_count = dp_count * tensor_count
    everyone = ("dp", "tensor")
    expert_count = router_matrix.shape[1]
    capacity = max(2, (5 * quarter + 4 * expert_count - 1) // (4 * expert_count))
    own_dp, own_tensor = lax.axis_index("dp"), lax.axis_index("tensor")
    share = router_matrix.shape[0]
    rows, grad_rows, length = inputs[0], cotangent[0], lengths[0]
    info = jnp.stack([own_tensor, length]).astype(jnp.int32)

    root_one = norm_root(rows)
    row_blocks = gather_relative((rows * root_one).astype(bf16), "tensor", [2, 1])
    weight_own = pack_columns(*attention_weight.astype(bf16))
    if dp_count <= 8:
        weight_blocks = gather_relative(weight_own, "dp", bits_of(dp_count)[::-1])
        weight = xor_order(jnp.stack(weight_blocks), own_dp).reshape(width, -1)
    else:
        weight = lax.all_gather(weight_own, "dp", axis=0, tiled=True)
    small = jnp.concatenate([norm_gains, router_matrix.T], axis=0)
    small = jnp.pad(small.reshape(-1), (0, -small.size % 1024)).reshape(-1, LANES)
    small = lax.all_to_all(
        jnp.broadcast_to(small[None], (device_count,) + small.shape), everyone, 0, 0, tiled=True
    )
    small = small.reshape(device_count, -1)[:, : (2 + expert_count) * share]
    small = small.reshape(device_count, 2 + expert_count, share).transpose(1, 0, 2).reshape(-1, width)
    gain_one, gain_two, router_rows = small[:1], small[1:2], small[2:]

    local_valid = own_tensor * quarter + jnp.arange(quarter) < length
    valid_scale = local_valid.astype(f32)[:, None]
    chosen = routes[0, :, 0]
    match = (chosen[:, None] == jnp.arange(expert_count)[None, :]).astype(f32)
    lower = (jnp.arange(quarter)[:, None] >= jnp.arange(quarter)[None, :]).astype(f32)
    rank = jnp.sum((mm(lower, match * valid_scale) - 1.0) * match, axis=1).astype(jnp.int32)
    slot = jnp.where(local_valid, chosen * capacity + rank, -1)
    slot_count = expert_count * capacity
    place = (jnp.arange(slot_count)[:, None] == slot[None, :]).astype(bf16)
    rankhot = (jnp.arange(LANES)[None, :] == rank[:, None]).astype(f32)

    def trade(values):
        blocks = values.reshape(expert_count, capacity, values.shape[1])
        return lax.all_to_all(blocks, "dp", 0, 0, tiled=True).reshape(values.shape)

    grad_slots, weight = lax.optimization_barrier((mm(place, grad_rows.astype(bf16)).astype(bf16), weight))
    expert_grads = trade(grad_slots)
    expert_low = expert_weight[0].astype(bf16)
    expert_all = lax.all_gather(expert_low, "tensor", axis=0)

    out_weight = jnp.concatenate([weight[:, 3 * LANES : 4 * LANES], weight[:, 5 * LANES + DH :]], axis=1).T
    out_weights = gather_relative(out_weight, "tensor", [2, 1])
    context, chances, qkv = attention_forward(info, row_blocks, gain_one, weight)
    context_own = lax.all_to_all(context, "tensor", 0, 0, tiled=True)
    turned_rows, keys_turned, third_query, context_rows = turn(info, row_blocks, qkv, context)

    middle, root_two, shares, gate, slots, gates = middle_part(
        info, rows, context_own, out_weights, gain_two, router_rows, place, match, rankhot, valid_scale
    )
    expert_rows = trade(slots)
    gates_came = lax.all_to_all(gates, everyone, 0, 0, tiled=True)[:, 0, :capacity]
    gates_all = gates_came.reshape(dp_count, tensor_count, capacity).transpose(1, 0, 2)
    gates_all = gates_all.reshape(tensor_count, slot_count, 1)
    expert_outs, expert_back = expert_part(expert_rows, expert_grads, expert_all)
    expert_back = trade(expert_back)
    rows_all = lax.all_gather(expert_rows, "tensor", axis=0)
    grads_all = lax.all_gather(expert_grads, "tensor", axis=0)
    expert_grad, expert_square_sum = expert_gradient(rows_all, grads_all, gates_all, expert_low)

    middle_grad, middle_turned, context_parts, gain_two_grad, router_grad = return_part(
        info, expert_back, place, middle, root_two, shares, gate, match, grad_rows, gain_two, router_rows, out_weights
    )
    context_grad = lax.all_to_all(context_parts, "tensor", 0, 0, tiled=True)
    middle_all = lax.all_gather(middle_turned, "tensor", axis=0)
    expert_outs, context_parts = lax.optimization_barrier((expert_outs, context_parts))
    picked = mm_tn(place, trade(expert_outs))
    branch = gate * valid_scale * picked
    block_output = middle + branch

    packed = attention_backward(context_grad, context, chances, qkv, keys_turned, third_query)
    weight_grad, gain_one_grad = weight_gradient(
        turned_rows, packed, middle_all, context_rows, weight, gain_one.reshape(width, 1)
    )
    weight_came = lax.all_to_all(weight_grad.reshape(dp_count, -1, width), "dp", 0, 0, tiled=True)
    attention_grad = unpack_columns(jnp.sum(weight_came.astype(f32), axis=0))
    input_parts = mm_nt(packed, weight).astype(bf16).reshape(tensor_count, quarter, width)
    input_came = lax.all_to_all(input_parts, "tensor", 0, 0, tiled=True)
    first_grad = jnp.sum(input_came.astype(f32), axis=0)
    input_grad = middle_grad + norm_backward(rows, root_one, gain_one, first_grad)

    small_grad = jnp.concatenate([gain_one_grad.reshape(1, width), gain_two_grad, router_grad], axis=0)
    small_cut = small_grad.reshape(-1, device_count, share).transpose(1, 0, 2).reshape(device_count, -1)
    small_cut = jnp.pad(small_cut, ((0, 0), (0, -small_cut.shape[1] % 1024))).reshape(device_count, -1, LANES)
    small_own = jnp.sum(lax.all_to_all(small_cut, everyone, 0, 0, tiled=True), axis=0)
    small_own = small_own.reshape(-1)[: (2 + expert_count) * share].reshape(2 + expert_count, share)
    gains_grad, router_own = small_own[:2], small_own[2:].T

    square_sum = (
        jnp.sum(attention_grad * attention_grad) + jnp.sum(expert_square_sum) + jnp.sum(small_own * small_own)
    )
    square_sums = lax.all_to_all(jnp.full((device_count, 8, LANES), square_sum), everyone, 0, 0, tiled=True)
    grad_norm = jnp.sqrt(jnp.sum(square_sums[:, 0, 0]))
    factor = jnp.minimum(1.0, clip_limit / (grad_norm + norm_epsilon))
    attention_rate = jnp.array(
        [0.71 / math.sqrt(D), 0.71 / math.sqrt(D), 0.83 / math.sqrt(D), 0.79 / math.sqrt(H * DH)],
        f32,
    ).reshape(4, 1, 1)
    expert_rate = jnp.array(
        [0.4 * math.sqrt(expert_count / D), 1.38 * math.sqrt(expert_count / FF)], f32
    ).reshape(1, 2, 1, 1)
    attention_new = adam_update(
        attention_weight, attention_mean, attention_square, attention_grad * factor, attention_rate
    )
    expert_new = adam_update(
        expert_weight, expert_mean, expert_square, expert_grad[None] * factor, expert_rate
    )
    router_new = adam_update(
        router_matrix, router_mean, router_square, router_own * factor, 0.24 / math.sqrt(D)
    )
    gains_new = adam_update(norm_gains, gains_mean, gains_square, gains_grad * factor, 0.5)
    return (
        block_output[None],
        input_grad[None],
        grad_norm,
        *attention_new,
        *expert_new,
        *router_new,
        *gains_new,
        branch[None],
    )


def solution(mesh):
    rows = P("dp", "tensor", None)
    attention = P(None, "dp", "tensor")
    expert = P("dp", None, None, "tensor")
    router = P(("dp", "tensor"), None)
    gains = P(None, ("dp", "tensor"))
    weights = (attention,) * 3 + (expert,) * 3 + (router,) * 3 + (gains,) * 3
    return jax.shard_map(
        on_device,
        mesh=mesh,
        in_specs=(rows, rows, P("dp"), rows) + weights,
        out_specs=(rows, rows, P()) + weights + (rows,),
        check_vma=False,
    )
```

```python
import math

import jax
import jax.numpy as jnp
from jax import lax
from jax.experimental import pallas as pl
from jax.experimental.pallas import tpu as pltpu
from jax.sharding import PartitionSpec as P

D = 768
H = 12
DH = 64
FF = 3072
STEP = 10

HIGHEST = lax.Precision.HIGHEST
norm_epsilon = 1e-06
beta_first = 0.9
beta_second = 0.999
adam_epsilon = 1e-08
decay_factor = 0.01
clip_limit = 1.0
masked_score = -1e30
score_scale = 1.0 / math.sqrt(DH)
bf16 = jnp.bfloat16
f32 = jnp.float32
MIB = 1 << 20
LANES = 128


def swap(values, axis, mask):
    count = lax.axis_size(axis)
    return lax.ppermute(values, axis, [(i, i ^ mask) for i in range(count)])


def bits_of(count):
    return [1 << b for b in range(count.bit_length() - 1)]


def gather_relative(block, axis, order):
    held = {0: block}
    for mask in order:
        for j in list(held):
            held[j ^ mask] = swap(held[j], axis, mask)
    return [held[j] for j in range(len(held))]


def mm(a, b):
    return jnp.dot(a, b, preferred_element_type=f32)


def mm_nt(a, b, precision=None):
    return lax.dot_general(
        a, b, (((1,), (1,)), ((), ())), preferred_element_type=f32, precision=precision
    )


def mm_tn(a, b, precision=None):
    return lax.dot_general(
        a, b, (((0,), (0,)), ((), ())), preferred_element_type=f32, precision=precision
    )


def norm_root(values):
    return lax.rsqrt(jnp.mean(values * values, axis=-1, keepdims=True) + norm_epsilon)


def norm_backward(values, root, gain_row, grad):
    scaled = values * root
    inner = grad * gain_row
    centre = jnp.mean(inner * scaled, axis=-1, keepdims=True)
    return root * (inner - scaled * centre)


def gelu_pair(values):
    c = math.sqrt(2.0 / math.pi)
    square = values * values
    th = jnp.tanh(c * values * (1.0 + 0.044715 * square))
    half = 0.5 * (1.0 + th)
    slope = half + 0.5 * values * (1.0 - th * th) * c * (1.0 + 3.0 * 0.044715 * square)
    return values * half, slope


def adam_update(weight, moment_one, moment_two, gradient, step_rate):
    moment_one_next = beta_first * moment_one + (1.0 - beta_first) * gradient
    moment_two_next = beta_second * moment_two + (1.0 - beta_second) * gradient * gradient
    corrected_one = moment_one_next / (1.0 - beta_first**STEP)
    corrected_two = moment_two_next / (1.0 - beta_second**STEP)
    weight_next = weight - step_rate * (
        corrected_one / (jnp.sqrt(corrected_two) + adam_epsilon) + decay_factor * weight
    )
    return (weight_next, moment_one_next, moment_two_next)


def shape_of(shape, dtype):
    return jax.ShapeDtypeStruct(shape, dtype)


def whole(shape):
    return pl.BlockSpec(shape, lambda *_: (0,) * len(shape))


def scalars():
    return pl.BlockSpec(memory_space=pltpu.SMEM)


def params(limit):
    return pltpu.CompilerParams(vmem_limit_bytes=limit * MIB)


def pack_columns(q, k, v, o):
    wide = LANES
    return jnp.concatenate(
        [q[:, :wide], k[:, :wide], v[:, :wide], o[:, :wide], q[:, wide:], k[:, wide:], v[:, wide:], o[:, wide:]],
        axis=1,
    )


def unpack_columns(packed):
    wide, rest = LANES, DH
    end = 4 * wide
    return jnp.stack(
        [
            jnp.concatenate(
                [packed[:, i * wide : (i + 1) * wide], packed[:, end + i * rest : end + (i + 1) * rest]], axis=1
            )
            for i in range(4)
        ]
    )


def assemble_kernel(count, info, *refs):
    shards, weight, turned = refs[:count], refs[count], refs[count + 1]
    rows = shards[0].shape[0]
    for j, ref in enumerate(shards):
        start = pl.multiple_of((info[2] ^ j) * rows, rows) if count > 1 else 0
        weight[pl.ds(start, rows), :] = ref[...]
    turned[:LANES, :] = weight[:, 3 * LANES : 4 * LANES].T
    turned[LANES:, :] = weight[:, 5 * LANES :].T[DH:]


def assemble(info, shards):
    rows, columns = shards[0].shape
    shapes = [shape_of((rows * len(shards), columns), bf16), shape_of((3 * DH, rows * len(shards)), bf16)]
    return pl.pallas_call(
        lambda *refs: assemble_kernel(len(shards), *refs),
        in_specs=[scalars()] + [whole((rows, columns))] * len(shards),
        out_specs=[whole(s.shape) for s in shapes],
        out_shape=shapes,
        compiler_params=params(60),
        cost_estimate=pl.CostEstimate(flops=0, bytes_accessed=4 * MIB, transcendentals=0),
        name="assemble",
    )(info, *shards)


def attention_kernel(quarter, blocks, info, x0, x1, x2, x3, gain, weight, context, chances, totals, qkv, a, kaug, vt):
    step = pl.program_id(0)

    @pl.when(step == 0)
    def _():
        for j, ref in enumerate((x0, x1, x2, x3)):
            start = pl.multiple_of((info[0] ^ j) * quarter, quarter)
            a[pl.ds(start, quarter), :] = (ref[...].astype(f32) * gain[...]).astype(bf16)
        tail = (lax.broadcasted_iota(jnp.int32, (16, quarter), 0) == 0).astype(f32).astype(bf16)
        for j in range(blocks):
            rows = slice(j * quarter, (j + 1) * quarter)
            first = mm(a[rows, :], weight[:, : 3 * LANES]).astype(bf16)
            second = mm(a[rows, :], weight[:, 4 * LANES :]).astype(bf16)
            qkv[rows, : 3 * LANES] = first
            qkv[rows, 3 * LANES :] = second
            kaug[rows, :LANES] = first[:, LANES : 2 * LANES]
            lane = lax.broadcasted_iota(jnp.int32, (quarter, LANES), 1)
            row = lax.broadcasted_iota(jnp.int32, (quarter, LANES), 0) + j * quarter
            hidden = jnp.where((lane == 0) & (row >= info[1]), masked_score, 0.0)
            kaug[rows, LANES:] = jnp.where(lane < DH, hidden, second[:, :LANES].astype(f32)).astype(bf16)
            values = first[:, 2 * LANES :].T
            vt[0, :DH, rows] = values[:DH]
            vt[1, :DH, rows] = values[DH:]
            vt[2, :DH, rows] = second[:, LANES:].T[:DH]
            for h in range(3):
                vt[h, DH:, rows] = tail

    rows = pl.ds(pl.multiple_of(step * quarter, quarter), quarter)
    q01 = (qkv[rows, :LANES].astype(f32) * score_scale).T.astype(bf16)
    q2 = (qkv[rows, 3 * LANES : 4 * LANES].astype(f32) * score_scale).T.astype(bf16)[:DH]
    ones = (lax.broadcasted_iota(jnp.int32, (DH, quarter), 0) == 0).astype(f32).astype(bf16)
    zeros = jnp.zeros((DH, quarter), bf16)
    queries = (
        jnp.concatenate([q01[:DH], zeros, ones, zeros], axis=0),
        jnp.concatenate([zeros, q01[DH:], ones, zeros], axis=0),
        jnp.concatenate([zeros, zeros, ones, q2], axis=0),
    )
    for h in range(3):
        scores = mm(kaug[...], queries[h])
        top = jnp.max(scores, axis=0, keepdims=True)
        low = jnp.exp(scores - top).astype(bf16)
        chances[h] = low
        summed = mm(vt[h], low)
        part = 1.0 / summed[DH : DH + 1]
        totals[0, h : h + 1, :] = part
        context[0, h * DH : (h + 1) * DH, :] = (summed[:DH] * part).astype(bf16)


def attention_forward(info, rows, gain, weight):
    quarter, width = rows[0].shape
    blocks = len(rows)
    full_len = quarter * blocks
    inner = 3 * DH
    return pl.pallas_call(
        lambda *refs: attention_kernel(quarter, blocks, *refs),
        grid=(blocks,),
        in_specs=[scalars()] + [whole((quarter, width))] * 4 + [whole((1, width)), whole(weight.shape)],
        out_specs=[
            pl.BlockSpec((1, inner, quarter), lambda i: (i, 0, 0)),
            pl.BlockSpec((3, full_len, quarter), lambda i: (0, 0, i)),
            pl.BlockSpec((1, 3, quarter), lambda i: (i, 0, 0)),
            whole((full_len, 5 * LANES)),
        ],
        out_shape=[
            shape_of((blocks, inner, quarter), bf16),
            shape_of((3, full_len, full_len), bf16),
            shape_of((blocks, 3, quarter), f32),
            shape_of((full_len, 5 * LANES), bf16),
        ],
        scratch_shapes=[
            pltpu.VMEM((full_len, width), bf16),
            pltpu.VMEM((full_len, 2 * LANES), bf16),
            pltpu.VMEM((3, DH + 16, full_len), bf16),
        ],
        compiler_params=params(60),
        cost_estimate=pl.CostEstimate(
            flops=2 * full_len * (width * 5 * LANES + 2 * full_len * inner),
            bytes_accessed=12 * MIB,
            transcendentals=3 * full_len * full_len,
        ),
        name="attend",
    )(info, *rows, gain, weight)


def turn_kernel(quarter, blocks, info, x0, x1, x2, x3, qkv, context, xt, kt, q2, cn):
    for j, ref in enumerate((x0, x1, x2, x3)):
        xt[info[0] ^ j] = ref[...].T
    for j in range(blocks):
        rows = slice(j * quarter, (j + 1) * quarter)
        third = qkv[rows, 3 * LANES : 4 * LANES].T
        kt[:LANES, rows] = qkv[rows, LANES : 2 * LANES].T
        kt[LANES:, rows] = third[DH:]
        zeros = jnp.zeros((DH, quarter), bf16)
        q2[rows, :] = jnp.concatenate([zeros, third[:DH]], axis=0).T
        cn[rows, :LANES] = context[j, :LANES, :].T
        cn[rows, LANES:] = jnp.concatenate([zeros, context[j, LANES:, :]], axis=0).T


def turn(info, rows, qkv, context):
    quarter, width = rows[0].shape
    blocks = len(rows)
    full_len = quarter * blocks
    shapes = [
        shape_of((blocks, width, quarter), bf16),
        shape_of((3 * DH, full_len), bf16),
        shape_of((full_len, LANES), bf16),
        shape_of((full_len, 2 * LANES), bf16),
    ]
    return pl.pallas_call(
        lambda *refs: turn_kernel(quarter, blocks, *refs),
        in_specs=[scalars()] + [whole((quarter, width))] * 4 + [whole(qkv.shape), whole(context.shape)],
        out_specs=[whole(s.shape) for s in shapes],
        out_shape=shapes,
        compiler_params=params(60),
        cost_estimate=pl.CostEstimate(flops=0, bytes_accessed=8 * MIB, transcendentals=0),
        name="turn",
    )(info, *rows, qkv, context)


def two_columns(column):
    high = column.astype(bf16).astype(f32)
    lane = lax.broadcasted_iota(jnp.int32, (column.shape[0], LANES), 1)
    return jnp.where(lane == 0, high, jnp.where(lane == 1, column - high, 0.0)).astype(bf16)


def middle_kernel(
    info, rows, context, w0, w1, w2, w3, gain, router, place, match, valid, middle, root, chances, gate, slots
):
    total = rows[...]
    for j, ref in enumerate((w0, w1, w2, w3)):
        total = total + mm_tn(context[info[0] ^ j], ref[...])
    middle[...] = total
    scale = norm_root(total)
    root[...] = scale
    hidden = total * scale * gain[...]
    scores = mm_nt(hidden, router[...], HIGHEST)
    powers = jnp.exp(scores - jnp.max(scores, axis=-1, keepdims=True))
    share = powers / jnp.sum(powers, axis=-1, keepdims=True)
    chances[...] = share
    own = jnp.sum(share * match[...], axis=-1, keepdims=True)
    gate[...] = own
    width = rows.shape[1]
    slots[:, :width] = mm(place[...], hidden.astype(bf16)).astype(bf16)
    slots[:, width:] = mm(place[...], two_columns(own * valid[...])).astype(bf16)


def middle_part(info, rows, context, out_weights, gain, router, place, match, valid):
    quarter, width = rows.shape
    experts = router.shape[0]
    shapes = [
        shape_of((quarter, width), f32),
        shape_of((quarter, 1), f32),
        shape_of((quarter, experts), f32),
        shape_of((quarter, 1), f32),
        shape_of((place.shape[0], width + LANES), bf16),
    ]
    arrays = (rows, context, *out_weights, gain, router, place, match, valid)
    return pl.pallas_call(
        middle_kernel,
        in_specs=[scalars()] + [whole(a.shape) for a in arrays],
        out_specs=[whole(s.shape) for s in shapes],
        out_shape=shapes,
        compiler_params=params(60),
        cost_estimate=pl.CostEstimate(
            flops=4 * quarter * width * width, bytes_accessed=6 * MIB, transcendentals=0
        ),
        name="middle",
    )(info, *arrays)


def expert_kernel(rows, grads, w0, w1, w2, w3, out, back, held, arrived):
    width = grads.shape[1]
    sources = (w0, w1, w2, w3)
    copies = [pltpu.make_async_copy(ref, held.at[i], arrived.at[i]) for i, ref in enumerate(sources)]
    for copy in copies:
        copy.start()
    out_total, back_total = None, None
    for i, copy in enumerate(copies):
        copy.wait()
        inward, outward = held[i, 0], held[i, 1]
        grad = mm(grads[...], outward)
        active, slope = gelu_pair(mm(rows[:, :width], inward))
        part = mm_nt(active.astype(bf16), outward)
        back_part = mm_nt((grad * slope).astype(bf16), inward)
        out_total = part if i == 0 else out_total + part
        back_total = back_part if i == 0 else back_total + back_part
    result = out_total.astype(bf16)
    out[...] = result
    back[:, :width] = back_total.astype(bf16)
    match = jnp.sum(grads[...].astype(f32) * result.astype(f32), axis=-1, keepdims=True)
    back[:, width:] = two_columns(match)


def expert_part(rows, grads, weights):
    slots, width = grads.shape
    hidden = weights[0].shape[2]
    count = len(weights)
    shapes = [shape_of((slots, width), bf16), shape_of((slots, width + LANES), bf16)]
    return pl.pallas_call(
        expert_kernel,
        in_specs=[whole(rows.shape), whole(grads.shape)] + [pl.BlockSpec(memory_space=pl.ANY)] * count,
        out_specs=[whole(s.shape) for s in shapes],
        out_shape=shapes,
        scratch_shapes=[pltpu.VMEM((count,) + weights[0].shape, bf16), pltpu.SemaphoreType.DMA((count,))],
        compiler_params=params(60),
        cost_estimate=pl.CostEstimate(
            flops=8 * slots * width * hidden * count,
            bytes_accessed=12 * MIB,
            transcendentals=slots * hidden * count,
        ),
        name="experts",
    )(rows, grads, *weights)


def expert_grad_kernel(count, *refs):
    rows, grads, weight = refs[:count], refs[count : 2 * count], refs[2 * count]
    out, square, row_all, grad_all, inner_all, active_all = refs[2 * count + 1 :]
    slots, width = grads[0].shape
    for j in range(count):
        at = slice(j * slots, (j + 1) * slots)
        gate = rows[j][:, width : width + 1].astype(f32) + rows[j][:, width + 1 : width + 2].astype(f32)
        row_all[at, :] = rows[j][:, :width]
        grad_all[at, :] = (grads[j][...].astype(f32) * gate).astype(bf16)
        back = mm(grads[j][...], weight[1])
        active, slope = gelu_pair(mm(rows[j][:, :width], weight[0]))
        inner_all[at, :] = (back * slope * gate).astype(bf16)
        active_all[at, :] = active.astype(bf16)
    first = mm_tn(row_all[...], inner_all[...])
    out[0] = first
    second = mm_tn(grad_all[...], active_all[...])
    out[1] = second
    square[...] = jnp.sum(first * first + second * second, axis=0, keepdims=True)


def expert_gradient(rows, grads, weight):
    count = len(rows)
    slots, width = grads[0].shape
    hidden = weight.shape[2]
    arrays = (*rows, *grads, weight)
    shapes = [shape_of((2, width, hidden), f32), shape_of((1, hidden), f32)]
    return pl.pallas_call(
        lambda *refs: expert_grad_kernel(count, *refs),
        in_specs=[whole(a.shape) for a in arrays],
        out_specs=[whole(s.shape) for s in shapes],
        out_shape=shapes,
        scratch_shapes=[pltpu.VMEM((count * slots, width), bf16)] * 2 + [pltpu.VMEM((count * slots, hidden), bf16)] * 2,
        compiler_params=params(60),
        cost_estimate=pl.CostEstimate(
            flops=8 * slots * width * hidden * count,
            bytes_accessed=12 * MIB,
            transcendentals=slots * hidden * count,
        ),
        name="expert_gradient",
    )(*arrays)


def return_kernel(
    info, back, place, middle, root, chances, gate, match, cotangent, gain, router, w0, w1, w2, w3,
    grad, turned, parts, gain_grad, router_grad,
):
    width = middle.shape[1]
    came = mm_tn(place[...], back[...])
    gate_grad = came[:, width : width + 1] + came[:, width + 1 : width + 2]
    own = gate[...]
    score_grad = own * (match[...] - chances[...]) * gate_grad
    scaled = middle[...] * root[...]
    hidden = scaled * gain[...]
    router_grad[...] = mm_tn(score_grad, hidden, HIGHEST)
    second = own * came[:, :width] + jnp.dot(
        score_grad, router[...], precision=HIGHEST, preferred_element_type=f32
    )
    gain_grad[...] = jnp.sum(second * scaled, axis=0, keepdims=True)
    inner = second * gain[...]
    centre = jnp.mean(inner * scaled, axis=-1, keepdims=True)
    total = cotangent[...] + root[...] * (inner - scaled * centre)
    grad[...] = total
    low = total.astype(bf16)
    turned[...] = low.T
    for j, ref in enumerate((w0, w1, w2, w3)):
        parts[info[0] ^ j] = mm_nt(ref[...], low).astype(bf16)


def return_part(info, back, place, middle, root, chances, gate, match, cotangent, gain, router, out_weights):
    quarter, width = middle.shape
    experts = router.shape[0]
    inner = out_weights[0].shape[0]
    shapes = [
        shape_of((quarter, width), f32),
        shape_of((width, quarter), bf16),
        shape_of((len(out_weights), inner, quarter), bf16),
        shape_of((1, width), f32),
        shape_of((experts, width), f32),
    ]
    arrays = (back, place, middle, root, chances, gate, match, cotangent, gain, router, *out_weights)
    return pl.pallas_call(
        return_kernel,
        in_specs=[scalars()] + [whole(a.shape) for a in arrays],
        out_specs=[whole(s.shape) for s in shapes],
        out_shape=shapes,
        compiler_params=params(60),
        cost_estimate=pl.CostEstimate(
            flops=4 * quarter * width * width, bytes_accessed=7 * MIB, transcendentals=0
        ),
        name="returned",
    )(info, *arrays)


def attention_back_kernel(blocks, grads, context, chances, totals, qkv, kt, q2, packed, vaug, k01, k2, v01, v2):
    step = pl.program_id(0)
    quarter = grads.shape[2]

    @pl.when(step == 0)
    def _():
        vaug[:, :LANES] = qkv[:, 2 * LANES : 3 * LANES]
        lane = lax.broadcasted_iota(jnp.int32, (vaug.shape[0], LANES), 1)
        ones = jnp.where(lane < DH + 2, 1.0, 0.0)
        vaug[:, LANES:] = jnp.where(lane < DH, qkv[:, 4 * LANES :].astype(f32), ones).astype(bf16)
        for ref in (k01, k2, v01, v2):
            ref[...] = jnp.zeros(ref.shape, f32)

    rows = pl.ds(pl.multiple_of(step * quarter, quarter), quarter)
    raw = grads[0].astype(f32)
    scale = totals[0]
    scaled = [raw[h * DH : (h + 1) * DH] * scale[h : h + 1] for h in range(3)]
    heads = jnp.concatenate(scaled, axis=0).astype(bf16)
    lane = lax.broadcasted_iota(jnp.int32, (quarter, LANES), 1)
    row = lax.broadcasted_iota(jnp.int32, (DH, quarter), 0)
    zeros = jnp.zeros((DH, quarter), bf16)
    q01 = qkv[rows, :LANES].astype(f32)
    g01 = heads[:LANES].T.astype(f32)
    g2 = jnp.concatenate([heads[LANES:], zeros], axis=0).T
    query_parts = []
    for h in range(3):
        part = heads[h * DH : (h + 1) * DH]
        centre = -jnp.sum(
            part.astype(f32) * context[0, h * DH : (h + 1) * DH, :].astype(f32), axis=0, keepdims=True
        )
        high = centre.astype(bf16).astype(f32)
        tail = jnp.where(row == 0, high, jnp.where(row == 1, centre - high, 0.0)).astype(bf16)
        pieces = [zeros, zeros, zeros, tail]
        pieces[h] = part
        chance_grad = mm(vaug[...], jnp.concatenate(pieces, axis=0))
        low = chances[h]
        score_grad = (low.astype(f32) * chance_grad).astype(bf16)
        query_parts.append(mm(kt[h * DH : (h + 1) * DH, :], score_grad) * score_scale)
        if h < 2:
            inside = (lane >= h * DH) & (lane < (h + 1) * DH)
            k01[...] += mm(score_grad, jnp.where(inside, q01, 0.0).astype(bf16))
            v01[...] += mm(low, jnp.where(inside, g01, 0.0).astype(bf16))
        else:
            k2[...] += mm(score_grad, q2[rows, :])
            v2[...] += mm(low, g2)
    packed[rows, :LANES] = jnp.concatenate(query_parts[:2], axis=0).T.astype(bf16)
    packed[rows, 4 * LANES : 5 * LANES] = (
        jnp.concatenate([query_parts[2], jnp.zeros((DH, quarter), f32)], axis=0).T.astype(bf16)
    )

    @pl.when(step == blocks - 1)
    def _():
        packed[:, LANES : 2 * LANES] = (k01[...] * score_scale).astype(bf16)
        packed[:, 2 * LANES : 3 * LANES] = v01[...].astype(bf16)
        packed[:, 3 * LANES : 4 * LANES] = jnp.zeros(k01.shape, bf16)
        packed[:, 4 * LANES : 5 * LANES] = packed[:, 4 * LANES : 5 * LANES] + (k2[...] * score_scale).astype(bf16)
        packed[:, 5 * LANES :] = v2[...].astype(bf16)


def attention_backward(grads, context, chances, totals, qkv, kt, q2):
    blocks, inner, quarter = grads.shape
    full_len = quarter * blocks
    block = pl.BlockSpec((1, inner, quarter), lambda i: (i, 0, 0))
    return pl.pallas_call(
        lambda *refs: attention_back_kernel(blocks, *refs),
        grid=(blocks,),
        in_specs=[
            block,
            block,
            pl.BlockSpec((3, full_len, quarter), lambda i: (0, 0, i)),
            pl.BlockSpec((1, 3, quarter), lambda i: (i, 0, 0)),
            whole(qkv.shape),
            whole(kt.shape),
            whole(q2.shape),
        ],
        out_specs=whole((full_len, 6 * LANES)),
        out_shape=shape_of((full_len, 6 * LANES), bf16),
        scratch_shapes=[pltpu.VMEM((full_len, 2 * LANES), bf16)] + [pltpu.VMEM((full_len, LANES), f32)] * 4,
        compiler_params=params(60),
        cost_estimate=pl.CostEstimate(
            flops=8 * full_len * full_len * inner, bytes_accessed=12 * MIB, transcendentals=0
        ),
        name="attend_back",
    )(grads, context, chances, totals, qkv, kt, q2)


def weight_grad_kernel(blocks, info, xt, packed, g0, g1, g2, g3, cn, weight, gain, out, gain_grad):
    quarter = xt.shape[2]
    total, outer = None, None
    for j, ref in enumerate((g0, g1, g2, g3)):
        rows = slice(j * quarter, (j + 1) * quarter)
        there = pl.ds(pl.multiple_of((info[0] ^ j) * quarter, quarter), quarter)
        part = mm(xt[j], packed[rows, :])
        own = mm(ref[...], cn[there, :])
        total = part if total is None else total + part
        outer = own if outer is None else outer + own
    gain_grad[...] = jnp.sum(total * weight[...].astype(f32), axis=1, keepdims=True)
    total = total * gain[...]
    out[:, : 3 * LANES] = total[:, : 3 * LANES].astype(bf16)
    out[:, 3 * LANES : 4 * LANES] = outer[:, :LANES].astype(bf16)
    out[:, 4 * LANES : 5 * LANES] = total[:, 4 * LANES : 5 * LANES].astype(bf16)
    out[:, 5 * LANES :] = (total[:, 5 * LANES :] + outer[:, LANES:]).astype(bf16)


def weight_gradient(info, xt, packed, grads, cn, weight, gain):
    blocks, width, quarter = xt.shape
    tall = 256
    full_len = quarter * blocks
    return pl.pallas_call(
        lambda *refs: weight_grad_kernel(blocks, *refs),
        grid=(width // tall,),
        in_specs=[
            scalars(),
            pl.BlockSpec((blocks, tall, quarter), lambda i: (0, i, 0)),
            whole(packed.shape),
            *[pl.BlockSpec((tall, quarter), lambda i: (i, 0))] * blocks,
            whole(cn.shape),
            pl.BlockSpec((tall, 6 * LANES), lambda i: (i, 0)),
            pl.BlockSpec((tall, 1), lambda i: (i, 0)),
        ],
        out_specs=[pl.BlockSpec((tall, 6 * LANES), lambda i: (i, 0)), pl.BlockSpec((tall, 1), lambda i: (i, 0))],
        out_shape=[shape_of((width, 6 * LANES), bf16), shape_of((width, 1), f32)],
        compiler_params=params(60),
        cost_estimate=pl.CostEstimate(
            flops=2 * full_len * width * 8 * LANES, bytes_accessed=8 * MIB, transcendentals=0
        ),
        name="weight_gradient",
    )(info, xt, packed, *grads, cn, weight, gain)


def adam_kernel(rates, weight, first, second, gradient, weight_out, first_out, second_out):
    grad = gradient[...] * rates[0]
    rate = rates[1 + pl.program_id(0)]
    result = adam_update(weight[...], first[...], second[...], grad, rate)
    weight_out[...], first_out[...], second_out[...] = result


def adam_experts(factor, rates, weight, first, second, gradient):
    _, tall, wide = weight.shape
    cut = tall // 4
    block = pl.BlockSpec((1, cut, wide), lambda i, j: (i, j, 0))
    return pl.pallas_call(
        adam_kernel,
        grid=(2, 4),
        in_specs=[scalars()] + [block] * 4,
        out_specs=[block] * 3,
        out_shape=[shape_of(weight.shape, f32)] * 3,
        compiler_params=params(60),
        cost_estimate=pl.CostEstimate(flops=2 * weight.size * 20, bytes_accessed=28 * MIB, transcendentals=0),
        name="adam",
    )(jnp.concatenate([factor[None], rates]), weight, first, second, gradient)


def after(value, *others):
    return lax.optimization_barrier((value, *others))[0]


def on_device(
    inputs,
    cotangent,
    lengths,
    routes,
    attention_weight,
    attention_mean,
    attention_square,
    expert_weight,
    expert_mean,
    expert_square,
    router_matrix,
    router_mean,
    router_square,
    norm_gains,
    gains_mean,
    gains_square,
):
    quarter, width = inputs.shape[1:]
    dp_count, tensor_count = lax.axis_size("dp"), lax.axis_size("tensor")
    device_count = dp_count * tensor_count
    everyone = ("dp", "tensor")
    expert_count = router_matrix.shape[1]
    capacity = max(2, (5 * quarter + 4 * expert_count - 1) // (4 * expert_count))
    own_dp, own_tensor = lax.axis_index("dp"), lax.axis_index("tensor")
    share = router_matrix.shape[0]
    rows, grad_rows, length = inputs[0], cotangent[0], lengths[0]
    info = jnp.stack([own_tensor, length, own_dp]).astype(jnp.int32)

    weight_own = pack_columns(*attention_weight.astype(bf16))
    root_one = norm_root(rows)
    scaled_one = (rows * root_one).astype(bf16)
    few = dp_count <= 8
    if few:
        shards = gather_relative(weight_own, "dp", bits_of(dp_count)[::-1])
        early, late = shards[dp_count // 2], shards[dp_count - 2]
    row_blocks = gather_relative(scaled_one, "tensor", [2, 1])
    if not few:
        shards = [lax.all_gather(weight_own, "dp", axis=0, tiled=True)]
        early = late = row_blocks[2]
    weight, out_weight = assemble(info, shards)
    small = jnp.concatenate([norm_gains, router_matrix.T], axis=0)
    small = jnp.pad(small.reshape(-1), (0, -small.size % 1024)).reshape(-1, LANES)
    small = lax.all_to_all(
        jnp.broadcast_to(small[None], (device_count,) + small.shape), everyone, 0, 0, tiled=True
    )
    small = small.reshape(device_count, -1)[:, : (2 + expert_count) * share]
    small = small.reshape(device_count, 2 + expert_count, share).transpose(1, 0, 2).reshape(-1, width)
    gain_one, gain_two, router_rows = small[:1], small[1:2], small[2:]

    local_valid = own_tensor * quarter + jnp.arange(quarter) < length
    valid_scale = local_valid.astype(f32)[:, None]
    chosen = routes[0, :, 0]
    match = (chosen[:, None] == jnp.arange(expert_count)[None, :]).astype(f32)
    lower = (jnp.arange(quarter)[:, None] >= jnp.arange(quarter)[None, :]).astype(f32)
    rank = jnp.sum((mm(lower, match * valid_scale) - 1.0) * match, axis=1).astype(jnp.int32)
    slot = jnp.where(local_valid, chosen * capacity + rank, -1)
    slot_count = expert_count * capacity
    place = (jnp.arange(slot_count)[:, None] == slot[None, :]).astype(bf16)

    def trade(values):
        blocks = values.reshape(expert_count, capacity, values.shape[1])
        return lax.all_to_all(blocks, "dp", 0, 0, tiled=True).reshape(values.shape)

    expert_low = after(expert_weight, early)[0].astype(bf16)
    expert_all = gather_relative(expert_low, "tensor", [2, 1])
    expert_grads = trade(after(mm(place, grad_rows.astype(bf16)).astype(bf16), late))

    out_weights = [out_weight] + [swap(out_weight, "tensor", j) for j in range(1, tensor_count)]
    context, chances, totals, qkv = attention_forward(info, row_blocks, gain_one, weight)
    context, expert_grads, out_weights = lax.optimization_barrier((context, expert_grads, out_weights))
    context_own = lax.all_to_all(context, "tensor", 0, 0, tiled=True)

    middle, root_two, shares, gate, slots = middle_part(
        info, rows, context_own, out_weights, gain_two, router_rows, place, match, valid_scale
    )
    expert_rows = trade(slots)
    turned_rows, keys_turned, third_query, context_rows = turn(info, row_blocks, after(qkv, slots), context)
    grads_all = gather_relative(expert_grads, "tensor", [2, 1])
    expert_rows, turned_rows, grads_all, expert_all = lax.optimization_barrier(
        (expert_rows, turned_rows, grads_all, expert_all)
    )
    expert_outs, expert_back = expert_part(expert_rows, expert_grads, expert_all)
    rows_all = gather_relative(expert_rows, "tensor", [2, 1])
    expert_grad, expert_square_sum = expert_gradient(rows_all, grads_all, after(expert_low, expert_back))
    expert_back = after(trade(expert_back), expert_grad)

    middle_grad, middle_turned, context_parts, gain_two_grad, router_grad = return_part(
        info, expert_back, place, middle, root_two, shares, gate, match, grad_rows, gain_two, router_rows, out_weights
    )
    context_grad = lax.all_to_all(context_parts, "tensor", 0, 0, tiled=True)
    middle_all = gather_relative(middle_turned, "tensor", [2, 1])
    expert_outs = trade(after(expert_outs, context_parts))

    packed = attention_backward(context_grad, context, chances, totals, qkv, keys_turned, third_query)
    weight_grad, gain_one_grad = weight_gradient(
        info, turned_rows, packed, middle_all, context_rows, weight, gain_one.reshape(width, 1)
    )
    weight_grad, packed, expert_outs = lax.optimization_barrier((weight_grad, packed, expert_outs))
    weight_came = lax.all_to_all(weight_grad.reshape(dp_count, -1, width), "dp", 0, 0, tiled=True)
    attention_grad = unpack_columns(jnp.sum(weight_came.astype(f32), axis=0))
    input_parts = mm_nt(packed, weight).astype(bf16).reshape(tensor_count, quarter, width)
    gain_one_grad = after(gain_one_grad, input_parts)
    input_came = lax.all_to_all(input_parts, "tensor", 0, 0, tiled=True)
    first_grad = jnp.sum(input_came.astype(f32), axis=0)
    input_grad = middle_grad + norm_backward(rows, root_one, gain_one, first_grad)
    picked = mm_tn(place, expert_outs)
    branch = gate * valid_scale * picked
    block_output = middle + branch

    small_grad = jnp.concatenate([gain_one_grad.reshape(1, width), gain_two_grad, router_grad], axis=0)
    small_cut = small_grad.reshape(-1, device_count, share).transpose(1, 0, 2).reshape(device_count, -1)
    small_cut = jnp.pad(small_cut, ((0, 0), (0, -small_cut.shape[1] % 1024))).reshape(device_count, -1, LANES)
    small_own = jnp.sum(lax.all_to_all(small_cut, everyone, 0, 0, tiled=True), axis=0)
    small_own = small_own.reshape(-1)[: (2 + expert_count) * share].reshape(2 + expert_count, share)
    gains_grad, router_own = small_own[:2], small_own[2:].T

    square_sum = (
        jnp.sum(attention_grad * attention_grad) + jnp.sum(expert_square_sum) + jnp.sum(small_own * small_own)
    )
    square_sums = lax.all_to_all(jnp.full((device_count, 8, LANES), square_sum), everyone, 0, 0, tiled=True)
    grad_norm = jnp.sqrt(jnp.sum(square_sums[:, 0, 0]))
    factor = jnp.minimum(1.0, clip_limit / (grad_norm + norm_epsilon))
    attention_rate = jnp.array(
        [0.71 / math.sqrt(D), 0.71 / math.sqrt(D), 0.83 / math.sqrt(D), 0.79 / math.sqrt(H * DH)],
        f32,
    ).reshape(4, 1, 1)
    expert_rate = jnp.array([0.4 * math.sqrt(expert_count / D), 1.38 * math.sqrt(expert_count / FF)], f32)
    attention_new = adam_update(
        attention_weight, attention_mean, attention_square, attention_grad * factor, attention_rate
    )
    expert_new = adam_experts(
        factor, expert_rate, expert_weight[0], expert_mean[0], expert_square[0], expert_grad
    )
    router_new = adam_update(
        router_matrix, router_mean, router_square, router_own * factor, 0.24 / math.sqrt(D)
    )
    gains_new = adam_update(norm_gains, gains_mean, gains_square, gains_grad * factor, 0.5)
    return (
        block_output[None],
        input_grad[None],
        grad_norm,
        *attention_new,
        *[part[None] for part in expert_new],
        *router_new,
        *gains_new,
        branch[None],
    )


def solution(mesh):
    rows = P("dp", "tensor", None)
    attention = P(None, "dp", "tensor")
    expert = P("dp", None, None, "tensor")
    router = P(("dp", "tensor"), None)
    gains = P(None, ("dp", "tensor"))
    weights = (attention,) * 3 + (expert,) * 3 + (router,) * 3 + (gains,) * 3
    return jax.shard_map(
        on_device,
        mesh=mesh,
        in_specs=(rows, rows, P("dp"), rows) + weights,
        out_specs=(rows, rows, P()) + weights + (rows,),
        check_vma=False,
    )
```

```python
import math

import jax
import jax.numpy as jnp
from jax import lax
from jax.experimental import pallas as pl
from jax.experimental.pallas import tpu as pltpu
from jax.sharding import PartitionSpec as P

D = 768
H = 12
DH = 64
FF = 3072
STEP = 10

HIGHEST = lax.Precision.HIGHEST
norm_epsilon = 1e-06
beta_first = 0.9
beta_second = 0.999
adam_epsilon = 1e-08
decay_factor = 0.01
clip_limit = 1.0
masked_score = -1e30
score_scale = 1.0 / math.sqrt(DH)
bf16 = jnp.bfloat16
f32 = jnp.float32
MIB = 1 << 20
LANES = 128


DP = ("dh", "dl")
TENSOR = ("th", "tl")
EVERYONE = DP + TENSOR


def swap(values, axis, mask):
    count = lax.axis_size(axis)
    return lax.ppermute(values, axis, [(i, i ^ mask) for i in range(count)])


def bits_of(count):
    return [1 << b for b in range(count.bit_length() - 1)]


def gather_relative(block, axis, order):
    held = {0: block}
    for mask in order:
        for j in list(held):
            held[j ^ mask] = swap(held[j], axis, mask)
    return [held[j] for j in range(len(held))]


def mm(a, b):
    return jnp.dot(a, b, preferred_element_type=f32)


def mm_nt(a, b, precision=None):
    return lax.dot_general(
        a, b, (((1,), (1,)), ((), ())), preferred_element_type=f32, precision=precision
    )


def mm_tn(a, b, precision=None):
    return lax.dot_general(
        a, b, (((0,), (0,)), ((), ())), preferred_element_type=f32, precision=precision
    )


def norm_root(values):
    return lax.rsqrt(jnp.mean(values * values, axis=-1, keepdims=True) + norm_epsilon)


def norm_backward(values, root, gain_row, grad):
    scaled = values * root
    inner = grad * gain_row
    centre = jnp.mean(inner * scaled, axis=-1, keepdims=True)
    return root * (inner - scaled * centre)


def gelu_pair(values):
    c = math.sqrt(2.0 / math.pi)
    square = values * values
    th = jnp.tanh(c * values * (1.0 + 0.044715 * square))
    half = 0.5 * (1.0 + th)
    slope = half + 0.5 * values * (1.0 - th * th) * c * (1.0 + 3.0 * 0.044715 * square)
    return values * half, slope


def adam_update(weight, moment_one, moment_two, gradient, step_rate):
    moment_one_next = beta_first * moment_one + (1.0 - beta_first) * gradient
    moment_two_next = beta_second * moment_two + (1.0 - beta_second) * gradient * gradient
    corrected_one = moment_one_next / (1.0 - beta_first**STEP)
    corrected_two = moment_two_next / (1.0 - beta_second**STEP)
    weight_next = weight - step_rate * (
        corrected_one / (jnp.sqrt(corrected_two) + adam_epsilon) + decay_factor * weight
    )
    return (weight_next, moment_one_next, moment_two_next)


def shape_of(shape, dtype):
    return jax.ShapeDtypeStruct(shape, dtype)


def whole(shape):
    return pl.BlockSpec(shape, lambda *_: (0,) * len(shape))


def scalars():
    return pl.BlockSpec(memory_space=pltpu.SMEM)


def params(limit):
    return pltpu.CompilerParams(vmem_limit_bytes=limit * MIB)


def pack_columns(q, k, v, o):
    wide = LANES
    return jnp.concatenate(
        [q[:, :wide], k[:, :wide], v[:, :wide], o[:, :wide], q[:, wide:], k[:, wide:], v[:, wide:], o[:, wide:]],
        axis=1,
    )


def unpack_columns(packed):
    wide, rest = LANES, DH
    end = 4 * wide
    return jnp.stack(
        [
            jnp.concatenate(
                [packed[:, i * wide : (i + 1) * wide], packed[:, end + i * rest : end + (i + 1) * rest]], axis=1
            )
            for i in range(4)
        ]
    )


def assemble_kernel(count, info, *refs):
    shards, weight, turned = refs[:count], refs[count], refs[count + 1]
    rows = shards[0].shape[0]
    for j, ref in enumerate(shards):
        start = pl.multiple_of((info[2] ^ j) * rows, rows) if count > 1 else 0
        weight[pl.ds(start, rows), :] = ref[...]
    turned[:LANES, :] = weight[:, 3 * LANES : 4 * LANES].T
    turned[LANES:, :] = weight[:, 5 * LANES :].T[DH:]


def assemble(info, shards):
    rows, columns = shards[0].shape
    shapes = [shape_of((rows * len(shards), columns), bf16), shape_of((3 * DH, rows * len(shards)), bf16)]
    return pl.pallas_call(
        lambda *refs: assemble_kernel(len(shards), *refs),
        in_specs=[scalars()] + [whole((rows, columns))] * len(shards),
        out_specs=[whole(s.shape) for s in shapes],
        out_shape=shapes,
        compiler_params=params(12),
        cost_estimate=pl.CostEstimate(flops=0, bytes_accessed=4 * MIB, transcendentals=0),
        name="assemble",
    )(info, *shards)


def project_kernel(quarter, blocks, info, x0, x1, x2, x3, gain, weight, qkv, kaug, vt):
    for j, ref in enumerate((x0, x1, x2, x3)):
        start = pl.multiple_of((info[0] ^ j) * quarter, quarter)
        rows = pl.ds(start, quarter)
        scaled = (ref[...].astype(f32) * gain[...]).astype(bf16)
        first = mm(scaled, weight[:, : 3 * LANES]).astype(bf16)
        second = mm(scaled, weight[:, 4 * LANES :]).astype(bf16)
        qkv[rows, : 3 * LANES] = first
        qkv[rows, 3 * LANES :] = second
        kaug[rows, :LANES] = first[:, LANES : 2 * LANES]
        lane = lax.broadcasted_iota(jnp.int32, (quarter, LANES), 1)
        row = lax.broadcasted_iota(jnp.int32, (quarter, LANES), 0) + start
        hidden = jnp.where((lane == 0) & (row >= info[1]), masked_score, 0.0)
        kaug[rows, LANES:] = jnp.where(lane < DH, hidden, second[:, :LANES].astype(f32)).astype(bf16)
        values = first[:, 2 * LANES :].T
        vt[0, :DH, rows] = values[:DH]
        vt[1, :DH, rows] = values[DH:]
        vt[2, :DH, rows] = second[:, LANES:].T[:DH]
    full_len = quarter * blocks
    tail = (lax.broadcasted_iota(jnp.int32, (16, full_len), 0) == 0).astype(f32).astype(bf16)
    for h in range(3):
        vt[h, DH:, :] = tail


def project(info, rows, gain, weight):
    quarter, width = rows[0].shape
    blocks = len(rows)
    full_len = quarter * blocks
    shapes = [
        shape_of((full_len, 5 * LANES), bf16),
        shape_of((full_len, 2 * LANES), bf16),
        shape_of((3, DH + 16, full_len), bf16),
    ]
    return pl.pallas_call(
        lambda *refs: project_kernel(quarter, blocks, *refs),
        in_specs=[scalars()] + [whole((quarter, width))] * 4 + [whole((1, width)), whole(weight.shape)],
        out_specs=[whole(s.shape) for s in shapes],
        out_shape=shapes,
        compiler_params=params(16),
        cost_estimate=pl.CostEstimate(
            flops=2 * full_len * width * 5 * LANES, bytes_accessed=5 * MIB, transcendentals=0
        ),
        name="project",
    )(info, *rows, gain, weight)


def attention_kernel(qkv, kaug, vt, context, chances, totals):
    quarter = context.shape[2]
    step = pl.program_id(0)
    rows = pl.ds(pl.multiple_of(step * quarter, quarter), quarter)
    q01 = (qkv[rows, :LANES].astype(f32) * score_scale).T.astype(bf16)
    q2 = (qkv[rows, 3 * LANES : 4 * LANES].astype(f32) * score_scale).T.astype(bf16)[:DH]
    ones = (lax.broadcasted_iota(jnp.int32, (DH, quarter), 0) == 0).astype(f32).astype(bf16)
    zeros = jnp.zeros((DH, quarter), bf16)
    queries = (
        jnp.concatenate([q01[:DH], zeros, ones, zeros], axis=0),
        jnp.concatenate([zeros, q01[DH:], ones, zeros], axis=0),
        jnp.concatenate([zeros, zeros, ones, q2], axis=0),
    )
    for h in range(3):
        scores = mm(kaug[...], queries[h])
        top = jnp.max(scores, axis=0, keepdims=True)
        low = jnp.exp(scores - top).astype(bf16)
        chances[h] = low
        summed = mm(vt[h], low)
        part = 1.0 / summed[DH : DH + 1]
        totals[0, h : h + 1, :] = part
        context[0, h * DH : (h + 1) * DH, :] = (summed[:DH] * part).astype(bf16)


def attention_forward(qkv, kaug, vt, blocks):
    full_len = qkv.shape[0]
    quarter = full_len // blocks
    inner = 3 * DH
    return pl.pallas_call(
        attention_kernel,
        grid=(blocks,),
        in_specs=[whole(qkv.shape), whole(kaug.shape), whole(vt.shape)],
        out_specs=[
            pl.BlockSpec((1, inner, quarter), lambda i: (i, 0, 0)),
            pl.BlockSpec((3, full_len, quarter), lambda i: (0, 0, i)),
            pl.BlockSpec((1, 3, quarter), lambda i: (i, 0, 0)),
        ],
        out_shape=[
            shape_of((blocks, inner, quarter), bf16),
            shape_of((3, full_len, full_len), bf16),
            shape_of((blocks, 3, quarter), f32),
        ],
        compiler_params=params(18),
        cost_estimate=pl.CostEstimate(
            flops=2 * full_len * 2 * full_len * inner,
            bytes_accessed=10 * MIB,
            transcendentals=3 * full_len * full_len,
        ),
        name="attend",
    )(qkv, kaug, vt)


def turn_kernel(quarter, blocks, info, x0, x1, x2, x3, qkv, context, xt, kt, q2, cn):
    for j, ref in enumerate((x0, x1, x2, x3)):
        xt[info[0] ^ j] = ref[...].T
    for j in range(blocks):
        rows = slice(j * quarter, (j + 1) * quarter)
        third = qkv[rows, 3 * LANES : 4 * LANES].T
        kt[:LANES, rows] = qkv[rows, LANES : 2 * LANES].T
        kt[LANES:, rows] = third[DH:]
        zeros = jnp.zeros((DH, quarter), bf16)
        q2[rows, :] = jnp.concatenate([zeros, third[:DH]], axis=0).T
        cn[rows, :LANES] = context[j, :LANES, :].T
        cn[rows, LANES:] = jnp.concatenate([zeros, context[j, LANES:, :]], axis=0).T


def turn(info, rows, qkv, context):
    quarter, width = rows[0].shape
    blocks = len(rows)
    full_len = quarter * blocks
    shapes = [
        shape_of((blocks, width, quarter), bf16),
        shape_of((3 * DH, full_len), bf16),
        shape_of((full_len, LANES), bf16),
        shape_of((full_len, 2 * LANES), bf16),
    ]
    return pl.pallas_call(
        lambda *refs: turn_kernel(quarter, blocks, *refs),
        in_specs=[scalars()] + [whole((quarter, width))] * 4 + [whole(qkv.shape), whole(context.shape)],
        out_specs=[whole(s.shape) for s in shapes],
        out_shape=shapes,
        compiler_params=params(14),
        cost_estimate=pl.CostEstimate(flops=0, bytes_accessed=8 * MIB, transcendentals=0),
        name="turn",
    )(info, *rows, qkv, context)


def two_columns(column):
    high = column.astype(bf16).astype(f32)
    lane = lax.broadcasted_iota(jnp.int32, (column.shape[0], LANES), 1)
    return jnp.where(lane == 0, high, jnp.where(lane == 1, column - high, 0.0)).astype(bf16)


def middle_kernel(
    info, rows, context, w0, w1, w2, w3, gain, router, place, match, valid, middle, root, chances, gate, slots
):
    total = rows[...]
    for j, ref in enumerate((w0, w1, w2, w3)):
        total = total + mm_tn(context[info[0] ^ j], ref[...])
    middle[...] = total
    scale = norm_root(total)
    root[...] = scale
    hidden = total * scale * gain[...]
    scores = mm_nt(hidden, router[...], HIGHEST)
    powers = jnp.exp(scores - jnp.max(scores, axis=-1, keepdims=True))
    share = powers / jnp.sum(powers, axis=-1, keepdims=True)
    chances[...] = share
    own = jnp.sum(share * match[...], axis=-1, keepdims=True)
    gate[...] = own
    width = rows.shape[1]
    slots[:, :width] = mm(place[...], hidden.astype(bf16)).astype(bf16)
    slots[:, width:] = mm(place[...], two_columns(own * valid[...])).astype(bf16)


def middle_part(info, rows, context, out_weights, gain, router, place, match, valid):
    quarter, width = rows.shape
    experts = router.shape[0]
    shapes = [
        shape_of((quarter, width), f32),
        shape_of((quarter, 1), f32),
        shape_of((quarter, experts), f32),
        shape_of((quarter, 1), f32),
        shape_of((place.shape[0], width + LANES), bf16),
    ]
    arrays = (rows, context, *out_weights, gain, router, place, match, valid)
    return pl.pallas_call(
        middle_kernel,
        in_specs=[scalars()] + [whole(a.shape) for a in arrays],
        out_specs=[whole(s.shape) for s in shapes],
        out_shape=shapes,
        compiler_params=params(16),
        cost_estimate=pl.CostEstimate(
            flops=4 * quarter * width * width, bytes_accessed=6 * MIB, transcendentals=0
        ),
        name="middle",
    )(info, *arrays)


def expert_kernel(rows, grads, near, other, out, back, held, arrived):
    width = grads.shape[1]
    sources = (near.at[0], near.at[1], other.at[0], other.at[1])
    copies = [pltpu.make_async_copy(ref, held.at[i], arrived.at[i]) for i, ref in enumerate(sources)]
    for copy in copies:
        copy.start()
    out_total, back_total = None, None
    for i, copy in enumerate(copies):
        copy.wait()
        inward, outward = held[i, 0], held[i, 1]
        grad = mm(grads[...], outward)
        active, slope = gelu_pair(mm(rows[:, :width], inward))
        part = mm_nt(active.astype(bf16), outward)
        back_part = mm_nt((grad * slope).astype(bf16), inward)
        out_total = part if i == 0 else out_total + part
        back_total = back_part if i == 0 else back_total + back_part
    result = out_total.astype(bf16)
    out[...] = result
    back[:, :width] = back_total.astype(bf16)
    match = jnp.sum(grads[...].astype(f32) * result.astype(f32), axis=-1, keepdims=True)
    back[:, width:] = two_columns(match)


def expert_part(rows, grads, weights):
    slots, width = grads.shape
    hidden = weights[0].shape[3]
    count = 2 * len(weights)
    shapes = [shape_of((slots, width), bf16), shape_of((slots, width + LANES), bf16)]
    return pl.pallas_call(
        expert_kernel,
        in_specs=[whole(rows.shape), whole(grads.shape)] + [pl.BlockSpec(memory_space=pl.ANY)] * 2,
        out_specs=[whole(s.shape) for s in shapes],
        out_shape=shapes,
        scratch_shapes=[pltpu.VMEM((count,) + weights[0].shape[1:], bf16), pltpu.SemaphoreType.DMA((count,))],
        compiler_params=params(30),
        cost_estimate=pl.CostEstimate(
            flops=8 * slots * width * hidden * count,
            bytes_accessed=12 * MIB,
            transcendentals=slots * hidden * count,
        ),
        name="experts",
    )(rows, grads, *weights)


def expert_grad_kernel(count, *refs):
    rows, grads, weight = refs[:count], refs[count : 2 * count], refs[2 * count]
    out, square, row_all, grad_all, inner_all, active_all = refs[2 * count + 1 :]
    slots, width = grads[0].shape
    for j in range(count):
        at = slice(j * slots, (j + 1) * slots)
        gate = rows[j][:, width : width + 1].astype(f32) + rows[j][:, width + 1 : width + 2].astype(f32)
        row_all[at, :] = rows[j][:, :width]
        grad_all[at, :] = (grads[j][...].astype(f32) * gate).astype(bf16)
        back = mm(grads[j][...], weight[1])
        active, slope = gelu_pair(mm(rows[j][:, :width], weight[0]))
        inner_all[at, :] = (back * slope * gate).astype(bf16)
        active_all[at, :] = active.astype(bf16)
    first = mm_tn(row_all[...], inner_all[...])
    out[0] = first
    second = mm_tn(grad_all[...], active_all[...])
    out[1] = second
    square[...] = jnp.sum(first * first + second * second, axis=0, keepdims=True)


def expert_gradient(rows, grads, weight):
    count = len(rows)
    slots, width = grads[0].shape
    hidden = weight.shape[2]
    arrays = (*rows, *grads, weight)
    shapes = [shape_of((2, width, hidden), f32), shape_of((1, hidden), f32)]
    return pl.pallas_call(
        lambda *refs: expert_grad_kernel(count, *refs),
        in_specs=[whole(a.shape) for a in arrays],
        out_specs=[whole(s.shape) for s in shapes],
        out_shape=shapes,
        scratch_shapes=[pltpu.VMEM((count * slots, width), bf16)] * 2 + [pltpu.VMEM((count * slots, hidden), bf16)] * 2,
        compiler_params=params(38),
        cost_estimate=pl.CostEstimate(
            flops=8 * slots * width * hidden * count,
            bytes_accessed=12 * MIB,
            transcendentals=slots * hidden * count,
        ),
        name="expert_gradient",
    )(*arrays)


def return_kernel(
    info, back, place, middle, root, chances, gate, match, cotangent, gain, router, w0, w1, w2, w3,
    grad, turned, parts, gain_grad, router_grad,
):
    width = middle.shape[1]
    came = mm_tn(place[...], back[...])
    gate_grad = came[:, width : width + 1] + came[:, width + 1 : width + 2]
    own = gate[...]
    score_grad = own * (match[...] - chances[...]) * gate_grad
    scaled = middle[...] * root[...]
    hidden = scaled * gain[...]
    router_grad[...] = mm_tn(score_grad, hidden, HIGHEST)
    second = own * came[:, :width] + jnp.dot(
        score_grad, router[...], precision=HIGHEST, preferred_element_type=f32
    )
    gain_grad[...] = jnp.sum(second * scaled, axis=0, keepdims=True)
    inner = second * gain[...]
    centre = jnp.mean(inner * scaled, axis=-1, keepdims=True)
    total = cotangent[...] + root[...] * (inner - scaled * centre)
    grad[...] = total
    low = total.astype(bf16)
    turned[...] = low.T
    for j, ref in enumerate((w0, w1, w2, w3)):
        parts[info[0] ^ j] = mm_nt(ref[...], low).astype(bf16)


def return_part(info, back, place, middle, root, chances, gate, match, cotangent, gain, router, out_weights):
    quarter, width = middle.shape
    experts = router.shape[0]
    inner = out_weights[0].shape[0]
    shapes = [
        shape_of((quarter, width), f32),
        shape_of((width, quarter), bf16),
        shape_of((len(out_weights), inner, quarter), bf16),
        shape_of((1, width), f32),
        shape_of((experts, width), f32),
    ]
    arrays = (back, place, middle, root, chances, gate, match, cotangent, gain, router, *out_weights)
    return pl.pallas_call(
        return_kernel,
        in_specs=[scalars()] + [whole(a.shape) for a in arrays],
        out_specs=[whole(s.shape) for s in shapes],
        out_shape=shapes,
        compiler_params=params(16),
        cost_estimate=pl.CostEstimate(
            flops=4 * quarter * width * width, bytes_accessed=7 * MIB, transcendentals=0
        ),
        name="returned",
    )(info, *arrays)


def attention_back_kernel(blocks, grads, context, chances, totals, qkv, kt, q2, packed, vaug, k01, k2, v01, v2):
    step = pl.program_id(0)
    quarter = grads.shape[2]

    @pl.when(step == 0)
    def _():
        vaug[:, :LANES] = qkv[:, 2 * LANES : 3 * LANES]
        lane = lax.broadcasted_iota(jnp.int32, (vaug.shape[0], LANES), 1)
        ones = jnp.where(lane < DH + 2, 1.0, 0.0)
        vaug[:, LANES:] = jnp.where(lane < DH, qkv[:, 4 * LANES :].astype(f32), ones).astype(bf16)
        for ref in (k01, k2, v01, v2):
            ref[...] = jnp.zeros(ref.shape, f32)

    rows = pl.ds(pl.multiple_of(step * quarter, quarter), quarter)
    raw = grads[0].astype(f32)
    scale = totals[0]
    scaled = [raw[h * DH : (h + 1) * DH] * scale[h : h + 1] for h in range(3)]
    heads = jnp.concatenate(scaled, axis=0).astype(bf16)
    lane = lax.broadcasted_iota(jnp.int32, (quarter, LANES), 1)
    row = lax.broadcasted_iota(jnp.int32, (DH, quarter), 0)
    zeros = jnp.zeros((DH, quarter), bf16)
    q01 = qkv[rows, :LANES].astype(f32)
    g01 = heads[:LANES].T.astype(f32)
    g2 = jnp.concatenate([heads[LANES:], zeros], axis=0).T
    query_parts = []
    for h in range(3):
        part = heads[h * DH : (h + 1) * DH]
        centre = -jnp.sum(
            part.astype(f32) * context[0, h * DH : (h + 1) * DH, :].astype(f32), axis=0, keepdims=True
        )
        high = centre.astype(bf16).astype(f32)
        tail = jnp.where(row == 0, high, jnp.where(row == 1, centre - high, 0.0)).astype(bf16)
        pieces = [zeros, zeros, zeros, tail]
        pieces[h] = part
        chance_grad = mm(vaug[...], jnp.concatenate(pieces, axis=0))
        low = chances[h]
        score_grad = (low.astype(f32) * chance_grad).astype(bf16)
        query_parts.append(mm(kt[h * DH : (h + 1) * DH, :], score_grad) * score_scale)
        if h < 2:
            inside = (lane >= h * DH) & (lane < (h + 1) * DH)
            k01[...] += mm(score_grad, jnp.where(inside, q01, 0.0).astype(bf16))
            v01[...] += mm(low, jnp.where(inside, g01, 0.0).astype(bf16))
        else:
            k2[...] += mm(score_grad, q2[rows, :])
            v2[...] += mm(low, g2)
    packed[rows, :LANES] = jnp.concatenate(query_parts[:2], axis=0).T.astype(bf16)
    packed[rows, 4 * LANES : 5 * LANES] = (
        jnp.concatenate([query_parts[2], jnp.zeros((DH, quarter), f32)], axis=0).T.astype(bf16)
    )

    @pl.when(step == blocks - 1)
    def _():
        packed[:, LANES : 2 * LANES] = (k01[...] * score_scale).astype(bf16)
        packed[:, 2 * LANES : 3 * LANES] = v01[...].astype(bf16)
        packed[:, 3 * LANES : 4 * LANES] = jnp.zeros(k01.shape, bf16)
        packed[:, 4 * LANES : 5 * LANES] = packed[:, 4 * LANES : 5 * LANES] + (k2[...] * score_scale).astype(bf16)
        packed[:, 5 * LANES :] = v2[...].astype(bf16)


def attention_backward(grads, context, chances, totals, qkv, kt, q2):
    blocks, inner, quarter = grads.shape
    full_len = quarter * blocks
    block = pl.BlockSpec((1, inner, quarter), lambda i: (i, 0, 0))
    return pl.pallas_call(
        lambda *refs: attention_back_kernel(blocks, *refs),
        grid=(blocks,),
        in_specs=[
            block,
            block,
            pl.BlockSpec((3, full_len, quarter), lambda i: (0, 0, i)),
            pl.BlockSpec((1, 3, quarter), lambda i: (i, 0, 0)),
            whole(qkv.shape),
            whole(kt.shape),
            whole(q2.shape),
        ],
        out_specs=whole((full_len, 6 * LANES)),
        out_shape=shape_of((full_len, 6 * LANES), bf16),
        scratch_shapes=[pltpu.VMEM((full_len, 2 * LANES), bf16)] + [pltpu.VMEM((full_len, LANES), f32)] * 4,
        compiler_params=params(22),
        cost_estimate=pl.CostEstimate(
            flops=8 * full_len * full_len * inner, bytes_accessed=12 * MIB, transcendentals=0
        ),
        name="attend_back",
    )(grads, context, chances, totals, qkv, kt, q2)


def weight_grad_kernel(blocks, info, xt, packed, g0, g1, g2, g3, cn, weight, gain, out, gain_grad):
    quarter = xt.shape[2]
    total, outer = None, None
    for j, ref in enumerate((g0, g1, g2, g3)):
        rows = slice(j * quarter, (j + 1) * quarter)
        there = pl.ds(pl.multiple_of((info[0] ^ j) * quarter, quarter), quarter)
        part = mm(xt[j], packed[rows, :])
        own = mm(ref[...], cn[there, :])
        total = part if total is None else total + part
        outer = own if outer is None else outer + own
    gain_grad[...] = jnp.sum(total * weight[...].astype(f32), axis=1, keepdims=True)
    total = total * gain[...]
    out[:, : 3 * LANES] = total[:, : 3 * LANES].astype(bf16)
    out[:, 3 * LANES : 4 * LANES] = outer[:, :LANES].astype(bf16)
    out[:, 4 * LANES : 5 * LANES] = total[:, 4 * LANES : 5 * LANES].astype(bf16)
    out[:, 5 * LANES :] = (total[:, 5 * LANES :] + outer[:, LANES:]).astype(bf16)


def weight_gradient(info, xt, packed, grads, cn, weight, gain):
    blocks, width, quarter = xt.shape
    tall = 256
    full_len = quarter * blocks
    return pl.pallas_call(
        lambda *refs: weight_grad_kernel(blocks, *refs),
        grid=(width // tall,),
        in_specs=[
            scalars(),
            pl.BlockSpec((blocks, tall, quarter), lambda i: (0, i, 0)),
            whole(packed.shape),
            *[pl.BlockSpec((tall, quarter), lambda i: (i, 0))] * blocks,
            whole(cn.shape),
            pl.BlockSpec((tall, 6 * LANES), lambda i: (i, 0)),
            pl.BlockSpec((tall, 1), lambda i: (i, 0)),
        ],
        out_specs=[pl.BlockSpec((tall, 6 * LANES), lambda i: (i, 0)), pl.BlockSpec((tall, 1), lambda i: (i, 0))],
        out_shape=[shape_of((width, 6 * LANES), bf16), shape_of((width, 1), f32)],
        compiler_params=params(16),
        cost_estimate=pl.CostEstimate(
            flops=2 * full_len * width * 8 * LANES, bytes_accessed=8 * MIB, transcendentals=0
        ),
        name="weight_gradient",
    )(info, xt, packed, *grads, cn, weight, gain)


def adam_kernel(rates, weight, first, second, gradient, weight_out, first_out, second_out):
    grad = gradient[...] * rates[0]
    rate = rates[1 + pl.program_id(0)]
    result = adam_update(weight[...], first[...], second[...], grad, rate)
    weight_out[...], first_out[...], second_out[...] = result


def adam_experts(factor, rates, weight, first, second, gradient):
    _, tall, wide = weight.shape
    cut = tall // 4
    block = pl.BlockSpec((1, cut, wide), lambda i, j: (i, j, 0))
    return pl.pallas_call(
        adam_kernel,
        grid=(2, 4),
        in_specs=[scalars()] + [block] * 4,
        out_specs=[block] * 3,
        out_shape=[shape_of(weight.shape, f32)] * 3,
        compiler_params=params(12),
        cost_estimate=pl.CostEstimate(flops=2 * weight.size * 20, bytes_accessed=28 * MIB, transcendentals=0),
        name="adam",
    )(jnp.concatenate([factor[None], rates]), weight, first, second, gradient)


def after(value, *others):
    return lax.optimization_barrier((value, *others))[0]


def on_device(
    inputs,
    cotangent,
    lengths,
    routes,
    attention_weight,
    attention_mean,
    attention_square,
    expert_weight,
    expert_mean,
    expert_square,
    router_matrix,
    router_mean,
    router_square,
    norm_gains,
    gains_mean,
    gains_square,
):
    quarter, width = inputs.shape[1:]
    dp_count, tensor_count = lax.axis_size(DP), lax.axis_size(TENSOR)
    device_count = dp_count * tensor_count
    expert_count = router_matrix.shape[1]
    capacity = max(2, (5 * quarter + 4 * expert_count - 1) // (4 * expert_count))
    own_dp, own_tensor = lax.axis_index(DP), lax.axis_index(TENSOR)
    share = router_matrix.shape[0]
    rows, grad_rows, length = inputs[0], cotangent[0], lengths[0]
    info = jnp.stack([own_tensor, length, own_dp]).astype(jnp.int32)

    weight_own = pack_columns(*attention_weight.astype(bf16))
    root_one = norm_root(rows)
    scaled_one = (rows * root_one).astype(bf16)
    few = dp_count <= 8
    if few:
        shards = gather_relative(weight_own, DP, bits_of(dp_count)[::-1])
        late = shards[dp_count - 2]
    row_blocks = gather_relative(scaled_one, TENSOR, [2, 1])
    if not few:
        shards = [lax.all_gather(weight_own, DP, axis=0, tiled=True)]
        late = row_blocks[2]
    weight, out_weight = assemble(info, shards)
    small = jnp.concatenate([norm_gains, router_matrix.T], axis=0)
    small = jnp.pad(small.reshape(-1), (0, -small.size % 1024)).reshape(-1, LANES)
    small = lax.all_to_all(
        jnp.broadcast_to(small[None], (device_count,) + small.shape), EVERYONE, 0, 0, tiled=True
    )
    small = small.reshape(device_count, -1)[:, : (2 + expert_count) * share]
    small = small.reshape(device_count, 2 + expert_count, share).transpose(1, 0, 2).reshape(-1, width)
    gain_one, gain_two, router_rows = small[:1], small[1:2], small[2:]

    local_valid = own_tensor * quarter + jnp.arange(quarter) < length
    valid_scale = local_valid.astype(f32)[:, None]
    chosen = routes[0, :, 0]
    match = (chosen[:, None] == jnp.arange(expert_count)[None, :]).astype(f32)
    lower = (jnp.arange(quarter)[:, None] >= jnp.arange(quarter)[None, :]).astype(f32)
    rank = jnp.sum((mm(lower, match * valid_scale) - 1.0) * match, axis=1).astype(jnp.int32)
    slot = jnp.where(local_valid, chosen * capacity + rank, -1)
    slot_count = expert_count * capacity
    place = (jnp.arange(slot_count)[:, None] == slot[None, :]).astype(bf16)

    def trade(values):
        blocks = values.reshape(expert_count, capacity, values.shape[1])
        return lax.all_to_all(blocks, DP, 0, 0, tiled=True).reshape(values.shape)

    expert_low = after(expert_weight, scaled_one)[0].astype(bf16)
    expert_near = lax.all_to_all(jnp.stack([expert_low] * 2), "th", 0, 0, tiled=True)
    expert_grads = trade(after(mm(place, grad_rows.astype(bf16)).astype(bf16), late))

    out_weights = [out_weight] + [swap(out_weight, TENSOR, j) for j in range(1, tensor_count)]
    qkv, keys_wide, values_turned = project(info, row_blocks, gain_one, weight)
    context, chances, totals = attention_forward(qkv, keys_wide, values_turned, tensor_count)
    context, expert_grads, out_weights = lax.optimization_barrier((context, expert_grads, out_weights))
    context_own = lax.all_to_all(context, TENSOR, 0, 0, tiled=True)

    middle, root_two, shares, gate, slots = middle_part(
        info, rows, context_own, out_weights, gain_two, router_rows, place, match, valid_scale
    )
    expert_rows = trade(slots)
    turned_rows, keys_turned, third_query, context_rows = turn(info, row_blocks, after(qkv, slots), context)
    expert_other = swap(after(expert_near, slots), TENSOR, 1)
    grads_all = gather_relative(after(expert_grads, slots), TENSOR, [2, 1])
    expert_rows, turned_rows = lax.optimization_barrier((expert_rows, turned_rows))
    expert_outs, expert_back = expert_part(expert_rows, expert_grads, [expert_near, expert_other])
    expert_rows, expert_back = lax.optimization_barrier((expert_rows, expert_back))
    rows_all = gather_relative(expert_rows, TENSOR, [2, 1])
    expert_back = trade(expert_back)

    middle_grad, middle_turned, context_parts, gain_two_grad, router_grad = return_part(
        info, expert_back, place, middle, root_two, shares, gate, match, grad_rows, gain_two, router_rows, out_weights
    )
    context_grad = lax.all_to_all(context_parts, TENSOR, 0, 0, tiled=True)
    middle_all = gather_relative(middle_turned, TENSOR, [2, 1])
    small_grad = jnp.concatenate([gain_two_grad, router_grad], axis=0)
    small_cut = small_grad.reshape(-1, device_count, share).transpose(1, 0, 2).reshape(device_count, -1)
    small_cut = jnp.pad(small_cut, ((0, 0), (0, -small_cut.shape[1] % 1024))).reshape(device_count, -1, LANES)
    small_own = jnp.sum(lax.all_to_all(small_cut, EVERYONE, 0, 0, tiled=True), axis=0)
    small_own = small_own.reshape(-1)[: (1 + expert_count) * share].reshape(1 + expert_count, share)
    expert_outs = trade(after(expert_outs, context_parts))

    packed = attention_backward(context_grad, context, chances, totals, qkv, keys_turned, third_query)
    weight_grad, gain_one_grad = weight_gradient(
        info, turned_rows, packed, middle_all, context_rows, weight, gain_one.reshape(width, 1)
    )
    weight_grad, expert_outs, small_own, rows_all, expert_low = lax.optimization_barrier(
        (weight_grad, expert_outs, small_own, rows_all, expert_low)
    )
    weight_came = lax.all_to_all(weight_grad.reshape(dp_count, -1, width), DP, 0, 0, tiled=True)
    expert_grad, expert_square_sum = expert_gradient(rows_all, grads_all, expert_low)
    picked = mm_tn(place, expert_outs)
    branch = gate * valid_scale * picked
    block_output = middle + branch
    attention_grad = unpack_columns(jnp.sum(weight_came.astype(f32), axis=0))

    square_sum = (
        jnp.sum(attention_grad * attention_grad) + jnp.sum(expert_square_sum) + jnp.sum(small_own * small_own)
    )
    last = jnp.concatenate([gain_one_grad.reshape(-1, LANES), jnp.full((1, LANES), square_sum)], axis=0)
    last = jnp.pad(last, ((0, -last.shape[0] % 8), (0, 0)))
    last, packed = lax.optimization_barrier((last, packed))
    last_all = lax.all_to_all(jnp.broadcast_to(last[None], (device_count,) + last.shape), EVERYONE, 0, 0, tiled=True)
    last_sum = jnp.sum(last_all, axis=0)
    gain_one_full = last_sum[: width // LANES].reshape(1, width)
    gain_one_own = lax.dynamic_slice_in_dim(gain_one_full, lax.axis_index(EVERYONE) * share, share, axis=1)
    gains_grad = jnp.concatenate([gain_one_own, small_own[:1]], axis=0)
    router_own = small_own[1:].T
    grad_norm = jnp.sqrt(last_sum[width // LANES, 0] + jnp.sum(gain_one_full * gain_one_full))

    input_parts = mm_nt(packed, weight).astype(bf16)
    input_parts = [
        lax.dynamic_slice_in_dim(input_parts, (own_tensor ^ j) * quarter, quarter) for j in range(tensor_count)
    ]
    first_half = input_parts[0].astype(f32) + swap(input_parts[1], TENSOR, 1).astype(f32)
    second_half = input_parts[2].astype(f32) + swap(input_parts[3], TENSOR, 1).astype(f32)
    came = swap(second_half.astype(bf16), TENSOR, 2)
    input_grad = middle_grad + norm_backward(rows, root_one, gain_one, first_half + came.astype(f32))

    factor = jnp.minimum(1.0, clip_limit / (grad_norm + norm_epsilon))
    attention_rate = jnp.array(
        [0.71 / math.sqrt(D), 0.71 / math.sqrt(D), 0.83 / math.sqrt(D), 0.79 / math.sqrt(H * DH)],
        f32,
    ).reshape(4, 1, 1)
    expert_rate = jnp.array([0.4 * math.sqrt(expert_count / D), 1.38 * math.sqrt(expert_count / FF)], f32)
    attention_new = adam_update(
        attention_weight, attention_mean, attention_square, attention_grad * factor, attention_rate
    )
    expert_new = adam_experts(
        factor, expert_rate, expert_weight[0], expert_mean[0], expert_square[0], expert_grad
    )
    router_new = adam_update(
        router_matrix, router_mean, router_square, router_own * factor, 0.24 / math.sqrt(D)
    )
    gains_new = adam_update(norm_gains, gains_mean, gains_square, gains_grad * factor, 0.5)
    return (
        block_output[None],
        input_grad[None],
        grad_norm,
        *attention_new,
        *[part[None] for part in expert_new],
        *router_new,
        *gains_new,
        branch[None],
    )


def solution(mesh):
    names = mesh.axis_names
    dp_count, tensor_count = mesh.shape[names[0]], mesh.shape[names[1]]
    cut = jax.sharding.Mesh(mesh.devices.reshape(dp_count // 2, 2, tensor_count // 2, 2), EVERYONE)
    rows = P(DP, TENSOR, None)
    attention = P(None, DP, TENSOR)
    expert = P(DP, None, None, TENSOR)
    router = P(EVERYONE, None)
    gains = P(None, EVERYONE)
    weights = (attention,) * 3 + (expert,) * 3 + (router,) * 3 + (gains,) * 3
    return jax.shard_map(
        on_device,
        mesh=cut,
        in_specs=(rows, rows, P(DP), rows) + weights,
        out_specs=(rows, rows, P()) + weights + (rows,),
        check_vma=False,
    )
```

```python
import math

import jax
import jax.numpy as jnp
from jax import lax
from jax.experimental import pallas as pl
from jax.experimental.pallas import tpu as pltpu
from jax.sharding import PartitionSpec as P

D = 768
H = 12
DH = 64
FF = 3072
STEP = 10

HIGHEST = lax.Precision.HIGHEST
norm_epsilon = 1e-06
beta_first = 0.9
beta_second = 0.999
adam_epsilon = 1e-08
decay_factor = 0.01
clip_limit = 1.0
masked_score = -1e30
score_scale = 1.0 / math.sqrt(DH)
bf16 = jnp.bfloat16
f32 = jnp.float32
MIB = 1 << 20
LANES = 128


DP = ("dh", "dl")
TENSOR = ("th", "tl")
EVERYONE = DP + TENSOR


def swap(values, axis, mask):
    count = lax.axis_size(axis)
    return lax.ppermute(values, axis, [(i, i ^ mask) for i in range(count)])


def bits_of(count):
    return [1 << b for b in range(count.bit_length() - 1)]


def gather_relative(block, axis, order):
    held = {0: block}
    for mask in order:
        for j in list(held):
            held[j ^ mask] = swap(held[j], axis, mask)
    return [held[j] for j in range(len(held))]


def mm(a, b):
    return jnp.dot(a, b, preferred_element_type=f32)


def mm_nt(a, b, precision=None):
    return lax.dot_general(
        a, b, (((1,), (1,)), ((), ())), preferred_element_type=f32, precision=precision
    )


def mm_tn(a, b, precision=None):
    return lax.dot_general(
        a, b, (((0,), (0,)), ((), ())), preferred_element_type=f32, precision=precision
    )


def norm_root(values):
    return lax.rsqrt(jnp.mean(values * values, axis=-1, keepdims=True) + norm_epsilon)


def norm_backward(values, root, gain_row, grad):
    scaled = values * root
    inner = grad * gain_row
    centre = jnp.mean(inner * scaled, axis=-1, keepdims=True)
    return root * (inner - scaled * centre)


def gelu_pair(values):
    c = math.sqrt(2.0 / math.pi)
    square = values * values
    th = jnp.tanh(c * values * (1.0 + 0.044715 * square))
    half = 0.5 * (1.0 + th)
    slope = half + 0.5 * values * (1.0 - th * th) * c * (1.0 + 3.0 * 0.044715 * square)
    return values * half, slope


def adam_update(weight, moment_one, moment_two, gradient, step_rate):
    moment_one_next = beta_first * moment_one + (1.0 - beta_first) * gradient
    moment_two_next = beta_second * moment_two + (1.0 - beta_second) * gradient * gradient
    corrected_one = moment_one_next / (1.0 - beta_first**STEP)
    corrected_two = moment_two_next / (1.0 - beta_second**STEP)
    weight_next = weight - step_rate * (
        corrected_one / (jnp.sqrt(corrected_two) + adam_epsilon) + decay_factor * weight
    )
    return (weight_next, moment_one_next, moment_two_next)


def shape_of(shape, dtype):
    return jax.ShapeDtypeStruct(shape, dtype)


def whole(shape):
    return pl.BlockSpec(shape, lambda *_: (0,) * len(shape))


def scalars():
    return pl.BlockSpec(memory_space=pltpu.SMEM)


LIGHT = pl.CostEstimate(flops=1, bytes_accessed=1, transcendentals=0)


def params(limit):
    return pltpu.CompilerParams(vmem_limit_bytes=limit * MIB)


def prologue_kernel(inputs, attention, gains, router, scaled, root, packed, payload):
    values = inputs[...]
    scale = norm_root(values)
    root[...] = scale
    scaled[...] = (values * scale).astype(bf16)
    parts = [attention[i].astype(bf16) for i in range(4)]
    packed[...] = jnp.concatenate(
        [part[:, :LANES] for part in parts] + [part[:, LANES:] for part in parts], axis=1
    )
    share, experts = router.shape
    groups = -(-(2 + experts) // 8)
    wide = jnp.concatenate([gains[...], router[...].T], axis=0)
    wide = jnp.pad(wide, ((0, 8 * groups - 2 - experts), (0, 0)))
    row = jnp.concatenate([wide[8 * k : 8 * k + 8] for k in range(groups)], axis=1)
    row = jnp.pad(row, ((0, 0), (0, LANES - groups * share)))
    payload[...] = jnp.broadcast_to(row[None], payload.shape)


def prologue(inputs, attention, gains, router, device_count):
    quarter, width = inputs.shape
    tall = attention.shape[1]
    shapes = [
        shape_of((quarter, width), bf16),
        shape_of((quarter, 1), f32),
        shape_of((tall, 6 * LANES), bf16),
        shape_of((device_count, 8, LANES), f32),
    ]
    arrays = (inputs, attention, gains, router)
    return pl.pallas_call(
        prologue_kernel,
        in_specs=[whole(a.shape) for a in arrays],
        out_specs=[whole(s.shape) for s in shapes],
        out_shape=shapes,
        compiler_params=params(60),
        cost_estimate=LIGHT,
        name="prologue",
    )(*arrays)


def slots_kernel(capacity, info, routes, grads, place, match, valid, slots):
    quarter = routes.shape[0]
    experts = match.shape[1]
    row = lax.broadcasted_iota(jnp.int32, (quarter, 1), 0) + info[0] * quarter
    inside = jnp.where(row < info[1], 1.0, 0.0)
    valid[...] = inside
    column = lax.broadcasted_iota(jnp.int32, (quarter, experts), 1)
    named = jnp.where(routes[...] == column, 1.0, 0.0)
    match[...] = named
    at = lax.broadcasted_iota(jnp.int32, (quarter, quarter), 0)
    before = lax.broadcasted_iota(jnp.int32, (quarter, quarter), 1)
    lower = jnp.where(at >= before, 1.0, 0.0).astype(bf16)
    rank = jnp.sum(mm(lower, (named * inside).astype(bf16)) * named, axis=1, keepdims=True) - 1.0
    slot = jnp.where(inside > 0.0, routes[...].astype(f32) * capacity + rank, -1.0)
    slot = jnp.broadcast_to(slot, (quarter, LANES)).T[:1]
    number = lax.broadcasted_iota(jnp.int32, place.shape, 0).astype(f32)
    chosen = jnp.where(number == slot, 1.0, 0.0).astype(bf16)
    place[...] = chosen
    slots[...] = mm(chosen, grads[...].astype(bf16)).astype(bf16)


def slots_part(info, routes, grads, experts, capacity):
    quarter, width = grads.shape
    shapes = [
        shape_of((experts * capacity, quarter), bf16),
        shape_of((quarter, experts), f32),
        shape_of((quarter, 1), f32),
        shape_of((experts * capacity, width), bf16),
    ]
    return pl.pallas_call(
        lambda *refs: slots_kernel(capacity, *refs),
        in_specs=[scalars(), whole(routes.shape), whole(grads.shape)],
        out_specs=[whole(s.shape) for s in shapes],
        out_shape=shapes,
        compiler_params=params(60),
        cost_estimate=LIGHT,
        name="slots",
    )(info, routes, grads)


def project_kernel(quarter, blocks, count, share, info, came, x0, x1, x2, x3, *refs):
    shards, (small, weight, out_weight, qkv, kaug, vt) = refs[:count], refs[count:]
    tall = shards[0].shape[0]
    width = weight.shape[0]
    for j, ref in enumerate(shards):
        start = pl.multiple_of((info[2] ^ j) * tall, tall) if count > 1 else 0
        weight[pl.ds(start, tall), :] = ref[...]
    out_weight[:LANES, :] = weight[:, 3 * LANES : 4 * LANES].T
    out_weight[LANES:, :] = weight[:, 5 * LANES :].T[DH:]
    groups = small.shape[0] // 8
    devices = came.shape[0]
    flat = came[...].reshape(devices * 8, LANES)
    lane = lax.broadcasted_iota(jnp.int32, (LANES, width), 0)
    column = lax.broadcasted_iota(jnp.int32, (LANES, width), 1)
    inside = lax.rem(column, share)
    owner = lax.broadcasted_iota(jnp.int32, (devices, 1, width), 2) - share * lax.broadcasted_iota(
        jnp.int32, (devices, 1, width), 0
    )
    owner = jnp.where((owner >= 0) & (owner < share), 1.0, 0.0)
    for k in range(groups):
        pick = jnp.where(lane == inside + k * share, 1.0, 0.0)
        spread = jnp.dot(flat, pick, precision=HIGHEST, preferred_element_type=f32)
        small[8 * k : 8 * k + 8, :] = jnp.sum(spread.reshape(devices, 8, width) * owner, axis=0)
    gain = small[:1, :]
    for j, ref in enumerate((x0, x1, x2, x3)):
        start = pl.multiple_of((info[0] ^ j) * quarter, quarter)
        rows = pl.ds(start, quarter)
        scaled = (ref[...].astype(f32) * gain).astype(bf16)
        first = mm(scaled, weight[:, : 3 * LANES]).astype(bf16)
        second = mm(scaled, weight[:, 4 * LANES :]).astype(bf16)
        qkv[rows, : 3 * LANES] = first
        qkv[rows, 3 * LANES :] = second
        kaug[rows, :LANES] = first[:, LANES : 2 * LANES]
        lane = lax.broadcasted_iota(jnp.int32, (quarter, LANES), 1)
        row = lax.broadcasted_iota(jnp.int32, (quarter, LANES), 0) + start
        hidden = jnp.where((lane == 0) & (row >= info[1]), masked_score, 0.0)
        kaug[rows, LANES:] = jnp.where(lane < DH, hidden, second[:, :LANES].astype(f32)).astype(bf16)
        values = first[:, 2 * LANES :].T
        vt[0, :DH, rows] = values[:DH]
        vt[1, :DH, rows] = values[DH:]
        vt[2, :DH, rows] = second[:, LANES:].T[:DH]
    full_len = quarter * blocks
    tail = (lax.broadcasted_iota(jnp.int32, (16, full_len), 0) == 0).astype(f32).astype(bf16)
    for h in range(3):
        vt[h, DH:, :] = tail


def project(info, came, rows, shards, share, experts):
    quarter, width = rows[0].shape
    blocks = len(rows)
    full_len = quarter * blocks
    shapes = [
        shape_of((8 * -(-(2 + experts) // 8), width), f32),
        shape_of((width, 6 * LANES), bf16),
        shape_of((3 * DH, width), bf16),
        shape_of((full_len, 5 * LANES), bf16),
        shape_of((full_len, 2 * LANES), bf16),
        shape_of((3, DH + 16, full_len), bf16),
    ]
    arrays = (came, *rows, *shards)
    return pl.pallas_call(
        lambda *refs: project_kernel(quarter, blocks, len(shards), share, *refs),
        in_specs=[scalars()] + [whole(a.shape) for a in arrays],
        out_specs=[whole(s.shape) for s in shapes],
        out_shape=shapes,
        compiler_params=params(60),
        cost_estimate=LIGHT,
        name="project",
    )(info, *arrays)


def attention_kernel(qkv, kaug, vt, context, chances, totals):
    quarter = context.shape[2]
    step = pl.program_id(0)
    rows = pl.ds(pl.multiple_of(step * quarter, quarter), quarter)
    q01 = (qkv[rows, :LANES].astype(f32) * score_scale).T.astype(bf16)
    q2 = (qkv[rows, 3 * LANES : 4 * LANES].astype(f32) * score_scale).T.astype(bf16)[:DH]
    ones = (lax.broadcasted_iota(jnp.int32, (DH, quarter), 0) == 0).astype(f32).astype(bf16)
    zeros = jnp.zeros((DH, quarter), bf16)
    queries = (
        jnp.concatenate([q01[:DH], zeros, ones, zeros], axis=0),
        jnp.concatenate([zeros, q01[DH:], ones, zeros], axis=0),
        jnp.concatenate([zeros, zeros, ones, q2], axis=0),
    )
    full_len = kaug.shape[0]
    all_scores = [mm(kaug[...], queries[h]) for h in range(3)]
    for h in range(3):
        scores = all_scores[h]
        top = jnp.max(jnp.max(scores.reshape(8, full_len // 8, quarter), axis=0), axis=0, keepdims=True)
        low = jnp.exp(scores - top).astype(bf16)
        chances[h] = low
        summed = mm(vt[h], low)
        part = 1.0 / summed[DH : DH + 1]
        totals[0, h : h + 1, :] = part
        context[0, h * DH : (h + 1) * DH, :] = (summed[:DH] * part).astype(bf16)


def attention_forward(qkv, kaug, vt, blocks):
    full_len = qkv.shape[0]
    quarter = full_len // blocks
    inner = 3 * DH
    return pl.pallas_call(
        attention_kernel,
        grid=(blocks,),
        in_specs=[whole(qkv.shape), whole(kaug.shape), whole(vt.shape)],
        out_specs=[
            pl.BlockSpec((1, inner, quarter), lambda i: (i, 0, 0)),
            pl.BlockSpec((3, full_len, quarter), lambda i: (0, 0, i)),
            pl.BlockSpec((1, 3, quarter), lambda i: (i, 0, 0)),
        ],
        out_shape=[
            shape_of((blocks, inner, quarter), bf16),
            shape_of((3, full_len, full_len), bf16),
            shape_of((blocks, 3, quarter), f32),
        ],
        compiler_params=params(60),
        cost_estimate=LIGHT,
        name="attend",
    )(qkv, kaug, vt)


def turn_kernel(quarter, blocks, info, x0, x1, x2, x3, qkv, context, xt, kt, q2, cn):
    for j, ref in enumerate((x0, x1, x2, x3)):
        xt[info[0] ^ j] = ref[...].T
    for j in range(blocks):
        rows = slice(j * quarter, (j + 1) * quarter)
        third = qkv[rows, 3 * LANES : 4 * LANES].T
        kt[:LANES, rows] = qkv[rows, LANES : 2 * LANES].T
        kt[LANES:, rows] = third[DH:]
        zeros = jnp.zeros((DH, quarter), bf16)
        q2[rows, :] = jnp.concatenate([zeros, third[:DH]], axis=0).T
        cn[rows, :LANES] = context[j, :LANES, :].T
        cn[rows, LANES:] = jnp.concatenate([zeros, context[j, LANES:, :]], axis=0).T


def turn(info, rows, qkv, context):
    quarter, width = rows[0].shape
    blocks = len(rows)
    full_len = quarter * blocks
    shapes = [
        shape_of((blocks, width, quarter), bf16),
        shape_of((3 * DH, full_len), bf16),
        shape_of((full_len, LANES), bf16),
        shape_of((full_len, 2 * LANES), bf16),
    ]
    return pl.pallas_call(
        lambda *refs: turn_kernel(quarter, blocks, *refs),
        in_specs=[scalars()] + [whole((quarter, width))] * 4 + [whole(qkv.shape), whole(context.shape)],
        out_specs=[whole(s.shape) for s in shapes],
        out_shape=shapes,
        compiler_params=params(60),
        cost_estimate=LIGHT,
        name="turn",
    )(info, *rows, qkv, context)


def two_columns(column):
    high = column.astype(bf16).astype(f32)
    lane = lax.broadcasted_iota(jnp.int32, (column.shape[0], LANES), 1)
    return jnp.where(lane == 0, high, jnp.where(lane == 1, column - high, 0.0)).astype(bf16)


def middle_kernel(
    info, rows, context, w0, w1, w2, w3, small, place, match, valid, middle, root, chances, gate, slots
):
    gain, router = small[1:2, :], small[2 : 2 + match.shape[1], :]
    total = rows[...]
    for j, ref in enumerate((w0, w1, w2, w3)):
        total = total + mm_tn(context[info[0] ^ j], ref[...])
    middle[...] = total
    scale = norm_root(total)
    root[...] = scale
    hidden = total * scale * gain
    scores = mm_nt(hidden, router, HIGHEST)
    powers = jnp.exp(scores - jnp.max(scores, axis=-1, keepdims=True))
    share = powers / jnp.sum(powers, axis=-1, keepdims=True)
    chances[...] = share
    own = jnp.sum(share * match[...], axis=-1, keepdims=True)
    gate[...] = own
    width = rows.shape[1]
    slots[:, :width] = mm(place[...], hidden.astype(bf16)).astype(bf16)
    slots[:, width:] = mm(place[...], two_columns(own * valid[...])).astype(bf16)


def middle_part(info, rows, context, out_weights, small, place, match, valid):
    quarter, width = rows.shape
    experts = match.shape[1]
    shapes = [
        shape_of((quarter, width), f32),
        shape_of((quarter, 1), f32),
        shape_of((quarter, experts), f32),
        shape_of((quarter, 1), f32),
        shape_of((place.shape[0], width + LANES), bf16),
    ]
    arrays = (rows, context, *out_weights, small, place, match, valid)
    return pl.pallas_call(
        middle_kernel,
        in_specs=[scalars()] + [whole(a.shape) for a in arrays],
        out_specs=[whole(s.shape) for s in shapes],
        out_shape=shapes,
        compiler_params=params(60),
        cost_estimate=LIGHT,
        name="middle",
    )(info, *arrays)


def expert_kernel(rows, grads, near, other, out, back, held, arrived):
    width = grads.shape[1]
    sources = (near.at[0], near.at[1], other.at[0], other.at[1])
    copies = [pltpu.make_async_copy(ref, held.at[i], arrived.at[i]) for i, ref in enumerate(sources)]
    for copy in copies:
        copy.start()
    out_total, back_total = None, None
    for i, copy in enumerate(copies):
        copy.wait()
        inward, outward = held[i, 0], held[i, 1]
        grad = mm(grads[...], outward)
        active, slope = gelu_pair(mm(rows[:, :width], inward))
        part = mm_nt(active.astype(bf16), outward)
        back_part = mm_nt((grad * slope).astype(bf16), inward)
        out_total = part if i == 0 else out_total + part
        back_total = back_part if i == 0 else back_total + back_part
    result = out_total.astype(bf16)
    out[...] = result
    back[:, :width] = back_total.astype(bf16)
    match = jnp.sum(grads[...].astype(f32) * result.astype(f32), axis=-1, keepdims=True)
    back[:, width:] = two_columns(match)


def expert_part(rows, grads, weights):
    slots, width = grads.shape
    hidden = weights[0].shape[3]
    count = 2 * len(weights)
    shapes = [shape_of((slots, width), bf16), shape_of((slots, width + LANES), bf16)]
    return pl.pallas_call(
        expert_kernel,
        in_specs=[whole(rows.shape), whole(grads.shape)] + [pl.BlockSpec(memory_space=pl.ANY)] * 2,
        out_specs=[whole(s.shape) for s in shapes],
        out_shape=shapes,
        scratch_shapes=[pltpu.VMEM((count,) + weights[0].shape[1:], bf16), pltpu.SemaphoreType.DMA((count,))],
        compiler_params=params(60),
        cost_estimate=LIGHT,
        name="experts",
    )(rows, grads, *weights)


def expert_grad_kernel(count, *refs):
    info, rows, grads, near = refs[0], refs[1 : count + 1], refs[count + 1 : 2 * count + 1], refs[2 * count + 1]
    out, square, weight, row_all, grad_all, inner_all, active_all, arrived = refs[2 * count + 2 :]
    copy = pltpu.make_async_copy(near.at[lax.div(info[0], 2)], weight, arrived)
    copy.start()
    copy.wait()
    slots, width = grads[0].shape
    for j in range(count):
        at = slice(j * slots, (j + 1) * slots)
        gate = rows[j][:, width : width + 1].astype(f32) + rows[j][:, width + 1 : width + 2].astype(f32)
        row_all[at, :] = rows[j][:, :width]
        grad_all[at, :] = (grads[j][...].astype(f32) * gate).astype(bf16)
        back = mm(grads[j][...], weight[1])
        active, slope = gelu_pair(mm(rows[j][:, :width], weight[0]))
        inner_all[at, :] = (back * slope * gate).astype(bf16)
        active_all[at, :] = active.astype(bf16)
    first = mm_tn(row_all[...], inner_all[...])
    out[0] = first
    second = mm_tn(grad_all[...], active_all[...])
    out[1] = second
    square[...] = jnp.sum(first * first + second * second, axis=0, keepdims=True)


def expert_gradient(info, rows, grads, near):
    count = len(rows)
    slots, width = grads[0].shape
    hidden = near.shape[3]
    arrays = (*rows, *grads)
    shapes = [shape_of((2, width, hidden), f32), shape_of((1, hidden), f32)]
    return pl.pallas_call(
        lambda *refs: expert_grad_kernel(count, *refs),
        in_specs=[scalars()] + [whole(a.shape) for a in arrays] + [pl.BlockSpec(memory_space=pl.ANY)],
        out_specs=[whole(s.shape) for s in shapes],
        out_shape=shapes,
        scratch_shapes=[pltpu.VMEM(near.shape[1:], bf16)]
        + [pltpu.VMEM((count * slots, width), bf16)] * 2
        + [pltpu.VMEM((count * slots, hidden), bf16)] * 2
        + [pltpu.SemaphoreType.DMA],
        compiler_params=params(60),
        cost_estimate=LIGHT,
        name="expert_gradient",
    )(info, *arrays, near)


def return_kernel(
    info, back, place, middle, root, chances, gate, match, cotangent, small, w0, w1, w2, w3,
    grad, turned, parts, small_grad,
):
    experts = match.shape[1]
    gain, router = small[1:2, :], small[2 : 2 + experts, :]
    width = middle.shape[1]
    came = mm_tn(place[...], back[...])
    gate_grad = came[:, width : width + 1] + came[:, width + 1 : width + 2]
    own = gate[...]
    score_grad = own * (match[...] - chances[...]) * gate_grad
    scaled = middle[...] * root[...]
    hidden = scaled * gain
    small_grad[1:, :] = mm_tn(score_grad, hidden, HIGHEST)
    second = own * came[:, :width] + jnp.dot(
        score_grad, router, precision=HIGHEST, preferred_element_type=f32
    )
    small_grad[:1, :] = jnp.sum(second * scaled, axis=0, keepdims=True)
    inner = second * gain
    centre = jnp.mean(inner * scaled, axis=-1, keepdims=True)
    total = cotangent[...] + root[...] * (inner - scaled * centre)
    grad[...] = total
    low = total.astype(bf16)
    turned[...] = low.T
    for j, ref in enumerate((w0, w1, w2, w3)):
        parts[info[0] ^ j] = mm_nt(ref[...], low).astype(bf16)


def return_part(info, back, place, middle, root, chances, gate, match, cotangent, small, out_weights):
    quarter, width = middle.shape
    experts = match.shape[1]
    inner = out_weights[0].shape[0]
    shapes = [
        shape_of((quarter, width), f32),
        shape_of((width, quarter), bf16),
        shape_of((len(out_weights), inner, quarter), bf16),
        shape_of((1 + experts, width), f32),
    ]
    arrays = (back, place, middle, root, chances, gate, match, cotangent, small, *out_weights)
    return pl.pallas_call(
        return_kernel,
        in_specs=[scalars()] + [whole(a.shape) for a in arrays],
        out_specs=[whole(s.shape) for s in shapes],
        out_shape=shapes,
        compiler_params=params(60),
        cost_estimate=LIGHT,
        name="returned",
    )(info, *arrays)


def attention_back_kernel(blocks, grads, context, chances, totals, qkv, kt, q2, packed, vaug, k01, k2, v01, v2):
    step = pl.program_id(0)
    quarter = grads.shape[2]

    @pl.when(step == 0)
    def _():
        vaug[:, :LANES] = qkv[:, 2 * LANES : 3 * LANES]
        lane = lax.broadcasted_iota(jnp.int32, (vaug.shape[0], LANES), 1)
        ones = jnp.where(lane < DH + 2, 1.0, 0.0)
        vaug[:, LANES:] = jnp.where(lane < DH, qkv[:, 4 * LANES :].astype(f32), ones).astype(bf16)
        for ref in (k01, k2, v01, v2):
            ref[...] = jnp.zeros(ref.shape, f32)

    rows = pl.ds(pl.multiple_of(step * quarter, quarter), quarter)
    raw = grads[0].astype(f32)
    scale = totals[0]
    scaled = [raw[h * DH : (h + 1) * DH] * scale[h : h + 1] for h in range(3)]
    heads = jnp.concatenate(scaled, axis=0).astype(bf16)
    lane = lax.broadcasted_iota(jnp.int32, (quarter, LANES), 1)
    row = lax.broadcasted_iota(jnp.int32, (DH, quarter), 0)
    zeros = jnp.zeros((DH, quarter), bf16)
    q01 = qkv[rows, :LANES].astype(f32)
    g01 = heads[:LANES].T.astype(f32)
    g2 = jnp.concatenate([heads[LANES:], zeros], axis=0).T
    query_parts = []
    for h in range(3):
        part = heads[h * DH : (h + 1) * DH]
        centre = -jnp.sum(
            part.astype(f32) * context[0, h * DH : (h + 1) * DH, :].astype(f32), axis=0, keepdims=True
        )
        high = centre.astype(bf16).astype(f32)
        tail = jnp.where(row == 0, high, jnp.where(row == 1, centre - high, 0.0)).astype(bf16)
        pieces = [zeros, zeros, zeros, tail]
        pieces[h] = part
        chance_grad = mm(vaug[...], jnp.concatenate(pieces, axis=0))
        low = chances[h]
        score_grad = (low.astype(f32) * chance_grad).astype(bf16)
        query_parts.append(mm(kt[h * DH : (h + 1) * DH, :], score_grad) * score_scale)
        if h < 2:
            inside = (lane >= h * DH) & (lane < (h + 1) * DH)
            k01[...] += mm(score_grad, jnp.where(inside, q01, 0.0).astype(bf16))
            v01[...] += mm(low, jnp.where(inside, g01, 0.0).astype(bf16))
        else:
            k2[...] += mm(score_grad, q2[rows, :])
            v2[...] += mm(low, g2)
    packed[rows, :LANES] = jnp.concatenate(query_parts[:2], axis=0).T.astype(bf16)
    packed[rows, 4 * LANES : 5 * LANES] = (
        jnp.concatenate([query_parts[2], jnp.zeros((DH, quarter), f32)], axis=0).T.astype(bf16)
    )

    @pl.when(step == blocks - 1)
    def _():
        packed[:, LANES : 2 * LANES] = (k01[...] * score_scale).astype(bf16)
        packed[:, 2 * LANES : 3 * LANES] = v01[...].astype(bf16)
        packed[:, 3 * LANES : 4 * LANES] = jnp.zeros(k01.shape, bf16)
        packed[:, 4 * LANES : 5 * LANES] = packed[:, 4 * LANES : 5 * LANES] + (k2[...] * score_scale).astype(bf16)
        packed[:, 5 * LANES :] = v2[...].astype(bf16)


def attention_backward(grads, context, chances, totals, qkv, kt, q2):
    blocks, inner, quarter = grads.shape
    full_len = quarter * blocks
    block = pl.BlockSpec((1, inner, quarter), lambda i: (i, 0, 0))
    return pl.pallas_call(
        lambda *refs: attention_back_kernel(blocks, *refs),
        grid=(blocks,),
        in_specs=[
            block,
            block,
            pl.BlockSpec((3, full_len, quarter), lambda i: (0, 0, i)),
            pl.BlockSpec((1, 3, quarter), lambda i: (i, 0, 0)),
            whole(qkv.shape),
            whole(kt.shape),
            whole(q2.shape),
        ],
        out_specs=whole((full_len, 6 * LANES)),
        out_shape=shape_of((full_len, 6 * LANES), bf16),
        scratch_shapes=[pltpu.VMEM((full_len, 2 * LANES), bf16)] + [pltpu.VMEM((full_len, LANES), f32)] * 4,
        compiler_params=params(60),
        cost_estimate=LIGHT,
        name="attend_back",
    )(grads, context, chances, totals, qkv, kt, q2)


def weight_grad_kernel(blocks, info, xt, packed, g0, g1, g2, g3, cn, weight, gain, out, gain_grad):
    quarter = xt.shape[2]
    total, outer = None, None
    for j, ref in enumerate((g0, g1, g2, g3)):
        rows = slice(j * quarter, (j + 1) * quarter)
        there = pl.ds(pl.multiple_of((info[0] ^ j) * quarter, quarter), quarter)
        part = mm(xt[j], packed[rows, :])
        own = mm(ref[...], cn[there, :])
        total = part if total is None else total + part
        outer = own if outer is None else outer + own
    gain_grad[...] = jnp.sum(total * weight[...].astype(f32), axis=1, keepdims=True)
    total = total * gain[...]
    out[:, : 3 * LANES] = total[:, : 3 * LANES].astype(bf16)
    out[:, 3 * LANES : 4 * LANES] = outer[:, :LANES].astype(bf16)
    out[:, 4 * LANES : 5 * LANES] = total[:, 4 * LANES : 5 * LANES].astype(bf16)
    out[:, 5 * LANES :] = (total[:, 5 * LANES :] + outer[:, LANES:]).astype(bf16)


def weight_gradient(info, xt, packed, grads, cn, weight, gain):
    blocks, width, quarter = xt.shape
    tall = 256
    full_len = quarter * blocks
    return pl.pallas_call(
        lambda *refs: weight_grad_kernel(blocks, *refs),
        grid=(width // tall,),
        in_specs=[
            scalars(),
            pl.BlockSpec((blocks, tall, quarter), lambda i: (0, i, 0)),
            whole(packed.shape),
            *[pl.BlockSpec((tall, quarter), lambda i: (i, 0))] * blocks,
            whole(cn.shape),
            pl.BlockSpec((tall, 6 * LANES), lambda i: (i, 0)),
            pl.BlockSpec((tall, 1), lambda i: (i, 0)),
        ],
        out_specs=[pl.BlockSpec((tall, 6 * LANES), lambda i: (i, 0)), pl.BlockSpec((tall, 1), lambda i: (i, 0))],
        out_shape=[shape_of((width, 6 * LANES), bf16), shape_of((width, 1), f32)],
        compiler_params=params(60),
        cost_estimate=LIGHT,
        name="weight_gradient",
    )(info, xt, packed, *grads, cn, weight, gain)


def sums_kernel(came, squares, small, gain_grad, gradient, payload):
    count = came.shape[0]
    total = came[0].astype(f32)
    for i in range(1, count):
        total = total + came[i].astype(f32)
    gradient[...] = total
    own = jnp.sum(small[...], axis=0)
    square = (
        jnp.sum(total * total, keepdims=True)
        + jnp.sum(squares[...], keepdims=True)
        + jnp.sum(own * own, keepdims=True)
    )
    rows = gain_grad.shape[0]
    row = lax.broadcasted_iota(jnp.int32, (8, LANES), 0)
    gain = jnp.concatenate([gain_grad[...], jnp.zeros((8 - rows, LANES), f32)], axis=0)
    payload[...] = jnp.broadcast_to(jnp.where(row < rows, gain, square)[None], payload.shape)


def sums_part(came, squares, small, gain_grad, device_count):
    shapes = [shape_of(came.shape[1:], f32), shape_of((device_count, 8, LANES), f32)]
    arrays = (came, squares, small, gain_grad)
    return pl.pallas_call(
        sums_kernel,
        in_specs=[whole(a.shape) for a in arrays],
        out_specs=[whole(s.shape) for s in shapes],
        out_shape=shapes,
        compiler_params=params(60),
        cost_estimate=LIGHT,
        name="sums",
    )(*arrays)


def adam_kernel(rows, expert_rates, info, last, dense, dense_first, dense_second, dense_grad,
                weight, first, second, gradient,
                stats, gain_sum, dense_out, dense_first_out, dense_second_out,
                weight_out, first_out, second_out, factor):
    matrix, part = pl.program_id(0), pl.program_id(1)

    @pl.when((matrix == 0) & (part == 0))
    def _():
        total = jnp.sum(last[...], axis=0)
        gain_sum[...] = total
        row = lax.broadcasted_iota(jnp.int32, (8, LANES), 0)
        squares = jnp.sum(jnp.where(row < rows, total * total, 0.0), keepdims=True)
        norm = jnp.sqrt(squares + total[7:8, :1])
        scale = jnp.minimum(1.0, clip_limit / (norm + norm_epsilon))
        stats[...] = jnp.where(row == 0, norm, scale)
        factor[...] = jnp.broadcast_to(scale, (8, LANES))
        rates = (0.71 / math.sqrt(D), 0.71 / math.sqrt(D), 0.83 / math.sqrt(D), 0.79 / math.sqrt(H * DH))
        for i, rate in enumerate(rates):
            grad = jnp.concatenate(
                [
                    dense_grad[:, i * LANES : (i + 1) * LANES],
                    dense_grad[:, 4 * LANES + i * DH : 4 * LANES + (i + 1) * DH],
                ],
                axis=1,
            )
            result = adam_update(dense[i], dense_first[i], dense_second[i], grad * scale, rate)
            dense_out[i], dense_first_out[i], dense_second_out[i] = result

    rate = jnp.where(matrix == 0, expert_rates[0], expert_rates[1])
    result = adam_update(weight[...], first[...], second[...], gradient[...] * factor[:1, :1], rate)
    weight_out[...], first_out[...], second_out[...] = result


def adam(info, last, dense, dense_grad, expert, expert_grad, rates):
    _, tall, wide = expert_grad.shape
    parts = 4
    block = pl.BlockSpec((1, tall // parts, wide), lambda i, j: (i, j, 0))
    small = shape_of((8, LANES), f32)
    dense_shape = shape_of(dense[0].shape, f32)
    whole_dense = whole(dense[0].shape)
    return pl.pallas_call(
        lambda *refs: adam_kernel(tall // LANES, rates, *refs),
        grid=(2, parts),
        in_specs=[scalars(), whole(last.shape)] + [whole_dense] * 3 + [whole(dense_grad.shape)] + [block] * 4,
        out_specs=[whole((8, LANES))] * 2 + [whole_dense] * 3 + [block] * 3,
        out_shape=[small] * 2 + [dense_shape] * 3 + [shape_of(expert_grad.shape, f32)] * 3,
        scratch_shapes=[pltpu.VMEM((8, LANES), f32)],
        compiler_params=params(60),
        cost_estimate=LIGHT,
        name="adam",
    )(info, last, *dense, dense_grad, *expert, expert_grad)


def after(value, *others):
    return lax.optimization_barrier((value, *others))[0]


def on_device(
    inputs,
    cotangent,
    lengths,
    routes,
    attention_weight,
    attention_mean,
    attention_square,
    expert_weight,
    expert_mean,
    expert_square,
    router_matrix,
    router_mean,
    router_square,
    norm_gains,
    gains_mean,
    gains_square,
):
    quarter, width = inputs.shape[1:]
    dp_count, tensor_count = lax.axis_size(DP), lax.axis_size(TENSOR)
    device_count = dp_count * tensor_count
    expert_count = router_matrix.shape[1]
    capacity = max(2, (5 * quarter + 4 * expert_count - 1) // (4 * expert_count))
    own_dp, own_tensor = lax.axis_index(DP), lax.axis_index(TENSOR)
    share = router_matrix.shape[0]
    rows, grad_rows, length = inputs[0], cotangent[0], lengths[0]
    info = jnp.stack([own_tensor, length, own_dp]).astype(jnp.int32)

    scaled_one, root_one, weight_own, payload = prologue(
        rows, attention_weight, norm_gains, router_matrix, device_count
    )
    block_two = swap(scaled_one, TENSOR, 2)
    if dp_count == 8:
        w4, w2, w1 = [swap(weight_own, DP, mask) for mask in (4, 2, 1)]
        w4, w2, w1 = lax.optimization_barrier((w4, w2, w1))
        w6, w5, w3 = swap(w4, DP, 2), swap(w4, DP, 1), swap(w2, DP, 1)
        w6, w5, w3, block_two = lax.optimization_barrier((w6, w5, w3, block_two))
        shards = [weight_own, w1, w2, w3, w4, w5, w6, swap(w6, DP, 1)]
    else:
        w6, block_two = lax.optimization_barrier((weight_own, block_two))
        shards = [lax.all_gather(weight_own, DP, axis=0, tiled=True)]
    row_blocks = [scaled_one, swap(scaled_one, TENSOR, 1), block_two, swap(block_two, TENSOR, 1)]
    small_came = lax.all_to_all(payload, EVERYONE, 0, 0, tiled=True)

    place, match, valid_scale, grad_slots = slots_part(info, routes[0], grad_rows, expert_count, capacity)
    slot_count = expert_count * capacity

    def trade(values):
        blocks = values.reshape(expert_count, capacity, values.shape[1])
        return lax.all_to_all(blocks, DP, 0, 0, tiled=True).reshape(values.shape)

    expert_low = after(expert_weight, scaled_one)[0].astype(bf16)
    expert_near = lax.all_to_all(jnp.stack([expert_low] * 2), "th", 0, 0, tiled=True)
    expert_grads = trade(after(grad_slots, w6))

    info_late = after(info, grad_slots, expert_low)
    small, weight, out_weight, qkv, keys_wide, values_turned = project(
        info_late, small_came, row_blocks, shards, share, expert_count
    )
    out_weights = [out_weight] + [swap(out_weight, TENSOR, j) for j in range(1, tensor_count)]
    context, chances, totals = attention_forward(qkv, keys_wide, values_turned, tensor_count)
    context, expert_grads, out_weights = lax.optimization_barrier((context, expert_grads, out_weights))
    context_own = lax.all_to_all(context, TENSOR, 0, 0, tiled=True)

    middle, root_two, shares, gate, slots = middle_part(
        info, rows, context_own, out_weights, small, place, match, valid_scale
    )
    expert_rows = trade(slots)
    turned_rows, keys_turned, third_query, context_rows = turn(info, row_blocks, after(qkv, slots), context)
    expert_other = swap(after(expert_near, slots), TENSOR, 1)
    grads_all = gather_relative(after(expert_grads, slots), TENSOR, [2, 1])
    expert_rows, turned_rows, expert_other, grads_all = lax.optimization_barrier(
        (expert_rows, turned_rows, expert_other, grads_all)
    )
    expert_outs, expert_back = expert_part(expert_rows, expert_grads, [expert_near, expert_other])
    expert_rows, expert_back = lax.optimization_barrier((expert_rows, expert_back))
    rows_all = gather_relative(expert_rows, TENSOR, [2, 1])
    expert_back, rows_all = lax.optimization_barrier((trade(expert_back), rows_all))

    middle_grad, middle_turned, context_parts, small_grad = return_part(
        info, expert_back, place, middle, root_two, shares, gate, match, grad_rows, small, out_weights
    )
    context_grad = lax.all_to_all(context_parts, TENSOR, 0, 0, tiled=True)
    middle_all = gather_relative(middle_turned, TENSOR, [2, 1])
    expert_outs = trade(after(expert_outs, context_parts))

    packed = attention_backward(context_grad, context, chances, totals, qkv, keys_turned, third_query)
    weight_grad, gain_one_grad = weight_gradient(
        info, turned_rows, packed, middle_all, context_rows, weight, small[:1].reshape(width, 1)
    )
    weight_grad, expert_outs, small_grad, expert_near = lax.optimization_barrier(
        (weight_grad, expert_outs, small_grad, expert_near)
    )
    weight_came = lax.all_to_all(weight_grad.reshape(dp_count, -1, width), DP, 0, 0, tiled=True)
    small_cut = small_grad.reshape(-1, device_count, share).transpose(1, 0, 2).reshape(device_count, -1)
    small_cut = jnp.pad(small_cut, ((0, 0), (0, 8 * LANES - small_cut.shape[1]))).reshape(device_count, 8, LANES)
    small_grads = lax.all_to_all(small_cut, EVERYONE, 0, 0, tiled=True)
    expert_grad, expert_squares = expert_gradient(info, rows_all, grads_all, expert_near)
    picked = mm_tn(place, expert_outs)
    branch = gate * valid_scale * picked
    block_output = middle + branch
    small_own = jnp.sum(small_grads, axis=0).reshape(-1)[: (1 + expert_count) * share]
    small_own = small_own.reshape(1 + expert_count, share)
    router_own = small_own[1:].T

    dense_grad, last = sums_part(
        weight_came, expert_squares, small_grads, gain_one_grad.reshape(-1, LANES), device_count
    )
    last, packed, block_output, router_own = lax.optimization_barrier((last, packed, block_output, router_own))
    last_all = lax.all_to_all(last, EVERYONE, 0, 0, tiled=True)

    input_parts = mm_nt(packed, weight).astype(bf16)
    input_parts = [
        lax.dynamic_slice_in_dim(input_parts, (own_tensor ^ j) * quarter, quarter) for j in range(tensor_count)
    ]
    first_half = input_parts[0].astype(f32) + swap(input_parts[1], TENSOR, 1).astype(f32)
    second_half = input_parts[2].astype(f32) + swap(input_parts[3], TENSOR, 1).astype(f32)
    second_half = second_half.astype(bf16)
    came = swap(second_half, TENSOR, 2)
    last_all = after(last_all, second_half)
    input_grad = middle_grad + norm_backward(rows, root_one, small[:1], first_half + came.astype(f32))

    rates = (0.4 * math.sqrt(expert_count / D), 1.38 * math.sqrt(expert_count / FF))
    stats, gain_sum, *updated = adam(
        info,
        last_all,
        (attention_weight, attention_mean, attention_square),
        dense_grad,
        (expert_weight[0], expert_mean[0], expert_square[0]),
        expert_grad,
        rates,
    )
    attention_new, expert_new = updated[:3], updated[3:]
    grad_norm, factor = stats[0, 0], stats[1, 0]
    gain_one_own = lax.dynamic_slice_in_dim(gain_sum.reshape(-1), lax.axis_index(EVERYONE) * share, share)
    gains_grad = jnp.stack([gain_one_own, small_own[0]])
    router_new = adam_update(
        router_matrix, router_mean, router_square, router_own * factor, 0.24 / math.sqrt(D)
    )
    gains_new = adam_update(norm_gains, gains_mean, gains_square, gains_grad * factor, 0.5)
    return (
        block_output[None],
        input_grad[None],
        grad_norm,
        *attention_new,
        *[part[None] for part in expert_new],
        *router_new,
        *gains_new,
        branch[None],
    )


def solution(mesh):
    names = mesh.axis_names
    dp_count, tensor_count = mesh.shape[names[0]], mesh.shape[names[1]]
    cut = jax.sharding.Mesh(mesh.devices.reshape(dp_count // 2, 2, tensor_count // 2, 2), EVERYONE)
    rows = P(DP, TENSOR, None)
    attention = P(None, DP, TENSOR)
    expert = P(DP, None, None, TENSOR)
    router = P(EVERYONE, None)
    gains = P(None, EVERYONE)
    weights = (attention,) * 3 + (expert,) * 3 + (router,) * 3 + (gains,) * 3
    return jax.shard_map(
        on_device,
        mesh=cut,
        in_specs=(rows, rows, P(DP), rows) + weights,
        out_specs=(rows, rows, P()) + weights + (rows,),
        check_vma=False,
    )
```

```python
import math

import jax
import jax.numpy as jnp
from jax import lax
from jax.experimental import pallas as pl
from jax.experimental.pallas import tpu as pltpu
from jax.sharding import PartitionSpec as P

D = 768
H = 12
DH = 64
FF = 3072
STEP = 10

HIGHEST = lax.Precision.HIGHEST
norm_epsilon = 1e-06
beta_first = 0.9
beta_second = 0.999
adam_epsilon = 1e-08
decay_factor = 0.01
clip_limit = 1.0
masked_score = -1e30
score_scale = 1.0 / math.sqrt(DH)
bf16 = jnp.bfloat16
f32 = jnp.float32
MIB = 1 << 20
LANES = 128


DP = ("dh", "dl")
TENSOR = ("th", "tl")
EVERYONE = DP + TENSOR


def swap(values, axis, mask):
    count = lax.axis_size(axis)
    return lax.ppermute(values, axis, [(i, i ^ mask) for i in range(count)])


def bits_of(count):
    return [1 << b for b in range(count.bit_length() - 1)]


def gather_relative(block, axis, order):
    held = {0: block}
    for mask in order:
        for j in list(held):
            held[j ^ mask] = swap(held[j], axis, mask)
    return [held[j] for j in range(len(held))]


def mm(a, b):
    return jnp.dot(a, b, preferred_element_type=f32)


def mm_nt(a, b, precision=None):
    return lax.dot_general(
        a, b, (((1,), (1,)), ((), ())), preferred_element_type=f32, precision=precision
    )


def mm_tn(a, b, precision=None):
    return lax.dot_general(
        a, b, (((0,), (0,)), ((), ())), preferred_element_type=f32, precision=precision
    )


def norm_root(values):
    return lax.rsqrt(jnp.mean(values * values, axis=-1, keepdims=True) + norm_epsilon)


def norm_backward(values, root, gain_row, grad):
    scaled = values * root
    inner = grad * gain_row
    centre = jnp.mean(inner * scaled, axis=-1, keepdims=True)
    return root * (inner - scaled * centre)


def gelu_pair(values):
    c = math.sqrt(2.0 / math.pi)
    square = values * values
    th = jnp.tanh(c * values * (1.0 + 0.044715 * square))
    half = 0.5 * (1.0 + th)
    slope = half + 0.5 * values * (1.0 - th * th) * c * (1.0 + 3.0 * 0.044715 * square)
    return values * half, slope


def adam_update(weight, moment_one, moment_two, gradient, step_rate):
    moment_one_next = beta_first * moment_one + (1.0 - beta_first) * gradient
    moment_two_next = beta_second * moment_two + (1.0 - beta_second) * gradient * gradient
    corrected_one = moment_one_next / (1.0 - beta_first**STEP)
    corrected_two = moment_two_next / (1.0 - beta_second**STEP)
    weight_next = weight - step_rate * (
        corrected_one / (jnp.sqrt(corrected_two) + adam_epsilon) + decay_factor * weight
    )
    return (weight_next, moment_one_next, moment_two_next)


def shape_of(shape, dtype):
    return jax.ShapeDtypeStruct(shape, dtype)


def whole(shape):
    return pl.BlockSpec(shape, lambda *_: (0,) * len(shape))


def scalars():
    return pl.BlockSpec(memory_space=pltpu.SMEM)


LIGHT = pl.CostEstimate(flops=1, bytes_accessed=1, transcendentals=0)


def params(limit):
    return pltpu.CompilerParams(vmem_limit_bytes=limit * MIB)


def prologue_kernel(inputs, attention, gains, router, scaled, root, packed, payload):
    values = inputs[...]
    scale = norm_root(values)
    root[...] = scale
    scaled[...] = (values * scale).astype(bf16)
    parts = [attention[i].astype(bf16) for i in range(4)]
    packed[...] = jnp.concatenate(
        [part[:, :LANES] for part in parts] + [part[:, LANES:] for part in parts], axis=1
    )
    experts, share = router.shape
    groups = -(-(2 + experts) // 8)
    wide = jnp.concatenate([gains[...], router[...]], axis=0)
    wide = jnp.pad(wide, ((0, 8 * groups - 2 - experts), (0, 0)))
    row = jnp.concatenate([wide[8 * k : 8 * k + 8] for k in range(groups)], axis=1)
    row = jnp.pad(row, ((0, 0), (0, LANES - groups * share)))
    payload[...] = jnp.broadcast_to(row[None], payload.shape)


def prologue(inputs, attention, gains, router, device_count):
    quarter, width = inputs.shape
    tall = attention.shape[1]
    shapes = [
        shape_of((quarter, width), bf16),
        shape_of((quarter, 1), f32),
        shape_of((tall, 6 * LANES), bf16),
        shape_of((device_count, 8, LANES), f32),
    ]
    arrays = (inputs, attention, gains, router)
    return pl.pallas_call(
        prologue_kernel,
        in_specs=[whole(a.shape) for a in arrays],
        out_specs=[whole(s.shape) for s in shapes],
        out_shape=shapes,
        compiler_params=params(60),
        cost_estimate=LIGHT,
        name="prologue",
    )(*arrays)


def slots_kernel(capacity, info, routes, grads, place, match, valid, slots):
    quarter = routes.shape[0]
    experts = match.shape[1]
    row = lax.broadcasted_iota(jnp.int32, (quarter, 1), 0) + info[0] * quarter
    inside = jnp.where(row < info[1], 1.0, 0.0)
    valid[...] = inside
    column = lax.broadcasted_iota(jnp.int32, (quarter, experts), 1)
    named = jnp.where(routes[...] == column, 1.0, 0.0)
    match[...] = named
    at = lax.broadcasted_iota(jnp.int32, (quarter, quarter), 0)
    before = lax.broadcasted_iota(jnp.int32, (quarter, quarter), 1)
    lower = jnp.where(at >= before, 1.0, 0.0).astype(bf16)
    rank = jnp.sum(mm(lower, (named * inside).astype(bf16)) * named, axis=1, keepdims=True) - 1.0
    slot = jnp.where(inside > 0.0, routes[...].astype(f32) * capacity + rank, -1.0)
    slot = jnp.broadcast_to(slot, (quarter, LANES)).T[:1]
    number = lax.broadcasted_iota(jnp.int32, place.shape, 0).astype(f32)
    chosen = jnp.where(number == slot, 1.0, 0.0).astype(bf16)
    place[...] = chosen
    slots[...] = mm(chosen, grads[...].astype(bf16)).astype(bf16)


def slots_part(info, routes, grads, experts, capacity):
    quarter, width = grads.shape
    shapes = [
        shape_of((experts * capacity, quarter), bf16),
        shape_of((quarter, experts), f32),
        shape_of((quarter, 1), f32),
        shape_of((experts * capacity, width), bf16),
    ]
    return pl.pallas_call(
        lambda *refs: slots_kernel(capacity, *refs),
        in_specs=[scalars(), whole(routes.shape), whole(grads.shape)],
        out_specs=[whole(s.shape) for s in shapes],
        out_shape=shapes,
        compiler_params=params(60),
        cost_estimate=LIGHT,
        name="slots",
    )(info, routes, grads)


def project_kernel(quarter, blocks, count, share, info, came, x0, x1, x2, x3, *refs):
    shards, (small, weight, out_weight, qkv, kaug, vt) = refs[:count], refs[count:]
    tall = shards[0].shape[0]
    width = weight.shape[0]
    for j, ref in enumerate(shards):
        start = pl.multiple_of((info[2] ^ j) * tall, tall) if count > 1 else 0
        weight[pl.ds(start, tall), :] = ref[...]
    out_weight[:LANES, :] = weight[:, 3 * LANES : 4 * LANES].T
    out_weight[LANES:, :] = weight[:, 5 * LANES :].T[DH:]
    groups = small.shape[0] // 8
    devices = came.shape[0]
    flat = came[...].reshape(devices * 8, LANES)
    lane = lax.broadcasted_iota(jnp.int32, (LANES, width), 0)
    column = lax.broadcasted_iota(jnp.int32, (LANES, width), 1)
    inside = lax.rem(column, share)
    owner = lax.broadcasted_iota(jnp.int32, (devices, 1, width), 2) - share * lax.broadcasted_iota(
        jnp.int32, (devices, 1, width), 0
    )
    owner = jnp.where((owner >= 0) & (owner < share), 1.0, 0.0)
    for k in range(groups):
        pick = jnp.where(lane == inside + k * share, 1.0, 0.0)
        spread = jnp.dot(flat, pick, precision=HIGHEST, preferred_element_type=f32)
        small[8 * k : 8 * k + 8, :] = jnp.sum(spread.reshape(devices, 8, width) * owner, axis=0)
    gain = small[:1, :]
    for j, ref in enumerate((x0, x1, x2, x3)):
        start = pl.multiple_of((info[0] ^ j) * quarter, quarter)
        rows = pl.ds(start, quarter)
        scaled = (ref[...].astype(f32) * gain).astype(bf16)
        first = mm(scaled, weight[:, : 3 * LANES]).astype(bf16)
        second = mm(scaled, weight[:, 4 * LANES :]).astype(bf16)
        qkv[rows, : 3 * LANES] = first
        qkv[rows, 3 * LANES :] = second
        kaug[rows, :LANES] = first[:, LANES : 2 * LANES]
        lane = lax.broadcasted_iota(jnp.int32, (quarter, LANES), 1)
        row = lax.broadcasted_iota(jnp.int32, (quarter, LANES), 0) + start
        hidden = jnp.where((lane == 0) & (row >= info[1]), masked_score, 0.0)
        kaug[rows, LANES:] = jnp.where(lane < DH, hidden, second[:, :LANES].astype(f32)).astype(bf16)
        values = first[:, 2 * LANES :].T
        vt[0, :DH, rows] = values[:DH]
        vt[1, :DH, rows] = values[DH:]
        vt[2, :DH, rows] = second[:, LANES:].T[:DH]
    full_len = quarter * blocks
    tail = (lax.broadcasted_iota(jnp.int32, (16, full_len), 0) == 0).astype(f32).astype(bf16)
    for h in range(3):
        vt[h, DH:, :] = tail


def project(info, came, rows, shards, share, experts):
    quarter, width = rows[0].shape
    blocks = len(rows)
    full_len = quarter * blocks
    shapes = [
        shape_of((8 * -(-(2 + experts) // 8), width), f32),
        shape_of((width, 6 * LANES), bf16),
        shape_of((3 * DH, width), bf16),
        shape_of((full_len, 5 * LANES), bf16),
        shape_of((full_len, 2 * LANES), bf16),
        shape_of((3, DH + 16, full_len), bf16),
    ]
    arrays = (came, *rows, *shards)
    return pl.pallas_call(
        lambda *refs: project_kernel(quarter, blocks, len(shards), share, *refs),
        in_specs=[scalars()] + [whole(a.shape) for a in arrays],
        out_specs=[whole(s.shape) for s in shapes],
        out_shape=shapes,
        compiler_params=params(60),
        cost_estimate=LIGHT,
        name="project",
    )(info, *arrays)


def attention_kernel(qkv, kaug, vt, context, chances, totals):
    quarter = context.shape[2]
    step = pl.program_id(0)
    rows = pl.ds(pl.multiple_of(step * quarter, quarter), quarter)
    q01 = (qkv[rows, :LANES].astype(f32) * score_scale).T.astype(bf16)
    q2 = (qkv[rows, 3 * LANES : 4 * LANES].astype(f32) * score_scale).T.astype(bf16)[:DH]
    ones = (lax.broadcasted_iota(jnp.int32, (DH, quarter), 0) == 0).astype(f32).astype(bf16)
    zeros = jnp.zeros((DH, quarter), bf16)
    queries = (
        jnp.concatenate([q01[:DH], zeros, ones, zeros], axis=0),
        jnp.concatenate([zeros, q01[DH:], ones, zeros], axis=0),
        jnp.concatenate([zeros, zeros, ones, q2], axis=0),
    )
    full_len = kaug.shape[0]
    all_scores = [mm(kaug[...], queries[h]) for h in range(3)]
    for h in range(3):
        scores = all_scores[h]
        top = jnp.max(jnp.max(scores.reshape(8, full_len // 8, quarter), axis=0), axis=0, keepdims=True)
        low = jnp.exp(scores - top).astype(bf16)
        chances[h] = low
        summed = mm(vt[h], low)
        part = 1.0 / summed[DH : DH + 1]
        totals[0, h : h + 1, :] = part
        context[0, h * DH : (h + 1) * DH, :] = (summed[:DH] * part).astype(bf16)


def attention_forward(qkv, kaug, vt, blocks):
    full_len = qkv.shape[0]
    quarter = full_len // blocks
    inner = 3 * DH
    return pl.pallas_call(
        attention_kernel,
        grid=(blocks,),
        in_specs=[whole(qkv.shape), whole(kaug.shape), whole(vt.shape)],
        out_specs=[
            pl.BlockSpec((1, inner, quarter), lambda i: (i, 0, 0)),
            pl.BlockSpec((3, full_len, quarter), lambda i: (0, 0, i)),
            pl.BlockSpec((1, 3, quarter), lambda i: (i, 0, 0)),
        ],
        out_shape=[
            shape_of((blocks, inner, quarter), bf16),
            shape_of((3, full_len, full_len), bf16),
            shape_of((blocks, 3, quarter), f32),
        ],
        compiler_params=params(60),
        cost_estimate=LIGHT,
        name="attend",
    )(qkv, kaug, vt)


def turn_kernel(quarter, blocks, info, x0, x1, x2, x3, qkv, context, xt, kt, q2, cn):
    for j, ref in enumerate((x0, x1, x2, x3)):
        xt[info[0] ^ j] = ref[...].T
    for j in range(blocks):
        rows = slice(j * quarter, (j + 1) * quarter)
        third = qkv[rows, 3 * LANES : 4 * LANES].T
        kt[:LANES, rows] = qkv[rows, LANES : 2 * LANES].T
        kt[LANES:, rows] = third[DH:]
        zeros = jnp.zeros((DH, quarter), bf16)
        q2[rows, :] = jnp.concatenate([zeros, third[:DH]], axis=0).T
        cn[rows, :LANES] = context[j, :LANES, :].T
        cn[rows, LANES:] = jnp.concatenate([zeros, context[j, LANES:, :]], axis=0).T


def turn(info, rows, qkv, context):
    quarter, width = rows[0].shape
    blocks = len(rows)
    full_len = quarter * blocks
    shapes = [
        shape_of((blocks, width, quarter), bf16),
        shape_of((3 * DH, full_len), bf16),
        shape_of((full_len, LANES), bf16),
        shape_of((full_len, 2 * LANES), bf16),
    ]
    return pl.pallas_call(
        lambda *refs: turn_kernel(quarter, blocks, *refs),
        in_specs=[scalars()] + [whole((quarter, width))] * 4 + [whole(qkv.shape), whole(context.shape)],
        out_specs=[whole(s.shape) for s in shapes],
        out_shape=shapes,
        compiler_params=params(60),
        cost_estimate=LIGHT,
        name="turn",
    )(info, *rows, qkv, context)


def two_columns(column):
    high = column.astype(bf16).astype(f32)
    lane = lax.broadcasted_iota(jnp.int32, (column.shape[0], LANES), 1)
    return jnp.where(lane == 0, high, jnp.where(lane == 1, column - high, 0.0)).astype(bf16)


def middle_kernel(
    info, rows, context, w0, w1, w2, w3, small, place, match, valid, middle, root, chances, gate, slots
):
    gain, router = small[1:2, :], small[2 : 2 + match.shape[1], :]
    total = rows[...]
    for j, ref in enumerate((w0, w1, w2, w3)):
        total = total + mm_tn(context[info[0] ^ j], ref[...])
    middle[...] = total
    scale = norm_root(total)
    root[...] = scale
    hidden = total * scale * gain
    scores = mm_nt(hidden, router, HIGHEST)
    powers = jnp.exp(scores - jnp.max(scores, axis=-1, keepdims=True))
    share = powers / jnp.sum(powers, axis=-1, keepdims=True)
    chances[...] = share
    own = jnp.sum(share * match[...], axis=-1, keepdims=True)
    gate[...] = own
    width = rows.shape[1]
    slots[:, :width] = mm(place[...], hidden.astype(bf16)).astype(bf16)
    slots[:, width:] = mm(place[...], two_columns(own * valid[...])).astype(bf16)


def middle_part(info, rows, context, out_weights, small, place, match, valid):
    quarter, width = rows.shape
    experts = match.shape[1]
    shapes = [
        shape_of((quarter, width), f32),
        shape_of((quarter, 1), f32),
        shape_of((quarter, experts), f32),
        shape_of((quarter, 1), f32),
        shape_of((place.shape[0], width + LANES), bf16),
    ]
    arrays = (rows, context, *out_weights, small, place, match, valid)
    return pl.pallas_call(
        middle_kernel,
        in_specs=[scalars()] + [whole(a.shape) for a in arrays],
        out_specs=[whole(s.shape) for s in shapes],
        out_shape=shapes,
        compiler_params=params(60),
        cost_estimate=LIGHT,
        name="middle",
    )(info, *arrays)


def expert_kernel(rows, grads, near, other, out, back, held, arrived):
    width = grads.shape[1]
    sources = (near.at[0], near.at[1], other.at[0], other.at[1])
    copies = [pltpu.make_async_copy(ref, held.at[i], arrived.at[i]) for i, ref in enumerate(sources)]
    for copy in copies:
        copy.start()
    out_total, back_total = None, None
    for i, copy in enumerate(copies):
        copy.wait()
        inward, outward = held[i, 0], held[i, 1]
        grad = mm(grads[...], outward)
        active, slope = gelu_pair(mm(rows[:, :width], inward))
        part = mm_nt(active.astype(bf16), outward)
        back_part = mm_nt((grad * slope).astype(bf16), inward)
        out_total = part if i == 0 else out_total + part
        back_total = back_part if i == 0 else back_total + back_part
    result = out_total.astype(bf16)
    out[...] = result
    back[:, :width] = back_total.astype(bf16)
    match = jnp.sum(grads[...].astype(f32) * result.astype(f32), axis=-1, keepdims=True)
    back[:, width:] = two_columns(match)


def expert_part(rows, grads, weights):
    slots, width = grads.shape
    hidden = weights[0].shape[3]
    count = 2 * len(weights)
    shapes = [shape_of((slots, width), bf16), shape_of((slots, width + LANES), bf16)]
    return pl.pallas_call(
        expert_kernel,
        in_specs=[whole(rows.shape), whole(grads.shape)] + [pl.BlockSpec(memory_space=pl.ANY)] * 2,
        out_specs=[whole(s.shape) for s in shapes],
        out_shape=shapes,
        scratch_shapes=[pltpu.VMEM((count,) + weights[0].shape[1:], bf16), pltpu.SemaphoreType.DMA((count,))],
        compiler_params=params(60),
        cost_estimate=LIGHT,
        name="experts",
    )(rows, grads, *weights)


def expert_grad_kernel(count, *refs):
    info, rows, grads, near = refs[0], refs[1 : count + 1], refs[count + 1 : 2 * count + 1], refs[2 * count + 1]
    out, square, weight, row_all, grad_all, inner_all, active_all, arrived = refs[2 * count + 2 :]
    copy = pltpu.make_async_copy(near.at[lax.div(info[0], 2)], weight, arrived)
    copy.start()
    copy.wait()
    slots, width = grads[0].shape
    for j in range(count):
        at = slice(j * slots, (j + 1) * slots)
        gate = rows[j][:, width : width + 1].astype(f32) + rows[j][:, width + 1 : width + 2].astype(f32)
        row_all[at, :] = rows[j][:, :width]
        grad_all[at, :] = (grads[j][...].astype(f32) * gate).astype(bf16)
        back = mm(grads[j][...], weight[1])
        active, slope = gelu_pair(mm(rows[j][:, :width], weight[0]))
        inner_all[at, :] = (back * slope * gate).astype(bf16)
        active_all[at, :] = active.astype(bf16)
    first = mm_tn(row_all[...], inner_all[...])
    out[0] = first
    second = mm_tn(grad_all[...], active_all[...])
    out[1] = second
    square[...] = jnp.sum(first * first + second * second, axis=0, keepdims=True)


def expert_gradient(info, rows, grads, near):
    count = len(rows)
    slots, width = grads[0].shape
    hidden = near.shape[3]
    arrays = (*rows, *grads)
    shapes = [pltpu.VMEM((2, width, hidden), f32), shape_of((1, hidden), f32)]
    return pl.pallas_call(
        lambda *refs: expert_grad_kernel(count, *refs),
        in_specs=[scalars()] + [whole(a.shape) for a in arrays] + [pl.BlockSpec(memory_space=pl.ANY)],
        out_specs=[pl.BlockSpec(memory_space=pltpu.VMEM), whole((1, hidden))],
        out_shape=shapes,
        scratch_shapes=[pltpu.VMEM(near.shape[1:], bf16)]
        + [pltpu.VMEM((count * slots, width), bf16)] * 2
        + [pltpu.VMEM((count * slots, hidden), bf16)] * 2
        + [pltpu.SemaphoreType.DMA],
        compiler_params=params(40),
        cost_estimate=LIGHT,
        name="expert_gradient",
    )(info, *arrays, near)


def return_kernel(
    info, back, place, middle, root, chances, gate, match, cotangent, small, w0, w1, w2, w3,
    grad, turned, parts, small_grad,
):
    experts = match.shape[1]
    gain, router = small[1:2, :], small[2 : 2 + experts, :]
    width = middle.shape[1]
    came = mm_tn(place[...], back[...])
    gate_grad = came[:, width : width + 1] + came[:, width + 1 : width + 2]
    own = gate[...]
    score_grad = own * (match[...] - chances[...]) * gate_grad
    scaled = middle[...] * root[...]
    hidden = scaled * gain
    small_grad[1:, :] = mm_tn(score_grad, hidden, HIGHEST)
    second = own * came[:, :width] + jnp.dot(
        score_grad, router, precision=HIGHEST, preferred_element_type=f32
    )
    small_grad[:1, :] = jnp.sum(second * scaled, axis=0, keepdims=True)
    inner = second * gain
    centre = jnp.mean(inner * scaled, axis=-1, keepdims=True)
    total = cotangent[...] + root[...] * (inner - scaled * centre)
    grad[...] = total
    low = total.astype(bf16)
    turned[...] = low.T
    for j, ref in enumerate((w0, w1, w2, w3)):
        parts[info[0] ^ j] = mm_nt(ref[...], low).astype(bf16)


def return_part(info, back, place, middle, root, chances, gate, match, cotangent, small, out_weights):
    quarter, width = middle.shape
    experts = match.shape[1]
    inner = out_weights[0].shape[0]
    shapes = [
        shape_of((quarter, width), f32),
        shape_of((width, quarter), bf16),
        shape_of((len(out_weights), inner, quarter), bf16),
        shape_of((1 + experts, width), f32),
    ]
    arrays = (back, place, middle, root, chances, gate, match, cotangent, small, *out_weights)
    return pl.pallas_call(
        return_kernel,
        in_specs=[scalars()] + [whole(a.shape) for a in arrays],
        out_specs=[whole(s.shape) for s in shapes],
        out_shape=shapes,
        compiler_params=params(60),
        cost_estimate=LIGHT,
        name="returned",
    )(info, *arrays)


def attention_back_kernel(blocks, grads, context, chances, totals, qkv, kt, q2, packed, vaug, k01, k2, v01, v2):
    step = pl.program_id(0)
    quarter = grads.shape[2]

    @pl.when(step == 0)
    def _():
        vaug[:, :LANES] = qkv[:, 2 * LANES : 3 * LANES]
        lane = lax.broadcasted_iota(jnp.int32, (vaug.shape[0], LANES), 1)
        ones = jnp.where(lane < DH + 2, 1.0, 0.0)
        vaug[:, LANES:] = jnp.where(lane < DH, qkv[:, 4 * LANES :].astype(f32), ones).astype(bf16)
        for ref in (k01, k2, v01, v2):
            ref[...] = jnp.zeros(ref.shape, f32)

    rows = pl.ds(pl.multiple_of(step * quarter, quarter), quarter)
    raw = grads[0].astype(f32)
    scale = totals[0]
    scaled = [raw[h * DH : (h + 1) * DH] * scale[h : h + 1] for h in range(3)]
    heads = jnp.concatenate(scaled, axis=0).astype(bf16)
    lane = lax.broadcasted_iota(jnp.int32, (quarter, LANES), 1)
    row = lax.broadcasted_iota(jnp.int32, (DH, quarter), 0)
    zeros = jnp.zeros((DH, quarter), bf16)
    q01 = qkv[rows, :LANES].astype(f32)
    g01 = heads[:LANES].T.astype(f32)
    g2 = jnp.concatenate([heads[LANES:], zeros], axis=0).T
    query_parts = []
    for h in range(3):
        part = heads[h * DH : (h + 1) * DH]
        centre = -jnp.sum(
            part.astype(f32) * context[0, h * DH : (h + 1) * DH, :].astype(f32), axis=0, keepdims=True
        )
        high = centre.astype(bf16).astype(f32)
        tail = jnp.where(row == 0, high, jnp.where(row == 1, centre - high, 0.0)).astype(bf16)
        pieces = [zeros, zeros, zeros, tail]
        pieces[h] = part
        chance_grad = mm(vaug[...], jnp.concatenate(pieces, axis=0))
        low = chances[h]
        score_grad = (low.astype(f32) * chance_grad).astype(bf16)
        query_parts.append(mm(kt[h * DH : (h + 1) * DH, :], score_grad) * score_scale)
        if h < 2:
            inside = (lane >= h * DH) & (lane < (h + 1) * DH)
            k01[...] += mm(score_grad, jnp.where(inside, q01, 0.0).astype(bf16))
            v01[...] += mm(low, jnp.where(inside, g01, 0.0).astype(bf16))
        else:
            k2[...] += mm(score_grad, q2[rows, :])
            v2[...] += mm(low, g2)
    packed[rows, :LANES] = jnp.concatenate(query_parts[:2], axis=0).T.astype(bf16)
    packed[rows, 4 * LANES : 5 * LANES] = (
        jnp.concatenate([query_parts[2], jnp.zeros((DH, quarter), f32)], axis=0).T.astype(bf16)
    )

    @pl.when(step == blocks - 1)
    def _():
        packed[:, LANES : 2 * LANES] = (k01[...] * score_scale).astype(bf16)
        packed[:, 2 * LANES : 3 * LANES] = v01[...].astype(bf16)
        packed[:, 3 * LANES : 4 * LANES] = jnp.zeros(k01.shape, bf16)
        packed[:, 4 * LANES : 5 * LANES] = packed[:, 4 * LANES : 5 * LANES] + (k2[...] * score_scale).astype(bf16)
        packed[:, 5 * LANES :] = v2[...].astype(bf16)


def attention_backward(grads, context, chances, totals, qkv, kt, q2):
    blocks, inner, quarter = grads.shape
    full_len = quarter * blocks
    block = pl.BlockSpec((1, inner, quarter), lambda i: (i, 0, 0))
    return pl.pallas_call(
        lambda *refs: attention_back_kernel(blocks, *refs),
        grid=(blocks,),
        in_specs=[
            block,
            block,
            pl.BlockSpec((3, full_len, quarter), lambda i: (0, 0, i)),
            pl.BlockSpec((1, 3, quarter), lambda i: (i, 0, 0)),
            whole(qkv.shape),
            whole(kt.shape),
            whole(q2.shape),
        ],
        out_specs=whole((full_len, 6 * LANES)),
        out_shape=shape_of((full_len, 6 * LANES), bf16),
        scratch_shapes=[pltpu.VMEM((full_len, 2 * LANES), bf16)] + [pltpu.VMEM((full_len, LANES), f32)] * 4,
        compiler_params=params(60),
        cost_estimate=LIGHT,
        name="attend_back",
    )(grads, context, chances, totals, qkv, kt, q2)


def weight_grad_kernel(blocks, info, xt, packed, g0, g1, g2, g3, cn, weight, gain, out, gain_grad):
    quarter = xt.shape[2]
    total, outer = None, None
    for j, ref in enumerate((g0, g1, g2, g3)):
        rows = slice(j * quarter, (j + 1) * quarter)
        there = pl.ds(pl.multiple_of((info[0] ^ j) * quarter, quarter), quarter)
        part = mm(xt[j], packed[rows, :])
        own = mm(ref[...], cn[there, :])
        total = part if total is None else total + part
        outer = own if outer is None else outer + own
    gain_grad[...] = jnp.sum(total * weight[...].astype(f32), axis=1, keepdims=True)
    total = total * gain[...]
    out[:, : 3 * LANES] = total[:, : 3 * LANES].astype(bf16)
    out[:, 3 * LANES : 4 * LANES] = outer[:, :LANES].astype(bf16)
    out[:, 4 * LANES : 5 * LANES] = total[:, 4 * LANES : 5 * LANES].astype(bf16)
    out[:, 5 * LANES :] = (total[:, 5 * LANES :] + outer[:, LANES:]).astype(bf16)


def weight_gradient(info, xt, packed, grads, cn, weight, gain):
    blocks, width, quarter = xt.shape
    tall = 256
    full_len = quarter * blocks
    return pl.pallas_call(
        lambda *refs: weight_grad_kernel(blocks, *refs),
        grid=(width // tall,),
        in_specs=[
            scalars(),
            pl.BlockSpec((blocks, tall, quarter), lambda i: (0, i, 0)),
            whole(packed.shape),
            *[pl.BlockSpec((tall, quarter), lambda i: (i, 0))] * blocks,
            whole(cn.shape),
            pl.BlockSpec((tall, 6 * LANES), lambda i: (i, 0)),
            pl.BlockSpec((tall, 1), lambda i: (i, 0)),
        ],
        out_specs=[pl.BlockSpec((tall, 6 * LANES), lambda i: (i, 0)), pl.BlockSpec((tall, 1), lambda i: (i, 0))],
        out_shape=[shape_of((width, 6 * LANES), bf16), shape_of((width, 1), f32)],
        compiler_params=params(60),
        cost_estimate=LIGHT,
        name="weight_gradient",
    )(info, xt, packed, *grads, cn, weight, gain)


def sums_kernel(came, squares, small, gain_grad, gradient, payload, small_sum):
    count = came.shape[0]
    total = came[0].astype(f32)
    for i in range(1, count):
        total = total + came[i].astype(f32)
    gradient[...] = total
    own = jnp.sum(small[...], axis=0)
    square = (
        jnp.sum(total * total, keepdims=True)
        + jnp.sum(squares[...], keepdims=True)
        + jnp.sum(own * own, keepdims=True)
    )
    small_sum[...] = own
    rows = gain_grad.shape[0]
    row = lax.broadcasted_iota(jnp.int32, (8, LANES), 0)
    gain = jnp.concatenate([gain_grad[...], jnp.zeros((8 - rows, LANES), f32)], axis=0)
    payload[...] = jnp.broadcast_to(jnp.where(row < rows, gain, square)[None], payload.shape)


def sums_part(came, squares, small, gain_grad, device_count):
    shapes = [
        shape_of(came.shape[1:], f32),
        shape_of((device_count, 8, LANES), f32),
        shape_of((8, LANES), f32),
    ]
    arrays = (came, squares, small, gain_grad)
    return pl.pallas_call(
        sums_kernel,
        in_specs=[whole(a.shape) for a in arrays],
        out_specs=[whole(s.shape) for s in shapes],
        out_shape=shapes,
        compiler_params=params(16),
        cost_estimate=LIGHT,
        name="sums",
    )(*arrays)


def stage_kernel(*refs):
    count = len(refs) // 2
    arrived = refs[-1]
    copies = [pltpu.make_async_copy(refs[i], refs[count + i], arrived.at[i]) for i in range(count)]
    for copy in copies:
        copy.start()
    for copy in copies:
        copy.wait()


def stage(*arrays):
    count = len(arrays)
    return pl.pallas_call(
        stage_kernel,
        in_specs=[pl.BlockSpec(memory_space=pltpu.HBM)] * count,
        out_specs=[pl.BlockSpec(memory_space=pltpu.VMEM)] * count,
        out_shape=[pltpu.VMEM(a.shape, a.dtype) for a in arrays],
        scratch_shapes=[pltpu.SemaphoreType.DMA((count,))],
        compiler_params=params(4),
        cost_estimate=LIGHT,
        name="stage",
    )(*arrays)


def adam_kernel(lanes, share, expert_rates, info, last, small_sum, *refs):
    held, outs, factor = refs[:14], refs[14:27], refs[27]
    dense, dense_grad, gains, router = held[:3], held[3], held[4:7], held[7:10]
    weight, first, second, gradient = held[10:14]
    stats, outs = outs[0], outs[1:]
    dense_out, gains_out, router_out, expert_out = outs[:3], outs[3:6], outs[6:9], outs[9:12]
    matrix, part = pl.program_id(0), pl.program_id(1)
    experts = router[0].shape[0]

    @pl.when((matrix == 0) & (part == 0))
    def _():
        total = jnp.sum(last[...], axis=0)
        row = lax.broadcasted_iota(jnp.int32, (8, LANES), 0)
        squares = jnp.sum(jnp.where(row < lanes, total * total, 0.0), keepdims=True)
        norm = jnp.sqrt(squares + total[7:8, :1])
        scale = jnp.minimum(1.0, clip_limit / (norm + norm_epsilon))
        stats[...] = jnp.where(row == 0, norm, scale)
        factor[...] = jnp.broadcast_to(scale, (8, LANES))
        rates = (0.71 / math.sqrt(D), 0.71 / math.sqrt(D), 0.83 / math.sqrt(D), 0.79 / math.sqrt(H * DH))
        for i, rate in enumerate(rates):
            grad = jnp.concatenate(
                [
                    dense_grad[:, i * LANES : (i + 1) * LANES],
                    dense_grad[:, 4 * LANES + i * DH : 4 * LANES + (i + 1) * DH],
                ],
                axis=1,
            )
            result = adam_update(*[ref[i] for ref in dense], grad * scale, rate)
            for ref, value in zip(dense_out, result):
                ref[i] = value
        column = lax.broadcasted_iota(jnp.int32, (LANES, LANES), 1)
        place = lax.broadcasted_iota(jnp.int32, (LANES, LANES), 0) - info[3] * share
        own = jnp.zeros((8, LANES), f32)
        for i in range(lanes):
            pick = jnp.where((column == place + i * LANES) & (column < share), 1.0, 0.0)
            own = own + jnp.dot(
                jnp.broadcast_to(total[i : i + 1], (8, LANES)), pick, precision=HIGHEST, preferred_element_type=f32
            )
        groups = -(-(1 + experts) // 8)
        table = small_sum[...]
        table = jnp.concatenate([table[:, k * share : (k + 1) * share] for k in range(groups)], axis=0)
        grad = jnp.concatenate([own[:1, :share], table[:1]], axis=0)
        for ref, value in zip(gains_out, adam_update(*[ref[...] for ref in gains], grad * scale, 0.5)):
            ref[...] = value
        grad = table[1 : 1 + experts]
        result = adam_update(*[ref[...] for ref in router], grad * scale, 0.24 / math.sqrt(D))
        for ref, value in zip(router_out, result):
            ref[...] = value

    rate = jnp.where(matrix == 0, expert_rates[0], expert_rates[1])
    tall = expert_out[0].shape[1]
    at = pl.ds(pl.multiple_of(part * tall, tall), tall)
    result = adam_update(
        weight[matrix, at, :], first[matrix, at, :], second[matrix, at, :], gradient[matrix, at, :] * factor[:1, :1], rate
    )
    for ref, value in zip(expert_out, result):
        ref[0] = value


def adam(info, last, small_sum, dense, dense_grad, gains, router, expert, expert_grad, rates):
    _, tall, wide = expert_grad.shape
    parts = 4
    block = pl.BlockSpec((1, tall // parts, wide), lambda i, j: (i, j, 0))
    held = pl.BlockSpec(memory_space=pltpu.VMEM)
    small = [*dense, *gains, *router]
    shapes = [shape_of((8, LANES), f32)] + [shape_of(a.shape, f32) for a in small]
    ins = (last, small_sum, *dense, dense_grad, *gains, *router)
    return pl.pallas_call(
        lambda *refs: adam_kernel(tall // LANES, gains[0].shape[1], rates, *refs),
        grid=(2, parts),
        in_specs=[scalars()] + [whole(a.shape) for a in ins] + [held] * 4,
        out_specs=[whole(a.shape) for a in shapes] + [block] * 3,
        out_shape=shapes + [shape_of(expert_grad.shape, f32)] * 3,
        scratch_shapes=[pltpu.VMEM((8, LANES), f32)],
        compiler_params=params(16),
        cost_estimate=LIGHT,
        name="adam",
    )(info, *ins, *expert, expert_grad)


def tie(*values):
    return lax.optimization_barrier(values)


def on_device(
    inputs,
    cotangent,
    lengths,
    routes,
    attention_weight,
    attention_mean,
    attention_square,
    expert_weight,
    expert_mean,
    expert_square,
    router_matrix,
    router_mean,
    router_square,
    norm_gains,
    gains_mean,
    gains_square,
):
    quarter, width = inputs.shape[1:]
    dp_count, tensor_count = lax.axis_size(DP), lax.axis_size(TENSOR)
    device_count = dp_count * tensor_count
    expert_count = router_matrix.shape[1]
    capacity = max(2, (5 * quarter + 4 * expert_count - 1) // (4 * expert_count))
    own_dp, own_tensor = lax.axis_index(DP), lax.axis_index(TENSOR)
    share = router_matrix.shape[0]
    rows, grad_rows, length = inputs[0], cotangent[0], lengths[0]
    info = jnp.stack([own_tensor, length, own_dp, lax.axis_index(EVERYONE)]).astype(jnp.int32)

    scaled_one, root_one, weight_own, payload = prologue(
        rows, attention_weight, norm_gains, router_matrix.T, device_count
    )
    block_two = swap(scaled_one, TENSOR, 2)
    if dp_count == 8:
        w4, w2, w1 = [swap(weight_own, DP, mask) for mask in (4, 2, 1)]
        w4, w2, w1 = tie(w4, w2, w1)
        w6, w5, w3 = swap(w4, DP, 2), swap(w4, DP, 1), swap(w2, DP, 1)
        w6, w5, w3, block_two = tie(w6, w5, w3, block_two)
        shards = [weight_own, w1, w2, w3, w4, w5, w6, swap(w6, DP, 1)]
    else:
        w6, block_two = tie(weight_own, block_two)
        shards = [lax.all_gather(weight_own, DP, axis=0, tiled=True)]
    row_blocks = [scaled_one, swap(scaled_one, TENSOR, 1), block_two, swap(block_two, TENSOR, 1)]
    small_came = lax.all_to_all(payload, EVERYONE, 0, 0, tiled=True)

    place, match, valid_scale, grad_slots = slots_part(info, routes[0], grad_rows, expert_count, capacity)
    slot_count = expert_count * capacity

    def trade(values):
        blocks = values.reshape(expert_count, capacity, values.shape[1])
        return lax.all_to_all(blocks, DP, 0, 0, tiled=True).reshape(values.shape)

    expert_pair = jnp.stack([expert_weight[0].astype(bf16)] * 2)
    expert_near = lax.all_to_all(expert_pair, "th", 0, 0, tiled=True)

    grad_slots, small_came, expert_pair = tie(grad_slots, small_came, expert_pair)
    small, weight, out_weight, qkv, keys_wide, values_turned = project(
        info, small_came, row_blocks, shards, share, expert_count
    )
    out_weights = [out_weight] + [swap(out_weight, TENSOR, j) for j in range(1, tensor_count)]
    context, chances, totals = attention_forward(qkv, keys_wide, values_turned, tensor_count)
    context, grad_slots = tie(context, grad_slots)
    context_own = lax.all_to_all(context, TENSOR, 0, 0, tiled=True)
    expert_grads = trade(grad_slots)

    middle, root_two, shares, gate, slots = middle_part(
        info, rows, context_own, out_weights, small, place, match, valid_scale
    )
    qkv, expert_near, slots = tie(qkv, expert_near, slots)
    expert_rows = trade(slots)
    turned_rows, keys_turned, third_query, context_rows = turn(info, row_blocks, qkv, context)
    expert_other = swap(expert_near, TENSOR, 1)
    grads_all = gather_relative(expert_grads, TENSOR, [2, 1])
    expert_rows, turned_rows, expert_other, grads_all = lax.optimization_barrier(
        (expert_rows, turned_rows, expert_other, grads_all)
    )
    expert_outs, expert_back = expert_part(expert_rows, expert_grads, [expert_near, expert_other])
    expert_rows, expert_back = tie(expert_rows, expert_back)
    rows_all = gather_relative(expert_rows, TENSOR, [2, 1])
    expert_back, rows_all = tie(trade(expert_back), rows_all)

    middle_grad, middle_turned, context_parts, small_grad = return_part(
        info, expert_back, place, middle, root_two, shares, gate, match, grad_rows, small, out_weights
    )
    expert_outs, context_parts = tie(expert_outs, context_parts)
    context_grad = lax.all_to_all(context_parts, TENSOR, 0, 0, tiled=True)
    middle_near, middle_far = swap(middle_turned, TENSOR, 1), swap(middle_turned, TENSOR, 2)
    expert_outs = trade(expert_outs)

    packed = attention_backward(context_grad, context, chances, totals, qkv, keys_turned, third_query)
    packed, middle_far = tie(packed, middle_far)
    middle_all = [middle_turned, middle_near, middle_far, swap(middle_far, TENSOR, 1)]
    weight_grad, gain_one_grad = weight_gradient(
        info, turned_rows, packed, middle_all, context_rows, weight, small[:1].reshape(width, 1)
    )
    weight_grad, expert_outs, expert_near = tie(weight_grad, expert_outs, expert_near)
    weight_came = lax.all_to_all(weight_grad.reshape(dp_count, -1, width), DP, 0, 0, tiled=True)
    expert_grad, expert_squares = expert_gradient(info, rows_all, grads_all, expert_near)
    expert_squares, small_grad, packed, expert_outs, *expert_state = tie(
        expert_squares, small_grad, packed, expert_outs, expert_weight[0], expert_mean[0], expert_square[0]
    )
    groups = -(-(1 + expert_count) // 8)
    small_cut = jnp.pad(small_grad, ((0, 8 * groups - 1 - expert_count), (0, 0)))
    small_cut = small_cut.reshape(groups, 8, device_count, share).transpose(2, 1, 0, 3).reshape(device_count, 8, -1)
    small_cut = jnp.pad(small_cut, ((0, 0), (0, 0), (0, LANES - groups * share)))
    small_grads = lax.all_to_all(small_cut, EVERYONE, 0, 0, tiled=True)

    input_parts = mm_nt(packed, weight).astype(bf16)
    input_parts = [
        lax.dynamic_slice_in_dim(input_parts, (own_tensor ^ j) * quarter, quarter) for j in range(tensor_count)
    ]
    first_half = input_parts[0].astype(f32) + swap(input_parts[1], TENSOR, 1).astype(f32)
    second_half = input_parts[2].astype(f32) + swap(input_parts[3], TENSOR, 1).astype(f32)
    came = swap(second_half.astype(bf16), TENSOR, 2)
    input_grad = middle_grad + norm_backward(rows, root_one, small[:1], first_half + came.astype(f32))
    picked = mm_tn(place, expert_outs)
    branch = gate * valid_scale * picked
    block_output = middle + branch
    staged = stage(*expert_state)

    weight_came, input_grad, block_output, branch, staged = tie(weight_came, input_grad, block_output, branch, staged)
    dense_grad, last, small_sum = sums_part(
        weight_came, expert_squares, small_grads, gain_one_grad.reshape(-1, LANES), device_count
    )
    last_all = lax.all_to_all(last, EVERYONE, 0, 0, tiled=True)

    rates = (0.4 * math.sqrt(expert_count / D), 1.38 * math.sqrt(expert_count / FF))
    stats, *updated = adam(
        info,
        last_all,
        small_sum,
        (attention_weight, attention_mean, attention_square),
        dense_grad,
        (norm_gains, gains_mean, gains_square),
        (router_matrix.T, router_mean.T, router_square.T),
        staged,
        expert_grad,
        rates,
    )
    attention_new, gains_new, router_new, expert_new = updated[:3], updated[3:6], updated[6:9], updated[9:]
    router_new = [part.T for part in router_new]
    grad_norm = stats[0, 0]
    return (
        block_output[None],
        input_grad[None],
        grad_norm,
        *attention_new,
        *[part[None] for part in expert_new],
        *router_new,
        *gains_new,
        branch[None],
    )


def solution(mesh):
    names = mesh.axis_names
    dp_count, tensor_count = mesh.shape[names[0]], mesh.shape[names[1]]
    cut = jax.sharding.Mesh(mesh.devices.reshape(dp_count // 2, 2, tensor_count // 2, 2), EVERYONE)
    rows = P(DP, TENSOR, None)
    attention = P(None, DP, TENSOR)
    expert = P(DP, None, None, TENSOR)
    router = P(EVERYONE, None)
    gains = P(None, EVERYONE)
    weights = (attention,) * 3 + (expert,) * 3 + (router,) * 3 + (gains,) * 3
    return jax.shard_map(
        on_device,
        mesh=cut,
        in_specs=(rows, rows, P(DP), rows) + weights,
        out_specs=(rows, rows, P()) + weights + (rows,),
        check_vma=False,
    )
```

```python
import math

import jax
import jax.numpy as jnp
from jax import lax
from jax.experimental import pallas as pl
from jax.experimental.pallas import tpu as pltpu
from jax.sharding import PartitionSpec as P

D = 768
H = 12
DH = 64
FF = 3072
STEP = 10

HIGHEST = lax.Precision.HIGHEST
norm_epsilon = 1e-06
beta_first = 0.9
beta_second = 0.999
adam_epsilon = 1e-08
decay_factor = 0.01
clip_limit = 1.0
masked_score = -1e30
score_scale = 1.0 / math.sqrt(DH)
bf16 = jnp.bfloat16
f32 = jnp.float32
MIB = 1 << 20
LANES = 128


DP = ("dh", "dl")
TENSOR = ("th", "tl")
EVERYONE = DP + TENSOR


def swap(values, axis, mask):
    count = lax.axis_size(axis)
    return lax.ppermute(values, axis, [(i, i ^ mask) for i in range(count)])


def bits_of(count):
    return [1 << b for b in range(count.bit_length() - 1)]


def gather_relative(block, axis, order):
    held = {0: block}
    for mask in order:
        for j in list(held):
            held[j ^ mask] = swap(held[j], axis, mask)
    return [held[j] for j in range(len(held))]


def mm(a, b):
    return jnp.dot(a, b, preferred_element_type=f32)


def mm_nt(a, b, precision=None):
    return lax.dot_general(
        a, b, (((1,), (1,)), ((), ())), preferred_element_type=f32, precision=precision
    )


def mm_tn(a, b, precision=None):
    return lax.dot_general(
        a, b, (((0,), (0,)), ((), ())), preferred_element_type=f32, precision=precision
    )


def norm_root(values):
    return lax.rsqrt(jnp.mean(values * values, axis=-1, keepdims=True) + norm_epsilon)


def norm_backward(values, root, gain_row, grad):
    scaled = values * root
    inner = grad * gain_row
    centre = jnp.mean(inner * scaled, axis=-1, keepdims=True)
    return root * (inner - scaled * centre)


def gelu_pair(values):
    c = math.sqrt(2.0 / math.pi)
    square = values * values
    th = jnp.tanh(c * values * (1.0 + 0.044715 * square))
    half = 0.5 * (1.0 + th)
    slope = half + 0.5 * values * (1.0 - th * th) * c * (1.0 + 3.0 * 0.044715 * square)
    return values * half, slope


def adam_update(weight, moment_one, moment_two, gradient, step_rate):
    moment_one_next = beta_first * moment_one + (1.0 - beta_first) * gradient
    moment_two_next = beta_second * moment_two + (1.0 - beta_second) * gradient * gradient
    corrected_one = moment_one_next / (1.0 - beta_first**STEP)
    corrected_two = moment_two_next / (1.0 - beta_second**STEP)
    weight_next = weight - step_rate * (
        corrected_one / (jnp.sqrt(corrected_two) + adam_epsilon) + decay_factor * weight
    )
    return (weight_next, moment_one_next, moment_two_next)


def shape_of(shape, dtype):
    return jax.ShapeDtypeStruct(shape, dtype)


def whole(shape):
    return pl.BlockSpec(shape, lambda *_: (0,) * len(shape))


def scalars():
    return pl.BlockSpec(memory_space=pltpu.SMEM)


LIGHT = pl.CostEstimate(flops=1, bytes_accessed=1, transcendentals=0)


def params(limit):
    return pltpu.CompilerParams(vmem_limit_bytes=limit * MIB)


def prologue_kernel(inputs, attention, gains, router, scaled, root, packed, payload):
    values = inputs[...]
    scale = norm_root(values)
    root[...] = scale
    scaled[...] = (values * scale).astype(bf16)
    parts = [attention[i].astype(bf16) for i in range(4)]
    packed[...] = jnp.concatenate(
        [part[:, :LANES] for part in parts] + [part[:, LANES:] for part in parts], axis=1
    )
    experts, share = router.shape
    groups = -(-(2 + experts) // 8)
    wide = jnp.concatenate([gains[...], router[...]], axis=0)
    wide = jnp.pad(wide, ((0, 8 * groups - 2 - experts), (0, 0)))
    row = jnp.concatenate([wide[8 * k : 8 * k + 8] for k in range(groups)], axis=1)
    row = jnp.pad(row, ((0, 0), (0, LANES - groups * share)))
    payload[...] = jnp.broadcast_to(row[None], payload.shape)


def prologue(inputs, attention, gains, router, device_count):
    quarter, width = inputs.shape
    tall = attention.shape[1]
    shapes = [
        shape_of((quarter, width), bf16),
        shape_of((quarter, 1), f32),
        shape_of((tall, 6 * LANES), bf16),
        shape_of((device_count, 8, LANES), f32),
    ]
    arrays = (inputs, attention, gains, router)
    return pl.pallas_call(
        prologue_kernel,
        in_specs=[whole(a.shape) for a in arrays],
        out_specs=[whole(s.shape) for s in shapes],
        out_shape=shapes,
        compiler_params=params(60),
        cost_estimate=LIGHT,
        name="prologue",
    )(*arrays)


def slots_kernel(capacity, info, routes, grads, place, match, valid, slots):
    quarter = routes.shape[0]
    experts = match.shape[1]
    row = lax.broadcasted_iota(jnp.int32, (quarter, 1), 0) + info[0] * quarter
    inside = jnp.where(row < info[1], 1.0, 0.0)
    valid[...] = inside
    column = lax.broadcasted_iota(jnp.int32, (quarter, experts), 1)
    named = jnp.where(routes[...] == column, 1.0, 0.0)
    match[...] = named
    at = lax.broadcasted_iota(jnp.int32, (quarter, quarter), 0)
    before = lax.broadcasted_iota(jnp.int32, (quarter, quarter), 1)
    lower = jnp.where(at >= before, 1.0, 0.0).astype(bf16)
    rank = jnp.sum(mm(lower, (named * inside).astype(bf16)) * named, axis=1, keepdims=True) - 1.0
    slot = jnp.where(inside > 0.0, routes[...].astype(f32) * capacity + rank, -1.0)
    slot = jnp.broadcast_to(slot, (quarter, LANES)).T[:1]
    number = lax.broadcasted_iota(jnp.int32, place.shape, 0).astype(f32)
    chosen = jnp.where(number == slot, 1.0, 0.0).astype(bf16)
    place[...] = chosen
    slots[...] = mm(chosen, grads[...].astype(bf16)).astype(bf16)


def slots_part(info, routes, grads, experts, capacity):
    quarter, width = grads.shape
    shapes = [
        shape_of((experts * capacity, quarter), bf16),
        shape_of((quarter, experts), f32),
        shape_of((quarter, 1), f32),
        shape_of((experts * capacity, width), bf16),
    ]
    return pl.pallas_call(
        lambda *refs: slots_kernel(capacity, *refs),
        in_specs=[scalars(), whole(routes.shape), whole(grads.shape)],
        out_specs=[whole(s.shape) for s in shapes],
        out_shape=shapes,
        compiler_params=params(60),
        cost_estimate=LIGHT,
        name="slots",
    )(info, routes, grads)


def project_kernel(quarter, blocks, count, share, info, came, x0, x1, x2, x3, *refs):
    shards, (small, weight, out_weight, qkv, kaug, vt) = refs[:count], refs[count:]
    tall = shards[0].shape[0]
    width = weight.shape[0]
    for j, ref in enumerate(shards):
        start = pl.multiple_of((info[2] ^ j) * tall, tall) if count > 1 else 0
        weight[pl.ds(start, tall), :] = ref[...]
    out_weight[:LANES, :] = weight[:, 3 * LANES : 4 * LANES].T
    out_weight[LANES:, :] = weight[:, 5 * LANES :].T[DH:]
    groups = small.shape[0] // 8
    devices = came.shape[0]
    flat = came[...].reshape(devices * 8, LANES)
    lane = lax.broadcasted_iota(jnp.int32, (LANES, width), 0)
    column = lax.broadcasted_iota(jnp.int32, (LANES, width), 1)
    inside = lax.rem(column, share)
    owner = lax.broadcasted_iota(jnp.int32, (devices, 1, width), 2) - share * lax.broadcasted_iota(
        jnp.int32, (devices, 1, width), 0
    )
    owner = jnp.where((owner >= 0) & (owner < share), 1.0, 0.0)
    for k in range(groups):
        pick = jnp.where(lane == inside + k * share, 1.0, 0.0)
        spread = jnp.dot(flat, pick, precision=HIGHEST, preferred_element_type=f32)
        small[8 * k : 8 * k + 8, :] = jnp.sum(spread.reshape(devices, 8, width) * owner, axis=0)
    gain = small[:1, :]
    for j, ref in enumerate((x0, x1, x2, x3)):
        start = pl.multiple_of((info[0] ^ j) * quarter, quarter)
        rows = pl.ds(start, quarter)
        scaled = (ref[...].astype(f32) * gain).astype(bf16)
        first = mm(scaled, weight[:, : 3 * LANES]).astype(bf16)
        second = mm(scaled, weight[:, 4 * LANES :]).astype(bf16)
        qkv[rows, : 3 * LANES] = first
        qkv[rows, 3 * LANES :] = second
        kaug[rows, :LANES] = first[:, LANES : 2 * LANES]
        lane = lax.broadcasted_iota(jnp.int32, (quarter, LANES), 1)
        row = lax.broadcasted_iota(jnp.int32, (quarter, LANES), 0) + start
        hidden = jnp.where((lane == 0) & (row >= info[1]), masked_score, 0.0)
        kaug[rows, LANES:] = jnp.where(lane < DH, hidden, second[:, :LANES].astype(f32)).astype(bf16)
        values = first[:, 2 * LANES :].T
        vt[0, :DH, rows] = values[:DH]
        vt[1, :DH, rows] = values[DH:]
        vt[2, :DH, rows] = second[:, LANES:].T[:DH]
    full_len = quarter * blocks
    tail = (lax.broadcasted_iota(jnp.int32, (16, full_len), 0) == 0).astype(f32).astype(bf16)
    for h in range(3):
        vt[h, DH:, :] = tail


def project(info, came, rows, shards, share, experts):
    quarter, width = rows[0].shape
    blocks = len(rows)
    full_len = quarter * blocks
    shapes = [
        shape_of((8 * -(-(2 + experts) // 8), width), f32),
        shape_of((width, 6 * LANES), bf16),
        shape_of((3 * DH, width), bf16),
        shape_of((full_len, 5 * LANES), bf16),
        shape_of((full_len, 2 * LANES), bf16),
        shape_of((3, DH + 16, full_len), bf16),
    ]
    arrays = (came, *rows, *shards)
    return pl.pallas_call(
        lambda *refs: project_kernel(quarter, blocks, len(shards), share, *refs),
        in_specs=[scalars()] + [whole(a.shape) for a in arrays],
        out_specs=[whole(s.shape) for s in shapes],
        out_shape=shapes,
        compiler_params=params(60),
        cost_estimate=LIGHT,
        name="project",
    )(info, *arrays)


def attention_kernel(qkv, kaug, vt, context, chances, totals):
    quarter = context.shape[2]
    step = pl.program_id(0)
    rows = pl.ds(pl.multiple_of(step * quarter, quarter), quarter)
    q01 = (qkv[rows, :LANES].astype(f32) * score_scale).T.astype(bf16)
    q2 = (qkv[rows, 3 * LANES : 4 * LANES].astype(f32) * score_scale).T.astype(bf16)[:DH]
    ones = (lax.broadcasted_iota(jnp.int32, (DH, quarter), 0) == 0).astype(f32).astype(bf16)
    zeros = jnp.zeros((DH, quarter), bf16)
    queries = (
        jnp.concatenate([q01[:DH], zeros, ones, zeros], axis=0),
        jnp.concatenate([zeros, q01[DH:], ones, zeros], axis=0),
        jnp.concatenate([zeros, zeros, ones, q2], axis=0),
    )
    full_len = kaug.shape[0]
    all_scores = [mm(kaug[...], queries[h]) for h in range(3)]
    for h in range(3):
        scores = all_scores[h]
        top = jnp.max(jnp.max(scores.reshape(8, full_len // 8, quarter), axis=0), axis=0, keepdims=True)
        low = jnp.exp(scores - top).astype(bf16)
        chances[h] = low
        summed = mm(vt[h], low)
        part = 1.0 / summed[DH : DH + 1]
        totals[0, h : h + 1, :] = part
        context[0, h * DH : (h + 1) * DH, :] = (summed[:DH] * part).astype(bf16)


def attention_forward(qkv, kaug, vt, blocks):
    full_len = qkv.shape[0]
    quarter = full_len // blocks
    inner = 3 * DH
    return pl.pallas_call(
        attention_kernel,
        grid=(blocks,),
        in_specs=[whole(qkv.shape), whole(kaug.shape), whole(vt.shape)],
        out_specs=[
            pl.BlockSpec((1, inner, quarter), lambda i: (i, 0, 0)),
            pl.BlockSpec((3, full_len, quarter), lambda i: (0, 0, i)),
            pl.BlockSpec((1, 3, quarter), lambda i: (i, 0, 0)),
        ],
        out_shape=[
            shape_of((blocks, inner, quarter), bf16),
            shape_of((3, full_len, full_len), bf16),
            shape_of((blocks, 3, quarter), f32),
        ],
        compiler_params=params(60),
        cost_estimate=LIGHT,
        name="attend",
    )(qkv, kaug, vt)


def turn_kernel(quarter, blocks, info, x0, x1, x2, x3, qkv, context, xt, kt, q2, cn):
    for j, ref in enumerate((x0, x1, x2, x3)):
        xt[info[0] ^ j] = ref[...].T
    for j in range(blocks):
        rows = slice(j * quarter, (j + 1) * quarter)
        third = qkv[rows, 3 * LANES : 4 * LANES].T
        kt[:LANES, rows] = qkv[rows, LANES : 2 * LANES].T
        kt[LANES:, rows] = third[DH:]
        zeros = jnp.zeros((DH, quarter), bf16)
        q2[rows, :] = jnp.concatenate([zeros, third[:DH]], axis=0).T
        cn[rows, :LANES] = context[j, :LANES, :].T
        cn[rows, LANES:] = jnp.concatenate([zeros, context[j, LANES:, :]], axis=0).T


def turn(info, rows, qkv, context):
    quarter, width = rows[0].shape
    blocks = len(rows)
    full_len = quarter * blocks
    shapes = [
        shape_of((blocks, width, quarter), bf16),
        shape_of((3 * DH, full_len), bf16),
        shape_of((full_len, LANES), bf16),
        shape_of((full_len, 2 * LANES), bf16),
    ]
    return pl.pallas_call(
        lambda *refs: turn_kernel(quarter, blocks, *refs),
        in_specs=[scalars()] + [whole((quarter, width))] * 4 + [whole(qkv.shape), whole(context.shape)],
        out_specs=[whole(s.shape) for s in shapes],
        out_shape=shapes,
        compiler_params=params(60),
        cost_estimate=LIGHT,
        name="turn",
    )(info, *rows, qkv, context)


def two_columns(column):
    high = column.astype(bf16).astype(f32)
    lane = lax.broadcasted_iota(jnp.int32, (column.shape[0], LANES), 1)
    return jnp.where(lane == 0, high, jnp.where(lane == 1, column - high, 0.0)).astype(bf16)


def middle_kernel(
    info, rows, context, w0, w1, w2, w3, small, place, match, valid, middle, root, chances, gate, slots
):
    gain, router = small[1:2, :], small[2 : 2 + match.shape[1], :]
    total = rows[...]
    for j, ref in enumerate((w0, w1, w2, w3)):
        total = total + mm_tn(context[info[0] ^ j], ref[...])
    middle[...] = total
    scale = norm_root(total)
    root[...] = scale
    hidden = total * scale * gain
    scores = mm_nt(hidden, router, HIGHEST)
    powers = jnp.exp(scores - jnp.max(scores, axis=-1, keepdims=True))
    share = powers / jnp.sum(powers, axis=-1, keepdims=True)
    chances[...] = share
    own = jnp.sum(share * match[...], axis=-1, keepdims=True)
    gate[...] = own
    width = rows.shape[1]
    slots[:, :width] = mm(place[...], hidden.astype(bf16)).astype(bf16)
    slots[:, width:] = mm(place[...], two_columns(own * valid[...])).astype(bf16)


def middle_part(info, rows, context, out_weights, small, place, match, valid):
    quarter, width = rows.shape
    experts = match.shape[1]
    shapes = [
        shape_of((quarter, width), f32),
        shape_of((quarter, 1), f32),
        shape_of((quarter, experts), f32),
        shape_of((quarter, 1), f32),
        shape_of((place.shape[0], width + LANES), bf16),
    ]
    arrays = (rows, context, *out_weights, small, place, match, valid)
    return pl.pallas_call(
        middle_kernel,
        in_specs=[scalars()] + [whole(a.shape) for a in arrays],
        out_specs=[whole(s.shape) for s in shapes],
        out_shape=shapes,
        compiler_params=params(60),
        cost_estimate=LIGHT,
        name="middle",
    )(info, *arrays)


def expert_kernel(rows, grads, near_in, near_out, other_in, other_out, out, back, held, arrived):
    width = grads.shape[1]
    copies = []
    for i, (inward, outward) in enumerate(((near_in, near_out), (other_in, other_out))):
        for j in range(2):
            at = 2 * i + j
            copies.append(
                (
                    pltpu.make_async_copy(outward.at[j], held.at[at, 1], arrived.at[at, 1]),
                    pltpu.make_async_copy(inward.at[j], held.at[at, 0], arrived.at[at, 0]),
                )
            )
    for pair in copies:
        for copy in pair:
            copy.start()
    out_total, back_total = None, None
    for i, pair in enumerate(copies):
        for copy in pair:
            copy.wait()
        inward, outward = held[i, 0], held[i, 1]
        grad = mm(grads[...], outward)
        active, slope = gelu_pair(mm(rows[:, :width], inward))
        part = mm_nt(active.astype(bf16), outward)
        back_part = mm_nt((grad * slope).astype(bf16), inward)
        out_total = part if i == 0 else out_total + part
        back_total = back_part if i == 0 else back_total + back_part
    result = out_total.astype(bf16)
    out[...] = result
    back[:, :width] = back_total.astype(bf16)
    match = jnp.sum(grads[...].astype(f32) * result.astype(f32), axis=-1, keepdims=True)
    back[:, width:] = two_columns(match)


def expert_part(rows, grads, weights):
    slots, width = grads.shape
    hidden = weights[0].shape[2]
    count = len(weights)
    shapes = [shape_of((slots, width), bf16), shape_of((slots, width + LANES), bf16)]
    return pl.pallas_call(
        expert_kernel,
        in_specs=[whole(rows.shape), whole(grads.shape)] + [pl.BlockSpec(memory_space=pl.ANY)] * count,
        out_specs=[whole(s.shape) for s in shapes],
        out_shape=shapes,
        scratch_shapes=[pltpu.VMEM((count, 2) + weights[0].shape[1:], bf16), pltpu.SemaphoreType.DMA((count, 2))],
        compiler_params=params(60),
        cost_estimate=LIGHT,
        name="experts",
    )(rows, grads, *weights)


def pack_small(small, cut):
    devices = cut.shape[0]
    rows, width = small.shape
    share = width // devices
    groups = rows // 8
    column = lax.broadcasted_iota(jnp.int32, (devices, 1, width), 2)
    owner = column - share * lax.broadcasted_iota(jnp.int32, (devices, 1, width), 0)
    owner = jnp.where((owner >= 0) & (owner < share), 1.0, 0.0)
    lane = lax.broadcasted_iota(jnp.int32, (width, LANES), 1)
    inside = lax.rem(lax.broadcasted_iota(jnp.int32, (width, LANES), 0), share)
    total = None
    for k in range(groups):
        pick = jnp.where(lane == inside + k * share, 1.0, 0.0)
        spread = (small[8 * k : 8 * k + 8, :][None] * owner).reshape(devices * 8, width)
        part = jnp.dot(spread, pick, precision=HIGHEST, preferred_element_type=f32)
        total = part if total is None else total + part
    cut[...] = total.reshape(devices, 8, LANES)


def expert_grad_kernel(count, *refs):
    info, rows, grads = refs[0], refs[1 : count + 1], refs[count + 1 : 2 * count + 1]
    small, near_in, near_out, out, square, cut, weight, row_all, grad_all, inner_all, active_all, arrived = refs[
        2 * count + 1 :
    ]
    copies = [
        pltpu.make_async_copy(ref.at[lax.div(info[0], 2)], weight.at[i], arrived.at[i])
        for i, ref in enumerate((near_in, near_out))
    ]
    for copy in copies:
        copy.start()
    pack_small(small, cut)
    for copy in copies:
        copy.wait()
    slots, width = grads[0].shape
    for j in range(count):
        at = slice(j * slots, (j + 1) * slots)
        gate = rows[j][:, width : width + 1].astype(f32) + rows[j][:, width + 1 : width + 2].astype(f32)
        row_all[at, :] = rows[j][:, :width]
        grad_all[at, :] = (grads[j][...].astype(f32) * gate).astype(bf16)
        back = mm(grads[j][...], weight[1])
        active, slope = gelu_pair(mm(rows[j][:, :width], weight[0]))
        inner_all[at, :] = (back * slope * gate).astype(bf16)
        active_all[at, :] = active.astype(bf16)
    first = mm_tn(row_all[...], inner_all[...])
    out[0] = first
    second = mm_tn(grad_all[...], active_all[...])
    out[1] = second
    square[...] = jnp.sum(first * first + second * second, axis=0, keepdims=True)


def expert_gradient(info, rows, grads, small, near_in, near_out, device_count):
    count = len(rows)
    slots, width = grads[0].shape
    hidden = near_in.shape[2]
    arrays = (*rows, *grads, small)
    shapes = [
        shape_of((2, width, hidden), f32),
        shape_of((1, hidden), f32),
        shape_of((device_count, 8, LANES), f32),
    ]
    return pl.pallas_call(
        lambda *refs: expert_grad_kernel(count, *refs),
        in_specs=[scalars()] + [whole(a.shape) for a in arrays] + [pl.BlockSpec(memory_space=pl.ANY)] * 2,
        out_specs=[whole(s.shape) for s in shapes],
        out_shape=shapes,
        scratch_shapes=[pltpu.VMEM((2, width, hidden), bf16)]
        + [pltpu.VMEM((count * slots, width), bf16)] * 2
        + [pltpu.VMEM((count * slots, hidden), bf16)] * 2
        + [pltpu.SemaphoreType.DMA((2,))],
        compiler_params=params(60),
        cost_estimate=LIGHT,
        name="expert_gradient",
    )(info, *arrays, near_in, near_out)


def return_kernel(
    info, back, place, middle, root, chances, gate, match, cotangent, small, w0, w1, w2, w3,
    grad, turned, parts, small_grad,
):
    experts = match.shape[1]
    gain, router = small[1:2, :], small[2 : 2 + experts, :]
    width = middle.shape[1]
    came = mm_tn(place[...], back[...])
    gate_grad = came[:, width : width + 1] + came[:, width + 1 : width + 2]
    own = gate[...]
    score_grad = own * (match[...] - chances[...]) * gate_grad
    scaled = middle[...] * root[...]
    hidden = scaled * gain
    tall = small_grad.shape[0]
    small_grad[1 : 1 + experts, :] = mm_tn(score_grad, hidden, HIGHEST)
    small_grad[1 + experts :, :] = jnp.zeros((tall - 1 - experts, hidden.shape[1]), f32)
    second = own * came[:, :width] + jnp.dot(
        score_grad, router, precision=HIGHEST, preferred_element_type=f32
    )
    small_grad[:1, :] = jnp.sum(second * scaled, axis=0, keepdims=True)
    inner = second * gain
    centre = jnp.mean(inner * scaled, axis=-1, keepdims=True)
    total = cotangent[...] + root[...] * (inner - scaled * centre)
    grad[...] = total
    low = total.astype(bf16)
    turned[...] = low.T
    for j, ref in enumerate((w0, w1, w2, w3)):
        parts[info[0] ^ j] = mm_nt(ref[...], low).astype(bf16)


def return_part(info, back, place, middle, root, chances, gate, match, cotangent, small, out_weights):
    quarter, width = middle.shape
    experts = match.shape[1]
    inner = out_weights[0].shape[0]
    shapes = [
        shape_of((quarter, width), f32),
        shape_of((width, quarter), bf16),
        shape_of((len(out_weights), inner, quarter), bf16),
        shape_of((8 * -(-(1 + experts) // 8), width), f32),
    ]
    arrays = (back, place, middle, root, chances, gate, match, cotangent, small, *out_weights)
    return pl.pallas_call(
        return_kernel,
        in_specs=[scalars()] + [whole(a.shape) for a in arrays],
        out_specs=[whole(s.shape) for s in shapes],
        out_shape=shapes,
        compiler_params=params(60),
        cost_estimate=LIGHT,
        name="returned",
    )(info, *arrays)


def attention_back_kernel(blocks, grads, context, chances, totals, qkv, kt, q2, packed, vaug, k01, k2, v01, v2):
    step = pl.program_id(0)
    quarter = grads.shape[2]

    @pl.when(step == 0)
    def _():
        vaug[:, :LANES] = qkv[:, 2 * LANES : 3 * LANES]
        lane = lax.broadcasted_iota(jnp.int32, (vaug.shape[0], LANES), 1)
        ones = jnp.where(lane < DH + 2, 1.0, 0.0)
        vaug[:, LANES:] = jnp.where(lane < DH, qkv[:, 4 * LANES :].astype(f32), ones).astype(bf16)
        for ref in (k01, k2, v01, v2):
            ref[...] = jnp.zeros(ref.shape, f32)

    rows = pl.ds(pl.multiple_of(step * quarter, quarter), quarter)
    raw = grads[0].astype(f32)
    scale = totals[0]
    scaled = [raw[h * DH : (h + 1) * DH] * scale[h : h + 1] for h in range(3)]
    heads = jnp.concatenate(scaled, axis=0).astype(bf16)
    lane = lax.broadcasted_iota(jnp.int32, (quarter, LANES), 1)
    row = lax.broadcasted_iota(jnp.int32, (DH, quarter), 0)
    zeros = jnp.zeros((DH, quarter), bf16)
    q01 = qkv[rows, :LANES].astype(f32)
    g01 = heads[:LANES].T.astype(f32)
    g2 = jnp.concatenate([heads[LANES:], zeros], axis=0).T
    query_parts = []
    for h in range(3):
        part = heads[h * DH : (h + 1) * DH]
        centre = -jnp.sum(
            part.astype(f32) * context[0, h * DH : (h + 1) * DH, :].astype(f32), axis=0, keepdims=True
        )
        high = centre.astype(bf16).astype(f32)
        tail = jnp.where(row == 0, high, jnp.where(row == 1, centre - high, 0.0)).astype(bf16)
        pieces = [zeros, zeros, zeros, tail]
        pieces[h] = part
        chance_grad = mm(vaug[...], jnp.concatenate(pieces, axis=0))
        low = chances[h]
        score_grad = (low.astype(f32) * chance_grad).astype(bf16)
        query_parts.append(mm(kt[h * DH : (h + 1) * DH, :], score_grad) * score_scale)
        if h < 2:
            inside = (lane >= h * DH) & (lane < (h + 1) * DH)
            k01[...] += mm(score_grad, jnp.where(inside, q01, 0.0).astype(bf16))
            v01[...] += mm(low, jnp.where(inside, g01, 0.0).astype(bf16))
        else:
            k2[...] += mm(score_grad, q2[rows, :])
            v2[...] += mm(low, g2)
    packed[rows, :LANES] = jnp.concatenate(query_parts[:2], axis=0).T.astype(bf16)
    packed[rows, 4 * LANES : 5 * LANES] = (
        jnp.concatenate([query_parts[2], jnp.zeros((DH, quarter), f32)], axis=0).T.astype(bf16)
    )

    @pl.when(step == blocks - 1)
    def _():
        packed[:, LANES : 2 * LANES] = (k01[...] * score_scale).astype(bf16)
        packed[:, 2 * LANES : 3 * LANES] = v01[...].astype(bf16)
        packed[:, 3 * LANES : 4 * LANES] = jnp.zeros(k01.shape, bf16)
        packed[:, 4 * LANES : 5 * LANES] = packed[:, 4 * LANES : 5 * LANES] + (k2[...] * score_scale).astype(bf16)
        packed[:, 5 * LANES :] = v2[...].astype(bf16)


def attention_backward(grads, context, chances, totals, qkv, kt, q2):
    blocks, inner, quarter = grads.shape
    full_len = quarter * blocks
    block = pl.BlockSpec((1, inner, quarter), lambda i: (i, 0, 0))
    return pl.pallas_call(
        lambda *refs: attention_back_kernel(blocks, *refs),
        grid=(blocks,),
        in_specs=[
            block,
            block,
            pl.BlockSpec((3, full_len, quarter), lambda i: (0, 0, i)),
            pl.BlockSpec((1, 3, quarter), lambda i: (i, 0, 0)),
            whole(qkv.shape),
            whole(kt.shape),
            whole(q2.shape),
        ],
        out_specs=whole((full_len, 6 * LANES)),
        out_shape=shape_of((full_len, 6 * LANES), bf16),
        scratch_shapes=[pltpu.VMEM((full_len, 2 * LANES), bf16)] + [pltpu.VMEM((full_len, LANES), f32)] * 4,
        compiler_params=params(60),
        cost_estimate=LIGHT,
        name="attend_back",
    )(grads, context, chances, totals, qkv, kt, q2)


def weight_grad_kernel(blocks, info, xt, packed, g0, g1, g2, g3, cn, weight, gain, out, gain_grad):
    quarter = xt.shape[2]
    total, outer = None, None
    for j, ref in enumerate((g0, g1, g2, g3)):
        rows = slice(j * quarter, (j + 1) * quarter)
        there = pl.ds(pl.multiple_of((info[0] ^ j) * quarter, quarter), quarter)
        part = mm(xt[j], packed[rows, :])
        own = mm(ref[...], cn[there, :])
        total = part if total is None else total + part
        outer = own if outer is None else outer + own
    gain_grad[...] = jnp.sum(total * weight[...].astype(f32), axis=1, keepdims=True)
    total = total * gain[...]
    out[:, : 3 * LANES] = total[:, : 3 * LANES].astype(bf16)
    out[:, 3 * LANES : 4 * LANES] = outer[:, :LANES].astype(bf16)
    out[:, 4 * LANES : 5 * LANES] = total[:, 4 * LANES : 5 * LANES].astype(bf16)
    out[:, 5 * LANES :] = (total[:, 5 * LANES :] + outer[:, LANES:]).astype(bf16)


def weight_gradient(info, xt, packed, grads, cn, weight, gain):
    blocks, width, quarter = xt.shape
    tall = 256
    full_len = quarter * blocks
    return pl.pallas_call(
        lambda *refs: weight_grad_kernel(blocks, *refs),
        grid=(width // tall,),
        in_specs=[
            scalars(),
            pl.BlockSpec((blocks, tall, quarter), lambda i: (0, i, 0)),
            whole(packed.shape),
            *[pl.BlockSpec((tall, quarter), lambda i: (i, 0))] * blocks,
            whole(cn.shape),
            pl.BlockSpec((tall, 6 * LANES), lambda i: (i, 0)),
            pl.BlockSpec((tall, 1), lambda i: (i, 0)),
        ],
        out_specs=[pl.BlockSpec((tall, 6 * LANES), lambda i: (i, 0)), pl.BlockSpec((tall, 1), lambda i: (i, 0))],
        out_shape=[shape_of((width, 6 * LANES), bf16), shape_of((width, 1), f32)],
        compiler_params=params(60),
        cost_estimate=LIGHT,
        name="weight_gradient",
    )(info, xt, packed, *grads, cn, weight, gain)


def sums_kernel(came, squares, small, gain_grad, gradient, payload, small_sum):
    count = came.shape[0]
    total = came[0].astype(f32)
    for i in range(1, count):
        total = total + came[i].astype(f32)
    gradient[...] = total
    own = jnp.sum(small[...], axis=0)
    square = (
        jnp.sum(total * total, keepdims=True)
        + jnp.sum(squares[...], keepdims=True)
        + jnp.sum(own * own, keepdims=True)
    )
    small_sum[...] = own
    rows = gain_grad.shape[0]
    row = lax.broadcasted_iota(jnp.int32, (8, LANES), 0)
    gain = jnp.concatenate([gain_grad[...], jnp.zeros((8 - rows, LANES), f32)], axis=0)
    payload[...] = jnp.broadcast_to(jnp.where(row < rows, gain, square)[None], payload.shape)


def sums_part(came, squares, small, gain_grad, device_count):
    shapes = [
        shape_of(came.shape[1:], f32),
        shape_of((device_count, 8, LANES), f32),
        shape_of((8, LANES), f32),
    ]
    arrays = (came, squares, small, gain_grad)
    return pl.pallas_call(
        sums_kernel,
        in_specs=[whole(a.shape) for a in arrays],
        out_specs=[whole(s.shape) for s in shapes],
        out_shape=shapes,
        compiler_params=params(16),
        cost_estimate=LIGHT,
        name="sums",
    )(*arrays)


def stage_kernel(*refs):
    count = len(refs) // 2
    arrived = refs[-1]
    copies = [pltpu.make_async_copy(refs[i], refs[count + i], arrived.at[i]) for i in range(count)]
    for copy in copies:
        copy.start()
    for copy in copies:
        copy.wait()


def stage(*arrays):
    count = len(arrays)
    return pl.pallas_call(
        stage_kernel,
        in_specs=[pl.BlockSpec(memory_space=pltpu.HBM)] * count,
        out_specs=[pl.BlockSpec(memory_space=pltpu.VMEM)] * count,
        out_shape=[pltpu.VMEM(a.shape, a.dtype) for a in arrays],
        scratch_shapes=[pltpu.SemaphoreType.DMA((count,))],
        compiler_params=params(4),
        cost_estimate=LIGHT,
        name="stage",
    )(*arrays)


def adam_kernel(lanes, share, expert_rates, info, last, small_sum, *refs):
    held, outs, factor = refs[:14], refs[14:27], refs[27]
    dense, dense_grad, gains, router = held[:3], held[3], held[4:7], held[7:10]
    weight, first, second, gradient = held[10:14]
    stats, outs = outs[0], outs[1:]
    dense_out, gains_out, router_out, expert_out = outs[:3], outs[3:6], outs[6:9], outs[9:12]
    matrix, part = pl.program_id(0), pl.program_id(1)
    experts = router[0].shape[0]

    @pl.when((matrix == 0) & (part == 0))
    def _():
        total = jnp.sum(last[...], axis=0)
        row = lax.broadcasted_iota(jnp.int32, (8, LANES), 0)
        squares = jnp.sum(jnp.where(row < lanes, total * total, 0.0), keepdims=True)
        norm = jnp.sqrt(squares + total[7:8, :1])
        scale = jnp.minimum(1.0, clip_limit / (norm + norm_epsilon))
        stats[...] = jnp.where(row == 0, norm, scale)
        factor[...] = jnp.broadcast_to(scale, (8, LANES))
        rates = (0.71 / math.sqrt(D), 0.71 / math.sqrt(D), 0.83 / math.sqrt(D), 0.79 / math.sqrt(H * DH))
        for i, rate in enumerate(rates):
            grad = jnp.concatenate(
                [
                    dense_grad[:, i * LANES : (i + 1) * LANES],
                    dense_grad[:, 4 * LANES + i * DH : 4 * LANES + (i + 1) * DH],
                ],
                axis=1,
            )
            result = adam_update(*[ref[i] for ref in dense], grad * scale, rate)
            for ref, value in zip(dense_out, result):
                ref[i] = value
        column = lax.broadcasted_iota(jnp.int32, (LANES, LANES), 1)
        place = lax.broadcasted_iota(jnp.int32, (LANES, LANES), 0) - info[3] * share
        own = jnp.zeros((8, LANES), f32)
        for i in range(lanes):
            pick = jnp.where((column == place + i * LANES) & (column < share), 1.0, 0.0)
            own = own + jnp.dot(
                jnp.broadcast_to(total[i : i + 1], (8, LANES)), pick, precision=HIGHEST, preferred_element_type=f32
            )
        groups = -(-(1 + experts) // 8)
        table = small_sum[...]
        table = jnp.concatenate([table[:, k * share : (k + 1) * share] for k in range(groups)], axis=0)
        grad = jnp.concatenate([own[:1, :share], table[:1]], axis=0)
        for ref, value in zip(gains_out, adam_update(*[ref[...] for ref in gains], grad * scale, 0.5)):
            ref[...] = value
        grad = table[1 : 1 + experts]
        result = adam_update(*[ref[...] for ref in router], grad * scale, 0.24 / math.sqrt(D))
        for ref, value in zip(router_out, result):
            ref[...] = value

    rate = jnp.where(matrix == 0, expert_rates[0], expert_rates[1])
    tall = expert_out[0].shape[1]
    at = pl.ds(pl.multiple_of(part * tall, tall), tall)
    result = adam_update(
        weight[matrix, at, :], first[matrix, at, :], second[matrix, at, :], gradient[matrix, at, :] * factor[:1, :1], rate
    )
    for ref, value in zip(expert_out, result):
        ref[0] = value


def adam(info, last, small_sum, dense, dense_grad, gains, router, expert, expert_grad, rates):
    _, tall, wide = expert_grad.shape
    parts = 4
    block = pl.BlockSpec((1, tall // parts, wide), lambda i, j: (i, j, 0))
    held = pl.BlockSpec(memory_space=pltpu.VMEM)
    small = [*dense, *gains, *router]
    shapes = [shape_of((8, LANES), f32)] + [shape_of(a.shape, f32) for a in small]
    ins = (last, small_sum, *dense, dense_grad, *gains, *router)
    return pl.pallas_call(
        lambda *refs: adam_kernel(tall // LANES, gains[0].shape[1], rates, *refs),
        grid=(2, parts),
        in_specs=[scalars()] + [whole(a.shape) for a in ins] + [held] * 4,
        out_specs=[whole(a.shape) for a in shapes] + [block] * 3,
        out_shape=shapes + [shape_of(expert_grad.shape, f32)] * 3,
        scratch_shapes=[pltpu.VMEM((8, LANES), f32)],
        compiler_params=params(16),
        cost_estimate=LIGHT,
        name="adam",
    )(info, *ins, *expert, expert_grad)


def tie(*values):
    return lax.optimization_barrier(values)


def on_device(
    inputs,
    cotangent,
    lengths,
    routes,
    attention_weight,
    attention_mean,
    attention_square,
    expert_weight,
    expert_mean,
    expert_square,
    router_matrix,
    router_mean,
    router_square,
    norm_gains,
    gains_mean,
    gains_square,
):
    quarter, width = inputs.shape[1:]
    dp_count, tensor_count = lax.axis_size(DP), lax.axis_size(TENSOR)
    device_count = dp_count * tensor_count
    expert_count = router_matrix.shape[1]
    capacity = max(2, (5 * quarter + 4 * expert_count - 1) // (4 * expert_count))
    own_dp, own_tensor = lax.axis_index(DP), lax.axis_index(TENSOR)
    share = router_matrix.shape[0]
    rows, grad_rows, length = inputs[0], cotangent[0], lengths[0]
    info = jnp.stack([own_tensor, length, own_dp, lax.axis_index(EVERYONE)]).astype(jnp.int32)

    scaled_one, root_one, weight_own, payload = prologue(
        rows, attention_weight, norm_gains, router_matrix.T, device_count
    )
    block_two = swap(scaled_one, TENSOR, 2)
    if dp_count == 8:
        w4, w2, w1 = [swap(weight_own, DP, mask) for mask in (4, 2, 1)]
        w4, w2, w1 = tie(w4, w2, w1)
        w6, w5, w3 = swap(w4, DP, 2), swap(w4, DP, 1), swap(w2, DP, 1)
        w6, w5, w3, block_two = tie(w6, w5, w3, block_two)
        shards = [weight_own, w1, w2, w3, w4, w5, w6, swap(w6, DP, 1)]
    else:
        w6, block_two = tie(weight_own, block_two)
        shards = [lax.all_gather(weight_own, DP, axis=0, tiled=True)]
    row_blocks = [scaled_one, swap(scaled_one, TENSOR, 1), block_two, swap(block_two, TENSOR, 1)]
    small_came = lax.all_to_all(payload, EVERYONE, 0, 0, tiled=True)

    place, match, valid_scale, grad_slots = slots_part(info, routes[0], grad_rows, expert_count, capacity)
    slot_count = expert_count * capacity

    def trade(values):
        blocks = values.reshape(expert_count, capacity, values.shape[1])
        return lax.all_to_all(blocks, DP, 0, 0, tiled=True).reshape(values.shape)

    inward_pair = jnp.stack([expert_weight[0, 0].astype(bf16)] * 2)
    inward_near = lax.all_to_all(inward_pair, "th", 0, 0, tiled=True)

    grad_slots, small_came, inward_pair = tie(grad_slots, small_came, inward_pair)
    small, weight, out_weight, qkv, keys_wide, values_turned = project(
        info, small_came, row_blocks, shards, share, expert_count
    )
    out_weights = gather_relative(out_weight, TENSOR, [2, 1])
    context, chances, totals = attention_forward(qkv, keys_wide, values_turned, tensor_count)
    outward_pair = jnp.stack([expert_weight[0, 1].astype(bf16)] * 2)
    context, grad_slots, inward_near, outward_pair = tie(context, grad_slots, inward_near, outward_pair)
    context_own = lax.all_to_all(context, TENSOR, 0, 0, tiled=True)
    expert_grads = trade(grad_slots)
    context_own, outward_pair = tie(context_own, outward_pair)
    outward_near = lax.all_to_all(outward_pair, "th", 0, 0, tiled=True)

    middle, root_two, shares, gate, slots = middle_part(
        info, rows, context_own, out_weights, small, place, match, valid_scale
    )
    qkv, expert_grads, slots, inward_near = tie(qkv, expert_grads, slots, inward_near)
    expert_rows = trade(slots)
    turned_rows, keys_turned, third_query, context_rows = turn(info, row_blocks, qkv, context)
    inward_other, outward_other = swap(inward_near, TENSOR, 1), swap(outward_near, TENSOR, 1)
    grads_all = gather_relative(expert_grads, TENSOR, [2, 1])
    expert_rows, turned_rows, inward_other, outward_other, grads_all = tie(
        expert_rows, turned_rows, inward_other, outward_other, grads_all
    )
    expert_outs, expert_back = expert_part(
        expert_rows, expert_grads, [inward_near, outward_near, inward_other, outward_other]
    )
    expert_rows, expert_back = tie(expert_rows, expert_back)
    rows_all = gather_relative(expert_rows, TENSOR, [2, 1])
    expert_back, rows_all = tie(trade(expert_back), rows_all)

    middle_grad, middle_turned, context_parts, small_grad = return_part(
        info, expert_back, place, middle, root_two, shares, gate, match, grad_rows, small, out_weights
    )
    expert_outs, context_parts = tie(expert_outs, context_parts)
    context_grad = lax.all_to_all(context_parts, TENSOR, 0, 0, tiled=True)
    middle_near, middle_far = swap(middle_turned, TENSOR, 1), swap(middle_turned, TENSOR, 2)
    expert_outs = trade(expert_outs)

    packed = attention_backward(context_grad, context, chances, totals, qkv, keys_turned, third_query)
    packed, middle_far = tie(packed, middle_far)
    middle_all = [middle_turned, middle_near, middle_far, swap(middle_far, TENSOR, 1)]
    weight_grad, gain_one_grad = weight_gradient(
        info, turned_rows, packed, middle_all, context_rows, weight, small[:1].reshape(width, 1)
    )
    weight_grad, expert_outs, inward_near, small_grad = tie(weight_grad, expert_outs, inward_near, small_grad)
    weight_came = lax.all_to_all(weight_grad.reshape(dp_count, -1, width), DP, 0, 0, tiled=True)
    expert_grad, expert_squares, small_cut = expert_gradient(
        info, rows_all, grads_all, small_grad, inward_near, outward_near, device_count
    )
    small_grads = lax.all_to_all(small_cut, EVERYONE, 0, 0, tiled=True)
    expert_squares, packed, expert_outs = tie(expert_squares, packed, expert_outs)

    input_parts = mm_nt(packed, weight).astype(bf16)
    input_parts = [
        lax.dynamic_slice_in_dim(input_parts, (own_tensor ^ j) * quarter, quarter) for j in range(tensor_count)
    ]
    first_half = input_parts[0].astype(f32) + swap(input_parts[1], TENSOR, 1).astype(f32)
    second_half = input_parts[2].astype(f32) + swap(input_parts[3], TENSOR, 1).astype(f32)
    came = swap(second_half.astype(bf16), TENSOR, 2)
    input_grad = middle_grad + norm_backward(rows, root_one, small[:1], first_half + came.astype(f32))
    picked = mm_tn(place, expert_outs)
    branch = gate * valid_scale * picked
    block_output = middle + branch

    weight_came, input_grad, block_output, branch = tie(weight_came, input_grad, block_output, branch)
    dense_grad, last, small_sum = sums_part(
        weight_came, expert_squares, small_grads, gain_one_grad.reshape(-1, LANES), device_count
    )
    last, *state = tie(last, expert_weight[0], expert_mean[0], expert_square[0], expert_grad)
    last_all = lax.all_to_all(last, EVERYONE, 0, 0, tiled=True)
    staged = stage(*state)

    rates = (0.4 * math.sqrt(expert_count / D), 1.38 * math.sqrt(expert_count / FF))
    stats, *updated = adam(
        info,
        last_all,
        small_sum,
        (attention_weight, attention_mean, attention_square),
        dense_grad,
        (norm_gains, gains_mean, gains_square),
        (router_matrix.T, router_mean.T, router_square.T),
        staged[:3],
        staged[3],
        rates,
    )
    attention_new, gains_new, router_new, expert_new = updated[:3], updated[3:6], updated[6:9], updated[9:]
    router_new = [part.T for part in router_new]
    grad_norm = stats[0, 0]
    return (
        block_output[None],
        input_grad[None],
        grad_norm,
        *attention_new,
        *[part[None] for part in expert_new],
        *router_new,
        *gains_new,
        branch[None],
    )


def solution(mesh):
    names = mesh.axis_names
    dp_count, tensor_count = mesh.shape[names[0]], mesh.shape[names[1]]
    cut = jax.sharding.Mesh(mesh.devices.reshape(dp_count // 2, 2, tensor_count // 2, 2), EVERYONE)
    rows = P(DP, TENSOR, None)
    attention = P(None, DP, TENSOR)
    expert = P(DP, None, None, TENSOR)
    router = P(EVERYONE, None)
    gains = P(None, EVERYONE)
    weights = (attention,) * 3 + (expert,) * 3 + (router,) * 3 + (gains,) * 3
    return jax.shard_map(
        on_device,
        mesh=cut,
        in_specs=(rows, rows, P(DP), rows) + weights,
        out_specs=(rows, rows, P()) + weights + (rows,),
        check_vma=False,
    )
```

```python
import math

import jax
import jax.numpy as jnp
from jax import lax
from jax.experimental import pallas as pl
from jax.experimental.pallas import tpu as pltpu
from jax.sharding import PartitionSpec as P

D = 768
H = 12
DH = 64
FF = 3072
STEP = 10

HIGHEST = lax.Precision.HIGHEST
norm_epsilon = 1e-06
beta_first = 0.9
beta_second = 0.999
adam_epsilon = 1e-08
decay_factor = 0.01
clip_limit = 1.0
masked_score = -1e30
score_scale = 1.0 / math.sqrt(DH)
bf16 = jnp.bfloat16
f32 = jnp.float32
MIB = 1 << 20
LANES = 128


DP = ("dh", "dl")
TENSOR = ("th", "tl")
EVERYONE = DP + TENSOR


def swap(values, axis, mask):
    count = lax.axis_size(axis)
    return lax.ppermute(values, axis, [(i, i ^ mask) for i in range(count)])


def bits_of(count):
    return [1 << b for b in range(count.bit_length() - 1)]


def gather_relative(block, axis, order):
    held = {0: block}
    for mask in order:
        for j in list(held):
            held[j ^ mask] = swap(held[j], axis, mask)
    return [held[j] for j in range(len(held))]


def mm(a, b):
    return jnp.dot(a, b, preferred_element_type=f32)


def mm_nt(a, b, precision=None):
    return lax.dot_general(
        a, b, (((1,), (1,)), ((), ())), preferred_element_type=f32, precision=precision
    )


def mm_tn(a, b, precision=None):
    return lax.dot_general(
        a, b, (((0,), (0,)), ((), ())), preferred_element_type=f32, precision=precision
    )


def norm_root(values):
    return lax.rsqrt(jnp.mean(values * values, axis=-1, keepdims=True) + norm_epsilon)


def norm_backward(values, root, gain_row, grad):
    scaled = values * root
    inner = grad * gain_row
    centre = jnp.mean(inner * scaled, axis=-1, keepdims=True)
    return root * (inner - scaled * centre)


def gelu_pair(values):
    c = math.sqrt(2.0 / math.pi)
    square = values * values
    th = jnp.tanh(c * values * (1.0 + 0.044715 * square))
    half = 0.5 * (1.0 + th)
    slope = half + 0.5 * values * (1.0 - th * th) * c * (1.0 + 3.0 * 0.044715 * square)
    return values * half, slope


def adam_update(weight, moment_one, moment_two, gradient, step_rate):
    moment_one_next = beta_first * moment_one + (1.0 - beta_first) * gradient
    moment_two_next = beta_second * moment_two + (1.0 - beta_second) * gradient * gradient
    corrected_one = moment_one_next / (1.0 - beta_first**STEP)
    corrected_two = moment_two_next / (1.0 - beta_second**STEP)
    weight_next = weight - step_rate * (
        corrected_one / (jnp.sqrt(corrected_two) + adam_epsilon) + decay_factor * weight
    )
    return (weight_next, moment_one_next, moment_two_next)


def shape_of(shape, dtype):
    return jax.ShapeDtypeStruct(shape, dtype)


def whole(shape):
    return pl.BlockSpec(shape, lambda *_: (0,) * len(shape))


def scalars():
    return pl.BlockSpec(memory_space=pltpu.SMEM)


LIGHT = pl.CostEstimate(flops=1, bytes_accessed=1, transcendentals=0)


def params(limit):
    return pltpu.CompilerParams(vmem_limit_bytes=limit * MIB)


def prologue_kernel(inputs, attention, gains, router, scaled, root, packed, payload):
    values = inputs[...]
    scale = norm_root(values)
    root[...] = scale
    scaled[...] = (values * scale).astype(bf16)
    parts = [attention[i].astype(bf16) for i in range(4)]
    packed[...] = jnp.concatenate(
        [part[:, :LANES] for part in parts] + [part[:, LANES:] for part in parts], axis=1
    )
    experts, share = router.shape
    groups = -(-(2 + experts) // 8)
    wide = jnp.concatenate([gains[...], router[...]], axis=0)
    wide = jnp.pad(wide, ((0, 8 * groups - 2 - experts), (0, 0)))
    row = jnp.concatenate([wide[8 * k : 8 * k + 8] for k in range(groups)], axis=1)
    row = jnp.pad(row, ((0, 0), (0, LANES - groups * share)))
    payload[...] = jnp.broadcast_to(row[None], payload.shape)


def prologue(inputs, attention, gains, router, device_count):
    quarter, width = inputs.shape
    tall = attention.shape[1]
    shapes = [
        shape_of((quarter, width), bf16),
        shape_of((quarter, 1), f32),
        shape_of((tall, 6 * LANES), bf16),
        shape_of((device_count, 8, LANES), f32),
    ]
    arrays = (inputs, attention, gains, router)
    return pl.pallas_call(
        prologue_kernel,
        in_specs=[whole(a.shape) for a in arrays],
        out_specs=[whole(s.shape) for s in shapes],
        out_shape=shapes,
        compiler_params=params(60),
        cost_estimate=LIGHT,
        name="prologue",
    )(*arrays)


def slots_kernel(capacity, info, routes, grads, place, match, valid, slots):
    quarter = routes.shape[0]
    experts = match.shape[1]
    row = lax.broadcasted_iota(jnp.int32, (quarter, 1), 0) + info[0] * quarter
    inside = jnp.where(row < info[1], 1.0, 0.0)
    valid[...] = inside
    column = lax.broadcasted_iota(jnp.int32, (quarter, experts), 1)
    named = jnp.where(routes[...] == column, 1.0, 0.0)
    match[...] = named
    at = lax.broadcasted_iota(jnp.int32, (quarter, quarter), 0)
    before = lax.broadcasted_iota(jnp.int32, (quarter, quarter), 1)
    lower = jnp.where(at >= before, 1.0, 0.0).astype(bf16)
    rank = jnp.sum(mm(lower, (named * inside).astype(bf16)) * named, axis=1, keepdims=True) - 1.0
    slot = jnp.where(inside > 0.0, routes[...].astype(f32) * capacity + rank, -1.0)
    slot = jnp.broadcast_to(slot, (quarter, LANES)).T[:1]
    number = lax.broadcasted_iota(jnp.int32, place.shape, 0).astype(f32)
    chosen = jnp.where(number == slot, 1.0, 0.0).astype(bf16)
    place[...] = chosen
    slots[...] = mm(chosen, grads[...].astype(bf16)).astype(bf16)


def slots_part(info, routes, grads, experts, capacity):
    quarter, width = grads.shape
    shapes = [
        shape_of((experts * capacity, quarter), bf16),
        shape_of((quarter, experts), f32),
        shape_of((quarter, 1), f32),
        shape_of((experts * capacity, width), bf16),
    ]
    return pl.pallas_call(
        lambda *refs: slots_kernel(capacity, *refs),
        in_specs=[scalars(), whole(routes.shape), whole(grads.shape)],
        out_specs=[whole(s.shape) for s in shapes],
        out_shape=shapes,
        compiler_params=params(60),
        cost_estimate=LIGHT,
        name="slots",
    )(info, routes, grads)


def project_kernel(quarter, blocks, count, share, info, came, x0, x1, x2, x3, *refs):
    shards, (small, column_gain, weight, out_weight, qkv, kaug, vt) = refs[:count], refs[count:]
    tall = shards[0].shape[0]
    width = weight.shape[0]
    for j, ref in enumerate(shards):
        start = pl.multiple_of((info[2] ^ j) * tall, tall) if count > 1 else 0
        weight[pl.ds(start, tall), :] = ref[...]
    out_weight[:LANES, :] = weight[:, 3 * LANES : 4 * LANES].T
    out_weight[LANES:, :] = weight[:, 5 * LANES :].T[DH:]
    groups = small.shape[0] // 8
    devices = came.shape[0]
    flat = came[...].reshape(devices * 8, LANES)
    lane = lax.broadcasted_iota(jnp.int32, (LANES, width), 0)
    column = lax.broadcasted_iota(jnp.int32, (LANES, width), 1)
    inside = lax.rem(column, share)
    owner = lax.broadcasted_iota(jnp.int32, (devices, 1, width), 2) - share * lax.broadcasted_iota(
        jnp.int32, (devices, 1, width), 0
    )
    owner = jnp.where((owner >= 0) & (owner < share), 1.0, 0.0)
    for k in range(groups):
        pick = jnp.where(lane == inside + k * share, 1.0, 0.0)
        spread = jnp.dot(flat, pick, precision=HIGHEST, preferred_element_type=f32)
        small[8 * k : 8 * k + 8, :] = jnp.sum(spread.reshape(devices, 8, width) * owner, axis=0)
    gain = small[:1, :]
    column_gain[...] = jnp.broadcast_to(gain, (LANES, width)).T[:, :1]
    for j, ref in enumerate((x0, x1, x2, x3)):
        start = pl.multiple_of((info[0] ^ j) * quarter, quarter)
        rows = pl.ds(start, quarter)
        scaled = (ref[...].astype(f32) * gain).astype(bf16)
        first = mm(scaled, weight[:, : 3 * LANES]).astype(bf16)
        second = mm(scaled, weight[:, 4 * LANES :]).astype(bf16)
        qkv[rows, : 3 * LANES] = first
        qkv[rows, 3 * LANES :] = second
        kaug[rows, :LANES] = first[:, LANES : 2 * LANES]
        lane = lax.broadcasted_iota(jnp.int32, (quarter, LANES), 1)
        row = lax.broadcasted_iota(jnp.int32, (quarter, LANES), 0) + start
        hidden = jnp.where((lane == 0) & (row >= info[1]), masked_score, 0.0)
        kaug[rows, LANES:] = jnp.where(lane < DH, hidden, second[:, :LANES].astype(f32)).astype(bf16)
        values = first[:, 2 * LANES :].T
        vt[0, :DH, rows] = values[:DH]
        vt[1, :DH, rows] = values[DH:]
        vt[2, :DH, rows] = second[:, LANES:].T[:DH]
    full_len = quarter * blocks
    tail = (lax.broadcasted_iota(jnp.int32, (16, full_len), 0) == 0).astype(f32).astype(bf16)
    for h in range(3):
        vt[h, DH:, :] = tail


def project(info, came, rows, shards, share, experts):
    quarter, width = rows[0].shape
    blocks = len(rows)
    full_len = quarter * blocks
    shapes = [
        shape_of((8 * -(-(2 + experts) // 8), width), f32),
        shape_of((width, 1), f32),
        shape_of((width, 6 * LANES), bf16),
        shape_of((3 * DH, width), bf16),
        shape_of((full_len, 5 * LANES), bf16),
        shape_of((full_len, 2 * LANES), bf16),
        shape_of((3, DH + 16, full_len), bf16),
    ]
    arrays = (came, *rows, *shards)
    return pl.pallas_call(
        lambda *refs: project_kernel(quarter, blocks, len(shards), share, *refs),
        in_specs=[scalars()] + [whole(a.shape) for a in arrays],
        out_specs=[whole(s.shape) for s in shapes],
        out_shape=shapes,
        compiler_params=params(60),
        cost_estimate=LIGHT,
        name="project",
    )(info, *arrays)


def attention_kernel(info, qkv, kaug, vt, context, chances, totals, *sent):
    quarter = context.shape[2]
    step = pl.program_id(0)
    rows = pl.ds(pl.multiple_of(step * quarter, quarter), quarter)
    q01 = (qkv[rows, :LANES].astype(f32) * score_scale).T.astype(bf16)
    q2 = (qkv[rows, 3 * LANES : 4 * LANES].astype(f32) * score_scale).T.astype(bf16)[:DH]
    ones = (lax.broadcasted_iota(jnp.int32, (DH, quarter), 0) == 0).astype(f32).astype(bf16)
    zeros = jnp.zeros((DH, quarter), bf16)
    queries = (
        jnp.concatenate([q01[:DH], zeros, ones, zeros], axis=0),
        jnp.concatenate([zeros, q01[DH:], ones, zeros], axis=0),
        jnp.concatenate([zeros, zeros, ones, q2], axis=0),
    )
    full_len = kaug.shape[0]
    all_scores = [mm(kaug[...], queries[h]) for h in range(3)]
    for h in range(3):
        scores = all_scores[h]
        top = jnp.max(jnp.max(scores.reshape(8, full_len // 8, quarter), axis=0), axis=0, keepdims=True)
        low = jnp.exp(scores - top).astype(bf16)
        chances[h] = low
        summed = mm(vt[h], low)
        part = 1.0 / summed[DH : DH + 1]
        totals[0, h : h + 1, :] = part
        context[0, h * DH : (h + 1) * DH, :] = (summed[:DH] * part).astype(bf16)
    for j, ref in enumerate(sent):

        @pl.when(step == info[0] ^ j)
        def _():
            ref[...] = context[0]


def attention_forward(info, qkv, kaug, vt, blocks):
    full_len = qkv.shape[0]
    quarter = full_len // blocks
    inner = 3 * DH
    return pl.pallas_call(
        attention_kernel,
        grid=(blocks,),
        in_specs=[scalars(), whole(qkv.shape), whole(kaug.shape), whole(vt.shape)],
        out_specs=[
            pl.BlockSpec((1, inner, quarter), lambda i: (i, 0, 0)),
            pl.BlockSpec((3, full_len, quarter), lambda i: (0, 0, i)),
            pl.BlockSpec((1, 3, quarter), lambda i: (i, 0, 0)),
        ]
        + [whole((inner, quarter))] * blocks,
        out_shape=[
            shape_of((blocks, inner, quarter), bf16),
            shape_of((3, full_len, full_len), bf16),
            shape_of((blocks, 3, quarter), f32),
        ]
        + [shape_of((inner, quarter), bf16)] * blocks,
        compiler_params=params(60),
        cost_estimate=LIGHT,
        name="attend",
    )(info, qkv, kaug, vt)


def turn_kernel(quarter, blocks, info, x0, x1, x2, x3, qkv, context, xt, kt, q2, cn):
    for j, ref in enumerate((x0, x1, x2, x3)):
        xt[info[0] ^ j] = ref[...].T
    for j in range(blocks):
        rows = slice(j * quarter, (j + 1) * quarter)
        third = qkv[rows, 3 * LANES : 4 * LANES].T
        kt[:LANES, rows] = qkv[rows, LANES : 2 * LANES].T
        kt[LANES:, rows] = third[DH:]
        zeros = jnp.zeros((DH, quarter), bf16)
        q2[rows, :] = jnp.concatenate([zeros, third[:DH]], axis=0).T
        cn[rows, :LANES] = context[j, :LANES, :].T
        cn[rows, LANES:] = jnp.concatenate([zeros, context[j, LANES:, :]], axis=0).T


def turn(info, rows, qkv, context):
    quarter, width = rows[0].shape
    blocks = len(rows)
    full_len = quarter * blocks
    shapes = [
        shape_of((blocks, width, quarter), bf16),
        shape_of((3 * DH, full_len), bf16),
        shape_of((full_len, LANES), bf16),
        shape_of((full_len, 2 * LANES), bf16),
    ]
    return pl.pallas_call(
        lambda *refs: turn_kernel(quarter, blocks, *refs),
        in_specs=[scalars()] + [whole((quarter, width))] * 4 + [whole(qkv.shape), whole(context.shape)],
        out_specs=[whole(s.shape) for s in shapes],
        out_shape=shapes,
        compiler_params=params(60),
        cost_estimate=LIGHT,
        name="turn",
    )(info, *rows, qkv, context)


def two_columns(column):
    high = column.astype(bf16).astype(f32)
    lane = lax.broadcasted_iota(jnp.int32, (column.shape[0], LANES), 1)
    return jnp.where(lane == 0, high, jnp.where(lane == 1, column - high, 0.0)).astype(bf16)


def middle_kernel(
    rows, c0, c1, c2, c3, w0, w1, w2, w3, small, place, match, valid, middle, root, chances, gate, slots
):
    gain, router = small[1:2, :], small[2 : 2 + match.shape[1], :]
    total = rows[...]
    for context, weight in zip((c0, c1, c2, c3), (w0, w1, w2, w3)):
        total = total + mm_tn(context[...], weight[...])
    middle[...] = total
    scale = norm_root(total)
    root[...] = scale
    hidden = total * scale * gain
    scores = mm_nt(hidden, router, HIGHEST)
    powers = jnp.exp(scores - jnp.max(scores, axis=-1, keepdims=True))
    share = powers / jnp.sum(powers, axis=-1, keepdims=True)
    chances[...] = share
    own = jnp.sum(share * match[...], axis=-1, keepdims=True)
    gate[...] = own
    width = rows.shape[1]
    slots[:, :width] = mm(place[...], hidden.astype(bf16)).astype(bf16)
    slots[:, width:] = mm(place[...], two_columns(own * valid[...])).astype(bf16)


def middle_part(rows, contexts, out_weights, small, place, match, valid):
    quarter, width = rows.shape
    experts = match.shape[1]
    shapes = [
        shape_of((quarter, width), f32),
        shape_of((quarter, 1), f32),
        shape_of((quarter, experts), f32),
        shape_of((quarter, 1), f32),
        shape_of((place.shape[0], width + LANES), bf16),
    ]
    arrays = (rows, *contexts, *out_weights, small, place, match, valid)
    return pl.pallas_call(
        middle_kernel,
        in_specs=[whole(a.shape) for a in arrays],
        out_specs=[whole(s.shape) for s in shapes],
        out_shape=shapes,
        compiler_params=params(60),
        cost_estimate=LIGHT,
        name="middle",
    )(*arrays)


def expert_kernel(rows, grads, near_in, near_out, other_in, other_out, out, back, held, arrived):
    width = grads.shape[1]
    copies = []
    for i, (inward, outward) in enumerate(((near_in, near_out), (other_in, other_out))):
        for j in range(2):
            at = 2 * i + j
            copies.append(
                (
                    pltpu.make_async_copy(outward.at[j], held.at[at, 1], arrived.at[at, 1]),
                    pltpu.make_async_copy(inward.at[j], held.at[at, 0], arrived.at[at, 0]),
                )
            )
    for pair in copies:
        for copy in pair:
            copy.start()
    out_total, back_total = None, None
    for i, pair in enumerate(copies):
        for copy in pair:
            copy.wait()
        inward, outward = held[i, 0], held[i, 1]
        grad = mm(grads[...], outward)
        active, slope = gelu_pair(mm(rows[:, :width], inward))
        part = mm_nt(active.astype(bf16), outward)
        back_part = mm_nt((grad * slope).astype(bf16), inward)
        out_total = part if i == 0 else out_total + part
        back_total = back_part if i == 0 else back_total + back_part
    result = out_total.astype(bf16)
    out[...] = result
    back[:, :width] = back_total.astype(bf16)
    match = jnp.sum(grads[...].astype(f32) * result.astype(f32), axis=-1, keepdims=True)
    back[:, width:] = two_columns(match)


def expert_part(rows, grads, weights):
    slots, width = grads.shape
    hidden = weights[0].shape[2]
    count = len(weights)
    shapes = [shape_of((slots, width), bf16), shape_of((slots, width + LANES), bf16)]
    return pl.pallas_call(
        expert_kernel,
        in_specs=[whole(rows.shape), whole(grads.shape)] + [pl.BlockSpec(memory_space=pl.ANY)] * count,
        out_specs=[whole(s.shape) for s in shapes],
        out_shape=shapes,
        scratch_shapes=[pltpu.VMEM((count, 2) + weights[0].shape[1:], bf16), pltpu.SemaphoreType.DMA((count, 2))],
        compiler_params=params(60),
        cost_estimate=LIGHT,
        name="experts",
    )(rows, grads, *weights)


def pack_small(small, cut):
    devices = cut.shape[0]
    rows, width = small.shape
    share = width // devices
    groups = rows // 8
    column = lax.broadcasted_iota(jnp.int32, (devices, 1, width), 2)
    owner = column - share * lax.broadcasted_iota(jnp.int32, (devices, 1, width), 0)
    owner = jnp.where((owner >= 0) & (owner < share), 1.0, 0.0)
    lane = lax.broadcasted_iota(jnp.int32, (width, LANES), 1)
    inside = lax.rem(lax.broadcasted_iota(jnp.int32, (width, LANES), 0), share)
    total = None
    for k in range(groups):
        pick = jnp.where(lane == inside + k * share, 1.0, 0.0)
        spread = (small[8 * k : 8 * k + 8, :][None] * owner).reshape(devices * 8, width)
        part = jnp.dot(spread, pick, precision=HIGHEST, preferred_element_type=f32)
        total = part if total is None else total + part
    cut[...] = total.reshape(devices, 8, LANES)


def expert_grad_kernel(count, *refs):
    info, rows, grads = refs[0], refs[1 : count + 1], refs[count + 1 : 2 * count + 1]
    small, near_in, near_out, out, square, cut, weight, row_all, grad_all, inner_all, active_all, arrived = refs[
        2 * count + 1 :
    ]
    copies = [
        pltpu.make_async_copy(ref.at[lax.div(info[0], 2)], weight.at[i], arrived.at[i])
        for i, ref in enumerate((near_in, near_out))
    ]
    for copy in copies:
        copy.start()
    pack_small(small, cut)
    for copy in copies:
        copy.wait()
    slots, width = grads[0].shape
    for j in range(count):
        at = slice(j * slots, (j + 1) * slots)
        gate = rows[j][:, width : width + 1].astype(f32) + rows[j][:, width + 1 : width + 2].astype(f32)
        row_all[at, :] = rows[j][:, :width]
        grad_all[at, :] = (grads[j][...].astype(f32) * gate).astype(bf16)
        back = mm(grads[j][...], weight[1])
        active, slope = gelu_pair(mm(rows[j][:, :width], weight[0]))
        inner_all[at, :] = (back * slope * gate).astype(bf16)
        active_all[at, :] = active.astype(bf16)
    first = mm_tn(row_all[...], inner_all[...])
    out[0] = first
    second = mm_tn(grad_all[...], active_all[...])
    out[1] = second
    square[...] = jnp.sum(first * first + second * second, axis=0, keepdims=True)


def expert_gradient(info, rows, grads, small, near_in, near_out, device_count):
    count = len(rows)
    slots, width = grads[0].shape
    hidden = near_in.shape[2]
    arrays = (*rows, *grads, small)
    shapes = [
        shape_of((2, width, hidden), f32),
        shape_of((1, hidden), f32),
        shape_of((device_count, 8, LANES), f32),
    ]
    return pl.pallas_call(
        lambda *refs: expert_grad_kernel(count, *refs),
        in_specs=[scalars()] + [whole(a.shape) for a in arrays] + [pl.BlockSpec(memory_space=pl.ANY)] * 2,
        out_specs=[whole(s.shape) for s in shapes],
        out_shape=shapes,
        scratch_shapes=[pltpu.VMEM((2, width, hidden), bf16)]
        + [pltpu.VMEM((count * slots, width), bf16)] * 2
        + [pltpu.VMEM((count * slots, hidden), bf16)] * 2
        + [pltpu.SemaphoreType.DMA((2,))],
        compiler_params=params(60),
        cost_estimate=LIGHT,
        name="expert_gradient",
    )(info, *arrays, near_in, near_out)


def return_kernel(
    back, place, middle, root, chances, gate, match, cotangent, small, w0, w1, w2, w3,
    grad, turned, small_grad, *parts,
):
    experts = match.shape[1]
    gain, router = small[1:2, :], small[2 : 2 + experts, :]
    width = middle.shape[1]
    came = mm_tn(place[...], back[...])
    gate_grad = came[:, width : width + 1] + came[:, width + 1 : width + 2]
    own = gate[...]
    score_grad = own * (match[...] - chances[...]) * gate_grad
    scaled = middle[...] * root[...]
    hidden = scaled * gain
    tall = small_grad.shape[0]
    small_grad[1 : 1 + experts, :] = mm_tn(score_grad, hidden, HIGHEST)
    small_grad[1 + experts :, :] = jnp.zeros((tall - 1 - experts, hidden.shape[1]), f32)
    second = own * came[:, :width] + jnp.dot(
        score_grad, router, precision=HIGHEST, preferred_element_type=f32
    )
    small_grad[:1, :] = jnp.sum(second * scaled, axis=0, keepdims=True)
    inner = second * gain
    centre = jnp.mean(inner * scaled, axis=-1, keepdims=True)
    total = cotangent[...] + root[...] * (inner - scaled * centre)
    grad[...] = total
    low = total.astype(bf16)
    turned[...] = low.T
    for ref, weight in zip(parts, (w0, w1, w2, w3)):
        ref[...] = mm_nt(weight[...], low).astype(bf16)


def return_part(back, place, middle, root, chances, gate, match, cotangent, small, out_weights):
    quarter, width = middle.shape
    experts = match.shape[1]
    inner = out_weights[0].shape[0]
    shapes = [
        shape_of((quarter, width), f32),
        shape_of((width, quarter), bf16),
        shape_of((8 * -(-(1 + experts) // 8), width), f32),
    ] + [shape_of((inner, quarter), bf16)] * len(out_weights)
    arrays = (back, place, middle, root, chances, gate, match, cotangent, small, *out_weights)
    return pl.pallas_call(
        return_kernel,
        in_specs=[whole(a.shape) for a in arrays],
        out_specs=[whole(s.shape) for s in shapes],
        out_shape=shapes,
        compiler_params=params(60),
        cost_estimate=LIGHT,
        name="returned",
    )(*arrays)


def attention_back_kernel(
    blocks, info, g0, g1, g2, g3, context, chances, totals, qkv, kt, q2, packed, grads, vaug, k01, k2, v01, v2
):
    step = pl.program_id(0)
    quarter = grads.shape[2]

    @pl.when(step == 0)
    def _():
        for j, ref in enumerate((g0, g1, g2, g3)):
            grads[info[0] ^ j] = ref[...]
        vaug[:, :LANES] = qkv[:, 2 * LANES : 3 * LANES]
        lane = lax.broadcasted_iota(jnp.int32, (vaug.shape[0], LANES), 1)
        ones = jnp.where(lane < DH + 2, 1.0, 0.0)
        vaug[:, LANES:] = jnp.where(lane < DH, qkv[:, 4 * LANES :].astype(f32), ones).astype(bf16)
        for ref in (k01, k2, v01, v2):
            ref[...] = jnp.zeros(ref.shape, f32)

    rows = pl.ds(pl.multiple_of(step * quarter, quarter), quarter)
    raw = grads[step].astype(f32)
    scale = totals[0]
    scaled = [raw[h * DH : (h + 1) * DH] * scale[h : h + 1] for h in range(3)]
    heads = jnp.concatenate(scaled, axis=0).astype(bf16)
    lane = lax.broadcasted_iota(jnp.int32, (quarter, LANES), 1)
    row = lax.broadcasted_iota(jnp.int32, (DH, quarter), 0)
    zeros = jnp.zeros((DH, quarter), bf16)
    q01 = qkv[rows, :LANES].astype(f32)
    g01 = heads[:LANES].T.astype(f32)
    third = jnp.concatenate([heads[LANES:], zeros], axis=0).T
    query_parts = []
    for h in range(3):
        part = heads[h * DH : (h + 1) * DH]
        centre = -jnp.sum(
            part.astype(f32) * context[0, h * DH : (h + 1) * DH, :].astype(f32), axis=0, keepdims=True
        )
        high = centre.astype(bf16).astype(f32)
        tail = jnp.where(row == 0, high, jnp.where(row == 1, centre - high, 0.0)).astype(bf16)
        pieces = [zeros, zeros, zeros, tail]
        pieces[h] = part
        chance_grad = mm(vaug[...], jnp.concatenate(pieces, axis=0))
        low = chances[h]
        score_grad = (low.astype(f32) * chance_grad).astype(bf16)
        query_parts.append(mm(kt[h * DH : (h + 1) * DH, :], score_grad) * score_scale)
        if h < 2:
            inside = (lane >= h * DH) & (lane < (h + 1) * DH)
            k01[...] += mm(score_grad, jnp.where(inside, q01, 0.0).astype(bf16))
            v01[...] += mm(low, jnp.where(inside, g01, 0.0).astype(bf16))
        else:
            k2[...] += mm(score_grad, q2[rows, :])
            v2[...] += mm(low, third)
    packed[rows, :LANES] = jnp.concatenate(query_parts[:2], axis=0).T.astype(bf16)
    packed[rows, 4 * LANES : 5 * LANES] = (
        jnp.concatenate([query_parts[2], jnp.zeros((DH, quarter), f32)], axis=0).T.astype(bf16)
    )

    @pl.when(step == blocks - 1)
    def _():
        packed[:, LANES : 2 * LANES] = (k01[...] * score_scale).astype(bf16)
        packed[:, 2 * LANES : 3 * LANES] = v01[...].astype(bf16)
        packed[:, 3 * LANES : 4 * LANES] = jnp.zeros(k01.shape, bf16)
        packed[:, 4 * LANES : 5 * LANES] = packed[:, 4 * LANES : 5 * LANES] + (k2[...] * score_scale).astype(bf16)
        packed[:, 5 * LANES :] = v2[...].astype(bf16)


def attention_backward(info, grads, context, chances, totals, qkv, kt, q2):
    blocks, inner, quarter = context.shape
    full_len = quarter * blocks
    block = pl.BlockSpec((1, inner, quarter), lambda i: (i, 0, 0))
    return pl.pallas_call(
        lambda *refs: attention_back_kernel(blocks, *refs),
        grid=(blocks,),
        in_specs=[
            scalars(),
            *[whole((inner, quarter))] * blocks,
            block,
            pl.BlockSpec((3, full_len, quarter), lambda i: (0, 0, i)),
            pl.BlockSpec((1, 3, quarter), lambda i: (i, 0, 0)),
            whole(qkv.shape),
            whole(kt.shape),
            whole(q2.shape),
        ],
        out_specs=whole((full_len, 6 * LANES)),
        out_shape=shape_of((full_len, 6 * LANES), bf16),
        scratch_shapes=[pltpu.VMEM(context.shape, bf16), pltpu.VMEM((full_len, 2 * LANES), bf16)]
        + [pltpu.VMEM((full_len, LANES), f32)] * 4,
        compiler_params=params(60),
        cost_estimate=LIGHT,
        name="attend_back",
    )(info, *grads, context, chances, totals, qkv, kt, q2)


def weight_grad_kernel(blocks, info, xt, packed, g0, g1, g2, g3, cn, weight, gain, out, gain_grad):
    quarter = xt.shape[2]
    total, outer = None, None
    for j, ref in enumerate((g0, g1, g2, g3)):
        rows = slice(j * quarter, (j + 1) * quarter)
        there = pl.ds(pl.multiple_of((info[0] ^ j) * quarter, quarter), quarter)
        part = mm(xt[j], packed[rows, :])
        own = mm(ref[...], cn[there, :])
        total = part if total is None else total + part
        outer = own if outer is None else outer + own
    gain_grad[...] = jnp.sum(total * weight[...].astype(f32), axis=1, keepdims=True)
    total = total * gain[...]
    out[:, : 3 * LANES] = total[:, : 3 * LANES].astype(bf16)
    out[:, 3 * LANES : 4 * LANES] = outer[:, :LANES].astype(bf16)
    out[:, 4 * LANES : 5 * LANES] = total[:, 4 * LANES : 5 * LANES].astype(bf16)
    out[:, 5 * LANES :] = (total[:, 5 * LANES :] + outer[:, LANES:]).astype(bf16)


def weight_gradient(info, xt, packed, grads, cn, weight, gain):
    blocks, width, quarter = xt.shape
    tall = 256
    full_len = quarter * blocks
    return pl.pallas_call(
        lambda *refs: weight_grad_kernel(blocks, *refs),
        grid=(width // tall,),
        in_specs=[
            scalars(),
            pl.BlockSpec((blocks, tall, quarter), lambda i: (0, i, 0)),
            whole(packed.shape),
            *[pl.BlockSpec((tall, quarter), lambda i: (i, 0))] * blocks,
            whole(cn.shape),
            pl.BlockSpec((tall, 6 * LANES), lambda i: (i, 0)),
            pl.BlockSpec((tall, 1), lambda i: (i, 0)),
        ],
        out_specs=[pl.BlockSpec((tall, 6 * LANES), lambda i: (i, 0)), pl.BlockSpec((tall, 1), lambda i: (i, 0))],
        out_shape=[shape_of((width, 6 * LANES), bf16), shape_of((width, 1), f32)],
        compiler_params=params(60),
        cost_estimate=LIGHT,
        name="weight_gradient",
    )(info, xt, packed, *grads, cn, weight, gain)


def input_grad_kernel(quarter, info, packed, weight, *parts):
    for j, ref in enumerate(parts):
        rows = pl.ds(pl.multiple_of((info[0] ^ j) * quarter, quarter), quarter)
        ref[...] = mm_nt(packed[rows, :], weight[...]).astype(bf16)


def input_gradient(info, packed, weight, blocks):
    quarter = packed.shape[0] // blocks
    shapes = [shape_of((quarter, weight.shape[0]), bf16)] * blocks
    return pl.pallas_call(
        lambda *refs: input_grad_kernel(quarter, *refs),
        in_specs=[scalars(), whole(packed.shape), whole(weight.shape)],
        out_specs=[whole(s.shape) for s in shapes],
        out_shape=shapes,
        compiler_params=params(60),
        cost_estimate=LIGHT,
        name="input_gradient",
    )(info, packed, weight)


def sums_kernel(came, squares, small, gain_grad, gradient, payload, small_sum):
    count = came.shape[0]
    total = came[0].astype(f32)
    for i in range(1, count):
        total = total + came[i].astype(f32)
    gradient[...] = total
    own = jnp.sum(small[...], axis=0)
    square = (
        jnp.sum(total * total, keepdims=True)
        + jnp.sum(squares[...], keepdims=True)
        + jnp.sum(own * own, keepdims=True)
    )
    small_sum[...] = own
    rows = gain_grad.shape[0]
    row = lax.broadcasted_iota(jnp.int32, (8, LANES), 0)
    gain = jnp.concatenate([gain_grad[...], jnp.zeros((8 - rows, LANES), f32)], axis=0)
    payload[...] = jnp.broadcast_to(jnp.where(row < rows, gain, square)[None], payload.shape)


def sums_part(came, squares, small, gain_grad, device_count):
    shapes = [
        shape_of(came.shape[1:], f32),
        shape_of((device_count, 8, LANES), f32),
        shape_of((8, LANES), f32),
    ]
    arrays = (came, squares, small, gain_grad)
    return pl.pallas_call(
        sums_kernel,
        in_specs=[whole(a.shape) for a in arrays],
        out_specs=[whole(s.shape) for s in shapes],
        out_shape=shapes,
        compiler_params=params(60),
        cost_estimate=LIGHT,
        name="sums",
    )(*arrays)


def adam_kernel(lanes, share, expert_rates, info, last, small_sum, *refs):
    held, outs, factor = refs[:14], refs[14:27], refs[27]
    dense, dense_grad, gains, router = held[:3], held[3], held[4:7], held[7:10]
    weight, first, second, gradient = held[10:14]
    stats, outs = outs[0], outs[1:]
    dense_out, gains_out, router_out, expert_out = outs[:3], outs[3:6], outs[6:9], outs[9:12]
    matrix, part = pl.program_id(0), pl.program_id(1)
    experts = router[0].shape[0]

    @pl.when((matrix == 0) & (part == 0))
    def _():
        total = jnp.sum(last[...], axis=0)
        row = lax.broadcasted_iota(jnp.int32, (8, LANES), 0)
        squares = jnp.sum(jnp.where(row < lanes, total * total, 0.0), keepdims=True)
        norm = jnp.sqrt(squares + total[7:8, :1])
        scale = jnp.minimum(1.0, clip_limit / (norm + norm_epsilon))
        stats[...] = jnp.where(row == 0, norm, scale)
        factor[...] = jnp.broadcast_to(scale, (8, LANES))
        rates = (0.71 / math.sqrt(D), 0.71 / math.sqrt(D), 0.83 / math.sqrt(D), 0.79 / math.sqrt(H * DH))
        for i, rate in enumerate(rates):
            grad = jnp.concatenate(
                [
                    dense_grad[:, i * LANES : (i + 1) * LANES],
                    dense_grad[:, 4 * LANES + i * DH : 4 * LANES + (i + 1) * DH],
                ],
                axis=1,
            )
            result = adam_update(*[ref[i] for ref in dense], grad * scale, rate)
            for ref, value in zip(dense_out, result):
                ref[i] = value
        column = lax.broadcasted_iota(jnp.int32, (LANES, LANES), 1)
        place = lax.broadcasted_iota(jnp.int32, (LANES, LANES), 0) - info[3] * share
        own = jnp.zeros((8, LANES), f32)
        for i in range(lanes):
            pick = jnp.where((column == place + i * LANES) & (column < share), 1.0, 0.0)
            own = own + jnp.dot(
                jnp.broadcast_to(total[i : i + 1], (8, LANES)), pick, precision=HIGHEST, preferred_element_type=f32
            )
        groups = -(-(1 + experts) // 8)
        table = small_sum[...]
        table = jnp.concatenate([table[:, k * share : (k + 1) * share] for k in range(groups)], axis=0)
        grad = jnp.concatenate([own[:1, :share], table[:1]], axis=0)
        for ref, value in zip(gains_out, adam_update(*[ref[...] for ref in gains], grad * scale, 0.5)):
            ref[...] = value
        grad = table[1 : 1 + experts]
        result = adam_update(*[ref[...] for ref in router], grad * scale, 0.24 / math.sqrt(D))
        for ref, value in zip(router_out, result):
            ref[...] = value

    rate = jnp.where(matrix == 0, expert_rates[0], expert_rates[1])
    result = adam_update(weight[...], first[...], second[...], gradient[...] * factor[:1, :1], rate)
    for ref, value in zip(expert_out, result):
        ref[...] = value


def adam(info, last, small_sum, dense, dense_grad, gains, router, expert, expert_grad, rates):
    _, tall, wide = expert_grad.shape
    parts = 4
    block = pl.BlockSpec((1, tall // parts, wide), lambda i, j: (i, j, 0))
    small = [*dense, *gains, *router]
    shapes = [shape_of((8, LANES), f32)] + [shape_of(a.shape, f32) for a in small]
    ins = (last, small_sum, *dense, dense_grad, *gains, *router)
    return pl.pallas_call(
        lambda *refs: adam_kernel(tall // LANES, gains[0].shape[1], rates, *refs),
        grid=(2, parts),
        in_specs=[scalars()] + [whole(a.shape) for a in ins] + [block] * 4,
        out_specs=[whole(a.shape) for a in shapes] + [block] * 3,
        out_shape=shapes + [shape_of(expert_grad.shape, f32)] * 3,
        scratch_shapes=[pltpu.VMEM((8, LANES), f32)],
        compiler_params=params(60),
        cost_estimate=LIGHT,
        name="adam",
    )(info, *ins, *expert, expert_grad)


def tie(*values):
    return lax.optimization_barrier(values)


def on_device(
    inputs,
    cotangent,
    lengths,
    routes,
    attention_weight,
    attention_mean,
    attention_square,
    expert_weight,
    expert_mean,
    expert_square,
    router_matrix,
    router_mean,
    router_square,
    norm_gains,
    gains_mean,
    gains_square,
):
    quarter, width = inputs.shape[1:]
    dp_count, tensor_count = lax.axis_size(DP), lax.axis_size(TENSOR)
    device_count = dp_count * tensor_count
    expert_count = router_matrix.shape[1]
    capacity = max(2, (5 * quarter + 4 * expert_count - 1) // (4 * expert_count))
    own_dp, own_tensor = lax.axis_index(DP), lax.axis_index(TENSOR)
    share = router_matrix.shape[0]
    rows, grad_rows, length = inputs[0], cotangent[0], lengths[0]
    info = jnp.stack([own_tensor, length, own_dp, lax.axis_index(EVERYONE)]).astype(jnp.int32)

    scaled_one, root_one, weight_own, payload = prologue(
        rows, attention_weight, norm_gains, router_matrix.T, device_count
    )
    block_two = swap(scaled_one, TENSOR, 2)
    inward_pair = jnp.stack([expert_weight[0, 0].astype(bf16)] * 2)
    if dp_count == 8:
        w4, w2, w1 = [swap(weight_own, DP, mask) for mask in (4, 2, 1)]
        w4, w2, w1, payload = tie(w4, w2, w1, payload)
        w6, w5, w3 = swap(w4, DP, 2), swap(w4, DP, 1), swap(w2, DP, 1)
        w6, w5, w3, block_two, inward_pair = tie(w6, w5, w3, block_two, inward_pair)
        w7 = swap(w6, DP, 1)
        shards = [weight_own, w1, w2, w3, w4, w5, w6, w7]
    else:
        block_two, inward_pair, weight_own = tie(block_two, inward_pair, weight_own)
        w7 = lax.all_gather(weight_own, DP, axis=0, tiled=True)
        shards = [w7]
    row_blocks = [scaled_one, swap(scaled_one, TENSOR, 1), block_two, swap(block_two, TENSOR, 1)]
    small_came = lax.all_to_all(payload, EVERYONE, 0, 0, tiled=True)
    inward_near = lax.all_to_all(inward_pair, "th", 0, 0, tiled=True)

    place, match, valid_scale, grad_slots = slots_part(info, routes[0], grad_rows, expert_count, capacity)
    slot_count = expert_count * capacity

    def trade(values):
        blocks = values.reshape(expert_count, capacity, values.shape[1])
        return lax.all_to_all(blocks, DP, 0, 0, tiled=True).reshape(values.shape)

    grad_slots, shards[-1] = tie(grad_slots, w7)
    expert_grads = trade(grad_slots)
    small, gain_column, weight, out_weight, qkv, keys_wide, values_turned = project(
        info, small_came, row_blocks, shards, share, expert_count
    )
    out_weights = gather_relative(out_weight, TENSOR, [2, 1])
    context, chances, totals, *sent = attention_forward(info, qkv, keys_wide, values_turned, tensor_count)
    outward_pair = jnp.stack([expert_weight[0, 1].astype(bf16)] * 2)
    expert_grads, inward_near, outward_pair, *sent = tie(expert_grads, inward_near, outward_pair, *sent)
    contexts = [sent[0]] + [swap(sent[j], TENSOR, j) for j in range(1, tensor_count)]
    outward_pair, *contexts = tie(outward_pair, *contexts)
    outward_near = lax.all_to_all(outward_pair, "th", 0, 0, tiled=True)

    middle, root_two, shares, gate, slots = middle_part(
        rows, contexts, out_weights, small, place, match, valid_scale
    )
    qkv, expert_grads, slots, inward_near = tie(qkv, expert_grads, slots, inward_near)
    expert_rows = trade(slots)
    turned_rows, keys_turned, third_query, context_rows = turn(info, row_blocks, qkv, context)
    inward_other, outward_other = swap(inward_near, TENSOR, 1), swap(outward_near, TENSOR, 1)
    grads_all = gather_relative(expert_grads, TENSOR, [2, 1])
    expert_rows, turned_rows, inward_other, outward_other, grads_all = tie(
        expert_rows, turned_rows, inward_other, outward_other, grads_all
    )
    expert_outs, expert_back = expert_part(
        expert_rows, expert_grads, [inward_near, outward_near, inward_other, outward_other]
    )
    expert_rows, expert_back = tie(expert_rows, expert_back)
    rows_all = gather_relative(expert_rows, TENSOR, [2, 1])
    expert_back, rows_all = tie(trade(expert_back), rows_all)

    middle_grad, middle_turned, small_grad, *parts = return_part(
        expert_back, place, middle, root_two, shares, gate, match, grad_rows, small, out_weights
    )
    expert_outs, middle_turned, *parts = tie(expert_outs, middle_turned, *parts)
    context_grads = [parts[0]] + [swap(parts[j], TENSOR, j) for j in range(1, tensor_count)]
    expert_outs = trade(expert_outs)
    middle_turned, *context_grads = tie(middle_turned, *context_grads)
    middle_near, middle_far = swap(middle_turned, TENSOR, 1), swap(middle_turned, TENSOR, 2)

    packed = attention_backward(info, context_grads, context, chances, totals, qkv, keys_turned, third_query)
    packed, middle_far = tie(packed, middle_far)
    middle_all = [middle_turned, middle_near, middle_far, swap(middle_far, TENSOR, 1)]
    weight_grad, gain_one_grad = weight_gradient(
        info, turned_rows, packed, middle_all, context_rows, weight, gain_column
    )
    weight_grad, expert_outs, inward_near, small_grad = tie(weight_grad, expert_outs, inward_near, small_grad)
    weight_came = lax.all_to_all(weight_grad.reshape(dp_count, -1, width), DP, 0, 0, tiled=True)
    expert_grad, expert_squares, small_cut = expert_gradient(
        info, rows_all, grads_all, small_grad, inward_near, outward_near, device_count
    )
    small_grads = lax.all_to_all(small_cut, EVERYONE, 0, 0, tiled=True)

    expert_squares, packed = tie(expert_squares, packed)
    input_parts = input_gradient(info, packed, weight, tensor_count)
    first_half = input_parts[0].astype(f32) + swap(input_parts[1], TENSOR, 1).astype(f32)
    second_half = (input_parts[2].astype(f32) + swap(input_parts[3], TENSOR, 1).astype(f32)).astype(bf16)

    weight_came, second_half = tie(weight_came, second_half)
    second_came = swap(second_half, TENSOR, 2)
    dense_grad, last, small_sum = sums_part(
        weight_came, expert_squares, small_grads, gain_one_grad.reshape(-1, LANES), device_count
    )
    last, expert_outs, first_half = tie(last, expert_outs, first_half)
    last_all = lax.all_to_all(last, EVERYONE, 0, 0, tiled=True)
    input_grad = middle_grad + norm_backward(rows, root_one, small[:1], first_half + second_came.astype(f32))
    picked = mm_tn(place, expert_outs)
    branch = gate * valid_scale * picked
    block_output = middle + branch
    last_all, input_grad, block_output, branch = tie(last_all, input_grad, block_output, branch)

    rates = (0.4 * math.sqrt(expert_count / D), 1.38 * math.sqrt(expert_count / FF))
    stats, *updated = adam(
        info,
        last_all,
        small_sum,
        (attention_weight, attention_mean, attention_square),
        dense_grad,
        (norm_gains, gains_mean, gains_square),
        (router_matrix.T, router_mean.T, router_square.T),
        (expert_weight[0], expert_mean[0], expert_square[0]),
        expert_grad,
        rates,
    )
    attention_new, gains_new, router_new, expert_new = updated[:3], updated[3:6], updated[6:9], updated[9:]
    router_new = [part.T for part in router_new]
    grad_norm = stats[0, 0]
    return (
        block_output[None],
        input_grad[None],
        grad_norm,
        *attention_new,
        *[part[None] for part in expert_new],
        *router_new,
        *gains_new,
        branch[None],
    )


def solution(mesh):
    names = mesh.axis_names
    dp_count, tensor_count = mesh.shape[names[0]], mesh.shape[names[1]]
    cut = jax.sharding.Mesh(mesh.devices.reshape(dp_count // 2, 2, tensor_count // 2, 2), EVERYONE)
    rows = P(DP, TENSOR, None)
    attention = P(None, DP, TENSOR)
    expert = P(DP, None, None, TENSOR)
    router = P(EVERYONE, None)
    gains = P(None, EVERYONE)
    weights = (attention,) * 3 + (expert,) * 3 + (router,) * 3 + (gains,) * 3
    return jax.shard_map(
        on_device,
        mesh=cut,
        in_specs=(rows, rows, P(DP), rows) + weights,
        out_specs=(rows, rows, P()) + weights + (rows,),
        check_vma=False,
    )
```

```python
import math

import jax
import jax.numpy as jnp
from jax import lax
from jax.experimental import pallas as pl
from jax.experimental.pallas import tpu as pltpu
from jax.sharding import PartitionSpec as P

D = 768
H = 12
DH = 64
FF = 3072
STEP = 10

HIGHEST = lax.Precision.HIGHEST
norm_epsilon = 1e-06
beta_first = 0.9
beta_second = 0.999
adam_epsilon = 1e-08
decay_factor = 0.01
clip_limit = 1.0
masked_score = -1e30
score_scale = 1.0 / math.sqrt(DH)
bf16 = jnp.bfloat16
f32 = jnp.float32
MIB = 1 << 20
LANES = 128
EARLY = 928


DP = ("dh", "dl")
TENSOR = ("th", "tl")
EVERYONE = DP + TENSOR


def swap(values, axis, mask):
    count = lax.axis_size(axis)
    return lax.ppermute(values, axis, [(i, i ^ mask) for i in range(count)])


def bits_of(count):
    return [1 << b for b in range(count.bit_length() - 1)]


def gather_relative(block, axis, order):
    held = {0: block}
    for mask in order:
        for j in list(held):
            held[j ^ mask] = swap(held[j], axis, mask)
    return [held[j] for j in range(len(held))]


def mm(a, b):
    return jnp.dot(a, b, preferred_element_type=f32)


def mm_nt(a, b, precision=None):
    return lax.dot_general(
        a, b, (((1,), (1,)), ((), ())), preferred_element_type=f32, precision=precision
    )


def mm_tn(a, b, precision=None):
    return lax.dot_general(
        a, b, (((0,), (0,)), ((), ())), preferred_element_type=f32, precision=precision
    )


def norm_root(values):
    return lax.rsqrt(jnp.mean(values * values, axis=-1, keepdims=True) + norm_epsilon)


def norm_backward(values, root, gain_row, grad):
    scaled = values * root
    inner = grad * gain_row
    centre = jnp.mean(inner * scaled, axis=-1, keepdims=True)
    return root * (inner - scaled * centre)


def gelu_pair(values):
    c = math.sqrt(2.0 / math.pi)
    square = values * values
    th = jnp.tanh(c * values * (1.0 + 0.044715 * square))
    half = 0.5 * (1.0 + th)
    slope = half + 0.5 * values * (1.0 - th * th) * c * (1.0 + 3.0 * 0.044715 * square)
    return values * half, slope


def adam_update(weight, moment_one, moment_two, gradient, step_rate):
    moment_one_next = beta_first * moment_one + (1.0 - beta_first) * gradient
    moment_two_next = beta_second * moment_two + (1.0 - beta_second) * gradient * gradient
    corrected_one = moment_one_next / (1.0 - beta_first**STEP)
    corrected_two = moment_two_next / (1.0 - beta_second**STEP)
    weight_next = weight - step_rate * (
        corrected_one / (jnp.sqrt(corrected_two) + adam_epsilon) + decay_factor * weight
    )
    return (weight_next, moment_one_next, moment_two_next)


def shape_of(shape, dtype):
    return jax.ShapeDtypeStruct(shape, dtype)


def whole(shape):
    return pl.BlockSpec(shape, lambda *_: (0,) * len(shape))


def scalars():
    return pl.BlockSpec(memory_space=pltpu.SMEM)


LIGHT = pl.CostEstimate(flops=1, bytes_accessed=1, transcendentals=0)


def params(limit):
    return pltpu.CompilerParams(vmem_limit_bytes=limit * MIB)


def prologue_kernel(inputs, attention, gains, router, scaled, root, packed, payload):
    values = inputs[...]
    scale = norm_root(values)
    root[...] = scale
    scaled[...] = (values * scale).astype(bf16)
    parts = [attention[i].astype(bf16) for i in range(4)]
    packed[...] = jnp.concatenate(
        [part[:, :LANES] for part in parts] + [part[:, LANES:] for part in parts], axis=1
    )
    experts, share = router.shape
    groups = -(-(2 + experts) // 8)
    wide = jnp.concatenate([gains[...], router[...]], axis=0)
    wide = jnp.pad(wide, ((0, 8 * groups - 2 - experts), (0, 0)))
    row = jnp.concatenate([wide[8 * k : 8 * k + 8] for k in range(groups)], axis=1)
    row = jnp.pad(row, ((0, 0), (0, LANES - groups * share)))
    payload[...] = jnp.broadcast_to(row[None], payload.shape)


def prologue(inputs, attention, gains, router, device_count):
    quarter, width = inputs.shape
    tall = attention.shape[1]
    shapes = [
        shape_of((quarter, width), bf16),
        shape_of((quarter, 1), f32),
        shape_of((tall, 6 * LANES), bf16),
        shape_of((device_count, 8, LANES), f32),
    ]
    arrays = (inputs, attention, gains, router)
    return pl.pallas_call(
        prologue_kernel,
        in_specs=[whole(a.shape) for a in arrays],
        out_specs=[whole(s.shape) for s in shapes],
        out_shape=shapes,
        compiler_params=params(60),
        cost_estimate=LIGHT,
        name="prologue",
    )(*arrays)


def slots_kernel(capacity, info, routes, grads, place, match, valid, slots):
    quarter = routes.shape[0]
    experts = match.shape[1]
    row = lax.broadcasted_iota(jnp.int32, (quarter, 1), 0) + info[0] * quarter
    inside = jnp.where(row < info[1], 1.0, 0.0)
    valid[...] = inside
    column = lax.broadcasted_iota(jnp.int32, (quarter, experts), 1)
    named = jnp.where(routes[...] == column, 1.0, 0.0)
    match[...] = named
    at = lax.broadcasted_iota(jnp.int32, (quarter, quarter), 0)
    before = lax.broadcasted_iota(jnp.int32, (quarter, quarter), 1)
    lower = jnp.where(at >= before, 1.0, 0.0).astype(bf16)
    rank = jnp.sum(mm(lower, (named * inside).astype(bf16)) * named, axis=1, keepdims=True) - 1.0
    slot = jnp.where(inside > 0.0, routes[...].astype(f32) * capacity + rank, -1.0)
    slot = jnp.broadcast_to(slot, (quarter, LANES)).T[:1]
    number = lax.broadcasted_iota(jnp.int32, place.shape, 0).astype(f32)
    chosen = jnp.where(number == slot, 1.0, 0.0).astype(bf16)
    place[...] = chosen
    slots[...] = mm(chosen, grads[...].astype(bf16)).astype(bf16)


def slots_part(info, routes, grads, experts, capacity):
    quarter, width = grads.shape
    shapes = [
        shape_of((experts * capacity, quarter), bf16),
        shape_of((quarter, experts), f32),
        shape_of((quarter, 1), f32),
        shape_of((experts * capacity, width), bf16),
    ]
    return pl.pallas_call(
        lambda *refs: slots_kernel(capacity, *refs),
        in_specs=[scalars(), whole(routes.shape), whole(grads.shape)],
        out_specs=[whole(s.shape) for s in shapes],
        out_shape=shapes,
        compiler_params=params(60),
        cost_estimate=LIGHT,
        name="slots",
    )(info, routes, grads)


def project_kernel(quarter, blocks, count, share, info, came, x0, x1, x2, x3, *refs):
    shards, (small, column_gain, weight, out_weight, qkv, kaug, vt) = refs[:count], refs[count:]
    tall = shards[0].shape[0]
    width = weight.shape[0]
    for j, ref in enumerate(shards):
        start = pl.multiple_of((info[2] ^ j) * tall, tall) if count > 1 else 0
        weight[pl.ds(start, tall), :] = ref[...]
    out_weight[:LANES, :] = weight[:, 3 * LANES : 4 * LANES].T
    out_weight[LANES:, :] = weight[:, 5 * LANES :].T[DH:]
    groups = small.shape[0] // 8
    devices = came.shape[0]
    flat = came[...].reshape(devices * 8, LANES)
    lane = lax.broadcasted_iota(jnp.int32, (LANES, width), 0)
    column = lax.broadcasted_iota(jnp.int32, (LANES, width), 1)
    inside = lax.rem(column, share)
    owner = lax.broadcasted_iota(jnp.int32, (devices, 1, width), 2) - share * lax.broadcasted_iota(
        jnp.int32, (devices, 1, width), 0
    )
    owner = jnp.where((owner >= 0) & (owner < share), 1.0, 0.0)
    for k in range(groups):
        pick = jnp.where(lane == inside + k * share, 1.0, 0.0)
        spread = jnp.dot(flat, pick, precision=HIGHEST, preferred_element_type=f32)
        small[8 * k : 8 * k + 8, :] = jnp.sum(spread.reshape(devices, 8, width) * owner, axis=0)
    gain = small[:1, :]
    column_gain[...] = jnp.broadcast_to(gain, (LANES, width)).T[:, :1]
    for j, ref in enumerate((x0, x1, x2, x3)):
        start = pl.multiple_of((info[0] ^ j) * quarter, quarter)
        rows = pl.ds(start, quarter)
        scaled = (ref[...].astype(f32) * gain).astype(bf16)
        first = mm(scaled, weight[:, : 3 * LANES]).astype(bf16)
        second = mm(scaled, weight[:, 4 * LANES :]).astype(bf16)
        qkv[rows, : 3 * LANES] = first
        qkv[rows, 3 * LANES :] = second
        kaug[rows, :LANES] = first[:, LANES : 2 * LANES]
        lane = lax.broadcasted_iota(jnp.int32, (quarter, LANES), 1)
        row = lax.broadcasted_iota(jnp.int32, (quarter, LANES), 0) + start
        hidden = jnp.where((lane == 0) & (row >= info[1]), masked_score, 0.0)
        kaug[rows, LANES:] = jnp.where(lane < DH, hidden, second[:, :LANES].astype(f32)).astype(bf16)
        values = first[:, 2 * LANES :].T
        vt[0, :DH, rows] = values[:DH]
        vt[1, :DH, rows] = values[DH:]
        vt[2, :DH, rows] = second[:, LANES:].T[:DH]
    full_len = quarter * blocks
    tail = (lax.broadcasted_iota(jnp.int32, (16, full_len), 0) == 0).astype(f32).astype(bf16)
    for h in range(3):
        vt[h, DH:, :] = tail


def project(info, came, rows, shards, share, experts):
    quarter, width = rows[0].shape
    blocks = len(rows)
    full_len = quarter * blocks
    shapes = [
        shape_of((8 * -(-(2 + experts) // 8), width), f32),
        shape_of((width, 1), f32),
        shape_of((width, 6 * LANES), bf16),
        shape_of((3 * DH, width), bf16),
        shape_of((full_len, 5 * LANES), bf16),
        shape_of((full_len, 2 * LANES), bf16),
        shape_of((3, DH + 16, full_len), bf16),
    ]
    arrays = (came, *rows, *shards)
    return pl.pallas_call(
        lambda *refs: project_kernel(quarter, blocks, len(shards), share, *refs),
        in_specs=[scalars()] + [whole(a.shape) for a in arrays],
        out_specs=[whole(s.shape) for s in shapes],
        out_shape=shapes,
        compiler_params=params(60),
        cost_estimate=LIGHT,
        name="project",
    )(info, *arrays)


def attention_kernel(info, qkv, kaug, vt, context, chances, totals, *sent):
    quarter = context.shape[2]
    step = pl.program_id(0)
    rows = pl.ds(pl.multiple_of(step * quarter, quarter), quarter)
    q01 = (qkv[rows, :LANES].astype(f32) * score_scale).T.astype(bf16)
    q2 = (qkv[rows, 3 * LANES : 4 * LANES].astype(f32) * score_scale).T.astype(bf16)[:DH]
    ones = (lax.broadcasted_iota(jnp.int32, (DH, quarter), 0) == 0).astype(f32).astype(bf16)
    zeros = jnp.zeros((DH, quarter), bf16)
    queries = (
        jnp.concatenate([q01[:DH], zeros, ones, zeros], axis=0),
        jnp.concatenate([zeros, q01[DH:], ones, zeros], axis=0),
        jnp.concatenate([zeros, zeros, ones, q2], axis=0),
    )
    full_len = kaug.shape[0]
    all_scores = [mm(kaug[...], queries[h]) for h in range(3)]
    for h in range(3):
        scores = all_scores[h]
        top = jnp.max(jnp.max(scores.reshape(8, full_len // 8, quarter), axis=0), axis=0, keepdims=True)
        low = jnp.exp(scores - top).astype(bf16)
        chances[h] = low
        summed = mm(vt[h], low)
        part = 1.0 / summed[DH : DH + 1]
        totals[0, h : h + 1, :] = part
        context[0, h * DH : (h + 1) * DH, :] = (summed[:DH] * part).astype(bf16)
    for j, ref in enumerate(sent):

        @pl.when(step == info[0] ^ j)
        def _():
            ref[...] = context[0]


def attention_forward(info, qkv, kaug, vt, blocks):
    full_len = qkv.shape[0]
    quarter = full_len // blocks
    inner = 3 * DH
    return pl.pallas_call(
        attention_kernel,
        grid=(blocks,),
        in_specs=[scalars(), whole(qkv.shape), whole(kaug.shape), whole(vt.shape)],
        out_specs=[
            pl.BlockSpec((1, inner, quarter), lambda i: (i, 0, 0)),
            pl.BlockSpec((3, full_len, quarter), lambda i: (0, 0, i)),
            pl.BlockSpec((1, 3, quarter), lambda i: (i, 0, 0)),
        ]
        + [whole((inner, quarter))] * blocks,
        out_shape=[
            shape_of((blocks, inner, quarter), bf16),
            shape_of((3, full_len, full_len), bf16),
            shape_of((blocks, 3, quarter), f32),
        ]
        + [shape_of((inner, quarter), bf16)] * blocks,
        compiler_params=params(60),
        cost_estimate=LIGHT,
        name="attend",
    )(info, qkv, kaug, vt)


def turn_kernel(quarter, blocks, info, x0, x1, x2, x3, qkv, context, xt, kt, q2, cn):
    for j, ref in enumerate((x0, x1, x2, x3)):
        xt[info[0] ^ j] = ref[...].T
    for j in range(blocks):
        rows = slice(j * quarter, (j + 1) * quarter)
        third = qkv[rows, 3 * LANES : 4 * LANES].T
        kt[:LANES, rows] = qkv[rows, LANES : 2 * LANES].T
        kt[LANES:, rows] = third[DH:]
        zeros = jnp.zeros((DH, quarter), bf16)
        q2[rows, :] = jnp.concatenate([zeros, third[:DH]], axis=0).T
        cn[rows, :LANES] = context[j, :LANES, :].T
        cn[rows, LANES:] = jnp.concatenate([zeros, context[j, LANES:, :]], axis=0).T


def turn(info, rows, qkv, context):
    quarter, width = rows[0].shape
    blocks = len(rows)
    full_len = quarter * blocks
    shapes = [
        shape_of((blocks, width, quarter), bf16),
        shape_of((3 * DH, full_len), bf16),
        shape_of((full_len, LANES), bf16),
        shape_of((full_len, 2 * LANES), bf16),
    ]
    return pl.pallas_call(
        lambda *refs: turn_kernel(quarter, blocks, *refs),
        in_specs=[scalars()] + [whole((quarter, width))] * 4 + [whole(qkv.shape), whole(context.shape)],
        out_specs=[whole(s.shape) for s in shapes],
        out_shape=shapes,
        compiler_params=params(60),
        cost_estimate=LIGHT,
        name="turn",
    )(info, *rows, qkv, context)


def two_columns(column):
    high = column.astype(bf16).astype(f32)
    lane = lax.broadcasted_iota(jnp.int32, (column.shape[0], LANES), 1)
    return jnp.where(lane == 0, high, jnp.where(lane == 1, column - high, 0.0)).astype(bf16)


def middle_kernel(
    rows, c0, c1, c2, c3, w0, w1, w2, w3, small, place, match, valid, middle, root, chances, gate, slots
):
    gain, router = small[1:2, :], small[2 : 2 + match.shape[1], :]
    total = rows[...]
    for context, weight in zip((c0, c1, c2, c3), (w0, w1, w2, w3)):
        total = total + mm_tn(context[...], weight[...])
    middle[...] = total
    scale = norm_root(total)
    root[...] = scale
    hidden = total * scale * gain
    scores = mm_nt(hidden, router, HIGHEST)
    powers = jnp.exp(scores - jnp.max(scores, axis=-1, keepdims=True))
    share = powers / jnp.sum(powers, axis=-1, keepdims=True)
    chances[...] = share
    own = jnp.sum(share * match[...], axis=-1, keepdims=True)
    gate[...] = own
    width = rows.shape[1]
    slots[:, :width] = mm(place[...], hidden.astype(bf16)).astype(bf16)
    slots[:, width:] = mm(place[...], two_columns(own * valid[...])).astype(bf16)


def middle_part(rows, contexts, out_weights, small, place, match, valid):
    quarter, width = rows.shape
    experts = match.shape[1]
    shapes = [
        shape_of((quarter, width), f32),
        shape_of((quarter, 1), f32),
        shape_of((quarter, experts), f32),
        shape_of((quarter, 1), f32),
        shape_of((place.shape[0], width + LANES), bf16),
    ]
    arrays = (rows, *contexts, *out_weights, small, place, match, valid)
    return pl.pallas_call(
        middle_kernel,
        in_specs=[whole(a.shape) for a in arrays],
        out_specs=[whole(s.shape) for s in shapes],
        out_shape=shapes,
        compiler_params=params(60),
        cost_estimate=LIGHT,
        name="middle",
    )(*arrays)


def expert_kernel(rows, grads, near_in, near_out, other_in, other_out, out, back, held, arrived):
    width = grads.shape[1]
    early = near_in.shape[1]
    copies = []
    for i, pair in enumerate(((near_in, near_out), (other_in, other_out))):
        for j in range(2):
            at = 2 * i + j
            ends = (slice(0, early), slice(early, 2 * width))
            copies.append(
                [
                    pltpu.make_async_copy(ref.at[j], held.at[at, end, :], arrived.at[at, k])
                    for k, (ref, end) in enumerate(zip(pair, ends))
                ]
            )
    for pair in copies:
        for copy in pair:
            copy.start()
    out_total, back_total = None, None
    for i, pair in enumerate(copies):
        for copy in pair:
            copy.wait()
        inward, outward = held[i, :width, :], held[i, width:, :]
        grad = mm(grads[...], outward)
        active, slope = gelu_pair(mm(rows[:, :width], inward))
        part = mm_nt(active.astype(bf16), outward)
        back_part = mm_nt((grad * slope).astype(bf16), inward)
        out_total = part if i == 0 else out_total + part
        back_total = back_part if i == 0 else back_total + back_part
    result = out_total.astype(bf16)
    out[...] = result
    back[:, :width] = back_total.astype(bf16)
    match = jnp.sum(grads[...].astype(f32) * result.astype(f32), axis=-1, keepdims=True)
    back[:, width:] = two_columns(match)


def expert_part(rows, grads, weights):
    slots, width = grads.shape
    hidden = weights[0].shape[2]
    count = len(weights)
    shapes = [shape_of((slots, width), bf16), shape_of((slots, width + LANES), bf16)]
    return pl.pallas_call(
        expert_kernel,
        in_specs=[whole(rows.shape), whole(grads.shape)] + [pl.BlockSpec(memory_space=pl.ANY)] * count,
        out_specs=[whole(s.shape) for s in shapes],
        out_shape=shapes,
        scratch_shapes=[pltpu.VMEM((count, 2 * width, hidden), bf16), pltpu.SemaphoreType.DMA((count, 2))],
        compiler_params=params(60),
        cost_estimate=LIGHT,
        name="experts",
    )(rows, grads, *weights)


def pack_small(small, cut):
    devices = cut.shape[0]
    rows, width = small.shape
    share = width // devices
    groups = rows // 8
    column = lax.broadcasted_iota(jnp.int32, (devices, 1, width), 2)
    owner = column - share * lax.broadcasted_iota(jnp.int32, (devices, 1, width), 0)
    owner = jnp.where((owner >= 0) & (owner < share), 1.0, 0.0)
    lane = lax.broadcasted_iota(jnp.int32, (width, LANES), 1)
    inside = lax.rem(lax.broadcasted_iota(jnp.int32, (width, LANES), 0), share)
    total = None
    for k in range(groups):
        pick = jnp.where(lane == inside + k * share, 1.0, 0.0)
        spread = (small[8 * k : 8 * k + 8, :][None] * owner).reshape(devices * 8, width)
        part = jnp.dot(spread, pick, precision=HIGHEST, preferred_element_type=f32)
        total = part if total is None else total + part
    cut[...] = total.reshape(devices, 8, LANES)


def expert_grad_kernel(count, *refs):
    info, rows, grads = refs[0], refs[1 : count + 1], refs[count + 1 : 2 * count + 1]
    small, near_in, near_out, out, square, cut, weight, row_all, grad_all, inner_all, active_all, arrived = refs[
        2 * count + 1 :
    ]
    early = near_in.shape[1]
    ends = (slice(0, early), slice(early, weight.shape[0]))
    copies = [
        pltpu.make_async_copy(ref.at[lax.div(info[0], 2)], weight.at[end, :], arrived.at[i])
        for i, (ref, end) in enumerate(zip((near_in, near_out), ends))
    ]
    for copy in copies:
        copy.start()
    pack_small(small, cut)
    for copy in copies:
        copy.wait()
    slots, width = grads[0].shape
    for j in range(count):
        at = slice(j * slots, (j + 1) * slots)
        gate = rows[j][:, width : width + 1].astype(f32) + rows[j][:, width + 1 : width + 2].astype(f32)
        row_all[at, :] = rows[j][:, :width]
        grad_all[at, :] = (grads[j][...].astype(f32) * gate).astype(bf16)
        back = mm(grads[j][...], weight[width:, :])
        active, slope = gelu_pair(mm(rows[j][:, :width], weight[:width, :]))
        inner_all[at, :] = (back * slope * gate).astype(bf16)
        active_all[at, :] = active.astype(bf16)
    first = mm_tn(row_all[...], inner_all[...])
    out[0] = first
    second = mm_tn(grad_all[...], active_all[...])
    out[1] = second
    square[...] = jnp.sum(first * first + second * second, axis=0, keepdims=True)


def expert_gradient(info, rows, grads, small, near_in, near_out, device_count):
    count = len(rows)
    slots, width = grads[0].shape
    hidden = near_in.shape[2]
    arrays = (*rows, *grads, small)
    shapes = [
        shape_of((2, width, hidden), f32),
        shape_of((1, hidden), f32),
        shape_of((device_count, 8, LANES), f32),
    ]
    return pl.pallas_call(
        lambda *refs: expert_grad_kernel(count, *refs),
        in_specs=[scalars()] + [whole(a.shape) for a in arrays] + [pl.BlockSpec(memory_space=pl.ANY)] * 2,
        out_specs=[whole(s.shape) for s in shapes],
        out_shape=shapes,
        scratch_shapes=[pltpu.VMEM((2 * width, hidden), bf16)]
        + [pltpu.VMEM((count * slots, width), bf16)] * 2
        + [pltpu.VMEM((count * slots, hidden), bf16)] * 2
        + [pltpu.SemaphoreType.DMA((2,))],
        compiler_params=params(60),
        cost_estimate=LIGHT,
        name="expert_gradient",
    )(info, *arrays, near_in, near_out)


def return_kernel(
    back, place, middle, root, chances, gate, match, cotangent, small, w0, w1, w2, w3,
    grad, turned, small_grad, *parts,
):
    experts = match.shape[1]
    gain, router = small[1:2, :], small[2 : 2 + experts, :]
    width = middle.shape[1]
    came = mm_tn(place[...], back[...])
    gate_grad = came[:, width : width + 1] + came[:, width + 1 : width + 2]
    own = gate[...]
    score_grad = own * (match[...] - chances[...]) * gate_grad
    scaled = middle[...] * root[...]
    hidden = scaled * gain
    tall = small_grad.shape[0]
    small_grad[1 : 1 + experts, :] = mm_tn(score_grad, hidden, HIGHEST)
    small_grad[1 + experts :, :] = jnp.zeros((tall - 1 - experts, hidden.shape[1]), f32)
    second = own * came[:, :width] + jnp.dot(
        score_grad, router, precision=HIGHEST, preferred_element_type=f32
    )
    small_grad[:1, :] = jnp.sum(second * scaled, axis=0, keepdims=True)
    inner = second * gain
    centre = jnp.mean(inner * scaled, axis=-1, keepdims=True)
    total = cotangent[...] + root[...] * (inner - scaled * centre)
    grad[...] = total
    low = total.astype(bf16)
    turned[...] = low.T
    for ref, weight in zip(parts, (w0, w1, w2, w3)):
        ref[...] = mm_nt(weight[...], low).astype(bf16)


def return_part(back, place, middle, root, chances, gate, match, cotangent, small, out_weights):
    quarter, width = middle.shape
    experts = match.shape[1]
    inner = out_weights[0].shape[0]
    shapes = [
        shape_of((quarter, width), f32),
        shape_of((width, quarter), bf16),
        shape_of((8 * -(-(1 + experts) // 8), width), f32),
    ] + [shape_of((inner, quarter), bf16)] * len(out_weights)
    arrays = (back, place, middle, root, chances, gate, match, cotangent, small, *out_weights)
    return pl.pallas_call(
        return_kernel,
        in_specs=[whole(a.shape) for a in arrays],
        out_specs=[whole(s.shape) for s in shapes],
        out_shape=shapes,
        compiler_params=params(60),
        cost_estimate=LIGHT,
        name="returned",
    )(*arrays)


def attention_back_kernel(
    blocks, info, g0, g1, g2, g3, context, chances, totals, qkv, kt, q2, packed, grads, vaug, k01, k2, v01, v2
):
    step = pl.program_id(0)
    quarter = grads.shape[2]

    @pl.when(step == 0)
    def _():
        for j, ref in enumerate((g0, g1, g2, g3)):
            grads[info[0] ^ j] = ref[...]
        vaug[:, :LANES] = qkv[:, 2 * LANES : 3 * LANES]
        lane = lax.broadcasted_iota(jnp.int32, (vaug.shape[0], LANES), 1)
        ones = jnp.where(lane < DH + 2, 1.0, 0.0)
        vaug[:, LANES:] = jnp.where(lane < DH, qkv[:, 4 * LANES :].astype(f32), ones).astype(bf16)
        for ref in (k01, k2, v01, v2):
            ref[...] = jnp.zeros(ref.shape, f32)

    rows = pl.ds(pl.multiple_of(step * quarter, quarter), quarter)
    raw = grads[step].astype(f32)
    scale = totals[0]
    scaled = [raw[h * DH : (h + 1) * DH] * scale[h : h + 1] for h in range(3)]
    heads = jnp.concatenate(scaled, axis=0).astype(bf16)
    lane = lax.broadcasted_iota(jnp.int32, (quarter, LANES), 1)
    row = lax.broadcasted_iota(jnp.int32, (DH, quarter), 0)
    zeros = jnp.zeros((DH, quarter), bf16)
    q01 = qkv[rows, :LANES].astype(f32)
    g01 = heads[:LANES].T.astype(f32)
    third = jnp.concatenate([heads[LANES:], zeros], axis=0).T
    query_parts = []
    for h in range(3):
        part = heads[h * DH : (h + 1) * DH]
        centre = -jnp.sum(
            part.astype(f32) * context[0, h * DH : (h + 1) * DH, :].astype(f32), axis=0, keepdims=True
        )
        high = centre.astype(bf16).astype(f32)
        tail = jnp.where(row == 0, high, jnp.where(row == 1, centre - high, 0.0)).astype(bf16)
        pieces = [zeros, zeros, zeros, tail]
        pieces[h] = part
        chance_grad = mm(vaug[...], jnp.concatenate(pieces, axis=0))
        low = chances[h]
        score_grad = (low.astype(f32) * chance_grad).astype(bf16)
        query_parts.append(mm(kt[h * DH : (h + 1) * DH, :], score_grad) * score_scale)
        if h < 2:
            inside = (lane >= h * DH) & (lane < (h + 1) * DH)
            k01[...] += mm(score_grad, jnp.where(inside, q01, 0.0).astype(bf16))
            v01[...] += mm(low, jnp.where(inside, g01, 0.0).astype(bf16))
        else:
            k2[...] += mm(score_grad, q2[rows, :])
            v2[...] += mm(low, third)
    packed[rows, :LANES] = jnp.concatenate(query_parts[:2], axis=0).T.astype(bf16)
    packed[rows, 4 * LANES : 5 * LANES] = (
        jnp.concatenate([query_parts[2], jnp.zeros((DH, quarter), f32)], axis=0).T.astype(bf16)
    )

    @pl.when(step == blocks - 1)
    def _():
        packed[:, LANES : 2 * LANES] = (k01[...] * score_scale).astype(bf16)
        packed[:, 2 * LANES : 3 * LANES] = v01[...].astype(bf16)
        packed[:, 3 * LANES : 4 * LANES] = jnp.zeros(k01.shape, bf16)
        packed[:, 4 * LANES : 5 * LANES] = packed[:, 4 * LANES : 5 * LANES] + (k2[...] * score_scale).astype(bf16)
        packed[:, 5 * LANES :] = v2[...].astype(bf16)


def attention_backward(info, grads, context, chances, totals, qkv, kt, q2):
    blocks, inner, quarter = context.shape
    full_len = quarter * blocks
    block = pl.BlockSpec((1, inner, quarter), lambda i: (i, 0, 0))
    return pl.pallas_call(
        lambda *refs: attention_back_kernel(blocks, *refs),
        grid=(blocks,),
        in_specs=[
            scalars(),
            *[whole((inner, quarter))] * blocks,
            block,
            pl.BlockSpec((3, full_len, quarter), lambda i: (0, 0, i)),
            pl.BlockSpec((1, 3, quarter), lambda i: (i, 0, 0)),
            whole(qkv.shape),
            whole(kt.shape),
            whole(q2.shape),
        ],
        out_specs=whole((full_len, 6 * LANES)),
        out_shape=shape_of((full_len, 6 * LANES), bf16),
        scratch_shapes=[pltpu.VMEM(context.shape, bf16), pltpu.VMEM((full_len, 2 * LANES), bf16)]
        + [pltpu.VMEM((full_len, LANES), f32)] * 4,
        compiler_params=params(60),
        cost_estimate=LIGHT,
        name="attend_back",
    )(info, *grads, context, chances, totals, qkv, kt, q2)


def weight_grad_kernel(blocks, info, xt, packed, g0, g1, g2, g3, cn, weight, gain, out, gain_grad):
    quarter = xt.shape[2]
    total, outer = None, None
    for j, ref in enumerate((g0, g1, g2, g3)):
        rows = slice(j * quarter, (j + 1) * quarter)
        there = pl.ds(pl.multiple_of((info[0] ^ j) * quarter, quarter), quarter)
        part = mm(xt[j], packed[rows, :])
        own = mm(ref[...], cn[there, :])
        total = part if total is None else total + part
        outer = own if outer is None else outer + own
    gain_grad[...] = jnp.sum(total * weight[...].astype(f32), axis=1, keepdims=True)
    total = total * gain[...]
    out[:, : 3 * LANES] = total[:, : 3 * LANES].astype(bf16)
    out[:, 3 * LANES : 4 * LANES] = outer[:, :LANES].astype(bf16)
    out[:, 4 * LANES : 5 * LANES] = total[:, 4 * LANES : 5 * LANES].astype(bf16)
    out[:, 5 * LANES :] = (total[:, 5 * LANES :] + outer[:, LANES:]).astype(bf16)


def weight_gradient(info, xt, packed, grads, cn, weight, gain):
    blocks, width, quarter = xt.shape
    tall = 256
    full_len = quarter * blocks
    return pl.pallas_call(
        lambda *refs: weight_grad_kernel(blocks, *refs),
        grid=(width // tall,),
        in_specs=[
            scalars(),
            pl.BlockSpec((blocks, tall, quarter), lambda i: (0, i, 0)),
            whole(packed.shape),
            *[pl.BlockSpec((tall, quarter), lambda i: (i, 0))] * blocks,
            whole(cn.shape),
            pl.BlockSpec((tall, 6 * LANES), lambda i: (i, 0)),
            pl.BlockSpec((tall, 1), lambda i: (i, 0)),
        ],
        out_specs=[pl.BlockSpec((tall, 6 * LANES), lambda i: (i, 0)), pl.BlockSpec((tall, 1), lambda i: (i, 0))],
        out_shape=[shape_of((width, 6 * LANES), bf16), shape_of((width, 1), f32)],
        compiler_params=params(60),
        cost_estimate=LIGHT,
        name="weight_gradient",
    )(info, xt, packed, *grads, cn, weight, gain)


def input_grad_kernel(quarter, info, packed, weight, *parts):
    for j, ref in enumerate(parts):
        rows = pl.ds(pl.multiple_of((info[0] ^ j) * quarter, quarter), quarter)
        ref[...] = mm_nt(packed[rows, :], weight[...]).astype(bf16)


def input_gradient(info, packed, weight, blocks):
    quarter = packed.shape[0] // blocks
    shapes = [shape_of((quarter, weight.shape[0]), bf16)] * blocks
    return pl.pallas_call(
        lambda *refs: input_grad_kernel(quarter, *refs),
        in_specs=[scalars(), whole(packed.shape), whole(weight.shape)],
        out_specs=[whole(s.shape) for s in shapes],
        out_shape=shapes,
        compiler_params=params(60),
        cost_estimate=LIGHT,
        name="input_gradient",
    )(info, packed, weight)


def sums_kernel(came, squares, small, gain_grad, gradient, payload, small_sum):
    count = came.shape[0]
    total = came[0].astype(f32)
    for i in range(1, count):
        total = total + came[i].astype(f32)
    gradient[...] = total
    own = jnp.sum(small[...], axis=0)
    square = (
        jnp.sum(total * total, keepdims=True)
        + jnp.sum(squares[...], keepdims=True)
        + jnp.sum(own * own, keepdims=True)
    )
    small_sum[...] = own
    rows = gain_grad.shape[0]
    row = lax.broadcasted_iota(jnp.int32, (8, LANES), 0)
    gain = jnp.concatenate([gain_grad[...], jnp.zeros((8 - rows, LANES), f32)], axis=0)
    payload[...] = jnp.broadcast_to(jnp.where(row < rows, gain, square)[None], payload.shape)


def sums_part(came, squares, small, gain_grad, device_count):
    shapes = [
        shape_of(came.shape[1:], f32),
        shape_of((device_count, 8, LANES), f32),
        shape_of((8, LANES), f32),
    ]
    arrays = (came, squares, small, gain_grad)
    return pl.pallas_call(
        sums_kernel,
        in_specs=[whole(a.shape) for a in arrays],
        out_specs=[whole(s.shape) for s in shapes],
        out_shape=shapes,
        compiler_params=params(60),
        cost_estimate=LIGHT,
        name="sums",
    )(*arrays)


def adam_kernel(lanes, share, expert_rates, info, last, small_sum, *refs):
    held, outs, factor = refs[:14], refs[14:27], refs[27]
    dense, dense_grad, gains, router = held[:3], held[3], held[4:7], held[7:10]
    weight, first, second, gradient = held[10:14]
    norm_out, outs = outs[0], outs[1:]
    dense_out, gains_out, router_out, expert_out = outs[:3], outs[3:6], outs[6:9], outs[9:12]
    matrix, part = pl.program_id(0), pl.program_id(1)
    experts = router[0].shape[0]

    @pl.when((matrix == 0) & (part == 0))
    def _():
        total = jnp.sum(last[...], axis=0)
        row = lax.broadcasted_iota(jnp.int32, (8, LANES), 0)
        squares = jnp.sum(jnp.where(row < lanes, total * total, 0.0), keepdims=True)
        norm = jnp.sqrt(squares + total[7:8, :1])
        scale = jnp.minimum(1.0, clip_limit / (norm + norm_epsilon))
        norm_out[...] = norm
        factor[...] = jnp.broadcast_to(scale, (8, LANES))
        rates = (0.71 / math.sqrt(D), 0.71 / math.sqrt(D), 0.83 / math.sqrt(D), 0.79 / math.sqrt(H * DH))
        for i, rate in enumerate(rates):
            grad = jnp.concatenate(
                [
                    dense_grad[:, i * LANES : (i + 1) * LANES],
                    dense_grad[:, 4 * LANES + i * DH : 4 * LANES + (i + 1) * DH],
                ],
                axis=1,
            )
            result = adam_update(*[ref[i] for ref in dense], grad * scale, rate)
            for ref, value in zip(dense_out, result):
                ref[i] = value
        column = lax.broadcasted_iota(jnp.int32, (LANES, LANES), 1)
        place = lax.broadcasted_iota(jnp.int32, (LANES, LANES), 0) - info[3] * share
        own = jnp.zeros((8, LANES), f32)
        for i in range(lanes):
            pick = jnp.where((column == place + i * LANES) & (column < share), 1.0, 0.0)
            own = own + jnp.dot(
                jnp.broadcast_to(total[i : i + 1], (8, LANES)), pick, precision=HIGHEST, preferred_element_type=f32
            )
        groups = -(-(1 + experts) // 8)
        table = small_sum[...]
        table = jnp.concatenate([table[:, k * share : (k + 1) * share] for k in range(groups)], axis=0)
        grad = jnp.concatenate([own[:1, :share], table[:1]], axis=0)
        for ref, value in zip(gains_out, adam_update(*[ref[...] for ref in gains], grad * scale, 0.5)):
            ref[...] = value
        grad = table[1 : 1 + experts]
        result = adam_update(*[ref[...] for ref in router], grad * scale, 0.24 / math.sqrt(D))
        for ref, value in zip(router_out, result):
            ref[...] = value

    rate = jnp.where(matrix == 0, expert_rates[0], expert_rates[1])
    result = adam_update(weight[...], first[...], second[...], gradient[...] * factor[:1, :1], rate)
    for ref, value in zip(expert_out, result):
        ref[...] = value


def adam(info, last, small_sum, dense, dense_grad, gains, router, expert, expert_grad, rates):
    _, tall, wide = expert_grad.shape
    parts = 4
    block = pl.BlockSpec((1, tall // parts, wide), lambda i, j: (i, j, 0))
    small = [*dense, *gains, *router]
    shapes = [shape_of((1, 1), f32)] + [shape_of(a.shape, f32) for a in small]
    ins = (last, small_sum, *dense, dense_grad, *gains, *router)
    return pl.pallas_call(
        lambda *refs: adam_kernel(tall // LANES, gains[0].shape[1], rates, *refs),
        grid=(2, parts),
        in_specs=[scalars()] + [whole(a.shape) for a in ins] + [block] * 4,
        out_specs=[whole(a.shape) for a in shapes] + [block] * 3,
        out_shape=shapes + [shape_of(expert_grad.shape, f32)] * 3,
        scratch_shapes=[pltpu.VMEM((8, LANES), f32)],
        compiler_params=params(60),
        cost_estimate=LIGHT,
        name="adam",
    )(info, *ins, *expert, expert_grad)


def tie(*values):
    return lax.optimization_barrier(values)


def on_device(
    inputs,
    cotangent,
    lengths,
    routes,
    attention_weight,
    attention_mean,
    attention_square,
    expert_weight,
    expert_mean,
    expert_square,
    router_matrix,
    router_mean,
    router_square,
    norm_gains,
    gains_mean,
    gains_square,
):
    quarter, width = inputs.shape[1:]
    dp_count, tensor_count = lax.axis_size(DP), lax.axis_size(TENSOR)
    device_count = dp_count * tensor_count
    expert_count = router_matrix.shape[1]
    capacity = max(2, (5 * quarter + 4 * expert_count - 1) // (4 * expert_count))
    own_dp, own_tensor = lax.axis_index(DP), lax.axis_index(TENSOR)
    share = router_matrix.shape[0]
    rows, grad_rows, length = inputs[0], cotangent[0], lengths[0]
    info = jnp.stack([own_tensor, length, own_dp, lax.axis_index(EVERYONE)]).astype(jnp.int32)

    scaled_one, root_one, weight_own, payload = prologue(
        rows, attention_weight, norm_gains, router_matrix.T, device_count
    )
    block_two = swap(scaled_one, TENSOR, 2)
    expert_flat = expert_weight[0].reshape(2 * width, -1)
    inward_pair = jnp.stack([expert_flat[:EARLY].astype(bf16)] * 2)
    place, match, valid_scale, grad_slots = slots_part(info, routes[0], grad_rows, expert_count, capacity)
    if dp_count == 8:
        w4, w2, w1 = [swap(weight_own, DP, mask) for mask in (4, 2, 1)]
        w4, w2, w1, payload = tie(w4, w2, w1, payload)
        w6, w5, w3 = swap(w4, DP, 2), swap(w4, DP, 1), swap(w2, DP, 1)
        w6, w5, w3, block_two, inward_pair, grad_slots = tie(w6, w5, w3, block_two, inward_pair, grad_slots)
        shards = [weight_own, w1, w2, w3, w4, w5, w6, swap(w6, DP, 1)]
    else:
        block_two, inward_pair, weight_own, grad_slots = tie(block_two, inward_pair, weight_own, grad_slots)
        shards = [lax.all_gather(weight_own, DP, axis=0, tiled=True)]
    row_blocks = [scaled_one, swap(scaled_one, TENSOR, 1), block_two, swap(block_two, TENSOR, 1)]
    small_came = lax.all_to_all(payload, EVERYONE, 0, 0, tiled=True)
    inward_near = lax.all_to_all(inward_pair, "th", 0, 0, tiled=True)

    slot_count = expert_count * capacity

    def trade(values):
        blocks = values.reshape(expert_count, capacity, values.shape[1])
        return lax.all_to_all(blocks, DP, 0, 0, tiled=True).reshape(values.shape)

    expert_grads = trade(grad_slots)
    small, gain_column, weight, out_weight, qkv, keys_wide, values_turned = project(
        info, small_came, row_blocks, shards, share, expert_count
    )
    out_near, out_far = swap(out_weight, TENSOR, 1), swap(out_weight, TENSOR, 2)
    context, chances, totals, *sent = attention_forward(info, qkv, keys_wide, values_turned, tensor_count)
    outward_pair = jnp.stack([expert_flat[EARLY:].astype(bf16)] * 2)
    expert_grads, inward_near, out_near, out_far, *sent = tie(expert_grads, inward_near, out_near, out_far, *sent)
    contexts = [sent[0]] + [swap(sent[j], TENSOR, j) for j in range(1, tensor_count)]
    out_weights = [out_weight, out_near, out_far, swap(out_far, TENSOR, 1)]
    outward_pair, *contexts = tie(outward_pair, *contexts)
    outward_near = lax.all_to_all(outward_pair, "th", 0, 0, tiled=True)

    middle, root_two, shares, gate, slots = middle_part(
        rows, contexts, out_weights, small, place, match, valid_scale
    )
    qkv, expert_grads, slots, inward_near = tie(qkv, expert_grads, slots, inward_near)
    expert_rows = trade(slots)
    turned_rows, keys_turned, third_query, context_rows = turn(info, row_blocks, qkv, context)
    inward_other, outward_other = swap(inward_near, TENSOR, 1), swap(outward_near, TENSOR, 1)
    expert_rows, turned_rows, inward_other, outward_other = tie(
        expert_rows, turned_rows, inward_other, outward_other
    )
    expert_outs, expert_back = expert_part(
        expert_rows, expert_grads, [inward_near, outward_near, inward_other, outward_other]
    )
    expert_rows, expert_back = tie(expert_rows, expert_back)
    rows_all = gather_relative(expert_rows, TENSOR, [2, 1])
    expert_back, rows_all = tie(trade(expert_back), rows_all)

    middle_grad, middle_turned, small_grad, *parts = return_part(
        expert_back, place, middle, root_two, shares, gate, match, grad_rows, small, out_weights
    )
    expert_outs, middle_turned, *parts = tie(expert_outs, middle_turned, *parts)
    context_grads = [parts[0]] + [swap(parts[j], TENSOR, j) for j in range(1, tensor_count)]
    expert_outs = trade(expert_outs)
    middle_turned, expert_grads, *context_grads = tie(middle_turned, expert_grads, *context_grads)
    middle_near, middle_far = swap(middle_turned, TENSOR, 1), swap(middle_turned, TENSOR, 2)
    grads_near, grads_far = swap(expert_grads, TENSOR, 1), swap(expert_grads, TENSOR, 2)

    packed = attention_backward(info, context_grads, context, chances, totals, qkv, keys_turned, third_query)
    packed, middle_far = tie(packed, middle_far)
    middle_all = [middle_turned, middle_near, middle_far, swap(middle_far, TENSOR, 1)]
    weight_grad, gain_one_grad = weight_gradient(
        info, turned_rows, packed, middle_all, context_rows, weight, gain_column
    )
    weight_grad, expert_outs, inward_near, small_grad, grads_far = tie(
        weight_grad, expert_outs, inward_near, small_grad, grads_far
    )
    grads_all = [expert_grads, grads_near, grads_far, swap(grads_far, TENSOR, 1)]
    weight_came = lax.all_to_all(weight_grad.reshape(dp_count, -1, width), DP, 0, 0, tiled=True)
    expert_grad, expert_squares, small_cut = expert_gradient(
        info, rows_all, grads_all, small_grad, inward_near, outward_near, device_count
    )
    small_grads = lax.all_to_all(small_cut, EVERYONE, 0, 0, tiled=True)

    expert_squares, packed, small_grads = tie(expert_squares, packed, small_grads)
    input_parts = input_gradient(info, packed, weight, tensor_count)
    first_half = input_parts[0].astype(f32) + swap(input_parts[1], TENSOR, 1).astype(f32)
    second_half = (input_parts[2].astype(f32) + swap(input_parts[3], TENSOR, 1).astype(f32)).astype(bf16)

    weight_came, second_half = tie(weight_came, second_half)
    second_came = swap(second_half, TENSOR, 2)
    dense_grad, last, small_sum = sums_part(
        weight_came, expert_squares, small_grads, gain_one_grad.reshape(-1, LANES), device_count
    )
    last, expert_outs, first_half = tie(last, expert_outs, first_half)
    last_all = lax.all_to_all(last, EVERYONE, 0, 0, tiled=True)
    input_grad = middle_grad + norm_backward(rows, root_one, small[:1], first_half + second_came.astype(f32))
    picked = mm_tn(place, expert_outs)
    branch = gate * valid_scale * picked
    block_output = middle + branch
    last_all, input_grad, block_output, branch = tie(last_all, input_grad, block_output, branch)

    rates = (0.4 * math.sqrt(expert_count / D), 1.38 * math.sqrt(expert_count / FF))
    norm, *updated = adam(
        info,
        last_all,
        small_sum,
        (attention_weight, attention_mean, attention_square),
        dense_grad,
        (norm_gains, gains_mean, gains_square),
        (router_matrix.T, router_mean.T, router_square.T),
        (expert_weight[0], expert_mean[0], expert_square[0]),
        expert_grad,
        rates,
    )
    attention_new, gains_new, router_new, expert_new = updated[:3], updated[3:6], updated[6:9], updated[9:]
    router_new = [part.T for part in router_new]
    grad_norm = norm.reshape(())
    return (
        block_output[None],
        input_grad[None],
        grad_norm,
        *attention_new,
        *[part[None] for part in expert_new],
        *router_new,
        *gains_new,
        branch[None],
    )


def solution(mesh):
    names = mesh.axis_names
    dp_count, tensor_count = mesh.shape[names[0]], mesh.shape[names[1]]
    cut = jax.sharding.Mesh(mesh.devices.reshape(dp_count // 2, 2, tensor_count // 2, 2), EVERYONE)
    rows = P(DP, TENSOR, None)
    attention = P(None, DP, TENSOR)
    expert = P(DP, None, None, TENSOR)
    router = P(EVERYONE, None)
    gains = P(None, EVERYONE)
    weights = (attention,) * 3 + (expert,) * 3 + (router,) * 3 + (gains,) * 3
    return jax.shard_map(
        on_device,
        mesh=cut,
        in_specs=(rows, rows, P(DP), rows) + weights,
        out_specs=(rows, rows, P()) + weights + (rows,),
        check_vma=False,
    )
```

```python
import math

import jax
import jax.numpy as jnp
from jax import lax
from jax.experimental import pallas as pl
from jax.experimental.pallas import tpu as pltpu
from jax.sharding import PartitionSpec as P

D = 768
H = 12
DH = 64
FF = 3072
STEP = 10

HIGHEST = lax.Precision.HIGHEST
norm_epsilon = 1e-06
beta_first = 0.9
beta_second = 0.999
adam_epsilon = 1e-08
decay_factor = 0.01
clip_limit = 1.0
masked_score = -1e30
score_scale = 1.0 / math.sqrt(DH)
bf16 = jnp.bfloat16
f32 = jnp.float32
MIB = 1 << 20
LANES = 128
EARLY = 928


DP = ("dh", "dl")
TENSOR = ("th", "tl")
EVERYONE = DP + TENSOR


def swap(values, axis, mask):
    count = lax.axis_size(axis)
    return lax.ppermute(values, axis, [(i, i ^ mask) for i in range(count)])


def bits_of(count):
    return [1 << b for b in range(count.bit_length() - 1)]


def gather_relative(block, axis, order):
    held = {0: block}
    for mask in order:
        for j in list(held):
            held[j ^ mask] = swap(held[j], axis, mask)
    return [held[j] for j in range(len(held))]


def mm(a, b):
    return jnp.dot(a, b, preferred_element_type=f32)


def mm_nt(a, b, precision=None):
    return lax.dot_general(
        a, b, (((1,), (1,)), ((), ())), preferred_element_type=f32, precision=precision
    )


def mm_tn(a, b, precision=None):
    return lax.dot_general(
        a, b, (((0,), (0,)), ((), ())), preferred_element_type=f32, precision=precision
    )


def norm_root(values):
    return lax.rsqrt(jnp.mean(values * values, axis=-1, keepdims=True) + norm_epsilon)


def norm_backward(values, root, gain_row, grad):
    scaled = values * root
    inner = grad * gain_row
    centre = jnp.mean(inner * scaled, axis=-1, keepdims=True)
    return root * (inner - scaled * centre)


def gelu_pair(values):
    c = math.sqrt(2.0 / math.pi)
    square = values * values
    th = jnp.tanh(c * values * (1.0 + 0.044715 * square))
    half = 0.5 * (1.0 + th)
    slope = half + 0.5 * values * (1.0 - th * th) * c * (1.0 + 3.0 * 0.044715 * square)
    return values * half, slope


def adam_update(weight, moment_one, moment_two, gradient, step_rate):
    moment_one_next = beta_first * moment_one + (1.0 - beta_first) * gradient
    moment_two_next = beta_second * moment_two + (1.0 - beta_second) * gradient * gradient
    corrected_one = moment_one_next / (1.0 - beta_first**STEP)
    corrected_two = moment_two_next / (1.0 - beta_second**STEP)
    weight_next = weight - step_rate * (
        corrected_one / (jnp.sqrt(corrected_two) + adam_epsilon) + decay_factor * weight
    )
    return (weight_next, moment_one_next, moment_two_next)


def shape_of(shape, dtype):
    return jax.ShapeDtypeStruct(shape, dtype)


def whole(shape):
    return pl.BlockSpec(shape, lambda *_: (0,) * len(shape))


def scalars():
    return pl.BlockSpec(memory_space=pltpu.SMEM)


LIGHT = pl.CostEstimate(flops=1, bytes_accessed=1, transcendentals=0)


def params(limit):
    return pltpu.CompilerParams(vmem_limit_bytes=limit * MIB)


def prologue_kernel(inputs, attention, gains, router, scaled, root, packed, payload):
    values = inputs[...]
    scale = norm_root(values)
    root[...] = scale
    scaled[...] = (values * scale).astype(bf16)
    parts = [attention[i].astype(bf16) for i in range(4)]
    packed[...] = jnp.concatenate(
        [part[:, :LANES] for part in parts] + [part[:, LANES:] for part in parts], axis=1
    )
    experts, share = router.shape
    groups = -(-(2 + experts) // 8)
    wide = jnp.concatenate([gains[...], router[...]], axis=0)
    wide = jnp.pad(wide, ((0, 8 * groups - 2 - experts), (0, 0)))
    row = jnp.concatenate([wide[8 * k : 8 * k + 8] for k in range(groups)], axis=1)
    row = jnp.pad(row, ((0, 0), (0, LANES - groups * share)))
    payload[...] = jnp.broadcast_to(row[None], payload.shape)


def prologue(inputs, attention, gains, router, device_count):
    quarter, width = inputs.shape
    tall = attention.shape[1]
    shapes = [
        shape_of((quarter, width), bf16),
        shape_of((quarter, 1), f32),
        shape_of((tall, 6 * LANES), bf16),
        shape_of((device_count, 8, LANES), f32),
    ]
    arrays = (inputs, attention, gains, router)
    return pl.pallas_call(
        prologue_kernel,
        in_specs=[whole(a.shape) for a in arrays],
        out_specs=[whole(s.shape) for s in shapes],
        out_shape=shapes,
        compiler_params=params(60),
        cost_estimate=LIGHT,
        name="prologue",
    )(*arrays)


def slots_kernel(capacity, info, routes, grads, place, match, valid, slots):
    quarter = routes.shape[0]
    experts = match.shape[1]
    row = lax.broadcasted_iota(jnp.int32, (quarter, 1), 0) + info[0] * quarter
    inside = jnp.where(row < info[1], 1.0, 0.0)
    valid[...] = inside
    column = lax.broadcasted_iota(jnp.int32, (quarter, experts), 1)
    named = jnp.where(routes[...] == column, 1.0, 0.0)
    match[...] = named
    at = lax.broadcasted_iota(jnp.int32, (quarter, quarter), 0)
    before = lax.broadcasted_iota(jnp.int32, (quarter, quarter), 1)
    lower = jnp.where(at >= before, 1.0, 0.0).astype(bf16)
    rank = jnp.sum(mm(lower, (named * inside).astype(bf16)) * named, axis=1, keepdims=True) - 1.0
    slot = jnp.where(inside > 0.0, routes[...].astype(f32) * capacity + rank, -1.0)
    slot = jnp.broadcast_to(slot, (quarter, LANES)).T[:1]
    number = lax.broadcasted_iota(jnp.int32, place.shape, 0).astype(f32)
    chosen = jnp.where(number == slot, 1.0, 0.0).astype(bf16)
    place[...] = chosen
    slots[...] = mm(chosen, grads[...].astype(bf16)).astype(bf16)


def slots_part(info, routes, grads, experts, capacity):
    quarter, width = grads.shape
    shapes = [
        shape_of((experts * capacity, quarter), bf16),
        shape_of((quarter, experts), f32),
        shape_of((quarter, 1), f32),
        shape_of((experts * capacity, width), bf16),
    ]
    return pl.pallas_call(
        lambda *refs: slots_kernel(capacity, *refs),
        in_specs=[scalars(), whole(routes.shape), whole(grads.shape)],
        out_specs=[whole(s.shape) for s in shapes],
        out_shape=shapes,
        compiler_params=params(60),
        cost_estimate=LIGHT,
        name="slots",
    )(info, routes, grads)


def project_kernel(quarter, blocks, count, share, info, came, x0, x1, x2, x3, *refs):
    shards, (small, column_gain, weight, out_weight, qkv, kaug, vt) = refs[:count], refs[count:]
    tall = shards[0].shape[0]
    width = weight.shape[0]
    for j, ref in enumerate(shards):
        start = pl.multiple_of((info[2] ^ j) * tall, tall) if count > 1 else 0
        weight[pl.ds(start, tall), :] = ref[...]
    out_weight[:LANES, :] = weight[:, 3 * LANES : 4 * LANES].T
    out_weight[LANES:, :] = weight[:, 5 * LANES :].T[DH:]
    groups = small.shape[0] // 8
    devices = came.shape[0]
    flat = came[...].reshape(devices * 8, LANES)
    lane = lax.broadcasted_iota(jnp.int32, (LANES, width), 0)
    column = lax.broadcasted_iota(jnp.int32, (LANES, width), 1)
    inside = lax.rem(column, share)
    owner = lax.broadcasted_iota(jnp.int32, (devices, 1, width), 2) - share * lax.broadcasted_iota(
        jnp.int32, (devices, 1, width), 0
    )
    owner = jnp.where((owner >= 0) & (owner < share), 1.0, 0.0)
    for k in range(groups):
        pick = jnp.where(lane == inside + k * share, 1.0, 0.0)
        spread = jnp.dot(flat, pick, precision=HIGHEST, preferred_element_type=f32)
        small[8 * k : 8 * k + 8, :] = jnp.sum(spread.reshape(devices, 8, width) * owner, axis=0)
    gain = small[:1, :]
    column_gain[...] = jnp.broadcast_to(gain, (LANES, width)).T[:, :1]
    for j, ref in enumerate((x0, x1, x2, x3)):
        start = pl.multiple_of((info[0] ^ j) * quarter, quarter)
        rows = pl.ds(start, quarter)
        scaled = (ref[...].astype(f32) * gain).astype(bf16)
        first = mm(scaled, weight[:, : 3 * LANES]).astype(bf16)
        second = mm(scaled, weight[:, 4 * LANES :]).astype(bf16)
        qkv[rows, : 3 * LANES] = first
        qkv[rows, 3 * LANES :] = second
        kaug[rows, :LANES] = first[:, LANES : 2 * LANES]
        lane = lax.broadcasted_iota(jnp.int32, (quarter, LANES), 1)
        row = lax.broadcasted_iota(jnp.int32, (quarter, LANES), 0) + start
        hidden = jnp.where((lane == 0) & (row >= info[1]), masked_score, 0.0)
        kaug[rows, LANES:] = jnp.where(lane < DH, hidden, second[:, :LANES].astype(f32)).astype(bf16)
        values = first[:, 2 * LANES :].T
        vt[0, :DH, rows] = values[:DH]
        vt[1, :DH, rows] = values[DH:]
        vt[2, :DH, rows] = second[:, LANES:].T[:DH]
    full_len = quarter * blocks
    tail = (lax.broadcasted_iota(jnp.int32, (16, full_len), 0) == 0).astype(f32).astype(bf16)
    for h in range(3):
        vt[h, DH:, :] = tail


def project(info, came, rows, shards, share, experts):
    quarter, width = rows[0].shape
    blocks = len(rows)
    full_len = quarter * blocks
    shapes = [
        shape_of((8 * -(-(2 + experts) // 8), width), f32),
        shape_of((width, 1), f32),
        shape_of((width, 6 * LANES), bf16),
        shape_of((3 * DH, width), bf16),
        shape_of((full_len, 5 * LANES), bf16),
        shape_of((full_len, 2 * LANES), bf16),
        shape_of((3, DH + 16, full_len), bf16),
    ]
    arrays = (came, *rows, *shards)
    return pl.pallas_call(
        lambda *refs: project_kernel(quarter, blocks, len(shards), share, *refs),
        in_specs=[scalars()] + [whole(a.shape) for a in arrays],
        out_specs=[whole(s.shape) for s in shapes],
        out_shape=shapes,
        compiler_params=params(60),
        cost_estimate=LIGHT,
        name="project",
    )(info, *arrays)


def attention_kernel(info, qkv, kaug, vt, context, chances, totals, *sent):
    quarter = context.shape[2]
    step = pl.program_id(0)
    rows = pl.ds(pl.multiple_of(step * quarter, quarter), quarter)
    q01 = (qkv[rows, :LANES].astype(f32) * score_scale).T.astype(bf16)
    q2 = (qkv[rows, 3 * LANES : 4 * LANES].astype(f32) * score_scale).T.astype(bf16)[:DH]
    ones = (lax.broadcasted_iota(jnp.int32, (DH, quarter), 0) == 0).astype(f32).astype(bf16)
    zeros = jnp.zeros((DH, quarter), bf16)
    queries = (
        jnp.concatenate([q01[:DH], zeros, ones, zeros], axis=0),
        jnp.concatenate([zeros, q01[DH:], ones, zeros], axis=0),
        jnp.concatenate([zeros, zeros, ones, q2], axis=0),
    )
    full_len = kaug.shape[0]
    all_scores = [mm(kaug[...], queries[h]) for h in range(3)]
    for h in range(3):
        scores = all_scores[h]
        top = jnp.max(jnp.max(scores.reshape(8, full_len // 8, quarter), axis=0), axis=0, keepdims=True)
        low = jnp.exp(scores - top).astype(bf16)
        chances[h] = low
        summed = mm(vt[h], low)
        part = 1.0 / summed[DH : DH + 1]
        totals[0, h : h + 1, :] = part
        context[0, h * DH : (h + 1) * DH, :] = (summed[:DH] * part).astype(bf16)
    for j, ref in enumerate(sent):

        @pl.when(step == info[0] ^ j)
        def _():
            ref[...] = context[0]


def attention_forward(info, qkv, kaug, vt, blocks):
    full_len = qkv.shape[0]
    quarter = full_len // blocks
    inner = 3 * DH
    return pl.pallas_call(
        attention_kernel,
        grid=(blocks,),
        in_specs=[scalars(), whole(qkv.shape), whole(kaug.shape), whole(vt.shape)],
        out_specs=[
            pl.BlockSpec((1, inner, quarter), lambda i: (i, 0, 0)),
            pl.BlockSpec((3, full_len, quarter), lambda i: (0, 0, i)),
            pl.BlockSpec((1, 3, quarter), lambda i: (i, 0, 0)),
        ]
        + [whole((inner, quarter))] * blocks,
        out_shape=[
            shape_of((blocks, inner, quarter), bf16),
            shape_of((3, full_len, full_len), bf16),
            shape_of((blocks, 3, quarter), f32),
        ]
        + [shape_of((inner, quarter), bf16)] * blocks,
        compiler_params=params(60),
        cost_estimate=LIGHT,
        name="attend",
    )(info, qkv, kaug, vt)


def turn_kernel(quarter, blocks, info, x0, x1, x2, x3, qkv, context, xt, kt, q2, cn):
    for j, ref in enumerate((x0, x1, x2, x3)):
        xt[info[0] ^ j] = ref[...].T
    for j in range(blocks):
        rows = slice(j * quarter, (j + 1) * quarter)
        third = qkv[rows, 3 * LANES : 4 * LANES].T
        kt[:LANES, rows] = qkv[rows, LANES : 2 * LANES].T
        kt[LANES:, rows] = third[DH:]
        zeros = jnp.zeros((DH, quarter), bf16)
        q2[rows, :] = jnp.concatenate([zeros, third[:DH]], axis=0).T
        cn[rows, :LANES] = context[j, :LANES, :].T
        cn[rows, LANES:] = jnp.concatenate([zeros, context[j, LANES:, :]], axis=0).T


def turn(info, rows, qkv, context):
    quarter, width = rows[0].shape
    blocks = len(rows)
    full_len = quarter * blocks
    shapes = [
        shape_of((blocks, width, quarter), bf16),
        shape_of((3 * DH, full_len), bf16),
        shape_of((full_len, LANES), bf16),
        shape_of((full_len, 2 * LANES), bf16),
    ]
    return pl.pallas_call(
        lambda *refs: turn_kernel(quarter, blocks, *refs),
        in_specs=[scalars()] + [whole((quarter, width))] * 4 + [whole(qkv.shape), whole(context.shape)],
        out_specs=[whole(s.shape) for s in shapes],
        out_shape=shapes,
        compiler_params=params(60),
        cost_estimate=LIGHT,
        name="turn",
    )(info, *rows, qkv, context)


def two_columns(column):
    high = column.astype(bf16).astype(f32)
    lane = lax.broadcasted_iota(jnp.int32, (column.shape[0], LANES), 1)
    return jnp.where(lane == 0, high, jnp.where(lane == 1, column - high, 0.0)).astype(bf16)


def middle_kernel(
    rows, c0, c1, c2, c3, w0, w1, w2, w3, small, place, match, valid, middle, root, chances, gate, slots
):
    gain, router = small[1:2, :], small[2 : 2 + match.shape[1], :]
    total = rows[...]
    for context, weight in zip((c0, c1, c2, c3), (w0, w1, w2, w3)):
        total = total + mm_tn(context[...], weight[...])
    middle[...] = total
    scale = norm_root(total)
    root[...] = scale
    hidden = total * scale * gain
    scores = mm_nt(hidden, router, HIGHEST)
    powers = jnp.exp(scores - jnp.max(scores, axis=-1, keepdims=True))
    share = powers / jnp.sum(powers, axis=-1, keepdims=True)
    chances[...] = share
    own = jnp.sum(share * match[...], axis=-1, keepdims=True)
    gate[...] = own
    width = rows.shape[1]
    slots[:, :width] = mm(place[...], hidden.astype(bf16)).astype(bf16)
    slots[:, width:] = mm(place[...], two_columns(own * valid[...])).astype(bf16)


def middle_part(rows, contexts, out_weights, small, place, match, valid):
    quarter, width = rows.shape
    experts = match.shape[1]
    shapes = [
        shape_of((quarter, width), f32),
        shape_of((quarter, 1), f32),
        shape_of((quarter, experts), f32),
        shape_of((quarter, 1), f32),
        shape_of((place.shape[0], width + LANES), bf16),
    ]
    arrays = (rows, *contexts, *out_weights, small, place, match, valid)
    return pl.pallas_call(
        middle_kernel,
        in_specs=[whole(a.shape) for a in arrays],
        out_specs=[whole(s.shape) for s in shapes],
        out_shape=shapes,
        compiler_params=params(60),
        cost_estimate=LIGHT,
        name="middle",
    )(*arrays)


def expert_kernel(rows, grads, *refs):
    count = (len(refs) - 4) // 2
    early_parts, late_parts = refs[:count], refs[count : 2 * count]
    out, back, held, arrived = refs[2 * count :]
    width = grads.shape[1]
    early = early_parts[0].shape[0]
    ends = (slice(0, early), slice(early, 2 * width))
    copies = [
        [
            pltpu.make_async_copy(ref, held.at[i, end, :], arrived.at[i, k])
            for k, (ref, end) in enumerate(zip(pair, ends))
        ]
        for i, pair in enumerate(zip(early_parts, late_parts))
    ]
    for pair in copies:
        for copy in pair:
            copy.start()
    out_total, back_total = None, None
    for i, pair in enumerate(copies):
        for copy in pair:
            copy.wait()
        inward, outward = held[i, :width, :], held[i, width:, :]
        grad = mm(grads[...], outward)
        active, slope = gelu_pair(mm(rows[:, :width], inward))
        part = mm_nt(active.astype(bf16), outward)
        back_part = mm_nt((grad * slope).astype(bf16), inward)
        out_total = part if i == 0 else out_total + part
        back_total = back_part if i == 0 else back_total + back_part
    result = out_total.astype(bf16)
    out[...] = result
    back[:, :width] = back_total.astype(bf16)
    match = jnp.sum(grads[...].astype(f32) * result.astype(f32), axis=-1, keepdims=True)
    back[:, width:] = two_columns(match)


def expert_part(rows, grads, early_parts, late_parts):
    slots, width = grads.shape
    hidden = early_parts[0].shape[1]
    count = len(early_parts)
    shapes = [shape_of((slots, width), bf16), shape_of((slots, width + LANES), bf16)]
    return pl.pallas_call(
        expert_kernel,
        in_specs=[whole(rows.shape), whole(grads.shape)] + [pl.BlockSpec(memory_space=pl.ANY)] * (2 * count),
        out_specs=[whole(s.shape) for s in shapes],
        out_shape=shapes,
        scratch_shapes=[pltpu.VMEM((count, 2 * width, hidden), bf16), pltpu.SemaphoreType.DMA((count, 2))],
        compiler_params=params(60),
        cost_estimate=LIGHT,
        name="experts",
    )(rows, grads, *early_parts, *late_parts)


def pack_small(small, cut):
    devices = cut.shape[0]
    rows, width = small.shape
    share = width // devices
    groups = rows // 8
    column = lax.broadcasted_iota(jnp.int32, (devices, 1, width), 2)
    owner = column - share * lax.broadcasted_iota(jnp.int32, (devices, 1, width), 0)
    owner = jnp.where((owner >= 0) & (owner < share), 1.0, 0.0)
    lane = lax.broadcasted_iota(jnp.int32, (width, LANES), 1)
    inside = lax.rem(lax.broadcasted_iota(jnp.int32, (width, LANES), 0), share)
    total = None
    for k in range(groups):
        pick = jnp.where(lane == inside + k * share, 1.0, 0.0)
        spread = (small[8 * k : 8 * k + 8, :][None] * owner).reshape(devices * 8, width)
        part = jnp.dot(spread, pick, precision=HIGHEST, preferred_element_type=f32)
        total = part if total is None else total + part
    cut[...] = total.reshape(devices, 8, LANES)


def pack_part(small, device_count):
    shape = shape_of((device_count, 8, LANES), f32)
    return pl.pallas_call(
        pack_small,
        in_specs=[whole(small.shape)],
        out_specs=whole(shape.shape),
        out_shape=shape,
        compiler_params=params(60),
        cost_estimate=LIGHT,
        name="pack",
    )(small)


def expert_grad_kernel(count, *refs):
    rows, grads = refs[:count], refs[count : 2 * count]
    near_in, near_out, out, square, weight, row_all, grad_all, inner_all, active_all, arrived = refs[2 * count :]
    early = near_in.shape[0]
    ends = (slice(0, early), slice(early, weight.shape[0]))
    copies = [
        pltpu.make_async_copy(ref, weight.at[end, :], arrived.at[i])
        for i, (ref, end) in enumerate(zip((near_in, near_out), ends))
    ]
    for copy in copies:
        copy.start()
    for copy in copies:
        copy.wait()
    slots, width = grads[0].shape
    for j in range(count):
        at = slice(j * slots, (j + 1) * slots)
        gate = rows[j][:, width : width + 1].astype(f32) + rows[j][:, width + 1 : width + 2].astype(f32)
        row_all[at, :] = rows[j][:, :width]
        grad_all[at, :] = (grads[j][...].astype(f32) * gate).astype(bf16)
        back = mm(grads[j][...], weight[width:, :])
        active, slope = gelu_pair(mm(rows[j][:, :width], weight[:width, :]))
        inner_all[at, :] = (back * slope * gate).astype(bf16)
        active_all[at, :] = active.astype(bf16)
    first = mm_tn(row_all[...], inner_all[...])
    out[0] = first
    second = mm_tn(grad_all[...], active_all[...])
    out[1] = second
    square[...] = jnp.sum(first * first + second * second, axis=0, keepdims=True)


def expert_gradient(rows, grads, near_in, near_out):
    count = len(rows)
    slots, width = grads[0].shape
    hidden = near_in.shape[1]
    arrays = (*rows, *grads)
    shapes = [
        shape_of((2, width, hidden), f32),
        shape_of((1, hidden), f32),
    ]
    return pl.pallas_call(
        lambda *refs: expert_grad_kernel(count, *refs),
        in_specs=[whole(a.shape) for a in arrays] + [pl.BlockSpec(memory_space=pl.ANY)] * 2,
        out_specs=[whole(s.shape) for s in shapes],
        out_shape=shapes,
        scratch_shapes=[pltpu.VMEM((2 * width, hidden), bf16)]
        + [pltpu.VMEM((count * slots, width), bf16)] * 2
        + [pltpu.VMEM((count * slots, hidden), bf16)] * 2
        + [pltpu.SemaphoreType.DMA((2,))],
        compiler_params=params(60),
        cost_estimate=LIGHT,
        name="expert_gradient",
    )(*arrays, near_in, near_out)


def return_kernel(
    back, place, middle, root, chances, gate, match, cotangent, small, w0, w1, w2, w3,
    grad, turned, small_grad, *parts,
):
    experts = match.shape[1]
    gain, router = small[1:2, :], small[2 : 2 + experts, :]
    width = middle.shape[1]
    came = mm_tn(place[...], back[...])
    gate_grad = came[:, width : width + 1] + came[:, width + 1 : width + 2]
    own = gate[...]
    score_grad = own * (match[...] - chances[...]) * gate_grad
    scaled = middle[...] * root[...]
    hidden = scaled * gain
    tall = small_grad.shape[0]
    small_grad[1 : 1 + experts, :] = mm_tn(score_grad, hidden, HIGHEST)
    small_grad[1 + experts :, :] = jnp.zeros((tall - 1 - experts, hidden.shape[1]), f32)
    second = own * came[:, :width] + jnp.dot(
        score_grad, router, precision=HIGHEST, preferred_element_type=f32
    )
    small_grad[:1, :] = jnp.sum(second * scaled, axis=0, keepdims=True)
    inner = second * gain
    centre = jnp.mean(inner * scaled, axis=-1, keepdims=True)
    total = cotangent[...] + root[...] * (inner - scaled * centre)
    grad[...] = total
    low = total.astype(bf16)
    turned[...] = low.T
    for ref, weight in zip(parts, (w0, w1, w2, w3)):
        ref[...] = mm_nt(weight[...], low).astype(bf16)


def return_part(back, place, middle, root, chances, gate, match, cotangent, small, out_weights):
    quarter, width = middle.shape
    experts = match.shape[1]
    inner = out_weights[0].shape[0]
    shapes = [
        shape_of((quarter, width), f32),
        shape_of((width, quarter), bf16),
        shape_of((8 * -(-(1 + experts) // 8), width), f32),
    ] + [shape_of((inner, quarter), bf16)] * len(out_weights)
    arrays = (back, place, middle, root, chances, gate, match, cotangent, small, *out_weights)
    return pl.pallas_call(
        return_kernel,
        in_specs=[whole(a.shape) for a in arrays],
        out_specs=[whole(s.shape) for s in shapes],
        out_shape=shapes,
        compiler_params=params(60),
        cost_estimate=LIGHT,
        name="returned",
    )(*arrays)


def attention_back_kernel(
    blocks, info, g0, g1, g2, g3, context, chances, totals, qkv, kt, q2, packed, grads, vaug, k01, k2, v01, v2
):
    step = pl.program_id(0)
    quarter = grads.shape[2]

    @pl.when(step == 0)
    def _():
        for j, ref in enumerate((g0, g1, g2, g3)):
            grads[info[0] ^ j] = ref[...]
        vaug[:, :LANES] = qkv[:, 2 * LANES : 3 * LANES]
        lane = lax.broadcasted_iota(jnp.int32, (vaug.shape[0], LANES), 1)
        ones = jnp.where(lane < DH + 2, 1.0, 0.0)
        vaug[:, LANES:] = jnp.where(lane < DH, qkv[:, 4 * LANES :].astype(f32), ones).astype(bf16)
        for ref in (k01, k2, v01, v2):
            ref[...] = jnp.zeros(ref.shape, f32)

    rows = pl.ds(pl.multiple_of(step * quarter, quarter), quarter)
    raw = grads[step].astype(f32)
    scale = totals[0]
    scaled = [raw[h * DH : (h + 1) * DH] * scale[h : h + 1] for h in range(3)]
    heads = jnp.concatenate(scaled, axis=0).astype(bf16)
    lane = lax.broadcasted_iota(jnp.int32, (quarter, LANES), 1)
    row = lax.broadcasted_iota(jnp.int32, (DH, quarter), 0)
    zeros = jnp.zeros((DH, quarter), bf16)
    q01 = qkv[rows, :LANES].astype(f32)
    g01 = heads[:LANES].T.astype(f32)
    third = jnp.concatenate([heads[LANES:], zeros], axis=0).T
    query_parts = []
    for h in range(3):
        part = heads[h * DH : (h + 1) * DH]
        centre = -jnp.sum(
            part.astype(f32) * context[0, h * DH : (h + 1) * DH, :].astype(f32), axis=0, keepdims=True
        )
        high = centre.astype(bf16).astype(f32)
        tail = jnp.where(row == 0, high, jnp.where(row == 1, centre - high, 0.0)).astype(bf16)
        pieces = [zeros, zeros, zeros, tail]
        pieces[h] = part
        chance_grad = mm(vaug[...], jnp.concatenate(pieces, axis=0))
        low = chances[h]
        score_grad = (low.astype(f32) * chance_grad).astype(bf16)
        query_parts.append(mm(kt[h * DH : (h + 1) * DH, :], score_grad) * score_scale)
        if h < 2:
            inside = (lane >= h * DH) & (lane < (h + 1) * DH)
            k01[...] += mm(score_grad, jnp.where(inside, q01, 0.0).astype(bf16))
            v01[...] += mm(low, jnp.where(inside, g01, 0.0).astype(bf16))
        else:
            k2[...] += mm(score_grad, q2[rows, :])
            v2[...] += mm(low, third)
    packed[rows, :LANES] = jnp.concatenate(query_parts[:2], axis=0).T.astype(bf16)
    packed[rows, 4 * LANES : 5 * LANES] = (
        jnp.concatenate([query_parts[2], jnp.zeros((DH, quarter), f32)], axis=0).T.astype(bf16)
    )

    @pl.when(step == blocks - 1)
    def _():
        packed[:, LANES : 2 * LANES] = (k01[...] * score_scale).astype(bf16)
        packed[:, 2 * LANES : 3 * LANES] = v01[...].astype(bf16)
        packed[:, 3 * LANES : 4 * LANES] = jnp.zeros(k01.shape, bf16)
        packed[:, 4 * LANES : 5 * LANES] = packed[:, 4 * LANES : 5 * LANES] + (k2[...] * score_scale).astype(bf16)
        packed[:, 5 * LANES :] = v2[...].astype(bf16)


def attention_backward(info, grads, context, chances, totals, qkv, kt, q2):
    blocks, inner, quarter = context.shape
    full_len = quarter * blocks
    block = pl.BlockSpec((1, inner, quarter), lambda i: (i, 0, 0))
    return pl.pallas_call(
        lambda *refs: attention_back_kernel(blocks, *refs),
        grid=(blocks,),
        in_specs=[
            scalars(),
            *[whole((inner, quarter))] * blocks,
            block,
            pl.BlockSpec((3, full_len, quarter), lambda i: (0, 0, i)),
            pl.BlockSpec((1, 3, quarter), lambda i: (i, 0, 0)),
            whole(qkv.shape),
            whole(kt.shape),
            whole(q2.shape),
        ],
        out_specs=whole((full_len, 6 * LANES)),
        out_shape=shape_of((full_len, 6 * LANES), bf16),
        scratch_shapes=[pltpu.VMEM(context.shape, bf16), pltpu.VMEM((full_len, 2 * LANES), bf16)]
        + [pltpu.VMEM((full_len, LANES), f32)] * 4,
        compiler_params=params(60),
        cost_estimate=LIGHT,
        name="attend_back",
    )(info, *grads, context, chances, totals, qkv, kt, q2)


def weight_grad_kernel(blocks, info, xt, packed, g0, g1, g2, g3, cn, weight, gain, out, gain_grad):
    quarter = xt.shape[2]
    total, outer = None, None
    for j, ref in enumerate((g0, g1, g2, g3)):
        rows = slice(j * quarter, (j + 1) * quarter)
        there = pl.ds(pl.multiple_of((info[0] ^ j) * quarter, quarter), quarter)
        part = mm(xt[j], packed[rows, :])
        own = mm(ref[...], cn[there, :])
        total = part if total is None else total + part
        outer = own if outer is None else outer + own
    gain_grad[...] = jnp.sum(total * weight[...].astype(f32), axis=1, keepdims=True)
    total = total * gain[...]
    out[:, : 3 * LANES] = total[:, : 3 * LANES].astype(bf16)
    out[:, 3 * LANES : 4 * LANES] = outer[:, :LANES].astype(bf16)
    out[:, 4 * LANES : 5 * LANES] = total[:, 4 * LANES : 5 * LANES].astype(bf16)
    out[:, 5 * LANES :] = (total[:, 5 * LANES :] + outer[:, LANES:]).astype(bf16)


def weight_gradient(info, xt, packed, grads, cn, weight, gain):
    blocks, width, quarter = xt.shape
    tall = 256
    full_len = quarter * blocks
    return pl.pallas_call(
        lambda *refs: weight_grad_kernel(blocks, *refs),
        grid=(width // tall,),
        in_specs=[
            scalars(),
            pl.BlockSpec((blocks, tall, quarter), lambda i: (0, i, 0)),
            whole(packed.shape),
            *[pl.BlockSpec((tall, quarter), lambda i: (i, 0))] * blocks,
            whole(cn.shape),
            pl.BlockSpec((tall, 6 * LANES), lambda i: (i, 0)),
            pl.BlockSpec((tall, 1), lambda i: (i, 0)),
        ],
        out_specs=[pl.BlockSpec((tall, 6 * LANES), lambda i: (i, 0)), pl.BlockSpec((tall, 1), lambda i: (i, 0))],
        out_shape=[shape_of((width, 6 * LANES), bf16), shape_of((width, 1), f32)],
        compiler_params=params(60),
        cost_estimate=LIGHT,
        name="weight_gradient",
    )(info, xt, packed, *grads, cn, weight, gain)


def input_grad_kernel(quarter, info, packed, weight, *parts):
    for j, ref in enumerate(parts):
        rows = pl.ds(pl.multiple_of((info[0] ^ j) * quarter, quarter), quarter)
        ref[...] = mm_nt(packed[rows, :], weight[...]).astype(bf16)


def input_gradient(info, packed, weight, blocks):
    quarter = packed.shape[0] // blocks
    shapes = [shape_of((quarter, weight.shape[0]), bf16)] * blocks
    return pl.pallas_call(
        lambda *refs: input_grad_kernel(quarter, *refs),
        in_specs=[scalars(), whole(packed.shape), whole(weight.shape)],
        out_specs=[whole(s.shape) for s in shapes],
        out_shape=shapes,
        compiler_params=params(60),
        cost_estimate=LIGHT,
        name="input_gradient",
    )(info, packed, weight)


def sums_kernel(came, squares, small, gain_grad, gradient, payload, small_sum):
    count = came.shape[0]
    total = came[0].astype(f32)
    for i in range(1, count):
        total = total + came[i].astype(f32)
    gradient[...] = total
    own = jnp.sum(small[...], axis=0)
    square = (
        jnp.sum(total * total, keepdims=True)
        + jnp.sum(squares[...], keepdims=True)
        + jnp.sum(own * own, keepdims=True)
    )
    small_sum[...] = own
    rows = gain_grad.shape[0]
    row = lax.broadcasted_iota(jnp.int32, (8, LANES), 0)
    gain = jnp.concatenate([gain_grad[...], jnp.zeros((8 - rows, LANES), f32)], axis=0)
    payload[...] = jnp.broadcast_to(jnp.where(row < rows, gain, square)[None], payload.shape)


def sums_part(came, squares, small, gain_grad, device_count):
    shapes = [
        shape_of(came.shape[1:], f32),
        shape_of((device_count, 8, LANES), f32),
        shape_of((8, LANES), f32),
    ]
    arrays = (came, squares, small, gain_grad)
    return pl.pallas_call(
        sums_kernel,
        in_specs=[whole(a.shape) for a in arrays],
        out_specs=[whole(s.shape) for s in shapes],
        out_shape=shapes,
        compiler_params=params(60),
        cost_estimate=LIGHT,
        name="sums",
    )(*arrays)


def adam_kernel(lanes, share, expert_rates, info, last, small_sum, *refs):
    held, outs, factor = refs[:14], refs[14:27], refs[27]
    dense, dense_grad, gains, router = held[:3], held[3], held[4:7], held[7:10]
    weight, first, second, gradient = held[10:14]
    norm_out, outs = outs[0], outs[1:]
    dense_out, gains_out, router_out, expert_out = outs[:3], outs[3:6], outs[6:9], outs[9:12]
    matrix, part = pl.program_id(0), pl.program_id(1)
    experts = router[0].shape[0]

    @pl.when((matrix == 0) & (part == 0))
    def _():
        total = jnp.sum(last[...], axis=0)
        row = lax.broadcasted_iota(jnp.int32, (8, LANES), 0)
        squares = jnp.sum(jnp.where(row < lanes, total * total, 0.0), keepdims=True)
        norm = jnp.sqrt(squares + total[7:8, :1])
        scale = jnp.minimum(1.0, clip_limit / (norm + norm_epsilon))
        norm_out[...] = norm
        factor[...] = jnp.broadcast_to(scale, (8, LANES))
        rates = (0.71 / math.sqrt(D), 0.71 / math.sqrt(D), 0.83 / math.sqrt(D), 0.79 / math.sqrt(H * DH))
        for i, rate in enumerate(rates):
            grad = jnp.concatenate(
                [
                    dense_grad[:, i * LANES : (i + 1) * LANES],
                    dense_grad[:, 4 * LANES + i * DH : 4 * LANES + (i + 1) * DH],
                ],
                axis=1,
            )
            result = adam_update(*[ref[i] for ref in dense], grad * scale, rate)
            for ref, value in zip(dense_out, result):
                ref[i] = value
        column = lax.broadcasted_iota(jnp.int32, (LANES, LANES), 1)
        place = lax.broadcasted_iota(jnp.int32, (LANES, LANES), 0) - info[3] * share
        own = jnp.zeros((8, LANES), f32)
        for i in range(lanes):
            pick = jnp.where((column == place + i * LANES) & (column < share), 1.0, 0.0)
            own = own + jnp.dot(
                jnp.broadcast_to(total[i : i + 1], (8, LANES)), pick, precision=HIGHEST, preferred_element_type=f32
            )
        groups = -(-(1 + experts) // 8)
        table = small_sum[...]
        table = jnp.concatenate([table[:, k * share : (k + 1) * share] for k in range(groups)], axis=0)
        grad = jnp.concatenate([own[:1, :share], table[:1]], axis=0)
        for ref, value in zip(gains_out, adam_update(*[ref[...] for ref in gains], grad * scale, 0.5)):
            ref[...] = value
        grad = table[1 : 1 + experts]
        result = adam_update(*[ref[...] for ref in router], grad * scale, 0.24 / math.sqrt(D))
        for ref, value in zip(router_out, result):
            ref[...] = value

    rate = jnp.where(matrix == 0, expert_rates[0], expert_rates[1])
    result = adam_update(weight[...], first[...], second[...], gradient[...] * factor[:1, :1], rate)
    for ref, value in zip(expert_out, result):
        ref[...] = value


def adam(info, last, small_sum, dense, dense_grad, gains, router, expert, expert_grad, rates):
    _, tall, wide = expert_grad.shape
    parts = 4
    block = pl.BlockSpec((1, tall // parts, wide), lambda i, j: (i, j, 0))
    small = [*dense, *gains, *router]
    shapes = [shape_of((1, 1), f32)] + [shape_of(a.shape, f32) for a in small]
    ins = (last, small_sum, *dense, dense_grad, *gains, *router)
    return pl.pallas_call(
        lambda *refs: adam_kernel(tall // LANES, gains[0].shape[1], rates, *refs),
        grid=(2, parts),
        in_specs=[scalars()] + [whole(a.shape) for a in ins] + [block] * 4,
        out_specs=[whole(a.shape) for a in shapes] + [block] * 3,
        out_shape=shapes + [shape_of(expert_grad.shape, f32)] * 3,
        scratch_shapes=[pltpu.VMEM((8, LANES), f32)],
        compiler_params=params(60),
        cost_estimate=LIGHT,
        name="adam",
    )(info, *ins, *expert, expert_grad)


def tie(*values):
    return lax.optimization_barrier(values)


def on_device(
    inputs,
    cotangent,
    lengths,
    routes,
    attention_weight,
    attention_mean,
    attention_square,
    expert_weight,
    expert_mean,
    expert_square,
    router_matrix,
    router_mean,
    router_square,
    norm_gains,
    gains_mean,
    gains_square,
):
    quarter, width = inputs.shape[1:]
    dp_count, tensor_count = lax.axis_size(DP), lax.axis_size(TENSOR)
    device_count = dp_count * tensor_count
    expert_count = router_matrix.shape[1]
    capacity = max(2, (5 * quarter + 4 * expert_count - 1) // (4 * expert_count))
    own_dp, own_tensor = lax.axis_index(DP), lax.axis_index(TENSOR)
    share = router_matrix.shape[0]
    rows, grad_rows, length = inputs[0], cotangent[0], lengths[0]
    info = jnp.stack([own_tensor, length, own_dp, lax.axis_index(EVERYONE)]).astype(jnp.int32)

    scaled_one, root_one, weight_own, payload = prologue(
        rows, attention_weight, norm_gains, router_matrix.T, device_count
    )
    block_two = swap(scaled_one, TENSOR, 2)
    expert_flat = expert_weight[0].reshape(2 * width, -1)
    early_own, late_own = expert_flat[:EARLY].astype(bf16), expert_flat[EARLY:].astype(bf16)
    place, match, valid_scale, grad_slots = slots_part(info, routes[0], grad_rows, expert_count, capacity)
    if dp_count == 8:
        w4, w2, w1 = [swap(weight_own, DP, mask) for mask in (4, 2, 1)]
        w4, w2, w1, payload, early_own = tie(w4, w2, w1, payload, early_own)
        early_far = swap(early_own, TENSOR, 2)
        w6, w5, w3 = swap(w4, DP, 2), swap(w4, DP, 1), swap(w2, DP, 1)
        w6, w5, w3, block_two, scaled_one, grad_slots = tie(w6, w5, w3, block_two, scaled_one, grad_slots)
        shards = [weight_own, w1, w2, w3, w4, w5, w6, swap(w6, DP, 1)]
    else:
        block_two, early_own, weight_own, grad_slots = tie(block_two, early_own, weight_own, grad_slots)
        early_far = swap(early_own, TENSOR, 2)
        shards = [lax.all_gather(weight_own, DP, axis=0, tiled=True)]
    row_blocks = [scaled_one, swap(scaled_one, TENSOR, 1), block_two, swap(block_two, TENSOR, 1)]
    small_came = lax.all_to_all(payload, EVERYONE, 0, 0, tiled=True)

    slot_count = expert_count * capacity

    def trade(values):
        blocks = values.reshape(expert_count, capacity, values.shape[1])
        return lax.all_to_all(blocks, DP, 0, 0, tiled=True).reshape(values.shape)

    expert_grads = trade(grad_slots)
    small, gain_column, weight, out_weight, qkv, keys_wide, values_turned = project(
        info, small_came, row_blocks, shards, share, expert_count
    )
    out_near, out_far = swap(out_weight, TENSOR, 1), swap(out_weight, TENSOR, 2)
    context, chances, totals, *sent = attention_forward(info, qkv, keys_wide, values_turned, tensor_count)
    expert_grads, early_far, out_near, out_far, *sent = tie(expert_grads, early_far, out_near, out_far, *sent)
    contexts = [sent[0]] + [swap(sent[j], TENSOR, j) for j in range(1, tensor_count)]
    out_weights = [out_weight, out_near, out_far, swap(out_far, TENSOR, 1)]
    late_own, *contexts = tie(late_own, *contexts)
    late_far = swap(late_own, TENSOR, 2)

    middle, root_two, shares, gate, slots = middle_part(
        rows, contexts, out_weights, small, place, match, valid_scale
    )
    qkv, slots, early_own, early_far, late_own = tie(qkv, slots, early_own, early_far, late_own)
    expert_rows = trade(slots)
    turned_rows, keys_turned, third_query, context_rows = turn(info, row_blocks, qkv, context)
    early_parts = [early_own, early_far, swap(early_own, TENSOR, 1), swap(early_far, TENSOR, 1)]
    late_parts = [late_own, late_far, swap(late_own, TENSOR, 1), swap(late_far, TENSOR, 1)]
    expert_rows, turned_rows = tie(expert_rows, turned_rows)
    expert_outs, expert_back = expert_part(expert_rows, expert_grads, early_parts, late_parts)
    expert_rows, expert_back = tie(expert_rows, expert_back)
    rows_all = gather_relative(expert_rows, TENSOR, [2, 1])
    expert_back, rows_all = tie(trade(expert_back), rows_all)

    middle_grad, middle_turned, small_grad, *parts = return_part(
        expert_back, place, middle, root_two, shares, gate, match, grad_rows, small, out_weights
    )
    expert_outs, middle_turned, *parts = tie(expert_outs, middle_turned, *parts)
    context_grads = [parts[0]] + [swap(parts[j], TENSOR, j) for j in range(1, tensor_count)]
    expert_outs = trade(expert_outs)
    middle_turned, expert_grads, *context_grads = tie(middle_turned, expert_grads, *context_grads)
    middle_near, middle_far = swap(middle_turned, TENSOR, 1), swap(middle_turned, TENSOR, 2)
    grads_near, grads_far = swap(expert_grads, TENSOR, 1), swap(expert_grads, TENSOR, 2)

    packed = attention_backward(info, context_grads, context, chances, totals, qkv, keys_turned, third_query)
    small_cut = pack_part(small_grad, device_count)
    packed, middle_far, grads_far, small_cut, expert_outs = tie(packed, middle_far, grads_far, small_cut, expert_outs)
    middle_all = [middle_turned, middle_near, middle_far, swap(middle_far, TENSOR, 1)]
    grads_all = [expert_grads, grads_near, grads_far, swap(grads_far, TENSOR, 1)]
    small_grads = lax.all_to_all(small_cut, EVERYONE, 0, 0, tiled=True)
    weight_grad, gain_one_grad = weight_gradient(
        info, turned_rows, packed, middle_all, context_rows, weight, gain_column
    )
    weight_grad, early_own, small_grads = tie(weight_grad, early_own, small_grads)
    weight_came = lax.all_to_all(weight_grad.reshape(dp_count, -1, width), DP, 0, 0, tiled=True)
    expert_grad, expert_squares = expert_gradient(rows_all, grads_all, early_own, late_own)
    expert_squares, packed = tie(expert_squares, packed)

    input_parts = input_gradient(info, packed, weight, tensor_count)
    first_half = input_parts[0].astype(f32) + swap(input_parts[1], TENSOR, 1).astype(f32)
    second_half = (input_parts[2].astype(f32) + swap(input_parts[3], TENSOR, 1).astype(f32)).astype(bf16)

    weight_came, second_half = tie(weight_came, second_half)
    second_came = swap(second_half, TENSOR, 2)
    dense_grad, last, small_sum = sums_part(
        weight_came, expert_squares, small_grads, gain_one_grad.reshape(-1, LANES), device_count
    )
    last, expert_outs, first_half = tie(last, expert_outs, first_half)
    last_all = lax.all_to_all(last, EVERYONE, 0, 0, tiled=True)
    input_grad = middle_grad + norm_backward(rows, root_one, small[:1], first_half + second_came.astype(f32))
    picked = mm_tn(place, expert_outs)
    branch = gate * valid_scale * picked
    block_output = middle + branch
    last_all, input_grad, block_output, branch = tie(last_all, input_grad, block_output, branch)

    rates = (0.4 * math.sqrt(expert_count / D), 1.38 * math.sqrt(expert_count / FF))
    norm, *updated = adam(
        info,
        last_all,
        small_sum,
        (attention_weight, attention_mean, attention_square),
        dense_grad,
        (norm_gains, gains_mean, gains_square),
        (router_matrix.T, router_mean.T, router_square.T),
        (expert_weight[0], expert_mean[0], expert_square[0]),
        expert_grad,
        rates,
    )
    attention_new, gains_new, router_new, expert_new = updated[:3], updated[3:6], updated[6:9], updated[9:]
    router_new = [part.T for part in router_new]
    grad_norm = norm.reshape(())
    return (
        block_output[None],
        input_grad[None],
        grad_norm,
        *attention_new,
        *[part[None] for part in expert_new],
        *router_new,
        *gains_new,
        branch[None],
    )


def solution(mesh):
    names = mesh.axis_names
    dp_count, tensor_count = mesh.shape[names[0]], mesh.shape[names[1]]
    cut = jax.sharding.Mesh(mesh.devices.reshape(dp_count // 2, 2, tensor_count // 2, 2), EVERYONE)
    rows = P(DP, TENSOR, None)
    attention = P(None, DP, TENSOR)
    expert = P(DP, None, None, TENSOR)
    router = P(EVERYONE, None)
    gains = P(None, EVERYONE)
    weights = (attention,) * 3 + (expert,) * 3 + (router,) * 3 + (gains,) * 3
    return jax.shard_map(
        on_device,
        mesh=cut,
        in_specs=(rows, rows, P(DP), rows) + weights,
        out_specs=(rows, rows, P()) + weights + (rows,),
        check_vma=False,
    )
```

```python
import math

import jax
import jax.numpy as jnp
from jax import lax
from jax.experimental import pallas as pl
from jax.experimental.pallas import tpu as pltpu
from jax.sharding import PartitionSpec as P

D = 768
H = 12
DH = 64
FF = 3072
STEP = 10

HIGHEST = lax.Precision.HIGHEST
norm_epsilon = 1e-06
beta_first = 0.9
beta_second = 0.999
adam_epsilon = 1e-08
decay_factor = 0.01
clip_limit = 1.0
masked_score = -1e30
score_scale = 1.0 / math.sqrt(DH)
bf16 = jnp.bfloat16
f32 = jnp.float32
MIB = 1 << 20
LANES = 128
EARLY = 1200


DP = ("dh", "dl")
TENSOR = ("th", "tl")
EVERYONE = DP + TENSOR


def swap(values, axis, mask):
    count = lax.axis_size(axis)
    return lax.ppermute(values, axis, [(i, i ^ mask) for i in range(count)])


def bits_of(count):
    return [1 << b for b in range(count.bit_length() - 1)]


def gather_relative(block, axis, order):
    held = {0: block}
    for mask in order:
        for j in list(held):
            held[j ^ mask] = swap(held[j], axis, mask)
    return [held[j] for j in range(len(held))]


def mm(a, b):
    return jnp.dot(a, b, preferred_element_type=f32)


def mm_nt(a, b, precision=None):
    return lax.dot_general(
        a, b, (((1,), (1,)), ((), ())), preferred_element_type=f32, precision=precision
    )


def mm_tn(a, b, precision=None):
    return lax.dot_general(
        a, b, (((0,), (0,)), ((), ())), preferred_element_type=f32, precision=precision
    )


def norm_root(values):
    return lax.rsqrt(jnp.mean(values * values, axis=-1, keepdims=True) + norm_epsilon)


def norm_backward(values, root, gain_row, grad):
    scaled = values * root
    inner = grad * gain_row
    centre = jnp.mean(inner * scaled, axis=-1, keepdims=True)
    return root * (inner - scaled * centre)


def gelu_pair(values):
    c = math.sqrt(2.0 / math.pi)
    square = values * values
    th = jnp.tanh(c * values * (1.0 + 0.044715 * square))
    half = 0.5 * (1.0 + th)
    slope = half + 0.5 * values * (1.0 - th * th) * c * (1.0 + 3.0 * 0.044715 * square)
    return values * half, slope


def adam_update(weight, moment_one, moment_two, gradient, step_rate):
    moment_one_next = beta_first * moment_one + (1.0 - beta_first) * gradient
    moment_two_next = beta_second * moment_two + (1.0 - beta_second) * gradient * gradient
    corrected_one = moment_one_next / (1.0 - beta_first**STEP)
    corrected_two = moment_two_next / (1.0 - beta_second**STEP)
    weight_next = weight - step_rate * (
        corrected_one / (jnp.sqrt(corrected_two) + adam_epsilon) + decay_factor * weight
    )
    return (weight_next, moment_one_next, moment_two_next)


def shape_of(shape, dtype):
    return jax.ShapeDtypeStruct(shape, dtype)


def whole(shape):
    return pl.BlockSpec(shape, lambda *_: (0,) * len(shape))


def scalars():
    return pl.BlockSpec(memory_space=pltpu.SMEM)


LIGHT = pl.CostEstimate(flops=1, bytes_accessed=1, transcendentals=0)


def params(limit):
    return pltpu.CompilerParams(vmem_limit_bytes=limit * MIB)


def prologue_kernel(inputs, attention, gains, router, scaled, root, packed, payload):
    values = inputs[...]
    scale = norm_root(values)
    root[...] = scale
    scaled[...] = (values * scale).astype(bf16)
    parts = [attention[i].astype(bf16) for i in range(4)]
    packed[...] = jnp.concatenate(
        [part[:, :LANES] for part in parts] + [part[:, LANES:] for part in parts], axis=1
    )
    experts, share = router.shape
    groups = -(-(2 + experts) // 8)
    wide = jnp.concatenate([gains[...], router[...]], axis=0)
    wide = jnp.pad(wide, ((0, 8 * groups - 2 - experts), (0, 0)))
    row = jnp.concatenate([wide[8 * k : 8 * k + 8] for k in range(groups)], axis=1)
    row = jnp.pad(row, ((0, 0), (0, LANES - groups * share)))
    payload[...] = jnp.broadcast_to(row[None], payload.shape)


def prologue(inputs, attention, gains, router, device_count):
    quarter, width = inputs.shape
    tall = attention.shape[1]
    shapes = [
        shape_of((quarter, width), bf16),
        shape_of((quarter, 1), f32),
        shape_of((tall, 6 * LANES), bf16),
        shape_of((device_count, 8, LANES), f32),
    ]
    arrays = (inputs, attention, gains, router)
    return pl.pallas_call(
        prologue_kernel,
        in_specs=[whole(a.shape) for a in arrays],
        out_specs=[whole(s.shape) for s in shapes],
        out_shape=shapes,
        compiler_params=params(60),
        cost_estimate=LIGHT,
        name="prologue",
    )(*arrays)


def slots_kernel(capacity, info, routes, grads, place, match, valid, slots):
    quarter = routes.shape[0]
    experts = match.shape[1]
    row = lax.broadcasted_iota(jnp.int32, (quarter, 1), 0) + info[0] * quarter
    inside = jnp.where(row < info[1], 1.0, 0.0)
    valid[...] = inside
    column = lax.broadcasted_iota(jnp.int32, (quarter, experts), 1)
    named = jnp.where(routes[...] == column, 1.0, 0.0)
    match[...] = named
    at = lax.broadcasted_iota(jnp.int32, (quarter, quarter), 0)
    before = lax.broadcasted_iota(jnp.int32, (quarter, quarter), 1)
    lower = jnp.where(at >= before, 1.0, 0.0).astype(bf16)
    rank = jnp.sum(mm(lower, (named * inside).astype(bf16)) * named, axis=1, keepdims=True) - 1.0
    slot = jnp.where(inside > 0.0, routes[...].astype(f32) * capacity + rank, -1.0)
    slot = jnp.broadcast_to(slot, (quarter, LANES)).T[:1]
    number = lax.broadcasted_iota(jnp.int32, place.shape, 0).astype(f32)
    chosen = jnp.where(number == slot, 1.0, 0.0).astype(bf16)
    place[...] = chosen
    slots[...] = mm(chosen, grads[...].astype(bf16)).astype(bf16)


def slots_part(info, routes, grads, experts, capacity):
    quarter, width = grads.shape
    shapes = [
        shape_of((experts * capacity, quarter), bf16),
        shape_of((quarter, experts), f32),
        shape_of((quarter, 1), f32),
        shape_of((experts * capacity, width), bf16),
    ]
    return pl.pallas_call(
        lambda *refs: slots_kernel(capacity, *refs),
        in_specs=[scalars(), whole(routes.shape), whole(grads.shape)],
        out_specs=[whole(s.shape) for s in shapes],
        out_shape=shapes,
        compiler_params=params(60),
        cost_estimate=LIGHT,
        name="slots",
    )(info, routes, grads)


def project_kernel(quarter, blocks, count, share, info, came, x0, x1, x2, x3, *refs):
    shards, (small, column_gain, weight, out_weight, qkv, kaug, vt) = refs[:count], refs[count:]
    tall = shards[0].shape[0]
    width = weight.shape[0]
    for j, ref in enumerate(shards):
        start = pl.multiple_of((info[2] ^ j) * tall, tall) if count > 1 else 0
        weight[pl.ds(start, tall), :] = ref[...]
    out_weight[:LANES, :] = weight[:, 3 * LANES : 4 * LANES].T
    out_weight[LANES:, :] = weight[:, 5 * LANES :].T[DH:]
    groups = small.shape[0] // 8
    devices = came.shape[0]
    flat = came[...].reshape(devices * 8, LANES)
    lane = lax.broadcasted_iota(jnp.int32, (LANES, width), 0)
    column = lax.broadcasted_iota(jnp.int32, (LANES, width), 1)
    inside = lax.rem(column, share)
    owner = lax.broadcasted_iota(jnp.int32, (devices, 1, width), 2) - share * lax.broadcasted_iota(
        jnp.int32, (devices, 1, width), 0
    )
    owner = jnp.where((owner >= 0) & (owner < share), 1.0, 0.0)
    for k in range(groups):
        pick = jnp.where(lane == inside + k * share, 1.0, 0.0)
        spread = jnp.dot(flat, pick, precision=HIGHEST, preferred_element_type=f32)
        small[8 * k : 8 * k + 8, :] = jnp.sum(spread.reshape(devices, 8, width) * owner, axis=0)
    gain = small[:1, :]
    column_gain[...] = jnp.broadcast_to(gain, (LANES, width)).T[:, :1]
    for j, ref in enumerate((x0, x1, x2, x3)):
        start = pl.multiple_of((info[0] ^ j) * quarter, quarter)
        rows = pl.ds(start, quarter)
        scaled = (ref[...].astype(f32) * gain).astype(bf16)
        first = mm(scaled, weight[:, : 3 * LANES]).astype(bf16)
        second = mm(scaled, weight[:, 4 * LANES :]).astype(bf16)
        qkv[rows, : 3 * LANES] = first
        qkv[rows, 3 * LANES :] = second
        kaug[rows, :LANES] = first[:, LANES : 2 * LANES]
        lane = lax.broadcasted_iota(jnp.int32, (quarter, LANES), 1)
        row = lax.broadcasted_iota(jnp.int32, (quarter, LANES), 0) + start
        hidden = jnp.where((lane == 0) & (row >= info[1]), masked_score, 0.0)
        kaug[rows, LANES:] = jnp.where(lane < DH, hidden, second[:, :LANES].astype(f32)).astype(bf16)
        values = first[:, 2 * LANES :].T
        vt[0, :DH, rows] = values[:DH]
        vt[1, :DH, rows] = values[DH:]
        vt[2, :DH, rows] = second[:, LANES:].T[:DH]
    full_len = quarter * blocks
    tail = (lax.broadcasted_iota(jnp.int32, (16, full_len), 0) == 0).astype(f32).astype(bf16)
    for h in range(3):
        vt[h, DH:, :] = tail


def project(info, came, rows, shards, share, experts):
    quarter, width = rows[0].shape
    blocks = len(rows)
    full_len = quarter * blocks
    shapes = [
        shape_of((8 * -(-(2 + experts) // 8), width), f32),
        shape_of((width, 1), f32),
        shape_of((width, 6 * LANES), bf16),
        shape_of((3 * DH, width), bf16),
        shape_of((full_len, 5 * LANES), bf16),
        shape_of((full_len, 2 * LANES), bf16),
        shape_of((3, DH + 16, full_len), bf16),
    ]
    arrays = (came, *rows, *shards)
    return pl.pallas_call(
        lambda *refs: project_kernel(quarter, blocks, len(shards), share, *refs),
        in_specs=[scalars()] + [whole(a.shape) for a in arrays],
        out_specs=[whole(s.shape) for s in shapes],
        out_shape=shapes,
        compiler_params=params(60),
        cost_estimate=LIGHT,
        name="project",
    )(info, *arrays)


def attention_kernel(info, qkv, kaug, vt, context, chances, totals, *sent):
    quarter = context.shape[2]
    step = pl.program_id(0)
    rows = pl.ds(pl.multiple_of(step * quarter, quarter), quarter)
    q01 = (qkv[rows, :LANES].astype(f32) * score_scale).T.astype(bf16)
    q2 = (qkv[rows, 3 * LANES : 4 * LANES].astype(f32) * score_scale).T.astype(bf16)[:DH]
    ones = (lax.broadcasted_iota(jnp.int32, (DH, quarter), 0) == 0).astype(f32).astype(bf16)
    zeros = jnp.zeros((DH, quarter), bf16)
    queries = (
        jnp.concatenate([q01[:DH], zeros, ones, zeros], axis=0),
        jnp.concatenate([zeros, q01[DH:], ones, zeros], axis=0),
        jnp.concatenate([zeros, zeros, ones, q2], axis=0),
    )
    full_len = kaug.shape[0]
    all_scores = [mm(kaug[...], queries[h]) for h in range(3)]
    for h in range(3):
        scores = all_scores[h]
        top = jnp.max(jnp.max(scores.reshape(8, full_len // 8, quarter), axis=0), axis=0, keepdims=True)
        low = jnp.exp(scores - top).astype(bf16)
        chances[h] = low
        summed = mm(vt[h], low)
        part = 1.0 / summed[DH : DH + 1]
        totals[0, h : h + 1, :] = part
        context[0, h * DH : (h + 1) * DH, :] = (summed[:DH] * part).astype(bf16)
    for j, ref in enumerate(sent):

        @pl.when(step == info[0] ^ j)
        def _():
            ref[...] = context[0]


def attention_forward(info, qkv, kaug, vt, blocks):
    full_len = qkv.shape[0]
    quarter = full_len // blocks
    inner = 3 * DH
    return pl.pallas_call(
        attention_kernel,
        grid=(blocks,),
        in_specs=[scalars(), whole(qkv.shape), whole(kaug.shape), whole(vt.shape)],
        out_specs=[
            pl.BlockSpec((1, inner, quarter), lambda i: (i, 0, 0)),
            pl.BlockSpec((3, full_len, quarter), lambda i: (0, 0, i)),
            pl.BlockSpec((1, 3, quarter), lambda i: (i, 0, 0)),
        ]
        + [whole((inner, quarter))] * blocks,
        out_shape=[
            shape_of((blocks, inner, quarter), bf16),
            shape_of((3, full_len, full_len), bf16),
            shape_of((blocks, 3, quarter), f32),
        ]
        + [shape_of((inner, quarter), bf16)] * blocks,
        compiler_params=params(60),
        cost_estimate=LIGHT,
        name="attend",
    )(info, qkv, kaug, vt)


def turn_kernel(quarter, blocks, info, x0, x1, x2, x3, qkv, context, xt, kt, q2, cn):
    for j, ref in enumerate((x0, x1, x2, x3)):
        xt[info[0] ^ j] = ref[...].T
    for j in range(blocks):
        rows = slice(j * quarter, (j + 1) * quarter)
        third = qkv[rows, 3 * LANES : 4 * LANES].T
        kt[:LANES, rows] = qkv[rows, LANES : 2 * LANES].T
        kt[LANES:, rows] = third[DH:]
        zeros = jnp.zeros((DH, quarter), bf16)
        q2[rows, :] = jnp.concatenate([zeros, third[:DH]], axis=0).T
        cn[rows, :LANES] = context[j, :LANES, :].T
        cn[rows, LANES:] = jnp.concatenate([zeros, context[j, LANES:, :]], axis=0).T


def turn(info, rows, qkv, context):
    quarter, width = rows[0].shape
    blocks = len(rows)
    full_len = quarter * blocks
    shapes = [
        shape_of((blocks, width, quarter), bf16),
        shape_of((3 * DH, full_len), bf16),
        shape_of((full_len, LANES), bf16),
        shape_of((full_len, 2 * LANES), bf16),
    ]
    return pl.pallas_call(
        lambda *refs: turn_kernel(quarter, blocks, *refs),
        in_specs=[scalars()] + [whole((quarter, width))] * 4 + [whole(qkv.shape), whole(context.shape)],
        out_specs=[whole(s.shape) for s in shapes],
        out_shape=shapes,
        compiler_params=params(60),
        cost_estimate=LIGHT,
        name="turn",
    )(info, *rows, qkv, context)


def two_columns(column):
    high = column.astype(bf16).astype(f32)
    lane = lax.broadcasted_iota(jnp.int32, (column.shape[0], LANES), 1)
    return jnp.where(lane == 0, high, jnp.where(lane == 1, column - high, 0.0)).astype(bf16)


def middle_kernel(
    rows, c0, c1, c2, c3, w0, w1, w2, w3, small, place, match, valid, middle, root, chances, gate, slots
):
    gain, router = small[1:2, :], small[2 : 2 + match.shape[1], :]
    total = rows[...]
    for context, weight in zip((c0, c1, c2, c3), (w0, w1, w2, w3)):
        total = total + mm_tn(context[...], weight[...])
    middle[...] = total
    scale = norm_root(total)
    root[...] = scale
    hidden = total * scale * gain
    scores = mm_nt(hidden, router, HIGHEST)
    powers = jnp.exp(scores - jnp.max(scores, axis=-1, keepdims=True))
    share = powers / jnp.sum(powers, axis=-1, keepdims=True)
    chances[...] = share
    own = jnp.sum(share * match[...], axis=-1, keepdims=True)
    gate[...] = own
    width = rows.shape[1]
    slots[:, :width] = mm(place[...], hidden.astype(bf16)).astype(bf16)
    slots[:, width:] = mm(place[...], two_columns(own * valid[...])).astype(bf16)


def middle_part(rows, contexts, out_weights, small, place, match, valid):
    quarter, width = rows.shape
    experts = match.shape[1]
    shapes = [
        shape_of((quarter, width), f32),
        shape_of((quarter, 1), f32),
        shape_of((quarter, experts), f32),
        shape_of((quarter, 1), f32),
        shape_of((place.shape[0], width + LANES), bf16),
    ]
    arrays = (rows, *contexts, *out_weights, small, place, match, valid)
    return pl.pallas_call(
        middle_kernel,
        in_specs=[whole(a.shape) for a in arrays],
        out_specs=[whole(s.shape) for s in shapes],
        out_shape=shapes,
        compiler_params=params(60),
        cost_estimate=LIGHT,
        name="middle",
    )(*arrays)


def expert_kernel(rows, grads, *refs):
    count = (len(refs) - 4) // 2
    early_parts, late_parts = refs[:count], refs[count : 2 * count]
    out, back, held, arrived = refs[2 * count :]
    width = grads.shape[1]
    early = early_parts[0].shape[0]
    ends = (slice(0, early), slice(early, 2 * width))
    copies = [
        [
            pltpu.make_async_copy(ref, held.at[i, end, :], arrived.at[i, k])
            for k, (ref, end) in enumerate(zip(pair, ends))
        ]
        for i, pair in enumerate(zip(early_parts, late_parts))
    ]
    for pair in copies:
        for copy in pair:
            copy.start()
    def products(i):
        for copy in copies[i]:
            copy.wait()
        return mm(rows[:, :width], held[i, :width, :]), mm(grads[...], held[i, width:, :])

    out_total, back_total = None, None
    ahead = products(0)
    for i in range(count):
        inner, grad = ahead
        if i + 1 < count:
            ahead = products(i + 1)
        active, slope = gelu_pair(inner)
        part = mm_nt(active.astype(bf16), held[i, width:, :])
        back_part = mm_nt((grad * slope).astype(bf16), held[i, :width, :])
        out_total = part if i == 0 else out_total + part
        back_total = back_part if i == 0 else back_total + back_part
    result = out_total.astype(bf16)
    out[...] = result
    back[:, :width] = back_total.astype(bf16)
    match = jnp.sum(grads[...].astype(f32) * result.astype(f32), axis=-1, keepdims=True)
    back[:, width:] = two_columns(match)


def expert_part(rows, grads, early_parts, late_parts):
    slots, width = grads.shape
    hidden = early_parts[0].shape[1]
    count = len(early_parts)
    shapes = [shape_of((slots, width), bf16), shape_of((slots, width + LANES), bf16)]
    return pl.pallas_call(
        expert_kernel,
        in_specs=[whole(rows.shape), whole(grads.shape)] + [pl.BlockSpec(memory_space=pl.ANY)] * (2 * count),
        out_specs=[whole(s.shape) for s in shapes],
        out_shape=shapes,
        scratch_shapes=[pltpu.VMEM((count, 2 * width, hidden), bf16), pltpu.SemaphoreType.DMA((count, 2))],
        compiler_params=params(60),
        cost_estimate=LIGHT,
        name="experts",
    )(rows, grads, *early_parts, *late_parts)


def expert_grad_kernel(count, *refs):
    rows, grads = refs[:count], refs[count : 2 * count]
    near_in, near_out, out, square, weight, row_all, grad_all, inner_all, active_all, arrived = refs[2 * count :]
    early = near_in.shape[0]
    ends = (slice(0, early), slice(early, weight.shape[0]))
    copies = [
        pltpu.make_async_copy(ref, weight.at[end, :], arrived.at[i])
        for i, (ref, end) in enumerate(zip((near_in, near_out), ends))
    ]
    for copy in copies:
        copy.start()
    for copy in copies:
        copy.wait()
    slots, width = grads[0].shape
    for j in range(count):
        at = slice(j * slots, (j + 1) * slots)
        gate = rows[j][:, width : width + 1].astype(f32) + rows[j][:, width + 1 : width + 2].astype(f32)
        row_all[at, :] = rows[j][:, :width]
        grad_all[at, :] = (grads[j][...].astype(f32) * gate).astype(bf16)
        back = mm(grads[j][...], weight[width:, :])
        active, slope = gelu_pair(mm(rows[j][:, :width], weight[:width, :]))
        inner_all[at, :] = (back * slope * gate).astype(bf16)
        active_all[at, :] = active.astype(bf16)
    first = mm_tn(row_all[...], inner_all[...])
    out[0] = first.astype(bf16)
    second = mm_tn(grad_all[...], active_all[...])
    out[1] = second.astype(bf16)
    square[...] = jnp.sum(first * first + second * second, axis=0, keepdims=True)


def expert_gradient(rows, grads, near_in, near_out):
    count = len(rows)
    slots, width = grads[0].shape
    hidden = near_in.shape[1]
    arrays = (*rows, *grads)
    shapes = [
        shape_of((2, width, hidden), bf16),
        shape_of((1, hidden), f32),
    ]
    return pl.pallas_call(
        lambda *refs: expert_grad_kernel(count, *refs),
        in_specs=[whole(a.shape) for a in arrays] + [pl.BlockSpec(memory_space=pl.ANY)] * 2,
        out_specs=[whole(s.shape) for s in shapes],
        out_shape=shapes,
        scratch_shapes=[pltpu.VMEM((2 * width, hidden), bf16)]
        + [pltpu.VMEM((count * slots, width), bf16)] * 2
        + [pltpu.VMEM((count * slots, hidden), bf16)] * 2
        + [pltpu.SemaphoreType.DMA((2,))],
        compiler_params=params(60),
        cost_estimate=LIGHT,
        name="expert_gradient",
    )(*arrays, near_in, near_out)


def pack_small(small, cut):
    devices = cut.shape[0]
    rows, width = small.shape
    share = width // devices
    groups = rows // 8
    column = lax.broadcasted_iota(jnp.int32, (devices, 1, width), 2)
    owner = column - share * lax.broadcasted_iota(jnp.int32, (devices, 1, width), 0)
    owner = jnp.where((owner >= 0) & (owner < share), 1.0, 0.0)
    lane = lax.broadcasted_iota(jnp.int32, (width, LANES), 1)
    inside = lax.rem(lax.broadcasted_iota(jnp.int32, (width, LANES), 0), share)
    total = None
    for k in range(groups):
        pick = jnp.where(lane == inside + k * share, 1.0, 0.0)
        spread = (small[8 * k : 8 * k + 8, :][None] * owner).reshape(devices * 8, width)
        part = jnp.dot(spread, pick, precision=HIGHEST, preferred_element_type=f32)
        total = part if total is None else total + part
    cut[...] = total.reshape(devices, 8, LANES)


def return_kernel(
    back, place, middle, root, chances, gate, match, cotangent, small, w0, w1, w2, w3,
    grad, turned, cut, p0, p1, p2, p3, small_grad,
):
    experts = match.shape[1]
    gain, router = small[1:2, :], small[2 : 2 + experts, :]
    width = middle.shape[1]
    came = mm_tn(place[...], back[...])
    gate_grad = came[:, width : width + 1] + came[:, width + 1 : width + 2]
    own = gate[...]
    score_grad = own * (match[...] - chances[...]) * gate_grad
    scaled = middle[...] * root[...]
    hidden = scaled * gain
    tall = small_grad.shape[0]
    small_grad[1 : 1 + experts, :] = mm_tn(score_grad, hidden, HIGHEST)
    small_grad[1 + experts :, :] = jnp.zeros((tall - 1 - experts, hidden.shape[1]), f32)
    second = own * came[:, :width] + jnp.dot(
        score_grad, router, precision=HIGHEST, preferred_element_type=f32
    )
    small_grad[:1, :] = jnp.sum(second * scaled, axis=0, keepdims=True)
    inner = second * gain
    centre = jnp.mean(inner * scaled, axis=-1, keepdims=True)
    total = cotangent[...] + root[...] * (inner - scaled * centre)
    grad[...] = total
    low = total.astype(bf16)
    turned[...] = low.T
    for ref, weight in zip((p0, p1, p2, p3), (w0, w1, w2, w3)):
        ref[...] = mm_nt(weight[...], low).astype(bf16)
    pack_small(small_grad, cut)


def return_part(back, place, middle, root, chances, gate, match, cotangent, small, out_weights, device_count):
    quarter, width = middle.shape
    experts = match.shape[1]
    inner = out_weights[0].shape[0]
    shapes = [
        shape_of((quarter, width), f32),
        shape_of((width, quarter), bf16),
        shape_of((device_count, 8, LANES), f32),
    ] + [shape_of((inner, quarter), bf16)] * len(out_weights)
    arrays = (back, place, middle, root, chances, gate, match, cotangent, small, *out_weights)
    return pl.pallas_call(
        return_kernel,
        in_specs=[whole(a.shape) for a in arrays],
        out_specs=[whole(s.shape) for s in shapes],
        out_shape=shapes,
        scratch_shapes=[pltpu.VMEM((8 * -(-(1 + experts) // 8), width), f32)],
        compiler_params=params(60),
        cost_estimate=LIGHT,
        name="returned",
    )(*arrays)


def attention_back_kernel(
    blocks, info, g0, g1, g2, g3, context, chances, totals, qkv, kt, q2, packed, grads, vaug, k01, k2, v01, v2
):
    step = pl.program_id(0)
    quarter = grads.shape[2]

    @pl.when(step == 0)
    def _():
        for j, ref in enumerate((g0, g1, g2, g3)):
            grads[info[0] ^ j] = ref[...]
        vaug[:, :LANES] = qkv[:, 2 * LANES : 3 * LANES]
        lane = lax.broadcasted_iota(jnp.int32, (vaug.shape[0], LANES), 1)
        ones = jnp.where(lane < DH + 2, 1.0, 0.0)
        vaug[:, LANES:] = jnp.where(lane < DH, qkv[:, 4 * LANES :].astype(f32), ones).astype(bf16)
        for ref in (k01, k2, v01, v2):
            ref[...] = jnp.zeros(ref.shape, f32)

    rows = pl.ds(pl.multiple_of(step * quarter, quarter), quarter)
    raw = grads[step].astype(f32)
    scale = totals[0]
    scaled = [raw[h * DH : (h + 1) * DH] * scale[h : h + 1] for h in range(3)]
    heads = jnp.concatenate(scaled, axis=0).astype(bf16)
    lane = lax.broadcasted_iota(jnp.int32, (quarter, LANES), 1)
    row = lax.broadcasted_iota(jnp.int32, (DH, quarter), 0)
    zeros = jnp.zeros((DH, quarter), bf16)
    q01 = qkv[rows, :LANES].astype(f32)
    g01 = heads[:LANES].T.astype(f32)
    third = jnp.concatenate([heads[LANES:], zeros], axis=0).T
    query_parts = []
    for h in range(3):
        part = heads[h * DH : (h + 1) * DH]
        centre = -jnp.sum(
            part.astype(f32) * context[0, h * DH : (h + 1) * DH, :].astype(f32), axis=0, keepdims=True
        )
        high = centre.astype(bf16).astype(f32)
        tail = jnp.where(row == 0, high, jnp.where(row == 1, centre - high, 0.0)).astype(bf16)
        pieces = [zeros, zeros, zeros, tail]
        pieces[h] = part
        chance_grad = mm(vaug[...], jnp.concatenate(pieces, axis=0))
        low = chances[h]
        score_grad = (low.astype(f32) * chance_grad).astype(bf16)
        query_parts.append(mm(kt[h * DH : (h + 1) * DH, :], score_grad) * score_scale)
        if h < 2:
            inside = (lane >= h * DH) & (lane < (h + 1) * DH)
            k01[...] += mm(score_grad, jnp.where(inside, q01, 0.0).astype(bf16))
            v01[...] += mm(low, jnp.where(inside, g01, 0.0).astype(bf16))
        else:
            k2[...] += mm(score_grad, q2[rows, :])
            v2[...] += mm(low, third)
    packed[rows, :LANES] = jnp.concatenate(query_parts[:2], axis=0).T.astype(bf16)
    packed[rows, 4 * LANES : 5 * LANES] = (
        jnp.concatenate([query_parts[2], jnp.zeros((DH, quarter), f32)], axis=0).T.astype(bf16)
    )

    @pl.when(step == blocks - 1)
    def _():
        packed[:, LANES : 2 * LANES] = (k01[...] * score_scale).astype(bf16)
        packed[:, 2 * LANES : 3 * LANES] = v01[...].astype(bf16)
        packed[:, 3 * LANES : 4 * LANES] = jnp.zeros(k01.shape, bf16)
        packed[:, 4 * LANES : 5 * LANES] = packed[:, 4 * LANES : 5 * LANES] + (k2[...] * score_scale).astype(bf16)
        packed[:, 5 * LANES :] = v2[...].astype(bf16)


def attention_backward(info, grads, context, chances, totals, qkv, kt, q2):
    blocks, inner, quarter = context.shape
    full_len = quarter * blocks
    block = pl.BlockSpec((1, inner, quarter), lambda i: (i, 0, 0))
    return pl.pallas_call(
        lambda *refs: attention_back_kernel(blocks, *refs),
        grid=(blocks,),
        in_specs=[
            scalars(),
            *[whole((inner, quarter))] * blocks,
            block,
            pl.BlockSpec((3, full_len, quarter), lambda i: (0, 0, i)),
            pl.BlockSpec((1, 3, quarter), lambda i: (i, 0, 0)),
            whole(qkv.shape),
            whole(kt.shape),
            whole(q2.shape),
        ],
        out_specs=whole((full_len, 6 * LANES)),
        out_shape=shape_of((full_len, 6 * LANES), bf16),
        scratch_shapes=[pltpu.VMEM(context.shape, bf16), pltpu.VMEM((full_len, 2 * LANES), bf16)]
        + [pltpu.VMEM((full_len, LANES), f32)] * 4,
        compiler_params=params(60),
        cost_estimate=LIGHT,
        name="attend_back",
    )(info, *grads, context, chances, totals, qkv, kt, q2)


def weight_grad_kernel(blocks, info, xt, packed, g0, g1, g2, g3, cn, weight, gain, out, gain_grad):
    quarter = xt.shape[2]
    total, outer = None, None
    for j, ref in enumerate((g0, g1, g2, g3)):
        rows = slice(j * quarter, (j + 1) * quarter)
        there = pl.ds(pl.multiple_of((info[0] ^ j) * quarter, quarter), quarter)
        part = mm(xt[j], packed[rows, :])
        own = mm(ref[...], cn[there, :])
        total = part if total is None else total + part
        outer = own if outer is None else outer + own
    gain_grad[...] = jnp.sum(total * weight[...].astype(f32), axis=1, keepdims=True)
    total = total * gain[...]
    out[:, : 3 * LANES] = total[:, : 3 * LANES].astype(bf16)
    out[:, 3 * LANES : 4 * LANES] = outer[:, :LANES].astype(bf16)
    out[:, 4 * LANES : 5 * LANES] = total[:, 4 * LANES : 5 * LANES].astype(bf16)
    out[:, 5 * LANES :] = (total[:, 5 * LANES :] + outer[:, LANES:]).astype(bf16)


def weight_gradient(info, xt, packed, grads, cn, weight, gain):
    blocks, width, quarter = xt.shape
    tall = 256
    full_len = quarter * blocks
    return pl.pallas_call(
        lambda *refs: weight_grad_kernel(blocks, *refs),
        grid=(width // tall,),
        in_specs=[
            scalars(),
            pl.BlockSpec((blocks, tall, quarter), lambda i: (0, i, 0)),
            whole(packed.shape),
            *[pl.BlockSpec((tall, quarter), lambda i: (i, 0))] * blocks,
            whole(cn.shape),
            pl.BlockSpec((tall, 6 * LANES), lambda i: (i, 0)),
            pl.BlockSpec((tall, 1), lambda i: (i, 0)),
        ],
        out_specs=[pl.BlockSpec((tall, 6 * LANES), lambda i: (i, 0)), pl.BlockSpec((tall, 1), lambda i: (i, 0))],
        out_shape=[shape_of((width, 6 * LANES), bf16), shape_of((width, 1), f32)],
        compiler_params=params(60),
        cost_estimate=LIGHT,
        name="weight_gradient",
    )(info, xt, packed, *grads, cn, weight, gain)


def input_grad_kernel(quarter, info, packed, weight, *parts):
    for j, ref in enumerate(parts):
        rows = pl.ds(pl.multiple_of((info[0] ^ j) * quarter, quarter), quarter)
        ref[...] = mm_nt(packed[rows, :], weight[...]).astype(bf16)


def input_gradient(info, packed, weight, blocks):
    quarter = packed.shape[0] // blocks
    shapes = [shape_of((quarter, weight.shape[0]), bf16)] * blocks
    return pl.pallas_call(
        lambda *refs: input_grad_kernel(quarter, *refs),
        in_specs=[scalars(), whole(packed.shape), whole(weight.shape)],
        out_specs=[whole(s.shape) for s in shapes],
        out_shape=shapes,
        compiler_params=params(60),
        cost_estimate=LIGHT,
        name="input_gradient",
    )(info, packed, weight)


def sums_kernel(came, squares, small, gain_grad, gradient, payload, small_sum):
    count = came.shape[0]
    total = came[0].astype(f32)
    for i in range(1, count):
        total = total + came[i].astype(f32)
    gradient[...] = total
    own = jnp.sum(small[...], axis=0)
    square = (
        jnp.sum(total * total, keepdims=True)
        + jnp.sum(squares[...], keepdims=True)
        + jnp.sum(own * own, keepdims=True)
    )
    small_sum[...] = own
    rows = gain_grad.shape[0]
    row = lax.broadcasted_iota(jnp.int32, (8, LANES), 0)
    gain = jnp.concatenate([gain_grad[...], jnp.zeros((8 - rows, LANES), f32)], axis=0)
    payload[...] = jnp.broadcast_to(jnp.where(row < rows, gain, square)[None], payload.shape)


def sums_part(came, squares, small, gain_grad, device_count):
    shapes = [
        shape_of(came.shape[1:], f32),
        shape_of((device_count, 8, LANES), f32),
        shape_of((8, LANES), f32),
    ]
    arrays = (came, squares, small, gain_grad)
    return pl.pallas_call(
        sums_kernel,
        in_specs=[whole(a.shape) for a in arrays],
        out_specs=[whole(s.shape) for s in shapes],
        out_shape=shapes,
        compiler_params=params(60),
        cost_estimate=LIGHT,
        name="sums",
    )(*arrays)


def adam_kernel(lanes, share, expert_rates, info, last, small_sum, *refs):
    held, outs, factor = refs[:14], refs[14:27], refs[27]
    dense, dense_grad, gains, router = held[:3], held[3], held[4:7], held[7:10]
    weight, first, second, gradient = held[10:14]
    norm_out, outs = outs[0], outs[1:]
    dense_out, gains_out, router_out, expert_out = outs[:3], outs[3:6], outs[6:9], outs[9:12]
    matrix, part = pl.program_id(0), pl.program_id(1)
    experts = router[0].shape[0]

    @pl.when((matrix == 0) & (part == 0))
    def _():
        total = jnp.sum(last[...], axis=0)
        row = lax.broadcasted_iota(jnp.int32, (8, LANES), 0)
        squares = jnp.sum(jnp.where(row < lanes, total * total, 0.0), keepdims=True)
        norm = jnp.sqrt(squares + total[7:8, :1])
        scale = jnp.minimum(1.0, clip_limit / (norm + norm_epsilon))
        norm_out[...] = norm
        factor[...] = jnp.broadcast_to(scale, (8, LANES))
        rates = (0.71 / math.sqrt(D), 0.71 / math.sqrt(D), 0.83 / math.sqrt(D), 0.79 / math.sqrt(H * DH))
        for i, rate in enumerate(rates):
            grad = jnp.concatenate(
                [
                    dense_grad[:, i * LANES : (i + 1) * LANES],
                    dense_grad[:, 4 * LANES + i * DH : 4 * LANES + (i + 1) * DH],
                ],
                axis=1,
            )
            result = adam_update(*[ref[i] for ref in dense], grad * scale, rate)
            for ref, value in zip(dense_out, result):
                ref[i] = value
        column = lax.broadcasted_iota(jnp.int32, (LANES, LANES), 1)
        place = lax.broadcasted_iota(jnp.int32, (LANES, LANES), 0) - info[3] * share
        own = jnp.zeros((8, LANES), f32)
        for i in range(lanes):
            pick = jnp.where((column == place + i * LANES) & (column < share), 1.0, 0.0)
            own = own + jnp.dot(
                jnp.broadcast_to(total[i : i + 1], (8, LANES)), pick, precision=HIGHEST, preferred_element_type=f32
            )
        groups = -(-(1 + experts) // 8)
        table = small_sum[...]
        table = jnp.concatenate([table[:, k * share : (k + 1) * share] for k in range(groups)], axis=0)
        grad = jnp.concatenate([own[:1, :share], table[:1]], axis=0)
        for ref, value in zip(gains_out, adam_update(*[ref[...] for ref in gains], grad * scale, 0.5)):
            ref[...] = value
        grad = table[1 : 1 + experts]
        result = adam_update(*[ref[...] for ref in router], grad * scale, 0.24 / math.sqrt(D))
        for ref, value in zip(router_out, result):
            ref[...] = value

    rate = jnp.where(matrix == 0, expert_rates[0], expert_rates[1])
    grad = gradient[...].astype(f32) * factor[:1, :1]
    result = adam_update(weight[...], first[...], second[...], grad, rate)
    for ref, value in zip(expert_out, result):
        ref[...] = value


def adam(info, last, small_sum, dense, dense_grad, gains, router, expert, expert_grad, rates):
    _, tall, wide = expert_grad.shape
    parts = 4
    block = pl.BlockSpec((1, tall // parts, wide), lambda i, j: (i, j, 0))
    small = [*dense, *gains, *router]
    shapes = [shape_of((1, 1), f32)] + [shape_of(a.shape, f32) for a in small]
    ins = (last, small_sum, *dense, dense_grad, *gains, *router)
    return pl.pallas_call(
        lambda *refs: adam_kernel(tall // LANES, gains[0].shape[1], rates, *refs),
        grid=(2, parts),
        in_specs=[scalars()] + [whole(a.shape) for a in ins] + [block] * 4,
        out_specs=[whole(a.shape) for a in shapes] + [block] * 3,
        out_shape=shapes + [shape_of(expert_grad.shape, f32)] * 3,
        scratch_shapes=[pltpu.VMEM((8, LANES), f32)],
        compiler_params=params(60),
        cost_estimate=LIGHT,
        name="adam",
    )(info, *ins, *expert, expert_grad)


def tie(*values):
    return lax.optimization_barrier(values)


def on_device(
    inputs,
    cotangent,
    lengths,
    routes,
    attention_weight,
    attention_mean,
    attention_square,
    expert_weight,
    expert_mean,
    expert_square,
    router_matrix,
    router_mean,
    router_square,
    norm_gains,
    gains_mean,
    gains_square,
):
    quarter, width = inputs.shape[1:]
    dp_count, tensor_count = lax.axis_size(DP), lax.axis_size(TENSOR)
    device_count = dp_count * tensor_count
    expert_count = router_matrix.shape[1]
    capacity = max(2, (5 * quarter + 4 * expert_count - 1) // (4 * expert_count))
    own_dp, own_tensor = lax.axis_index(DP), lax.axis_index(TENSOR)
    share = router_matrix.shape[0]
    rows, grad_rows, length = inputs[0], cotangent[0], lengths[0]
    info = jnp.stack([own_tensor, length, own_dp, lax.axis_index(EVERYONE)]).astype(jnp.int32)

    scaled_one, root_one, weight_own, payload = prologue(
        rows, attention_weight, norm_gains, router_matrix.T, device_count
    )
    block_two = swap(scaled_one, TENSOR, 2)
    expert_flat = expert_weight[0].reshape(2 * width, -1)
    early_own, late_own = expert_flat[:EARLY].astype(bf16), expert_flat[EARLY:].astype(bf16)
    place, match, valid_scale, grad_slots = slots_part(info, routes[0], grad_rows, expert_count, capacity)
    if dp_count == 8:
        w4, w2, w1 = [swap(weight_own, DP, mask) for mask in (4, 2, 1)]
        w4, w2, w1, payload, early_own, block_two = tie(w4, w2, w1, payload, early_own, block_two)
        early_far = swap(early_own, TENSOR, 2)
        w6, w5, w3 = swap(w4, DP, 2), swap(w4, DP, 1), swap(w2, DP, 1)
        w6, w5, w3, scaled_one, grad_slots = tie(w6, w5, w3, scaled_one, grad_slots)
        shards = [weight_own, w1, w2, w3, w4, w5, w6, swap(w6, DP, 1)]
    else:
        block_two, early_own, weight_own, grad_slots = tie(block_two, early_own, weight_own, grad_slots)
        early_far = swap(early_own, TENSOR, 2)
        shards = [lax.all_gather(weight_own, DP, axis=0, tiled=True)]
    row_blocks = [scaled_one, swap(scaled_one, TENSOR, 1), block_two, swap(block_two, TENSOR, 1)]
    small_came = lax.all_to_all(payload, EVERYONE, 0, 0, tiled=True)

    slot_count = expert_count * capacity

    def trade(values):
        blocks = values.reshape(expert_count, capacity, values.shape[1])
        return lax.all_to_all(blocks, DP, 0, 0, tiled=True).reshape(values.shape)

    expert_grads = trade(grad_slots)
    small, gain_column, weight, out_weight, qkv, keys_wide, values_turned = project(
        info, small_came, row_blocks, shards, share, expert_count
    )
    out_near, out_far = swap(out_weight, TENSOR, 1), swap(out_weight, TENSOR, 2)
    context, chances, totals, *sent = attention_forward(info, qkv, keys_wide, values_turned, tensor_count)
    expert_grads, early_far, out_near, out_far, *sent = tie(expert_grads, early_far, out_near, out_far, *sent)
    contexts = [sent[0]] + [swap(sent[j], TENSOR, j) for j in range(1, tensor_count)]
    out_weights = [out_weight, out_near, out_far, swap(out_far, TENSOR, 1)]
    late_own, *contexts = tie(late_own, *contexts)
    late_far = swap(late_own, TENSOR, 2)

    middle, root_two, shares, gate, slots = middle_part(
        rows, contexts, out_weights, small, place, match, valid_scale
    )
    qkv, slots, early_own, early_far, late_own = tie(qkv, slots, early_own, early_far, late_own)
    expert_rows = trade(slots)
    turned_rows, keys_turned, third_query, context_rows = turn(info, row_blocks, qkv, context)
    early_parts = [early_own, early_far, swap(early_own, TENSOR, 1), swap(early_far, TENSOR, 1)]
    late_parts = [late_own, late_far, swap(late_own, TENSOR, 1), swap(late_far, TENSOR, 1)]
    expert_rows, turned_rows = tie(expert_rows, turned_rows)
    expert_outs, expert_back = expert_part(expert_rows, expert_grads, early_parts, late_parts)
    expert_rows, expert_back = tie(expert_rows, expert_back)
    rows_all = gather_relative(expert_rows, TENSOR, [2, 1])
    expert_back, rows_all = tie(trade(expert_back), rows_all)

    middle_grad, middle_turned, small_cut, *parts = return_part(
        expert_back, place, middle, root_two, shares, gate, match, grad_rows, small, out_weights, device_count
    )
    context_grads = [parts[0]] + [swap(parts[j], TENSOR, j) for j in range(1, tensor_count)]
    expert_outs, context_grads[1] = tie(expert_outs, context_grads[1])
    expert_outs = trade(expert_outs)
    middle_turned, expert_grads, *context_grads = tie(middle_turned, expert_grads, *context_grads)
    middle_near, middle_far = swap(middle_turned, TENSOR, 1), swap(middle_turned, TENSOR, 2)
    grads_near, grads_far = swap(expert_grads, TENSOR, 1), swap(expert_grads, TENSOR, 2)

    packed = attention_backward(info, context_grads, context, chances, totals, qkv, keys_turned, third_query)
    packed, middle_far, grads_far, small_cut, expert_outs = tie(packed, middle_far, grads_far, small_cut, expert_outs)
    middle_all = [middle_turned, middle_near, middle_far, swap(middle_far, TENSOR, 1)]
    grads_all = [expert_grads, grads_near, grads_far, swap(grads_far, TENSOR, 1)]
    small_grads = lax.all_to_all(small_cut, EVERYONE, 0, 0, tiled=True)
    weight_grad, gain_one_grad = weight_gradient(
        info, turned_rows, packed, middle_all, context_rows, weight, gain_column
    )
    weight_grad, early_own, small_grads = tie(weight_grad, early_own, small_grads)
    weight_came = lax.all_to_all(weight_grad.reshape(dp_count, -1, width), DP, 0, 0, tiled=True)
    expert_grad, expert_squares = expert_gradient(rows_all, grads_all, early_own, late_own)
    expert_squares, packed = tie(expert_squares, packed)

    input_parts = input_gradient(info, packed, weight, tensor_count)
    first_half = input_parts[0].astype(f32) + swap(input_parts[1], TENSOR, 1).astype(f32)
    second_half = (input_parts[2].astype(f32) + swap(input_parts[3], TENSOR, 1).astype(f32)).astype(bf16)

    weight_came, second_half = tie(weight_came, second_half)
    second_came = swap(second_half, TENSOR, 2)
    dense_grad, last, small_sum = sums_part(
        weight_came, expert_squares, small_grads, gain_one_grad.reshape(-1, LANES), device_count
    )
    last, expert_outs, first_half = tie(last, expert_outs, first_half)
    last_all = lax.all_to_all(last, EVERYONE, 0, 0, tiled=True)
    input_grad = middle_grad + norm_backward(rows, root_one, small[:1], first_half + second_came.astype(f32))
    picked = mm_tn(place, expert_outs)
    branch = gate * valid_scale * picked
    block_output = middle + branch
    last_all, input_grad, block_output, branch = tie(last_all, input_grad, block_output, branch)

    rates = (0.4 * math.sqrt(expert_count / D), 1.38 * math.sqrt(expert_count / FF))
    norm, *updated = adam(
        info,
        last_all,
        small_sum,
        (attention_weight, attention_mean, attention_square),
        dense_grad,
        (norm_gains, gains_mean, gains_square),
        (router_matrix.T, router_mean.T, router_square.T),
        (expert_weight[0], expert_mean[0], expert_square[0]),
        expert_grad,
        rates,
    )
    attention_new, gains_new, router_new, expert_new = updated[:3], updated[3:6], updated[6:9], updated[9:]
    router_new = [part.T for part in router_new]
    grad_norm = norm.reshape(())
    return (
        block_output[None],
        input_grad[None],
        grad_norm,
        *attention_new,
        *[part[None] for part in expert_new],
        *router_new,
        *gains_new,
        branch[None],
    )


def solution(mesh):
    names = mesh.axis_names
    dp_count, tensor_count = mesh.shape[names[0]], mesh.shape[names[1]]
    cut = jax.sharding.Mesh(mesh.devices.reshape(dp_count // 2, 2, tensor_count // 2, 2), EVERYONE)
    rows = P(DP, TENSOR, None)
    attention = P(None, DP, TENSOR)
    expert = P(DP, None, None, TENSOR)
    router = P(EVERYONE, None)
    gains = P(None, EVERYONE)
    weights = (attention,) * 3 + (expert,) * 3 + (router,) * 3 + (gains,) * 3
    return jax.shard_map(
        on_device,
        mesh=cut,
        in_specs=(rows, rows, P(DP), rows) + weights,
        out_specs=(rows, rows, P()) + weights + (rows,),
        check_vma=False,
    )
```

```python
import math

import jax
import jax.numpy as jnp
from jax import lax
from jax.experimental import pallas as pl
from jax.experimental.pallas import tpu as pltpu
from jax.sharding import PartitionSpec as P

D = 768
H = 12
DH = 64
FF = 3072
STEP = 10

HIGHEST = lax.Precision.HIGHEST
norm_epsilon = 1e-06
beta_first = 0.9
beta_second = 0.999
adam_epsilon = 1e-08
decay_factor = 0.01
clip_limit = 1.0
masked_score = -1e30
score_scale = 1.0 / math.sqrt(DH)
bf16 = jnp.bfloat16
f32 = jnp.float32
MIB = 1 << 20
LANES = 128
EARLY = 1200


DP = ("dh", "dl")
TENSOR = ("th", "tl")
EVERYONE = DP + TENSOR


def swap(values, axis, mask):
    count = lax.axis_size(axis)
    return lax.ppermute(values, axis, [(i, i ^ mask) for i in range(count)])


def bits_of(count):
    return [1 << b for b in range(count.bit_length() - 1)]


def gather_relative(block, axis, order):
    held = {0: block}
    for mask in order:
        for j in list(held):
            held[j ^ mask] = swap(held[j], axis, mask)
    return [held[j] for j in range(len(held))]


def mm(a, b):
    return jnp.dot(a, b, preferred_element_type=f32)


def mm_nt(a, b, precision=None):
    return lax.dot_general(
        a, b, (((1,), (1,)), ((), ())), preferred_element_type=f32, precision=precision
    )


def mm_tn(a, b, precision=None):
    return lax.dot_general(
        a, b, (((0,), (0,)), ((), ())), preferred_element_type=f32, precision=precision
    )


def norm_root(values):
    return lax.rsqrt(jnp.mean(values * values, axis=-1, keepdims=True) + norm_epsilon)


def norm_backward(values, root, gain_row, grad):
    scaled = values * root
    inner = grad * gain_row
    centre = jnp.mean(inner * scaled, axis=-1, keepdims=True)
    return root * (inner - scaled * centre)


def gelu_pair(values):
    c = math.sqrt(2.0 / math.pi)
    square = values * values
    th = jnp.tanh(c * values * (1.0 + 0.044715 * square))
    half = 0.5 * (1.0 + th)
    slope = half + 0.5 * values * (1.0 - th * th) * c * (1.0 + 3.0 * 0.044715 * square)
    return values * half, slope


def adam_update(weight, moment_one, moment_two, gradient, step_rate):
    moment_one_next = beta_first * moment_one + (1.0 - beta_first) * gradient
    moment_two_next = beta_second * moment_two + (1.0 - beta_second) * gradient * gradient
    corrected_one = moment_one_next / (1.0 - beta_first**STEP)
    corrected_two = moment_two_next / (1.0 - beta_second**STEP)
    weight_next = weight - step_rate * (
        corrected_one / (jnp.sqrt(corrected_two) + adam_epsilon) + decay_factor * weight
    )
    return (weight_next, moment_one_next, moment_two_next)


def shape_of(shape, dtype):
    return jax.ShapeDtypeStruct(shape, dtype)


def whole(shape):
    return pl.BlockSpec(shape, lambda *_: (0,) * len(shape))


def scalars():
    return pl.BlockSpec(memory_space=pltpu.SMEM)


LIGHT = pl.CostEstimate(flops=1, bytes_accessed=1, transcendentals=0)


def params(limit):
    return pltpu.CompilerParams(vmem_limit_bytes=limit * MIB)


def split_dot(values, picks, parts):
    total, left = None, values
    for _ in range(parts):
        high = left.astype(bf16)
        part = mm(high, picks)
        total = part if total is None else total + part
        left = left - high.astype(f32)
    return total


def prologue_kernel(inputs, attention, gains, router, scaled, root, packed, payload):
    values = inputs[...]
    scale = norm_root(values)
    root[...] = scale
    scaled[...] = (values * scale).astype(bf16)
    parts = [attention[i].astype(bf16) for i in range(4)]
    packed[...] = jnp.concatenate(
        [part[:, :LANES] for part in parts] + [part[:, LANES:] for part in parts], axis=1
    )
    experts, share = router.shape
    groups = -(-(2 + experts) // 8)
    wide = jnp.concatenate([gains[...], router[...]], axis=0)
    wide = jnp.pad(wide, ((0, 8 * groups - 2 - experts), (0, 0)))
    row = jnp.concatenate([wide[8 * k : 8 * k + 8] for k in range(groups)], axis=1)
    row = jnp.pad(row, ((0, 0), (0, LANES - groups * share)))
    payload[...] = jnp.broadcast_to(row[None], payload.shape)


def prologue(inputs, attention, gains, router, device_count):
    quarter, width = inputs.shape
    tall = attention.shape[1]
    shapes = [
        shape_of((quarter, width), bf16),
        shape_of((quarter, 1), f32),
        shape_of((tall, 6 * LANES), bf16),
        shape_of((device_count, 8, LANES), f32),
    ]
    arrays = (inputs, attention, gains, router)
    return pl.pallas_call(
        prologue_kernel,
        in_specs=[whole(a.shape) for a in arrays],
        out_specs=[whole(s.shape) for s in shapes],
        out_shape=shapes,
        compiler_params=params(60),
        cost_estimate=LIGHT,
        name="prologue",
    )(*arrays)


def slots_kernel(capacity, info, routes, grads, place, match, valid, slots):
    quarter = routes.shape[0]
    experts = match.shape[1]
    row = lax.broadcasted_iota(jnp.int32, (quarter, 1), 0) + info[0] * quarter
    inside = jnp.where(row < info[1], 1.0, 0.0)
    valid[...] = inside
    column = lax.broadcasted_iota(jnp.int32, (quarter, experts), 1)
    named = jnp.where(routes[...] == column, 1.0, 0.0)
    match[...] = named
    at = lax.broadcasted_iota(jnp.int32, (quarter, quarter), 0)
    before = lax.broadcasted_iota(jnp.int32, (quarter, quarter), 1)
    lower = jnp.where(at >= before, 1.0, 0.0).astype(bf16)
    rank = jnp.sum(mm(lower, (named * inside).astype(bf16)) * named, axis=1, keepdims=True) - 1.0
    slot = jnp.where(inside > 0.0, routes[...].astype(f32) * capacity + rank, -1.0)
    slot = jnp.broadcast_to(slot, (quarter, LANES)).T[:1]
    number = lax.broadcasted_iota(jnp.int32, place.shape, 0).astype(f32)
    chosen = jnp.where(number == slot, 1.0, 0.0).astype(bf16)
    place[...] = chosen
    slots[...] = mm(chosen, grads[...].astype(bf16)).astype(bf16)


def slots_part(info, routes, grads, experts, capacity):
    quarter, width = grads.shape
    shapes = [
        shape_of((experts * capacity, quarter), bf16),
        shape_of((quarter, experts), f32),
        shape_of((quarter, 1), f32),
        shape_of((experts * capacity, width), bf16),
    ]
    return pl.pallas_call(
        lambda *refs: slots_kernel(capacity, *refs),
        in_specs=[scalars(), whole(routes.shape), whole(grads.shape)],
        out_specs=[whole(s.shape) for s in shapes],
        out_shape=shapes,
        compiler_params=params(60),
        cost_estimate=LIGHT,
        name="slots",
    )(info, routes, grads)


def project_kernel(quarter, blocks, count, share, info, came, x0, x1, x2, x3, *refs):
    shards, (small, column_gain, weight, out_weight, qkv, kaug, vt) = refs[:count], refs[count:]
    tall = shards[0].shape[0]
    width = weight.shape[0]
    for j, ref in enumerate(shards):
        start = pl.multiple_of((info[2] ^ j) * tall, tall) if count > 1 else 0
        weight[pl.ds(start, tall), :] = ref[...]
    out_weight[:LANES, :] = weight[:, 3 * LANES : 4 * LANES].T
    out_weight[LANES:, :] = weight[:, 5 * LANES :].T[DH:]
    groups = small.shape[0] // 8
    devices = came.shape[0]
    flat = came[...].reshape(devices * 8, LANES)
    lane = lax.broadcasted_iota(jnp.int32, (LANES, width), 0)
    column = lax.broadcasted_iota(jnp.int32, (LANES, width), 1)
    inside = lax.rem(column, share)
    owner = lax.broadcasted_iota(jnp.int32, (devices, 1, width), 2) - share * lax.broadcasted_iota(
        jnp.int32, (devices, 1, width), 0
    )
    owner = jnp.where((owner >= 0) & (owner < share), 1.0, 0.0)
    for k in range(groups):
        pick = jnp.where(lane == inside + k * share, 1.0, 0.0).astype(bf16)
        spread = split_dot(flat, pick, 3)
        small[8 * k : 8 * k + 8, :] = jnp.sum(spread.reshape(devices, 8, width) * owner, axis=0)
    gain = small[:1, :]
    column_gain[...] = jnp.broadcast_to(gain, (LANES, width)).T[:, :1]
    for j, ref in enumerate((x0, x1, x2, x3)):
        start = pl.multiple_of((info[0] ^ j) * quarter, quarter)
        rows = pl.ds(start, quarter)
        scaled = (ref[...].astype(f32) * gain).astype(bf16)
        first = mm(scaled, weight[:, : 3 * LANES]).astype(bf16)
        second = mm(scaled, weight[:, 4 * LANES :]).astype(bf16)
        qkv[rows, : 3 * LANES] = first
        qkv[rows, 3 * LANES :] = second
        kaug[rows, :LANES] = first[:, LANES : 2 * LANES]
        lane = lax.broadcasted_iota(jnp.int32, (quarter, LANES), 1)
        row = lax.broadcasted_iota(jnp.int32, (quarter, LANES), 0) + start
        hidden = jnp.where((lane == 0) & (row >= info[1]), masked_score, 0.0)
        kaug[rows, LANES:] = jnp.where(lane < DH, hidden, second[:, :LANES].astype(f32)).astype(bf16)
        values = first[:, 2 * LANES :].T
        vt[0, :DH, rows] = values[:DH]
        vt[1, :DH, rows] = values[DH:]
        vt[2, :DH, rows] = second[:, LANES:].T[:DH]
    full_len = quarter * blocks
    tail = (lax.broadcasted_iota(jnp.int32, (16, full_len), 0) == 0).astype(f32).astype(bf16)
    for h in range(3):
        vt[h, DH:, :] = tail


def project(info, came, rows, shards, share, experts):
    quarter, width = rows[0].shape
    blocks = len(rows)
    full_len = quarter * blocks
    shapes = [
        shape_of((8 * -(-(2 + experts) // 8), width), f32),
        shape_of((width, 1), f32),
        shape_of((width, 6 * LANES), bf16),
        shape_of((3 * DH, width), bf16),
        shape_of((full_len, 5 * LANES), bf16),
        shape_of((full_len, 2 * LANES), bf16),
        shape_of((3, DH + 16, full_len), bf16),
    ]
    arrays = (came, *rows, *shards)
    return pl.pallas_call(
        lambda *refs: project_kernel(quarter, blocks, len(shards), share, *refs),
        in_specs=[scalars()] + [whole(a.shape) for a in arrays],
        out_specs=[whole(s.shape) for s in shapes],
        out_shape=shapes,
        compiler_params=params(60),
        cost_estimate=LIGHT,
        name="project",
    )(info, *arrays)


def attention_kernel(info, qkv, kaug, vt, context, chances, totals, *sent):
    quarter = context.shape[2]
    step = pl.program_id(0)
    rows = pl.ds(pl.multiple_of(step * quarter, quarter), quarter)
    q01 = (qkv[rows, :LANES].astype(f32) * score_scale).T.astype(bf16)
    q2 = (qkv[rows, 3 * LANES : 4 * LANES].astype(f32) * score_scale).T.astype(bf16)[:DH]
    ones = (lax.broadcasted_iota(jnp.int32, (DH, quarter), 0) == 0).astype(f32).astype(bf16)
    zeros = jnp.zeros((DH, quarter), bf16)
    queries = (
        jnp.concatenate([q01[:DH], zeros, ones, zeros], axis=0),
        jnp.concatenate([zeros, q01[DH:], ones, zeros], axis=0),
        jnp.concatenate([zeros, zeros, ones, q2], axis=0),
    )
    full_len = kaug.shape[0]
    all_scores = [mm(kaug[...], queries[h]) for h in range(3)]
    for h in range(3):
        scores = all_scores[h]
        top = jnp.max(jnp.max(scores.reshape(8, full_len // 8, quarter), axis=0), axis=0, keepdims=True)
        low = jnp.exp(scores - top).astype(bf16)
        chances[h] = low
        summed = mm(vt[h], low)
        part = 1.0 / summed[DH : DH + 1]
        totals[0, h : h + 1, :] = part
        context[0, h * DH : (h + 1) * DH, :] = (summed[:DH] * part).astype(bf16)
    for j, ref in enumerate(sent):

        @pl.when(step == info[0] ^ j)
        def _():
            ref[...] = context[0]


def attention_forward(info, qkv, kaug, vt, blocks):
    full_len = qkv.shape[0]
    quarter = full_len // blocks
    inner = 3 * DH
    return pl.pallas_call(
        attention_kernel,
        grid=(blocks,),
        in_specs=[scalars(), whole(qkv.shape), whole(kaug.shape), whole(vt.shape)],
        out_specs=[
            pl.BlockSpec((1, inner, quarter), lambda i: (i, 0, 0)),
            pl.BlockSpec((3, full_len, quarter), lambda i: (0, 0, i)),
            pl.BlockSpec((1, 3, quarter), lambda i: (i, 0, 0)),
        ]
        + [whole((inner, quarter))] * blocks,
        out_shape=[
            shape_of((blocks, inner, quarter), bf16),
            shape_of((3, full_len, full_len), bf16),
            shape_of((blocks, 3, quarter), f32),
        ]
        + [shape_of((inner, quarter), bf16)] * blocks,
        compiler_params=params(60),
        cost_estimate=LIGHT,
        name="attend",
    )(info, qkv, kaug, vt)


def turn_kernel(quarter, blocks, info, x0, x1, x2, x3, qkv, context, xt, kt, q2, cn):
    for j, ref in enumerate((x0, x1, x2, x3)):
        xt[info[0] ^ j] = ref[...].T
    for j in range(blocks):
        rows = slice(j * quarter, (j + 1) * quarter)
        third = qkv[rows, 3 * LANES : 4 * LANES].T
        kt[:LANES, rows] = qkv[rows, LANES : 2 * LANES].T
        kt[LANES:, rows] = third[DH:]
        zeros = jnp.zeros((DH, quarter), bf16)
        q2[rows, :] = jnp.concatenate([zeros, third[:DH]], axis=0).T
        cn[rows, :LANES] = context[j, :LANES, :].T
        cn[rows, LANES:] = jnp.concatenate([zeros, context[j, LANES:, :]], axis=0).T


def turn(info, rows, qkv, context):
    quarter, width = rows[0].shape
    blocks = len(rows)
    full_len = quarter * blocks
    shapes = [
        shape_of((blocks, width, quarter), bf16),
        shape_of((3 * DH, full_len), bf16),
        shape_of((full_len, LANES), bf16),
        shape_of((full_len, 2 * LANES), bf16),
    ]
    return pl.pallas_call(
        lambda *refs: turn_kernel(quarter, blocks, *refs),
        in_specs=[scalars()] + [whole((quarter, width))] * 4 + [whole(qkv.shape), whole(context.shape)],
        out_specs=[whole(s.shape) for s in shapes],
        out_shape=shapes,
        compiler_params=params(60),
        cost_estimate=LIGHT,
        name="turn",
    )(info, *rows, qkv, context)


def two_columns(column):
    high = column.astype(bf16).astype(f32)
    lane = lax.broadcasted_iota(jnp.int32, (column.shape[0], LANES), 1)
    return jnp.where(lane == 0, high, jnp.where(lane == 1, column - high, 0.0)).astype(bf16)


def middle_kernel(
    rows, c0, c1, c2, c3, w0, w1, w2, w3, small, place, match, valid, middle, root, chances, gate, slots
):
    gain, router = small[1:2, :], small[2 : 2 + match.shape[1], :]
    total = rows[...]
    for context, weight in zip((c0, c1, c2, c3), (w0, w1, w2, w3)):
        total = total + mm_tn(context[...], weight[...])
    middle[...] = total
    scale = norm_root(total)
    root[...] = scale
    hidden = total * scale * gain
    scores = mm_nt(hidden, router, HIGHEST)
    powers = jnp.exp(scores - jnp.max(scores, axis=-1, keepdims=True))
    share = powers / jnp.sum(powers, axis=-1, keepdims=True)
    chances[...] = share
    own = jnp.sum(share * match[...], axis=-1, keepdims=True)
    gate[...] = own
    width = rows.shape[1]
    slots[:, :width] = mm(place[...], hidden.astype(bf16)).astype(bf16)
    slots[:, width:] = mm(place[...], two_columns(own * valid[...])).astype(bf16)


def middle_part(rows, contexts, out_weights, small, place, match, valid):
    quarter, width = rows.shape
    experts = match.shape[1]
    shapes = [
        shape_of((quarter, width), f32),
        shape_of((quarter, 1), f32),
        shape_of((quarter, experts), f32),
        shape_of((quarter, 1), f32),
        shape_of((place.shape[0], width + LANES), bf16),
    ]
    arrays = (rows, *contexts, *out_weights, small, place, match, valid)
    return pl.pallas_call(
        middle_kernel,
        in_specs=[whole(a.shape) for a in arrays],
        out_specs=[whole(s.shape) for s in shapes],
        out_shape=shapes,
        compiler_params=params(60),
        cost_estimate=LIGHT,
        name="middle",
    )(*arrays)


def expert_kernel(rows, grads, *refs):
    count = (len(refs) - 4) // 2
    early_parts, late_parts = refs[:count], refs[count : 2 * count]
    out, back, held, arrived = refs[2 * count :]
    width = grads.shape[1]
    early = early_parts[0].shape[0]
    ends = (slice(0, early), slice(early, 2 * width))
    copies = [
        [
            pltpu.make_async_copy(ref, held.at[i, end, :], arrived.at[i, k])
            for k, (ref, end) in enumerate(zip(pair, ends))
        ]
        for i, pair in enumerate(zip(early_parts, late_parts))
    ]
    for pair in copies:
        for copy in pair:
            copy.start()
    def products(i):
        for copy in copies[i]:
            copy.wait()
        return mm(rows[:, :width], held[i, :width, :]), mm(grads[...], held[i, width:, :])

    out_total, back_total = None, None
    ahead = products(0)
    for i in range(count):
        inner, grad = ahead
        if i + 1 < count:
            ahead = products(i + 1)
        active, slope = gelu_pair(inner)
        part = mm_nt(active.astype(bf16), held[i, width:, :])
        back_part = mm_nt((grad * slope).astype(bf16), held[i, :width, :])
        out_total = part if i == 0 else out_total + part
        back_total = back_part if i == 0 else back_total + back_part
    result = out_total.astype(bf16)
    out[...] = result
    back[:, :width] = back_total.astype(bf16)
    match = jnp.sum(grads[...].astype(f32) * result.astype(f32), axis=-1, keepdims=True)
    back[:, width:] = two_columns(match)


def expert_part(rows, grads, early_parts, late_parts):
    slots, width = grads.shape
    hidden = early_parts[0].shape[1]
    count = len(early_parts)
    shapes = [shape_of((slots, width), bf16), shape_of((slots, width + LANES), bf16)]
    return pl.pallas_call(
        expert_kernel,
        in_specs=[whole(rows.shape), whole(grads.shape)] + [pl.BlockSpec(memory_space=pl.ANY)] * (2 * count),
        out_specs=[whole(s.shape) for s in shapes],
        out_shape=shapes,
        scratch_shapes=[pltpu.VMEM((count, 2 * width, hidden), bf16), pltpu.SemaphoreType.DMA((count, 2))],
        compiler_params=params(60),
        cost_estimate=LIGHT,
        name="experts",
    )(rows, grads, *early_parts, *late_parts)


def expert_grad_kernel(count, *refs):
    rows, grads = refs[:count], refs[count : 2 * count]
    near_in, near_out, out, square, weight, row_all, grad_all, inner_all, active_all, arrived = refs[2 * count :]
    early = near_in.shape[0]
    ends = (slice(0, early), slice(early, weight.shape[0]))
    copies = [
        pltpu.make_async_copy(ref, weight.at[end, :], arrived.at[i])
        for i, (ref, end) in enumerate(zip((near_in, near_out), ends))
    ]
    for copy in copies:
        copy.start()
    for copy in copies:
        copy.wait()
    slots, width = grads[0].shape
    for j in range(count):
        at = slice(j * slots, (j + 1) * slots)
        gate = rows[j][:, width : width + 1].astype(f32) + rows[j][:, width + 1 : width + 2].astype(f32)
        row_all[at, :] = rows[j][:, :width]
        grad_all[at, :] = (grads[j][...].astype(f32) * gate).astype(bf16)
        back = mm(grads[j][...], weight[width:, :])
        active, slope = gelu_pair(mm(rows[j][:, :width], weight[:width, :]))
        inner_all[at, :] = (back * slope * gate).astype(bf16)
        active_all[at, :] = active.astype(bf16)
    first = mm_tn(row_all[...], inner_all[...])
    out[0] = first.astype(bf16)
    second = mm_tn(grad_all[...], active_all[...])
    out[1] = second.astype(bf16)
    square[...] = jnp.sum(first * first + second * second, axis=0, keepdims=True)


def expert_gradient(rows, grads, near_in, near_out):
    count = len(rows)
    slots, width = grads[0].shape
    hidden = near_in.shape[1]
    arrays = (*rows, *grads)
    shapes = [
        shape_of((2, width, hidden), bf16),
        shape_of((1, hidden), f32),
    ]
    return pl.pallas_call(
        lambda *refs: expert_grad_kernel(count, *refs),
        in_specs=[whole(a.shape) for a in arrays] + [pl.BlockSpec(memory_space=pl.ANY)] * 2,
        out_specs=[whole(s.shape) for s in shapes],
        out_shape=shapes,
        scratch_shapes=[pltpu.VMEM((2 * width, hidden), bf16)]
        + [pltpu.VMEM((count * slots, width), bf16)] * 2
        + [pltpu.VMEM((count * slots, hidden), bf16)] * 2
        + [pltpu.SemaphoreType.DMA((2,))],
        compiler_params=params(60),
        cost_estimate=LIGHT,
        name="expert_gradient",
    )(*arrays, near_in, near_out)


def pack_small(small, cut):
    devices = cut.shape[0]
    rows, width = small.shape
    share = width // devices
    groups = rows // 8
    column = lax.broadcasted_iota(jnp.int32, (devices, 1, width), 2)
    owner = column - share * lax.broadcasted_iota(jnp.int32, (devices, 1, width), 0)
    owner = jnp.where((owner >= 0) & (owner < share), 1.0, 0.0)
    lane = lax.broadcasted_iota(jnp.int32, (width, LANES), 1)
    inside = lax.rem(lax.broadcasted_iota(jnp.int32, (width, LANES), 0), share)
    total = None
    for k in range(groups):
        pick = jnp.where(lane == inside + k * share, 1.0, 0.0).astype(bf16)
        spread = (small[8 * k : 8 * k + 8, :][None] * owner).reshape(devices * 8, width)
        part = split_dot(spread, pick, 2)
        total = part if total is None else total + part
    cut[...] = total.reshape(devices, 8, LANES)


def return_kernel(
    back, place, middle, root, chances, gate, match, cotangent, small, w0, w1, w2, w3,
    grad, turned, cut, p0, p1, p2, p3, small_grad,
):
    experts = match.shape[1]
    gain, router = small[1:2, :], small[2 : 2 + experts, :]
    width = middle.shape[1]
    came = mm_tn(place[...], back[...])
    gate_grad = came[:, width : width + 1] + came[:, width + 1 : width + 2]
    own = gate[...]
    score_grad = own * (match[...] - chances[...]) * gate_grad
    scaled = middle[...] * root[...]
    hidden = scaled * gain
    tall = small_grad.shape[0]
    small_grad[1 : 1 + experts, :] = mm_tn(score_grad, hidden, HIGHEST)
    small_grad[1 + experts :, :] = jnp.zeros((tall - 1 - experts, hidden.shape[1]), f32)
    second = own * came[:, :width] + jnp.dot(
        score_grad, router, precision=HIGHEST, preferred_element_type=f32
    )
    small_grad[:1, :] = jnp.sum(second * scaled, axis=0, keepdims=True)
    inner = second * gain
    centre = jnp.mean(inner * scaled, axis=-1, keepdims=True)
    total = cotangent[...] + root[...] * (inner - scaled * centre)
    grad[...] = total
    low = total.astype(bf16)
    turned[...] = low.T
    for ref, weight in zip((p0, p1, p2, p3), (w0, w1, w2, w3)):
        ref[...] = mm_nt(weight[...], low).astype(bf16)
    pack_small(small_grad, cut)


def return_part(back, place, middle, root, chances, gate, match, cotangent, small, out_weights, device_count):
    quarter, width = middle.shape
    experts = match.shape[1]
    inner = out_weights[0].shape[0]
    shapes = [
        shape_of((quarter, width), f32),
        shape_of((width, quarter), bf16),
        shape_of((device_count, 8, LANES), f32),
    ] + [shape_of((inner, quarter), bf16)] * len(out_weights)
    arrays = (back, place, middle, root, chances, gate, match, cotangent, small, *out_weights)
    return pl.pallas_call(
        return_kernel,
        in_specs=[whole(a.shape) for a in arrays],
        out_specs=[whole(s.shape) for s in shapes],
        out_shape=shapes,
        scratch_shapes=[pltpu.VMEM((8 * -(-(1 + experts) // 8), width), f32)],
        compiler_params=params(60),
        cost_estimate=LIGHT,
        name="returned",
    )(*arrays)


def attention_back_kernel(
    blocks, info, g0, g1, g2, g3, context, chances, totals, qkv, kt, q2, packed, grads, vaug, k01, k2, v01, v2
):
    step = pl.program_id(0)
    quarter = grads.shape[2]

    @pl.when(step == 0)
    def _():
        for j, ref in enumerate((g0, g1, g2, g3)):
            grads[info[0] ^ j] = ref[...]
        vaug[:, :LANES] = qkv[:, 2 * LANES : 3 * LANES]
        lane = lax.broadcasted_iota(jnp.int32, (vaug.shape[0], LANES), 1)
        ones = jnp.where(lane < DH + 2, 1.0, 0.0)
        vaug[:, LANES:] = jnp.where(lane < DH, qkv[:, 4 * LANES :].astype(f32), ones).astype(bf16)
        for ref in (k01, k2, v01, v2):
            ref[...] = jnp.zeros(ref.shape, f32)

    rows = pl.ds(pl.multiple_of(step * quarter, quarter), quarter)
    raw = grads[step].astype(f32)
    scale = totals[0]
    scaled = [raw[h * DH : (h + 1) * DH] * scale[h : h + 1] for h in range(3)]
    heads = jnp.concatenate(scaled, axis=0).astype(bf16)
    lane = lax.broadcasted_iota(jnp.int32, (quarter, LANES), 1)
    row = lax.broadcasted_iota(jnp.int32, (DH, quarter), 0)
    zeros = jnp.zeros((DH, quarter), bf16)
    q01 = qkv[rows, :LANES].astype(f32)
    g01 = heads[:LANES].T.astype(f32)
    third = jnp.concatenate([heads[LANES:], zeros], axis=0).T
    query_parts = []
    for h in range(3):
        part = heads[h * DH : (h + 1) * DH]
        centre = -jnp.sum(
            part.astype(f32) * context[0, h * DH : (h + 1) * DH, :].astype(f32), axis=0, keepdims=True
        )
        high = centre.astype(bf16).astype(f32)
        tail = jnp.where(row == 0, high, jnp.where(row == 1, centre - high, 0.0)).astype(bf16)
        pieces = [zeros, zeros, zeros, tail]
        pieces[h] = part
        chance_grad = mm(vaug[...], jnp.concatenate(pieces, axis=0))
        low = chances[h]
        score_grad = (low.astype(f32) * chance_grad).astype(bf16)
        query_parts.append(mm(kt[h * DH : (h + 1) * DH, :], score_grad) * score_scale)
        if h < 2:
            inside = (lane >= h * DH) & (lane < (h + 1) * DH)
            k01[...] += mm(score_grad, jnp.where(inside, q01, 0.0).astype(bf16))
            v01[...] += mm(low, jnp.where(inside, g01, 0.0).astype(bf16))
        else:
            k2[...] += mm(score_grad, q2[rows, :])
            v2[...] += mm(low, third)
    packed[rows, :LANES] = jnp.concatenate(query_parts[:2], axis=0).T.astype(bf16)
    packed[rows, 4 * LANES : 5 * LANES] = (
        jnp.concatenate([query_parts[2], jnp.zeros((DH, quarter), f32)], axis=0).T.astype(bf16)
    )

    @pl.when(step == blocks - 1)
    def _():
        packed[:, LANES : 2 * LANES] = (k01[...] * score_scale).astype(bf16)
        packed[:, 2 * LANES : 3 * LANES] = v01[...].astype(bf16)
        packed[:, 3 * LANES : 4 * LANES] = jnp.zeros(k01.shape, bf16)
        packed[:, 4 * LANES : 5 * LANES] = packed[:, 4 * LANES : 5 * LANES] + (k2[...] * score_scale).astype(bf16)
        packed[:, 5 * LANES :] = v2[...].astype(bf16)


def attention_backward(info, grads, context, chances, totals, qkv, kt, q2):
    blocks, inner, quarter = context.shape
    full_len = quarter * blocks
    block = pl.BlockSpec((1, inner, quarter), lambda i: (i, 0, 0))
    return pl.pallas_call(
        lambda *refs: attention_back_kernel(blocks, *refs),
        grid=(blocks,),
        in_specs=[
            scalars(),
            *[whole((inner, quarter))] * blocks,
            block,
            pl.BlockSpec((3, full_len, quarter), lambda i: (0, 0, i)),
            pl.BlockSpec((1, 3, quarter), lambda i: (i, 0, 0)),
            whole(qkv.shape),
            whole(kt.shape),
            whole(q2.shape),
        ],
        out_specs=whole((full_len, 6 * LANES)),
        out_shape=shape_of((full_len, 6 * LANES), bf16),
        scratch_shapes=[pltpu.VMEM(context.shape, bf16), pltpu.VMEM((full_len, 2 * LANES), bf16)]
        + [pltpu.VMEM((full_len, LANES), f32)] * 4,
        compiler_params=params(60),
        cost_estimate=LIGHT,
        name="attend_back",
    )(info, *grads, context, chances, totals, qkv, kt, q2)


def weight_grad_kernel(blocks, info, xt, packed, g0, g1, g2, g3, cn, weight, gain, out, gain_grad):
    quarter = xt.shape[2]
    total, outer = None, None
    for j, ref in enumerate((g0, g1, g2, g3)):
        rows = slice(j * quarter, (j + 1) * quarter)
        there = pl.ds(pl.multiple_of((info[0] ^ j) * quarter, quarter), quarter)
        part = mm(xt[j], packed[rows, :])
        own = mm(ref[...], cn[there, :])
        total = part if total is None else total + part
        outer = own if outer is None else outer + own
    gain_grad[...] = jnp.sum(total * weight[...].astype(f32), axis=1, keepdims=True)
    total = total * gain[...]
    out[:, : 3 * LANES] = total[:, : 3 * LANES].astype(bf16)
    out[:, 3 * LANES : 4 * LANES] = outer[:, :LANES].astype(bf16)
    out[:, 4 * LANES : 5 * LANES] = total[:, 4 * LANES : 5 * LANES].astype(bf16)
    out[:, 5 * LANES :] = (total[:, 5 * LANES :] + outer[:, LANES:]).astype(bf16)


def weight_gradient(info, xt, packed, grads, cn, weight, gain):
    blocks, width, quarter = xt.shape
    tall = 256
    full_len = quarter * blocks
    return pl.pallas_call(
        lambda *refs: weight_grad_kernel(blocks, *refs),
        grid=(width // tall,),
        in_specs=[
            scalars(),
            pl.BlockSpec((blocks, tall, quarter), lambda i: (0, i, 0)),
            whole(packed.shape),
            *[pl.BlockSpec((tall, quarter), lambda i: (i, 0))] * blocks,
            whole(cn.shape),
            pl.BlockSpec((tall, 6 * LANES), lambda i: (i, 0)),
            pl.BlockSpec((tall, 1), lambda i: (i, 0)),
        ],
        out_specs=[pl.BlockSpec((tall, 6 * LANES), lambda i: (i, 0)), pl.BlockSpec((tall, 1), lambda i: (i, 0))],
        out_shape=[shape_of((width, 6 * LANES), bf16), shape_of((width, 1), f32)],
        compiler_params=params(60),
        cost_estimate=LIGHT,
        name="weight_gradient",
    )(info, xt, packed, *grads, cn, weight, gain)


def input_grad_kernel(quarter, info, packed, weight, *parts):
    for j, ref in enumerate(parts):
        rows = pl.ds(pl.multiple_of((info[0] ^ j) * quarter, quarter), quarter)
        ref[...] = mm_nt(packed[rows, :], weight[...]).astype(bf16)


def input_gradient(info, packed, weight, blocks):
    quarter = packed.shape[0] // blocks
    shapes = [shape_of((quarter, weight.shape[0]), bf16)] * blocks
    return pl.pallas_call(
        lambda *refs: input_grad_kernel(quarter, *refs),
        in_specs=[scalars(), whole(packed.shape), whole(weight.shape)],
        out_specs=[whole(s.shape) for s in shapes],
        out_shape=shapes,
        compiler_params=params(60),
        cost_estimate=LIGHT,
        name="input_gradient",
    )(info, packed, weight)


def sums_kernel(came, squares, small, gain_grad, gradient, payload, small_sum):
    count = came.shape[0]
    total = came[0].astype(f32)
    for i in range(1, count):
        total = total + came[i].astype(f32)
    gradient[...] = total
    own = jnp.sum(small[...], axis=0)
    square = (
        jnp.sum(total * total, keepdims=True)
        + jnp.sum(squares[...], keepdims=True)
        + jnp.sum(own * own, keepdims=True)
    )
    small_sum[...] = own
    rows = gain_grad.shape[0]
    row = lax.broadcasted_iota(jnp.int32, (8, LANES), 0)
    gain = jnp.concatenate([gain_grad[...], jnp.zeros((8 - rows, LANES), f32)], axis=0)
    payload[...] = jnp.broadcast_to(jnp.where(row < rows, gain, square)[None], payload.shape)


def sums_part(came, squares, small, gain_grad, device_count):
    shapes = [
        shape_of(came.shape[1:], f32),
        shape_of((device_count, 8, LANES), f32),
        shape_of((8, LANES), f32),
    ]
    arrays = (came, squares, small, gain_grad)
    return pl.pallas_call(
        sums_kernel,
        in_specs=[whole(a.shape) for a in arrays],
        out_specs=[whole(s.shape) for s in shapes],
        out_shape=shapes,
        compiler_params=params(60),
        cost_estimate=LIGHT,
        name="sums",
    )(*arrays)


def adam_kernel(lanes, share, expert_rates, info, last, small_sum, *refs):
    held, outs, factor = refs[:14], refs[14:27], refs[27]
    dense, dense_grad, gains, router = held[:3], held[3], held[4:7], held[7:10]
    weight, first, second, gradient = held[10:14]
    norm_out, outs = outs[0], outs[1:]
    dense_out, gains_out, router_out, expert_out = outs[:3], outs[3:6], outs[6:9], outs[9:12]
    matrix, part = pl.program_id(0), pl.program_id(1)
    experts = router[0].shape[0]

    @pl.when((matrix == 0) & (part == 0))
    def _():
        total = jnp.sum(last[...], axis=0)
        row = lax.broadcasted_iota(jnp.int32, (8, LANES), 0)
        squares = jnp.sum(jnp.where(row < lanes, total * total, 0.0), keepdims=True)
        norm = jnp.sqrt(squares + total[7:8, :1])
        scale = jnp.minimum(1.0, clip_limit / (norm + norm_epsilon))
        norm_out[...] = norm
        factor[...] = jnp.broadcast_to(scale, (8, LANES))
        rates = (0.71 / math.sqrt(D), 0.71 / math.sqrt(D), 0.83 / math.sqrt(D), 0.79 / math.sqrt(H * DH))
        for i, rate in enumerate(rates):
            grad = jnp.concatenate(
                [
                    dense_grad[:, i * LANES : (i + 1) * LANES],
                    dense_grad[:, 4 * LANES + i * DH : 4 * LANES + (i + 1) * DH],
                ],
                axis=1,
            )
            result = adam_update(*[ref[i] for ref in dense], grad * scale, rate)
            for ref, value in zip(dense_out, result):
                ref[i] = value
        column = lax.broadcasted_iota(jnp.int32, (LANES, LANES), 1)
        place = lax.broadcasted_iota(jnp.int32, (LANES, LANES), 0) - info[3] * share
        own = jnp.zeros((8, LANES), f32)
        for i in range(lanes):
            pick = jnp.where((column == place + i * LANES) & (column < share), 1.0, 0.0)
            own = own + jnp.dot(
                jnp.broadcast_to(total[i : i + 1], (8, LANES)), pick, precision=HIGHEST, preferred_element_type=f32
            )
        groups = -(-(1 + experts) // 8)
        table = small_sum[...]
        table = jnp.concatenate([table[:, k * share : (k + 1) * share] for k in range(groups)], axis=0)
        grad = jnp.concatenate([own[:1, :share], table[:1]], axis=0)
        for ref, value in zip(gains_out, adam_update(*[ref[...] for ref in gains], grad * scale, 0.5)):
            ref[...] = value
        grad = table[1 : 1 + experts]
        result = adam_update(*[ref[...] for ref in router], grad * scale, 0.24 / math.sqrt(D))
        for ref, value in zip(router_out, result):
            ref[...] = value

    rate = jnp.where(matrix == 0, expert_rates[0], expert_rates[1])
    grad = gradient[...].astype(f32) * factor[:1, :1]
    result = adam_update(weight[...], first[...], second[...], grad, rate)
    for ref, value in zip(expert_out, result):
        ref[...] = value


def adam(info, last, small_sum, dense, dense_grad, gains, router, expert, expert_grad, rates):
    _, tall, wide = expert_grad.shape
    parts = 4
    block = pl.BlockSpec((1, tall // parts, wide), lambda i, j: (i, j, 0))
    small = [*dense, *gains, *router]
    shapes = [shape_of((1, 1), f32)] + [shape_of(a.shape, f32) for a in small]
    ins = (last, small_sum, *dense, dense_grad, *gains, *router)
    return pl.pallas_call(
        lambda *refs: adam_kernel(tall // LANES, gains[0].shape[1], rates, *refs),
        grid=(2, parts),
        in_specs=[scalars()] + [whole(a.shape) for a in ins] + [block] * 4,
        out_specs=[whole(a.shape) for a in shapes] + [block] * 3,
        out_shape=shapes + [shape_of(expert_grad.shape, f32)] * 3,
        scratch_shapes=[pltpu.VMEM((8, LANES), f32)],
        compiler_params=params(60),
        cost_estimate=LIGHT,
        name="adam",
    )(info, *ins, *expert, expert_grad)


def tie(*values):
    return lax.optimization_barrier(values)


def on_device(
    inputs,
    cotangent,
    lengths,
    routes,
    attention_weight,
    attention_mean,
    attention_square,
    expert_weight,
    expert_mean,
    expert_square,
    router_matrix,
    router_mean,
    router_square,
    norm_gains,
    gains_mean,
    gains_square,
):
    quarter, width = inputs.shape[1:]
    dp_count, tensor_count = lax.axis_size(DP), lax.axis_size(TENSOR)
    device_count = dp_count * tensor_count
    expert_count = router_matrix.shape[1]
    capacity = max(2, (5 * quarter + 4 * expert_count - 1) // (4 * expert_count))
    own_dp, own_tensor = lax.axis_index(DP), lax.axis_index(TENSOR)
    share = router_matrix.shape[0]
    rows, grad_rows, length = inputs[0], cotangent[0], lengths[0]
    info = jnp.stack([own_tensor, length, own_dp, lax.axis_index(EVERYONE)]).astype(jnp.int32)

    scaled_one, root_one, weight_own, payload = prologue(
        rows, attention_weight, norm_gains, router_matrix.T, device_count
    )
    block_two = swap(scaled_one, TENSOR, 2)
    small_came = lax.all_to_all(payload, EVERYONE, 0, 0, tiled=True)
    expert_flat = expert_weight[0].reshape(2 * width, -1)
    early_own, late_own = expert_flat[:EARLY].astype(bf16), expert_flat[EARLY:].astype(bf16)
    place, match, valid_scale, grad_slots = slots_part(info, routes[0], grad_rows, expert_count, capacity)
    if dp_count == 8:
        w4, w2, w1 = [swap(weight_own, DP, mask) for mask in (4, 2, 1)]
        w4, w2, w1, small_came, block_two, early_own = tie(w4, w2, w1, small_came, block_two, early_own)
        w6, w5, w3 = swap(w4, DP, 2), swap(w4, DP, 1), swap(w2, DP, 1)
        w6, w5, w3, scaled_one, grad_slots = tie(w6, w5, w3, scaled_one, grad_slots)
        shards = [weight_own, w1, w2, w3, w4, w5, w6, swap(w6, DP, 1)]
    else:
        weight_own, grad_slots, small_came, block_two, early_own = tie(
            weight_own, grad_slots, small_came, block_two, early_own
        )
        shards = [lax.all_gather(weight_own, DP, axis=0, tiled=True)]
    early_far = swap(early_own, TENSOR, 2)
    row_blocks = [scaled_one, swap(scaled_one, TENSOR, 1), block_two, swap(block_two, TENSOR, 1)]

    slot_count = expert_count * capacity

    def trade(values):
        blocks = values.reshape(expert_count, capacity, values.shape[1])
        return lax.all_to_all(blocks, DP, 0, 0, tiled=True).reshape(values.shape)

    expert_grads = trade(grad_slots)
    small, gain_column, weight, out_weight, qkv, keys_wide, values_turned = project(
        info, small_came, row_blocks, shards, share, expert_count
    )
    out_near, out_far = swap(out_weight, TENSOR, 1), swap(out_weight, TENSOR, 2)
    context, chances, totals, *sent = attention_forward(info, qkv, keys_wide, values_turned, tensor_count)
    expert_grads, early_far, out_near, out_far, *sent = tie(expert_grads, early_far, out_near, out_far, *sent)
    contexts = [sent[0]] + [swap(sent[j], TENSOR, j) for j in range(1, tensor_count)]
    out_weights = [out_weight, out_near, out_far, swap(out_far, TENSOR, 1)]
    late_own, *contexts = tie(late_own, *contexts)
    late_far = swap(late_own, TENSOR, 2)

    middle, root_two, shares, gate, slots = middle_part(
        rows, contexts, out_weights, small, place, match, valid_scale
    )
    qkv, slots, early_own, early_far, late_own = tie(qkv, slots, early_own, early_far, late_own)
    expert_rows = trade(slots)
    turned_rows, keys_turned, third_query, context_rows = turn(info, row_blocks, qkv, context)
    early_parts = [early_own, early_far, swap(early_own, TENSOR, 1), swap(early_far, TENSOR, 1)]
    late_parts = [late_own, late_far, swap(late_own, TENSOR, 1), swap(late_far, TENSOR, 1)]
    expert_rows, turned_rows = tie(expert_rows, turned_rows)
    expert_outs, expert_back = expert_part(expert_rows, expert_grads, early_parts, late_parts)
    expert_rows, expert_back = tie(expert_rows, expert_back)
    rows_near, rows_far = swap(expert_rows, TENSOR, 1), swap(expert_rows, TENSOR, 2)
    rows_far, expert_grads = tie(rows_far, expert_grads)
    rows_all = [expert_rows, rows_near, rows_far, swap(rows_far, TENSOR, 1)]
    grads_near, grads_far = swap(expert_grads, TENSOR, 1), swap(expert_grads, TENSOR, 2)
    expert_back, rows_all = tie(trade(expert_back), rows_all)

    middle_grad, middle_turned, small_cut, *parts = return_part(
        expert_back, place, middle, root_two, shares, gate, match, grad_rows, small, out_weights, device_count
    )
    expert_outs, middle_turned, *parts = tie(expert_outs, middle_turned, *parts)
    context_grads = [parts[0]] + [swap(parts[j], TENSOR, j) for j in range(1, tensor_count)]
    expert_outs = trade(expert_outs)
    middle_turned, *context_grads = tie(middle_turned, *context_grads)
    middle_near, middle_far = swap(middle_turned, TENSOR, 1), swap(middle_turned, TENSOR, 2)

    packed = attention_backward(info, context_grads, context, chances, totals, qkv, keys_turned, third_query)
    packed, middle_far, grads_far, small_cut, expert_outs = tie(packed, middle_far, grads_far, small_cut, expert_outs)
    middle_all = [middle_turned, middle_near, middle_far, swap(middle_far, TENSOR, 1)]
    grads_all = [expert_grads, grads_near, grads_far, swap(grads_far, TENSOR, 1)]
    small_grads = lax.all_to_all(small_cut, EVERYONE, 0, 0, tiled=True)
    weight_grad, gain_one_grad = weight_gradient(
        info, turned_rows, packed, middle_all, context_rows, weight, gain_column
    )
    weight_grad, early_own, small_grads = tie(weight_grad, early_own, small_grads)
    weight_came = lax.all_to_all(weight_grad.reshape(dp_count, -1, width), DP, 0, 0, tiled=True)
    expert_grad, expert_squares = expert_gradient(rows_all, grads_all, early_own, late_own)
    expert_squares, packed = tie(expert_squares, packed)

    input_parts = input_gradient(info, packed, weight, tensor_count)
    first_half = input_parts[0].astype(f32) + swap(input_parts[1], TENSOR, 1).astype(f32)
    second_half = (input_parts[2].astype(f32) + swap(input_parts[3], TENSOR, 1).astype(f32)).astype(bf16)

    second_came = swap(second_half, TENSOR, 2)
    dense_grad, last, small_sum = sums_part(
        weight_came, expert_squares, small_grads, gain_one_grad.reshape(-1, LANES), device_count
    )
    last, expert_outs = tie(last, expert_outs)
    last_all = lax.all_to_all(last, EVERYONE, 0, 0, tiled=True)
    input_grad = middle_grad + norm_backward(rows, root_one, small[:1], first_half + second_came.astype(f32))
    picked = mm_tn(place, expert_outs)
    branch = gate * valid_scale * picked
    block_output = middle + branch
    last_all, input_grad, block_output, branch = tie(last_all, input_grad, block_output, branch)

    rates = (0.4 * math.sqrt(expert_count / D), 1.38 * math.sqrt(expert_count / FF))
    norm, *updated = adam(
        info,
        last_all,
        small_sum,
        (attention_weight, attention_mean, attention_square),
        dense_grad,
        (norm_gains, gains_mean, gains_square),
        (router_matrix.T, router_mean.T, router_square.T),
        (expert_weight[0], expert_mean[0], expert_square[0]),
        expert_grad,
        rates,
    )
    attention_new, gains_new, router_new, expert_new = updated[:3], updated[3:6], updated[6:9], updated[9:]
    router_new = [part.T for part in router_new]
    grad_norm = norm.reshape(())
    return (
        block_output[None],
        input_grad[None],
        grad_norm,
        *attention_new,
        *[part[None] for part in expert_new],
        *router_new,
        *gains_new,
        branch[None],
    )


def solution(mesh):
    names = mesh.axis_names
    dp_count, tensor_count = mesh.shape[names[0]], mesh.shape[names[1]]
    cut = jax.sharding.Mesh(mesh.devices.reshape(dp_count // 2, 2, tensor_count // 2, 2), EVERYONE)
    rows = P(DP, TENSOR, None)
    attention = P(None, DP, TENSOR)
    expert = P(DP, None, None, TENSOR)
    router = P(EVERYONE, None)
    gains = P(None, EVERYONE)
    weights = (attention,) * 3 + (expert,) * 3 + (router,) * 3 + (gains,) * 3
    return jax.shard_map(
        on_device,
        mesh=cut,
        in_specs=(rows, rows, P(DP), rows) + weights,
        out_specs=(rows, rows, P()) + weights + (rows,),
        check_vma=False,
    )
```

```python
import math

import jax
import jax.numpy as jnp
from jax import lax
from jax.experimental import pallas as pl
from jax.experimental.pallas import tpu as pltpu
from jax.sharding import PartitionSpec as P

D = 768
H = 12
DH = 64
FF = 3072
STEP = 10

HIGHEST = lax.Precision.HIGHEST
norm_epsilon = 1e-06
beta_first = 0.9
beta_second = 0.999
adam_epsilon = 1e-08
decay_factor = 0.01
clip_limit = 1.0
masked_score = -1e30
score_scale = 1.0 / math.sqrt(DH)
bf16 = jnp.bfloat16
f32 = jnp.float32
MIB = 1 << 20
LANES = 128
EARLY = 848


DP = ("dh", "dl")
TENSOR = ("th", "tl")
EVERYONE = DP + TENSOR


def swap(values, axis, mask):
    count = lax.axis_size(axis)
    return lax.ppermute(values, axis, [(i, i ^ mask) for i in range(count)])


def bits_of(count):
    return [1 << b for b in range(count.bit_length() - 1)]


def gather_relative(block, axis, order):
    held = {0: block}
    for mask in order:
        for j in list(held):
            held[j ^ mask] = swap(held[j], axis, mask)
    return [held[j] for j in range(len(held))]


def mm(a, b):
    return jnp.dot(a, b, preferred_element_type=f32)


def mm_nt(a, b, precision=None):
    return lax.dot_general(
        a, b, (((1,), (1,)), ((), ())), preferred_element_type=f32, precision=precision
    )


def mm_tn(a, b, precision=None):
    return lax.dot_general(
        a, b, (((0,), (0,)), ((), ())), preferred_element_type=f32, precision=precision
    )


def norm_root(values):
    return lax.rsqrt(jnp.mean(values * values, axis=-1, keepdims=True) + norm_epsilon)


def norm_backward(values, root, gain_row, grad):
    scaled = values * root
    inner = grad * gain_row
    centre = jnp.mean(inner * scaled, axis=-1, keepdims=True)
    return root * (inner - scaled * centre)


def gelu_pair(values):
    c = math.sqrt(2.0 / math.pi)
    square = values * values
    th = jnp.tanh(c * values * (1.0 + 0.044715 * square))
    half = 0.5 * (1.0 + th)
    slope = half + 0.5 * values * (1.0 - th * th) * c * (1.0 + 3.0 * 0.044715 * square)
    return values * half, slope


def adam_update(weight, moment_one, moment_two, gradient, step_rate):
    moment_one_next = beta_first * moment_one + (1.0 - beta_first) * gradient
    moment_two_next = beta_second * moment_two + (1.0 - beta_second) * gradient * gradient
    corrected_one = moment_one_next / (1.0 - beta_first**STEP)
    corrected_two = moment_two_next / (1.0 - beta_second**STEP)
    weight_next = weight - step_rate * (
        corrected_one / (jnp.sqrt(corrected_two) + adam_epsilon) + decay_factor * weight
    )
    return (weight_next, moment_one_next, moment_two_next)


def shape_of(shape, dtype):
    return jax.ShapeDtypeStruct(shape, dtype)


def whole(shape):
    return pl.BlockSpec(shape, lambda *_: (0,) * len(shape))


def scalars():
    return pl.BlockSpec(memory_space=pltpu.SMEM)


LIGHT = pl.CostEstimate(flops=1, bytes_accessed=1, transcendentals=0)


def params(limit):
    return pltpu.CompilerParams(vmem_limit_bytes=limit * MIB)


def split_dot(values, picks, parts):
    total, left = None, values
    for _ in range(parts):
        high = left.astype(bf16)
        part = mm(high, picks)
        total = part if total is None else total + part
        left = left - high.astype(f32)
    return total


def prologue_kernel(inputs, attention, gains, router, scaled, root, packed, payload):
    values = inputs[...]
    scale = norm_root(values)
    root[...] = scale
    scaled[...] = (values * scale).astype(bf16)
    parts = [attention[i].astype(bf16) for i in range(4)]
    packed[...] = jnp.concatenate(
        [part[:, :LANES] for part in parts] + [part[:, LANES:] for part in parts], axis=1
    )
    experts, share = router.shape
    groups = -(-(2 + experts) // 8)
    wide = jnp.concatenate([gains[...], router[...]], axis=0)
    wide = jnp.pad(wide, ((0, 8 * groups - 2 - experts), (0, 0)))
    row = jnp.concatenate([wide[8 * k : 8 * k + 8] for k in range(groups)], axis=1)
    row = jnp.pad(row, ((0, 0), (0, LANES - groups * share)))
    payload[...] = jnp.broadcast_to(row[None], payload.shape)


def prologue(inputs, attention, gains, router, device_count):
    quarter, width = inputs.shape
    tall = attention.shape[1]
    shapes = [
        shape_of((quarter, width), bf16),
        shape_of((quarter, 1), f32),
        shape_of((tall, 6 * LANES), bf16),
        shape_of((device_count, 8, LANES), f32),
    ]
    arrays = (inputs, attention, gains, router)
    return pl.pallas_call(
        prologue_kernel,
        in_specs=[whole(a.shape) for a in arrays],
        out_specs=[whole(s.shape) for s in shapes],
        out_shape=shapes,
        compiler_params=params(60),
        cost_estimate=LIGHT,
        name="prologue",
    )(*arrays)


def slots_kernel(capacity, info, routes, grads, place, match, valid, slots):
    quarter = routes.shape[0]
    experts = match.shape[1]
    row = lax.broadcasted_iota(jnp.int32, (quarter, 1), 0) + info[0] * quarter
    inside = jnp.where(row < info[1], 1.0, 0.0)
    valid[...] = inside
    column = lax.broadcasted_iota(jnp.int32, (quarter, experts), 1)
    named = jnp.where(routes[...] == column, 1.0, 0.0)
    match[...] = named
    at = lax.broadcasted_iota(jnp.int32, (quarter, quarter), 0)
    before = lax.broadcasted_iota(jnp.int32, (quarter, quarter), 1)
    lower = jnp.where(at >= before, 1.0, 0.0).astype(bf16)
    rank = jnp.sum(mm(lower, (named * inside).astype(bf16)) * named, axis=1, keepdims=True) - 1.0
    slot = jnp.where(inside > 0.0, routes[...].astype(f32) * capacity + rank, -1.0)
    slot = jnp.broadcast_to(slot, (quarter, LANES)).T[:1]
    number = lax.broadcasted_iota(jnp.int32, place.shape, 0).astype(f32)
    chosen = jnp.where(number == slot, 1.0, 0.0).astype(bf16)
    place[...] = chosen
    slots[...] = mm(chosen, grads[...].astype(bf16)).astype(bf16)


def slots_part(info, routes, grads, experts, capacity):
    quarter, width = grads.shape
    shapes = [
        shape_of((experts * capacity, quarter), bf16),
        shape_of((quarter, experts), f32),
        shape_of((quarter, 1), f32),
        shape_of((experts * capacity, width), bf16),
    ]
    return pl.pallas_call(
        lambda *refs: slots_kernel(capacity, *refs),
        in_specs=[scalars(), whole(routes.shape), whole(grads.shape)],
        out_specs=[whole(s.shape) for s in shapes],
        out_shape=shapes,
        compiler_params=params(60),
        cost_estimate=LIGHT,
        name="slots",
    )(info, routes, grads)


def project_kernel(quarter, blocks, count, share, info, came, x0, x1, x2, x3, *refs):
    shards, (small, column_gain, weight, out_weight, qkv, kaug, vt) = refs[:count], refs[count:]
    tall = shards[0].shape[0]
    width = weight.shape[0]
    for j, ref in enumerate(shards):
        start = pl.multiple_of((info[2] ^ j) * tall, tall) if count > 1 else 0
        weight[pl.ds(start, tall), :] = ref[...]
    out_weight[:LANES, :] = weight[:, 3 * LANES : 4 * LANES].T
    out_weight[LANES:, :] = weight[:, 5 * LANES :].T[DH:]
    groups = small.shape[0] // 8
    devices = came.shape[0]
    flat = came[...].reshape(devices * 8, LANES)
    lane = lax.broadcasted_iota(jnp.int32, (LANES, width), 0)
    column = lax.broadcasted_iota(jnp.int32, (LANES, width), 1)
    inside = lax.rem(column, share)
    owner = lax.broadcasted_iota(jnp.int32, (devices, 1, width), 2) - share * lax.broadcasted_iota(
        jnp.int32, (devices, 1, width), 0
    )
    owner = jnp.where((owner >= 0) & (owner < share), 1.0, 0.0)
    for k in range(groups):
        pick = jnp.where(lane == inside + k * share, 1.0, 0.0).astype(bf16)
        spread = split_dot(flat, pick, 3)
        small[8 * k : 8 * k + 8, :] = jnp.sum(spread.reshape(devices, 8, width) * owner, axis=0)
    gain = small[:1, :]
    column_gain[...] = jnp.broadcast_to(gain, (LANES, width)).T[:, :1]
    for j, ref in enumerate((x0, x1, x2, x3)):
        start = pl.multiple_of((info[0] ^ j) * quarter, quarter)
        rows = pl.ds(start, quarter)
        scaled = (ref[...].astype(f32) * gain).astype(bf16)
        first = mm(scaled, weight[:, : 3 * LANES]).astype(bf16)
        second = mm(scaled, weight[:, 4 * LANES :]).astype(bf16)
        qkv[rows, : 3 * LANES] = first
        qkv[rows, 3 * LANES :] = second
        kaug[rows, :LANES] = first[:, LANES : 2 * LANES]
        lane = lax.broadcasted_iota(jnp.int32, (quarter, LANES), 1)
        row = lax.broadcasted_iota(jnp.int32, (quarter, LANES), 0) + start
        hidden = jnp.where((lane == 0) & (row >= info[1]), masked_score, 0.0)
        kaug[rows, LANES:] = jnp.where(lane < DH, hidden, second[:, :LANES].astype(f32)).astype(bf16)
        values = first[:, 2 * LANES :].T
        vt[0, :DH, rows] = values[:DH]
        vt[1, :DH, rows] = values[DH:]
        vt[2, :DH, rows] = second[:, LANES:].T[:DH]
    full_len = quarter * blocks
    tail = (lax.broadcasted_iota(jnp.int32, (16, full_len), 0) == 0).astype(f32).astype(bf16)
    for h in range(3):
        vt[h, DH:, :] = tail


def project(info, came, rows, shards, share, experts):
    quarter, width = rows[0].shape
    blocks = len(rows)
    full_len = quarter * blocks
    shapes = [
        shape_of((8 * -(-(2 + experts) // 8), width), f32),
        shape_of((width, 1), f32),
        shape_of((width, 6 * LANES), bf16),
        shape_of((3 * DH, width), bf16),
        shape_of((full_len, 5 * LANES), bf16),
        shape_of((full_len, 2 * LANES), bf16),
        shape_of((3, DH + 16, full_len), bf16),
    ]
    arrays = (came, *rows, *shards)
    return pl.pallas_call(
        lambda *refs: project_kernel(quarter, blocks, len(shards), share, *refs),
        in_specs=[scalars()] + [whole(a.shape) for a in arrays],
        out_specs=[whole(s.shape) for s in shapes],
        out_shape=shapes,
        compiler_params=params(60),
        cost_estimate=LIGHT,
        name="project",
    )(info, *arrays)


def attention_kernel(info, qkv, kaug, vt, context, chances, totals, *sent):
    quarter = context.shape[2]
    step = pl.program_id(0)
    rows = pl.ds(pl.multiple_of(step * quarter, quarter), quarter)
    q01 = (qkv[rows, :LANES].astype(f32) * score_scale).T.astype(bf16)
    q2 = (qkv[rows, 3 * LANES : 4 * LANES].astype(f32) * score_scale).T.astype(bf16)[:DH]
    ones = (lax.broadcasted_iota(jnp.int32, (DH, quarter), 0) == 0).astype(f32).astype(bf16)
    zeros = jnp.zeros((DH, quarter), bf16)
    queries = (
        jnp.concatenate([q01[:DH], zeros, ones, zeros], axis=0),
        jnp.concatenate([zeros, q01[DH:], ones, zeros], axis=0),
        jnp.concatenate([zeros, zeros, ones, q2], axis=0),
    )
    full_len = kaug.shape[0]
    all_scores = [mm(kaug[...], queries[h]) for h in range(3)]
    for h in range(3):
        scores = all_scores[h]
        top = jnp.max(jnp.max(scores.reshape(8, full_len // 8, quarter), axis=0), axis=0, keepdims=True)
        low = jnp.exp(scores - top).astype(bf16)
        chances[h] = low
        summed = mm(vt[h], low)
        part = 1.0 / summed[DH : DH + 1]
        totals[0, h : h + 1, :] = part
        context[0, h * DH : (h + 1) * DH, :] = (summed[:DH] * part).astype(bf16)
    for j, ref in enumerate(sent):

        @pl.when(step == info[0] ^ j)
        def _():
            ref[...] = context[0]


def attention_forward(info, qkv, kaug, vt, blocks):
    full_len = qkv.shape[0]
    quarter = full_len // blocks
    inner = 3 * DH
    return pl.pallas_call(
        attention_kernel,
        grid=(blocks,),
        in_specs=[scalars(), whole(qkv.shape), whole(kaug.shape), whole(vt.shape)],
        out_specs=[
            pl.BlockSpec((1, inner, quarter), lambda i: (i, 0, 0)),
            pl.BlockSpec((3, full_len, quarter), lambda i: (0, 0, i)),
            pl.BlockSpec((1, 3, quarter), lambda i: (i, 0, 0)),
        ]
        + [whole((inner, quarter))] * blocks,
        out_shape=[
            shape_of((blocks, inner, quarter), bf16),
            shape_of((3, full_len, full_len), bf16),
            shape_of((blocks, 3, quarter), f32),
        ]
        + [shape_of((inner, quarter), bf16)] * blocks,
        compiler_params=params(60),
        cost_estimate=LIGHT,
        name="attend",
    )(info, qkv, kaug, vt)


def turn_kernel(quarter, blocks, info, x0, x1, x2, x3, qkv, context, xt, kt, q2, cn):
    for j, ref in enumerate((x0, x1, x2, x3)):
        xt[info[0] ^ j] = ref[...].T
    for j in range(blocks):
        rows = slice(j * quarter, (j + 1) * quarter)
        third = qkv[rows, 3 * LANES : 4 * LANES].T
        kt[:LANES, rows] = qkv[rows, LANES : 2 * LANES].T
        kt[LANES:, rows] = third[DH:]
        zeros = jnp.zeros((DH, quarter), bf16)
        q2[rows, :] = jnp.concatenate([zeros, third[:DH]], axis=0).T
        cn[rows, :LANES] = context[j, :LANES, :].T
        cn[rows, LANES:] = jnp.concatenate([zeros, context[j, LANES:, :]], axis=0).T


def turn(info, rows, qkv, context):
    quarter, width = rows[0].shape
    blocks = len(rows)
    full_len = quarter * blocks
    shapes = [
        shape_of((blocks, width, quarter), bf16),
        shape_of((3 * DH, full_len), bf16),
        shape_of((full_len, LANES), bf16),
        shape_of((full_len, 2 * LANES), bf16),
    ]
    return pl.pallas_call(
        lambda *refs: turn_kernel(quarter, blocks, *refs),
        in_specs=[scalars()] + [whole((quarter, width))] * 4 + [whole(qkv.shape), whole(context.shape)],
        out_specs=[whole(s.shape) for s in shapes],
        out_shape=shapes,
        compiler_params=params(60),
        cost_estimate=LIGHT,
        name="turn",
    )(info, *rows, qkv, context)


def two_columns(column):
    high = column.astype(bf16).astype(f32)
    lane = lax.broadcasted_iota(jnp.int32, (column.shape[0], LANES), 1)
    return jnp.where(lane == 0, high, jnp.where(lane == 1, column - high, 0.0)).astype(bf16)


def middle_kernel(
    rows, c0, c1, c2, c3, w0, w1, w2, w3, small, place, match, valid, middle, root, chances, gate, slots
):
    gain, router = small[1:2, :], small[2 : 2 + match.shape[1], :]
    total = rows[...]
    for context, weight in zip((c0, c1, c2, c3), (w0, w1, w2, w3)):
        total = total + mm_tn(context[...], weight[...])
    middle[...] = total
    scale = norm_root(total)
    root[...] = scale
    hidden = total * scale * gain
    scores = mm_nt(hidden, router, HIGHEST)
    powers = jnp.exp(scores - jnp.max(scores, axis=-1, keepdims=True))
    share = powers / jnp.sum(powers, axis=-1, keepdims=True)
    chances[...] = share
    own = jnp.sum(share * match[...], axis=-1, keepdims=True)
    gate[...] = own
    width = rows.shape[1]
    slots[:, :width] = mm(place[...], hidden.astype(bf16)).astype(bf16)
    slots[:, width:] = mm(place[...], two_columns(own * valid[...])).astype(bf16)


def middle_part(rows, contexts, out_weights, small, place, match, valid):
    quarter, width = rows.shape
    experts = match.shape[1]
    shapes = [
        shape_of((quarter, width), f32),
        shape_of((quarter, 1), f32),
        shape_of((quarter, experts), f32),
        shape_of((quarter, 1), f32),
        shape_of((place.shape[0], width + LANES), bf16),
    ]
    arrays = (rows, *contexts, *out_weights, small, place, match, valid)
    return pl.pallas_call(
        middle_kernel,
        in_specs=[whole(a.shape) for a in arrays],
        out_specs=[whole(s.shape) for s in shapes],
        out_shape=shapes,
        compiler_params=params(60),
        cost_estimate=LIGHT,
        name="middle",
    )(*arrays)


def expert_kernel(rows, grads, *refs):
    count = (len(refs) - 4) // 2
    early_parts, late_parts = refs[:count], refs[count : 2 * count]
    out, back, held, arrived = refs[2 * count :]
    width = grads.shape[1]
    early = early_parts[0].shape[0]
    ends = (slice(0, early), slice(early, 2 * width))
    copies = [
        [
            pltpu.make_async_copy(ref, held.at[i, end, :], arrived.at[i, k])
            for k, (ref, end) in enumerate(zip(pair, ends))
        ]
        for i, pair in enumerate(zip(early_parts, late_parts))
    ]
    for pair in copies:
        for copy in pair:
            copy.start()
    out_total, back_total = None, None
    for i, pair in enumerate(copies):
        for copy in pair:
            copy.wait()
        grad = mm(grads[...], held[i, width:, :])
        active, slope = gelu_pair(mm(rows[:, :width], held[i, :width, :]))
        part = mm_nt(active.astype(bf16), held[i, width:, :])
        back_part = mm_nt((grad * slope).astype(bf16), held[i, :width, :])
        out_total = part if i == 0 else out_total + part
        back_total = back_part if i == 0 else back_total + back_part
    result = out_total.astype(bf16)
    out[...] = result
    back[:, :width] = back_total.astype(bf16)
    match = jnp.sum(grads[...].astype(f32) * result.astype(f32), axis=-1, keepdims=True)
    back[:, width:] = two_columns(match)


def expert_part(rows, grads, early_parts, late_parts):
    slots, width = grads.shape
    hidden = early_parts[0].shape[1]
    count = len(early_parts)
    shapes = [shape_of((slots, width), bf16), shape_of((slots, width + LANES), bf16)]
    return pl.pallas_call(
        expert_kernel,
        in_specs=[whole(rows.shape), whole(grads.shape)] + [pl.BlockSpec(memory_space=pl.ANY)] * (2 * count),
        out_specs=[whole(s.shape) for s in shapes],
        out_shape=shapes,
        scratch_shapes=[pltpu.VMEM((count, 2 * width, hidden), bf16), pltpu.SemaphoreType.DMA((count, 2))],
        compiler_params=params(60),
        cost_estimate=LIGHT,
        name="experts",
    )(rows, grads, *early_parts, *late_parts)


def expert_grad_kernel(count, *refs):
    rows, grads = refs[:count], refs[count : 2 * count]
    near_in, near_out, out, square, weight, row_all, grad_all, inner_all, active_all, arrived = refs[2 * count :]
    early = near_in.shape[0]
    ends = (slice(0, early), slice(early, weight.shape[0]))
    copies = [
        pltpu.make_async_copy(ref, weight.at[end, :], arrived.at[i])
        for i, (ref, end) in enumerate(zip((near_in, near_out), ends))
    ]
    for copy in copies:
        copy.start()
    for copy in copies:
        copy.wait()
    slots, width = grads[0].shape
    for j in range(count):
        at = slice(j * slots, (j + 1) * slots)
        gate = rows[j][:, width : width + 1].astype(f32) + rows[j][:, width + 1 : width + 2].astype(f32)
        row_all[at, :] = rows[j][:, :width]
        grad_all[at, :] = (grads[j][...].astype(f32) * gate).astype(bf16)
        back = mm(grads[j][...], weight[width:, :])
        active, slope = gelu_pair(mm(rows[j][:, :width], weight[:width, :]))
        inner_all[at, :] = (back * slope * gate).astype(bf16)
        active_all[at, :] = active.astype(bf16)
    first = mm_tn(row_all[...], inner_all[...])
    out[0] = first.astype(bf16)
    second = mm_tn(grad_all[...], active_all[...])
    out[1] = second.astype(bf16)
    square[...] = jnp.sum(first * first + second * second, axis=0, keepdims=True)


def expert_gradient(rows, grads, near_in, near_out):
    count = len(rows)
    slots, width = grads[0].shape
    hidden = near_in.shape[1]
    arrays = (*rows, *grads)
    shapes = [
        shape_of((2, width, hidden), bf16),
        shape_of((1, hidden), f32),
    ]
    return pl.pallas_call(
        lambda *refs: expert_grad_kernel(count, *refs),
        in_specs=[whole(a.shape) for a in arrays] + [pl.BlockSpec(memory_space=pl.ANY)] * 2,
        out_specs=[whole(s.shape) for s in shapes],
        out_shape=shapes,
        scratch_shapes=[pltpu.VMEM((2 * width, hidden), bf16)]
        + [pltpu.VMEM((count * slots, width), bf16)] * 2
        + [pltpu.VMEM((count * slots, hidden), bf16)] * 2
        + [pltpu.SemaphoreType.DMA((2,))],
        compiler_params=params(60),
        cost_estimate=LIGHT,
        name="expert_gradient",
    )(*arrays, near_in, near_out)


def pack_small(small, cut):
    devices = cut.shape[0]
    rows, width = small.shape
    share = width // devices
    groups = rows // 8
    column = lax.broadcasted_iota(jnp.int32, (devices, 1, width), 2)
    owner = column - share * lax.broadcasted_iota(jnp.int32, (devices, 1, width), 0)
    owner = jnp.where((owner >= 0) & (owner < share), 1.0, 0.0)
    lane = lax.broadcasted_iota(jnp.int32, (width, LANES), 1)
    inside = lax.rem(lax.broadcasted_iota(jnp.int32, (width, LANES), 0), share)
    total = None
    for k in range(groups):
        pick = jnp.where(lane == inside + k * share, 1.0, 0.0).astype(bf16)
        spread = (small[8 * k : 8 * k + 8, :][None] * owner).reshape(devices * 8, width)
        part = split_dot(spread, pick, 2)
        total = part if total is None else total + part
    cut[...] = total.reshape(devices, 8, LANES)


def return_kernel(
    back, place, middle, root, chances, gate, match, cotangent, small, w0, w1, w2, w3,
    grad, turned, cut, p0, p1, p2, p3, small_grad,
):
    experts = match.shape[1]
    gain, router = small[1:2, :], small[2 : 2 + experts, :]
    width = middle.shape[1]
    came = mm_tn(place[...], back[...])
    gate_grad = came[:, width : width + 1] + came[:, width + 1 : width + 2]
    own = gate[...]
    score_grad = own * (match[...] - chances[...]) * gate_grad
    scaled = middle[...] * root[...]
    hidden = scaled * gain
    tall = small_grad.shape[0]
    small_grad[1 : 1 + experts, :] = mm_tn(score_grad, hidden, HIGHEST)
    small_grad[1 + experts :, :] = jnp.zeros((tall - 1 - experts, hidden.shape[1]), f32)
    second = own * came[:, :width] + jnp.dot(
        score_grad, router, precision=HIGHEST, preferred_element_type=f32
    )
    small_grad[:1, :] = jnp.sum(second * scaled, axis=0, keepdims=True)
    inner = second * gain
    centre = jnp.mean(inner * scaled, axis=-1, keepdims=True)
    total = cotangent[...] + root[...] * (inner - scaled * centre)
    grad[...] = total
    low = total.astype(bf16)
    turned[...] = low.T
    for ref, weight in zip((p0, p1, p2, p3), (w0, w1, w2, w3)):
        ref[...] = mm_nt(weight[...], low).astype(bf16)
    pack_small(small_grad, cut)


def return_part(back, place, middle, root, chances, gate, match, cotangent, small, out_weights, device_count):
    quarter, width = middle.shape
    experts = match.shape[1]
    inner = out_weights[0].shape[0]
    shapes = [
        shape_of((quarter, width), f32),
        shape_of((width, quarter), bf16),
        shape_of((device_count, 8, LANES), f32),
    ] + [shape_of((inner, quarter), bf16)] * len(out_weights)
    arrays = (back, place, middle, root, chances, gate, match, cotangent, small, *out_weights)
    return pl.pallas_call(
        return_kernel,
        in_specs=[whole(a.shape) for a in arrays],
        out_specs=[whole(s.shape) for s in shapes],
        out_shape=shapes,
        scratch_shapes=[pltpu.VMEM((8 * -(-(1 + experts) // 8), width), f32)],
        compiler_params=params(60),
        cost_estimate=LIGHT,
        name="returned",
    )(*arrays)


def attention_back_kernel(
    blocks, info, g0, g1, g2, g3, context, chances, totals, qkv, kt, q2, packed, grads, vaug, k01, k2, v01, v2
):
    step = pl.program_id(0)
    quarter = grads.shape[2]

    @pl.when(step == 0)
    def _():
        for j, ref in enumerate((g0, g1, g2, g3)):
            grads[info[0] ^ j] = ref[...]
        vaug[:, :LANES] = qkv[:, 2 * LANES : 3 * LANES]
        lane = lax.broadcasted_iota(jnp.int32, (vaug.shape[0], LANES), 1)
        ones = jnp.where(lane < DH + 2, 1.0, 0.0)
        vaug[:, LANES:] = jnp.where(lane < DH, qkv[:, 4 * LANES :].astype(f32), ones).astype(bf16)
        for ref in (k01, k2, v01, v2):
            ref[...] = jnp.zeros(ref.shape, f32)

    rows = pl.ds(pl.multiple_of(step * quarter, quarter), quarter)
    raw = grads[step].astype(f32)
    scale = totals[0]
    scaled = [raw[h * DH : (h + 1) * DH] * scale[h : h + 1] for h in range(3)]
    heads = jnp.concatenate(scaled, axis=0).astype(bf16)
    lane = lax.broadcasted_iota(jnp.int32, (quarter, LANES), 1)
    row = lax.broadcasted_iota(jnp.int32, (DH, quarter), 0)
    zeros = jnp.zeros((DH, quarter), bf16)
    q01 = qkv[rows, :LANES].astype(f32)
    g01 = heads[:LANES].T.astype(f32)
    third = jnp.concatenate([heads[LANES:], zeros], axis=0).T
    query_parts = []
    for h in range(3):
        part = heads[h * DH : (h + 1) * DH]
        centre = -jnp.sum(
            part.astype(f32) * context[0, h * DH : (h + 1) * DH, :].astype(f32), axis=0, keepdims=True
        )
        high = centre.astype(bf16).astype(f32)
        tail = jnp.where(row == 0, high, jnp.where(row == 1, centre - high, 0.0)).astype(bf16)
        pieces = [zeros, zeros, zeros, tail]
        pieces[h] = part
        chance_grad = mm(vaug[...], jnp.concatenate(pieces, axis=0))
        low = chances[h]
        score_grad = (low.astype(f32) * chance_grad).astype(bf16)
        query_parts.append(mm(kt[h * DH : (h + 1) * DH, :], score_grad) * score_scale)
        if h < 2:
            inside = (lane >= h * DH) & (lane < (h + 1) * DH)
            k01[...] += mm(score_grad, jnp.where(inside, q01, 0.0).astype(bf16))
            v01[...] += mm(low, jnp.where(inside, g01, 0.0).astype(bf16))
        else:
            k2[...] += mm(score_grad, q2[rows, :])
            v2[...] += mm(low, third)
    packed[rows, :LANES] = jnp.concatenate(query_parts[:2], axis=0).T.astype(bf16)
    packed[rows, 4 * LANES : 5 * LANES] = (
        jnp.concatenate([query_parts[2], jnp.zeros((DH, quarter), f32)], axis=0).T.astype(bf16)
    )

    @pl.when(step == blocks - 1)
    def _():
        packed[:, LANES : 2 * LANES] = (k01[...] * score_scale).astype(bf16)
        packed[:, 2 * LANES : 3 * LANES] = v01[...].astype(bf16)
        packed[:, 3 * LANES : 4 * LANES] = jnp.zeros(k01.shape, bf16)
        packed[:, 4 * LANES : 5 * LANES] = packed[:, 4 * LANES : 5 * LANES] + (k2[...] * score_scale).astype(bf16)
        packed[:, 5 * LANES :] = v2[...].astype(bf16)


def attention_backward(info, grads, context, chances, totals, qkv, kt, q2):
    blocks, inner, quarter = context.shape
    full_len = quarter * blocks
    block = pl.BlockSpec((1, inner, quarter), lambda i: (i, 0, 0))
    return pl.pallas_call(
        lambda *refs: attention_back_kernel(blocks, *refs),
        grid=(blocks,),
        in_specs=[
            scalars(),
            *[whole((inner, quarter))] * blocks,
            block,
            pl.BlockSpec((3, full_len, quarter), lambda i: (0, 0, i)),
            pl.BlockSpec((1, 3, quarter), lambda i: (i, 0, 0)),
            whole(qkv.shape),
            whole(kt.shape),
            whole(q2.shape),
        ],
        out_specs=whole((full_len, 6 * LANES)),
        out_shape=shape_of((full_len, 6 * LANES), bf16),
        scratch_shapes=[pltpu.VMEM(context.shape, bf16), pltpu.VMEM((full_len, 2 * LANES), bf16)]
        + [pltpu.VMEM((full_len, LANES), f32)] * 4,
        compiler_params=params(60),
        cost_estimate=LIGHT,
        name="attend_back",
    )(info, *grads, context, chances, totals, qkv, kt, q2)


def weight_grad_kernel(blocks, info, xt, packed, g0, g1, g2, g3, cn, weight, gain, out, gain_grad):
    quarter = xt.shape[2]
    total, outer = None, None
    for j, ref in enumerate((g0, g1, g2, g3)):
        rows = slice(j * quarter, (j + 1) * quarter)
        there = pl.ds(pl.multiple_of((info[0] ^ j) * quarter, quarter), quarter)
        part = mm(xt[j], packed[rows, :])
        own = mm(ref[...], cn[there, :])
        total = part if total is None else total + part
        outer = own if outer is None else outer + own
    gain_grad[...] = jnp.sum(total * weight[...].astype(f32), axis=1, keepdims=True)
    total = total * gain[...]
    out[:, : 3 * LANES] = total[:, : 3 * LANES].astype(bf16)
    out[:, 3 * LANES : 4 * LANES] = outer[:, :LANES].astype(bf16)
    out[:, 4 * LANES : 5 * LANES] = total[:, 4 * LANES : 5 * LANES].astype(bf16)
    out[:, 5 * LANES :] = (total[:, 5 * LANES :] + outer[:, LANES:]).astype(bf16)


def weight_gradient(info, xt, packed, grads, cn, weight, gain):
    blocks, width, quarter = xt.shape
    tall = 256
    full_len = quarter * blocks
    return pl.pallas_call(
        lambda *refs: weight_grad_kernel(blocks, *refs),
        grid=(width // tall,),
        in_specs=[
            scalars(),
            pl.BlockSpec((blocks, tall, quarter), lambda i: (0, i, 0)),
            whole(packed.shape),
            *[pl.BlockSpec((tall, quarter), lambda i: (i, 0))] * blocks,
            whole(cn.shape),
            pl.BlockSpec((tall, 6 * LANES), lambda i: (i, 0)),
            pl.BlockSpec((tall, 1), lambda i: (i, 0)),
        ],
        out_specs=[pl.BlockSpec((tall, 6 * LANES), lambda i: (i, 0)), pl.BlockSpec((tall, 1), lambda i: (i, 0))],
        out_shape=[shape_of((width, 6 * LANES), bf16), shape_of((width, 1), f32)],
        compiler_params=params(60),
        cost_estimate=LIGHT,
        name="weight_gradient",
    )(info, xt, packed, *grads, cn, weight, gain)


def input_grad_kernel(quarter, info, packed, weight, *parts):
    for j, ref in enumerate(parts):
        rows = pl.ds(pl.multiple_of((info[0] ^ j) * quarter, quarter), quarter)
        ref[...] = mm_nt(packed[rows, :], weight[...]).astype(bf16)


def input_gradient(info, packed, weight, blocks):
    quarter = packed.shape[0] // blocks
    shapes = [shape_of((quarter, weight.shape[0]), bf16)] * blocks
    return pl.pallas_call(
        lambda *refs: input_grad_kernel(quarter, *refs),
        in_specs=[scalars(), whole(packed.shape), whole(weight.shape)],
        out_specs=[whole(s.shape) for s in shapes],
        out_shape=shapes,
        compiler_params=params(60),
        cost_estimate=LIGHT,
        name="input_gradient",
    )(info, packed, weight)


def sums_kernel(came, squares, small, gain_grad, gradient, payload, small_sum):
    count = came.shape[0]
    total = came[0].astype(f32)
    for i in range(1, count):
        total = total + came[i].astype(f32)
    gradient[...] = total
    own = jnp.sum(small[...], axis=0)
    square = (
        jnp.sum(total * total, keepdims=True)
        + jnp.sum(squares[...], keepdims=True)
        + jnp.sum(own * own, keepdims=True)
    )
    small_sum[...] = own
    rows = gain_grad.shape[0]
    row = lax.broadcasted_iota(jnp.int32, (8, LANES), 0)
    gain = jnp.concatenate([gain_grad[...], jnp.zeros((8 - rows, LANES), f32)], axis=0)
    payload[...] = jnp.broadcast_to(jnp.where(row < rows, gain, square)[None], payload.shape)


def sums_part(came, squares, small, gain_grad, device_count):
    shapes = [
        shape_of(came.shape[1:], f32),
        shape_of((device_count, 8, LANES), f32),
        shape_of((8, LANES), f32),
    ]
    arrays = (came, squares, small, gain_grad)
    return pl.pallas_call(
        sums_kernel,
        in_specs=[whole(a.shape) for a in arrays],
        out_specs=[whole(s.shape) for s in shapes],
        out_shape=shapes,
        compiler_params=params(60),
        cost_estimate=LIGHT,
        name="sums",
    )(*arrays)


def adam_kernel(lanes, share, expert_rates, info, last, small_sum, *refs):
    held, outs, factor = refs[:14], refs[14:27], refs[27]
    dense, dense_grad, gains, router = held[:3], held[3], held[4:7], held[7:10]
    weight, first, second, gradient = held[10:14]
    norm_out, outs = outs[0], outs[1:]
    dense_out, gains_out, router_out, expert_out = outs[:3], outs[3:6], outs[6:9], outs[9:12]
    matrix, part = pl.program_id(0), pl.program_id(1)
    experts = router[0].shape[0]

    @pl.when((matrix == 0) & (part == 0))
    def _():
        total = jnp.sum(last[...], axis=0)
        row = lax.broadcasted_iota(jnp.int32, (8, LANES), 0)
        squares = jnp.sum(jnp.where(row < lanes, total * total, 0.0), keepdims=True)
        norm = jnp.sqrt(squares + total[7:8, :1])
        scale = jnp.minimum(1.0, clip_limit / (norm + norm_epsilon))
        norm_out[...] = norm
        factor[...] = jnp.broadcast_to(scale, (8, LANES))
        rates = (0.71 / math.sqrt(D), 0.71 / math.sqrt(D), 0.83 / math.sqrt(D), 0.79 / math.sqrt(H * DH))
        for i, rate in enumerate(rates):
            grad = jnp.concatenate(
                [
                    dense_grad[:, i * LANES : (i + 1) * LANES],
                    dense_grad[:, 4 * LANES + i * DH : 4 * LANES + (i + 1) * DH],
                ],
                axis=1,
            )
            result = adam_update(*[ref[i] for ref in dense], grad * scale, rate)
            for ref, value in zip(dense_out, result):
                ref[i] = value
        column = lax.broadcasted_iota(jnp.int32, (LANES, LANES), 1)
        place = lax.broadcasted_iota(jnp.int32, (LANES, LANES), 0) - info[3] * share
        own = jnp.zeros((8, LANES), f32)
        for i in range(lanes):
            pick = jnp.where((column == place + i * LANES) & (column < share), 1.0, 0.0)
            own = own + jnp.dot(
                jnp.broadcast_to(total[i : i + 1], (8, LANES)), pick, precision=HIGHEST, preferred_element_type=f32
            )
        groups = -(-(1 + experts) // 8)
        table = small_sum[...]
        table = jnp.concatenate([table[:, k * share : (k + 1) * share] for k in range(groups)], axis=0)
        grad = jnp.concatenate([own[:1, :share], table[:1]], axis=0)
        for ref, value in zip(gains_out, adam_update(*[ref[...] for ref in gains], grad * scale, 0.5)):
            ref[...] = value
        grad = table[1 : 1 + experts]
        result = adam_update(*[ref[...] for ref in router], grad * scale, 0.24 / math.sqrt(D))
        for ref, value in zip(router_out, result):
            ref[...] = value

    rate = jnp.where(matrix == 0, expert_rates[0], expert_rates[1])
    grad = gradient[...].astype(f32) * factor[:1, :1]
    result = adam_update(weight[...], first[...], second[...], grad, rate)
    for ref, value in zip(expert_out, result):
        ref[...] = value


def adam(info, last, small_sum, dense, dense_grad, gains, router, expert, expert_grad, rates):
    _, tall, wide = expert_grad.shape
    parts = 4
    block = pl.BlockSpec((1, tall // parts, wide), lambda i, j: (i, j, 0))
    small = [*dense, *gains, *router]
    shapes = [shape_of((1, 1), f32)] + [shape_of(a.shape, f32) for a in small]
    ins = (last, small_sum, *dense, dense_grad, *gains, *router)
    return pl.pallas_call(
        lambda *refs: adam_kernel(tall // LANES, gains[0].shape[1], rates, *refs),
        grid=(2, parts),
        in_specs=[scalars()] + [whole(a.shape) for a in ins] + [block] * 4,
        out_specs=[whole(a.shape) for a in shapes] + [block] * 3,
        out_shape=shapes + [shape_of(expert_grad.shape, f32)] * 3,
        scratch_shapes=[pltpu.VMEM((8, LANES), f32)],
        compiler_params=params(60),
        cost_estimate=LIGHT,
        name="adam",
    )(info, *ins, *expert, expert_grad)


def tie(*values):
    return lax.optimization_barrier(values)


def on_device(
    inputs,
    cotangent,
    lengths,
    routes,
    attention_weight,
    attention_mean,
    attention_square,
    expert_weight,
    expert_mean,
    expert_square,
    router_matrix,
    router_mean,
    router_square,
    norm_gains,
    gains_mean,
    gains_square,
):
    quarter, width = inputs.shape[1:]
    dp_count, tensor_count = lax.axis_size(DP), lax.axis_size(TENSOR)
    device_count = dp_count * tensor_count
    expert_count = router_matrix.shape[1]
    capacity = max(2, (5 * quarter + 4 * expert_count - 1) // (4 * expert_count))
    own_dp, own_tensor = lax.axis_index(DP), lax.axis_index(TENSOR)
    share = router_matrix.shape[0]
    rows, grad_rows, length = inputs[0], cotangent[0], lengths[0]
    info = jnp.stack([own_tensor, length, own_dp, lax.axis_index(EVERYONE)]).astype(jnp.int32)

    scaled_one, root_one, weight_own, payload = prologue(
        rows, attention_weight, norm_gains, router_matrix.T, device_count
    )
    block_two = swap(scaled_one, TENSOR, 2)
    small_came = lax.all_to_all(payload, EVERYONE, 0, 0, tiled=True)
    expert_flat = expert_weight[0].reshape(2 * width, -1)
    early_own, late_own = expert_flat[:EARLY].astype(bf16), expert_flat[EARLY:].astype(bf16)
    place, match, valid_scale, grad_slots = slots_part(info, routes[0], grad_rows, expert_count, capacity)
    if dp_count == 8:
        w4, w2, w1 = [swap(weight_own, DP, mask) for mask in (4, 2, 1)]
        w4, w2, w1, small_came, block_two, early_own = tie(w4, w2, w1, small_came, block_two, early_own)
        w6, w5, w3 = swap(w4, DP, 2), swap(w4, DP, 1), swap(w2, DP, 1)
        w6, w5, w3, scaled_one, grad_slots = tie(w6, w5, w3, scaled_one, grad_slots)
        shards = [weight_own, w1, w2, w3, w4, w5, w6, swap(w6, DP, 1)]
    else:
        weight_own, grad_slots, small_came, block_two, early_own = tie(
            weight_own, grad_slots, small_came, block_two, early_own
        )
        shards = [lax.all_gather(weight_own, DP, axis=0, tiled=True)]
    early_far = swap(early_own, TENSOR, 2)
    row_blocks = [scaled_one, swap(scaled_one, TENSOR, 1), block_two, swap(block_two, TENSOR, 1)]

    slot_count = expert_count * capacity

    def trade(values):
        blocks = values.reshape(expert_count, capacity, values.shape[1])
        return lax.all_to_all(blocks, DP, 0, 0, tiled=True).reshape(values.shape)

    expert_grads = trade(grad_slots)
    small, gain_column, weight, out_weight, qkv, keys_wide, values_turned = project(
        info, small_came, row_blocks, shards, share, expert_count
    )
    out_weight, early_own = tie(out_weight, early_own)
    out_near, out_far = swap(out_weight, TENSOR, 1), swap(out_weight, TENSOR, 2)
    early_near = swap(early_own, TENSOR, 1)
    context, chances, totals, *sent = attention_forward(info, qkv, keys_wide, values_turned, tensor_count)
    expert_grads, early_far, out_near, out_far, *sent = tie(expert_grads, early_far, out_near, out_far, *sent)
    contexts = [sent[0]] + [swap(sent[j], TENSOR, j) for j in range(1, tensor_count)]
    out_weights = [out_weight, out_near, out_far, swap(out_far, TENSOR, 1)]
    late_own, early_far, *contexts = tie(late_own, early_far, *contexts)
    late_far = swap(late_own, TENSOR, 2)

    middle, root_two, shares, gate, slots = middle_part(
        rows, contexts, out_weights, small, place, match, valid_scale
    )
    qkv, slots, late_own = tie(qkv, slots, late_own)
    expert_rows = trade(slots)
    turned_rows, keys_turned, third_query, context_rows = turn(info, row_blocks, qkv, context)
    early_parts = [early_own, early_far, early_near, swap(early_far, TENSOR, 1)]
    late_parts = [late_own, late_far, swap(late_own, TENSOR, 1), swap(late_far, TENSOR, 1)]
    expert_rows, turned_rows = tie(expert_rows, turned_rows)
    expert_outs, expert_back = expert_part(expert_rows, expert_grads, early_parts, late_parts)
    expert_rows, expert_back = tie(expert_rows, expert_back)
    rows_near, rows_far = swap(expert_rows, TENSOR, 1), swap(expert_rows, TENSOR, 2)
    rows_far, expert_grads = tie(rows_far, expert_grads)
    rows_all = [expert_rows, rows_near, rows_far, swap(rows_far, TENSOR, 1)]
    grads_near, grads_far = swap(expert_grads, TENSOR, 1), swap(expert_grads, TENSOR, 2)
    expert_back, rows_all = tie(trade(expert_back), rows_all)

    middle_grad, middle_turned, small_cut, *parts = return_part(
        expert_back, place, middle, root_two, shares, gate, match, grad_rows, small, out_weights, device_count
    )
    expert_outs, middle_turned, *parts = tie(expert_outs, middle_turned, *parts)
    context_grads = [parts[0]] + [swap(parts[j], TENSOR, j) for j in range(1, tensor_count)]
    expert_outs = trade(expert_outs)
    middle_turned, *context_grads = tie(middle_turned, *context_grads)
    middle_near, middle_far = swap(middle_turned, TENSOR, 1), swap(middle_turned, TENSOR, 2)

    packed = attention_backward(info, context_grads, context, chances, totals, qkv, keys_turned, third_query)
    packed, middle_far, grads_far, small_cut, expert_outs = tie(packed, middle_far, grads_far, small_cut, expert_outs)
    middle_all = [middle_turned, middle_near, middle_far, swap(middle_far, TENSOR, 1)]
    grads_all = [expert_grads, grads_near, grads_far, swap(grads_far, TENSOR, 1)]
    small_grads = lax.all_to_all(small_cut, EVERYONE, 0, 0, tiled=True)
    weight_grad, gain_one_grad = weight_gradient(
        info, turned_rows, packed, middle_all, context_rows, weight, gain_column
    )
    weight_grad, early_own, small_grads = tie(weight_grad, early_own, small_grads)
    weight_came = lax.all_to_all(weight_grad.reshape(dp_count, -1, width), DP, 0, 0, tiled=True)
    expert_grad, expert_squares = expert_gradient(rows_all, grads_all, early_own, late_own)
    expert_squares, packed = tie(expert_squares, packed)

    input_parts = input_gradient(info, packed, weight, tensor_count)
    first_half = input_parts[0].astype(f32) + swap(input_parts[1], TENSOR, 1).astype(f32)
    second_half = (input_parts[2].astype(f32) + swap(input_parts[3], TENSOR, 1).astype(f32)).astype(bf16)

    second_came = swap(second_half, TENSOR, 2)
    dense_grad, last, small_sum = sums_part(
        weight_came, expert_squares, small_grads, gain_one_grad.reshape(-1, LANES), device_count
    )
    last, expert_outs, middle_grad = tie(last, expert_outs, middle_grad)
    last_all = lax.all_to_all(last, EVERYONE, 0, 0, tiled=True)
    input_grad = middle_grad + norm_backward(rows, root_one, small[:1], first_half + second_came.astype(f32))
    picked = mm_tn(place, expert_outs)
    branch = gate * valid_scale * picked
    block_output = middle + branch
    last_all, input_grad, block_output, branch = tie(last_all, input_grad, block_output, branch)

    rates = (0.4 * math.sqrt(expert_count / D), 1.38 * math.sqrt(expert_count / FF))
    norm, *updated = adam(
        info,
        last_all,
        small_sum,
        (attention_weight, attention_mean, attention_square),
        dense_grad,
        (norm_gains, gains_mean, gains_square),
        (router_matrix.T, router_mean.T, router_square.T),
        (expert_weight[0], expert_mean[0], expert_square[0]),
        expert_grad,
        rates,
    )
    attention_new, gains_new, router_new, expert_new = updated[:3], updated[3:6], updated[6:9], updated[9:]
    router_new = [part.T for part in router_new]
    grad_norm = norm.reshape(())
    return (
        block_output[None],
        input_grad[None],
        grad_norm,
        *attention_new,
        *[part[None] for part in expert_new],
        *router_new,
        *gains_new,
        branch[None],
    )


def solution(mesh):
    names = mesh.axis_names
    dp_count, tensor_count = mesh.shape[names[0]], mesh.shape[names[1]]
    cut = jax.sharding.Mesh(mesh.devices.reshape(dp_count // 2, 2, tensor_count // 2, 2), EVERYONE)
    rows = P(DP, TENSOR, None)
    attention = P(None, DP, TENSOR)
    expert = P(DP, None, None, TENSOR)
    router = P(EVERYONE, None)
    gains = P(None, EVERYONE)
    weights = (attention,) * 3 + (expert,) * 3 + (router,) * 3 + (gains,) * 3
    return jax.shard_map(
        on_device,
        mesh=cut,
        in_specs=(rows, rows, P(DP), rows) + weights,
        out_specs=(rows, rows, P()) + weights + (rows,),
        check_vma=False,
    )
```

```python
import math

import jax
import jax.numpy as jnp
from jax import lax
from jax.experimental import pallas as pl
from jax.experimental.pallas import tpu as pltpu
from jax.sharding import PartitionSpec as P

D = 768
H = 12
DH = 64
FF = 3072
STEP = 10

HIGHEST = lax.Precision.HIGHEST
norm_epsilon = 1e-06
beta_first = 0.9
beta_second = 0.999
adam_epsilon = 1e-08
decay_factor = 0.01
clip_limit = 1.0
masked_score = -1e30
score_scale = 1.0 / math.sqrt(DH)
bf16 = jnp.bfloat16
f32 = jnp.float32
MIB = 1 << 20
LANES = 128
EARLY = 848


DP = ("dh", "dl")
TENSOR = ("th", "tl")
EVERYONE = DP + TENSOR


def swap(values, axis, mask):
    count = lax.axis_size(axis)
    return lax.ppermute(values, axis, [(i, i ^ mask) for i in range(count)])


def bits_of(count):
    return [1 << b for b in range(count.bit_length() - 1)]


def gather_relative(block, axis, order):
    held = {0: block}
    for mask in order:
        for j in list(held):
            held[j ^ mask] = swap(held[j], axis, mask)
    return [held[j] for j in range(len(held))]


def mm(a, b):
    return jnp.dot(a, b, preferred_element_type=f32)


def mm_nt(a, b, precision=None):
    return lax.dot_general(
        a, b, (((1,), (1,)), ((), ())), preferred_element_type=f32, precision=precision
    )


def mm_tn(a, b, precision=None):
    return lax.dot_general(
        a, b, (((0,), (0,)), ((), ())), preferred_element_type=f32, precision=precision
    )


def norm_root(values):
    return lax.rsqrt(jnp.mean(values * values, axis=-1, keepdims=True) + norm_epsilon)


def norm_backward(values, root, gain_row, grad):
    scaled = values * root
    inner = grad * gain_row
    centre = jnp.mean(inner * scaled, axis=-1, keepdims=True)
    return root * (inner - scaled * centre)


def gelu_pair(values):
    c = math.sqrt(2.0 / math.pi)
    square = values * values
    th = jnp.tanh(c * values * (1.0 + 0.044715 * square))
    half = 0.5 * (1.0 + th)
    slope = half + 0.5 * values * (1.0 - th * th) * c * (1.0 + 3.0 * 0.044715 * square)
    return values * half, slope


def adam_update(weight, moment_one, moment_two, gradient, step_rate):
    moment_one_next = beta_first * moment_one + (1.0 - beta_first) * gradient
    moment_two_next = beta_second * moment_two + (1.0 - beta_second) * gradient * gradient
    corrected_one = moment_one_next / (1.0 - beta_first**STEP)
    corrected_two = moment_two_next / (1.0 - beta_second**STEP)
    weight_next = weight - step_rate * (
        corrected_one / (jnp.sqrt(corrected_two) + adam_epsilon) + decay_factor * weight
    )
    return (weight_next, moment_one_next, moment_two_next)


def shape_of(shape, dtype):
    return jax.ShapeDtypeStruct(shape, dtype)


def whole(shape):
    return pl.BlockSpec(shape, lambda *_: (0,) * len(shape))


def scalars():
    return pl.BlockSpec(memory_space=pltpu.SMEM)


LIGHT = pl.CostEstimate(flops=1, bytes_accessed=1, transcendentals=0)


def params(limit):
    return pltpu.CompilerParams(vmem_limit_bytes=limit * MIB)


def split_dot(values, picks, parts):
    total, left = None, values
    for _ in range(parts):
        high = left.astype(bf16)
        part = mm(high, picks)
        total = part if total is None else total + part
        left = left - high.astype(f32)
    return total


def prologue_kernel(inputs, attention, gains, router, scaled, root, packed, payload):
    values = inputs[...]
    scale = norm_root(values)
    root[...] = scale
    scaled[...] = (values * scale).astype(bf16)
    parts = [attention[i].astype(bf16) for i in range(4)]
    packed[...] = jnp.concatenate(
        [part[:, :LANES] for part in parts] + [part[:, LANES:] for part in parts], axis=1
    )
    experts, share = router.shape
    groups = -(-(2 + experts) // 8)
    wide = jnp.concatenate([gains[...], router[...]], axis=0)
    wide = jnp.pad(wide, ((0, 8 * groups - 2 - experts), (0, 0)))
    row = jnp.concatenate([wide[8 * k : 8 * k + 8] for k in range(groups)], axis=1)
    row = jnp.pad(row, ((0, 0), (0, LANES - groups * share)))
    payload[...] = jnp.broadcast_to(row[None], payload.shape)


def prologue(inputs, attention, gains, router, device_count):
    quarter, width = inputs.shape
    tall = attention.shape[1]
    shapes = [
        shape_of((quarter, width), bf16),
        shape_of((quarter, 1), f32),
        shape_of((tall, 6 * LANES), bf16),
        shape_of((device_count, 8, LANES), f32),
    ]
    arrays = (inputs, attention, gains, router)
    return pl.pallas_call(
        prologue_kernel,
        in_specs=[whole(a.shape) for a in arrays],
        out_specs=[whole(s.shape) for s in shapes],
        out_shape=shapes,
        compiler_params=params(60),
        cost_estimate=LIGHT,
        name="prologue",
    )(*arrays)


def slots_kernel(capacity, info, routes, grads, place, match, valid, slots):
    quarter = routes.shape[0]
    experts = match.shape[1]
    row = lax.broadcasted_iota(jnp.int32, (quarter, 1), 0) + info[0] * quarter
    inside = jnp.where(row < info[1], 1.0, 0.0)
    valid[...] = inside
    column = lax.broadcasted_iota(jnp.int32, (quarter, experts), 1)
    named = jnp.where(routes[...] == column, 1.0, 0.0)
    match[...] = named
    at = lax.broadcasted_iota(jnp.int32, (quarter, quarter), 0)
    before = lax.broadcasted_iota(jnp.int32, (quarter, quarter), 1)
    lower = jnp.where(at >= before, 1.0, 0.0).astype(bf16)
    rank = jnp.sum(mm(lower, (named * inside).astype(bf16)) * named, axis=1, keepdims=True) - 1.0
    slot = jnp.where(inside > 0.0, routes[...].astype(f32) * capacity + rank, -1.0)
    slot = jnp.broadcast_to(slot, (quarter, LANES)).T[:1]
    number = lax.broadcasted_iota(jnp.int32, place.shape, 0).astype(f32)
    chosen = jnp.where(number == slot, 1.0, 0.0).astype(bf16)
    place[...] = chosen
    slots[...] = mm(chosen, grads[...].astype(bf16)).astype(bf16)


def slots_part(info, routes, grads, experts, capacity):
    quarter, width = grads.shape
    shapes = [
        shape_of((experts * capacity, quarter), bf16),
        shape_of((quarter, experts), f32),
        shape_of((quarter, 1), f32),
        shape_of((experts * capacity, width), bf16),
    ]
    return pl.pallas_call(
        lambda *refs: slots_kernel(capacity, *refs),
        in_specs=[scalars(), whole(routes.shape), whole(grads.shape)],
        out_specs=[whole(s.shape) for s in shapes],
        out_shape=shapes,
        compiler_params=params(60),
        cost_estimate=LIGHT,
        name="slots",
    )(info, routes, grads)


def project_kernel(quarter, blocks, count, share, info, came, x0, x1, x2, x3, *refs):
    shards, (small, column_gain, weight, out_weight, qkv, kaug, vt) = refs[:count], refs[count:]
    tall = shards[0].shape[0]
    width = weight.shape[0]
    for j, ref in enumerate(shards):
        start = pl.multiple_of((info[2] ^ j) * tall, tall) if count > 1 else 0
        weight[pl.ds(start, tall), :] = ref[...]
    out_weight[:LANES, :] = weight[:, 3 * LANES : 4 * LANES].T
    out_weight[LANES:, :] = weight[:, 5 * LANES :].T[DH:]
    groups = small.shape[0] // 8
    devices = came.shape[0]
    flat = came[...].reshape(devices * 8, LANES)
    lane = lax.broadcasted_iota(jnp.int32, (LANES, width), 0)
    column = lax.broadcasted_iota(jnp.int32, (LANES, width), 1)
    inside = lax.rem(column, share)
    owner = lax.broadcasted_iota(jnp.int32, (devices, 1, width), 2) - share * lax.broadcasted_iota(
        jnp.int32, (devices, 1, width), 0
    )
    owner = jnp.where((owner >= 0) & (owner < share), 1.0, 0.0)
    for k in range(groups):
        pick = jnp.where(lane == inside + k * share, 1.0, 0.0).astype(bf16)
        spread = split_dot(flat, pick, 3)
        small[8 * k : 8 * k + 8, :] = jnp.sum(spread.reshape(devices, 8, width) * owner, axis=0)
    gain = small[:1, :]
    column_gain[...] = jnp.broadcast_to(gain, (LANES, width)).T[:, :1]
    for j, ref in enumerate((x0, x1, x2, x3)):
        start = pl.multiple_of((info[0] ^ j) * quarter, quarter)
        rows = pl.ds(start, quarter)
        scaled = (ref[...].astype(f32) * gain).astype(bf16)
        first = mm(scaled, weight[:, : 3 * LANES]).astype(bf16)
        second = mm(scaled, weight[:, 4 * LANES :]).astype(bf16)
        qkv[rows, : 3 * LANES] = first
        qkv[rows, 3 * LANES :] = second
        kaug[rows, :LANES] = first[:, LANES : 2 * LANES]
        lane = lax.broadcasted_iota(jnp.int32, (quarter, LANES), 1)
        row = lax.broadcasted_iota(jnp.int32, (quarter, LANES), 0) + start
        hidden = jnp.where((lane == 0) & (row >= info[1]), masked_score, 0.0)
        kaug[rows, LANES:] = jnp.where(lane < DH, hidden, second[:, :LANES].astype(f32)).astype(bf16)
        values = first[:, 2 * LANES :].T
        vt[0, :DH, rows] = values[:DH]
        vt[1, :DH, rows] = values[DH:]
        vt[2, :DH, rows] = second[:, LANES:].T[:DH]
    full_len = quarter * blocks
    tail = (lax.broadcasted_iota(jnp.int32, (16, full_len), 0) == 0).astype(f32).astype(bf16)
    for h in range(3):
        vt[h, DH:, :] = tail


def project(info, came, rows, shards, share, experts):
    quarter, width = rows[0].shape
    blocks = len(rows)
    full_len = quarter * blocks
    shapes = [
        shape_of((8 * -(-(2 + experts) // 8), width), f32),
        shape_of((width, 1), f32),
        shape_of((width, 6 * LANES), bf16),
        shape_of((3 * DH, width), bf16),
        shape_of((full_len, 5 * LANES), bf16),
        shape_of((full_len, 2 * LANES), bf16),
        shape_of((3, DH + 16, full_len), bf16),
    ]
    arrays = (came, *rows, *shards)
    return pl.pallas_call(
        lambda *refs: project_kernel(quarter, blocks, len(shards), share, *refs),
        in_specs=[scalars()] + [whole(a.shape) for a in arrays],
        out_specs=[whole(s.shape) for s in shapes],
        out_shape=shapes,
        compiler_params=params(60),
        cost_estimate=LIGHT,
        name="project",
    )(info, *arrays)


def attention_kernel(info, qkv, kaug, vt, context, chances, totals, *sent):
    quarter = context.shape[2]
    step = pl.program_id(0)
    rows = pl.ds(pl.multiple_of(step * quarter, quarter), quarter)
    q01 = (qkv[rows, :LANES].astype(f32) * score_scale).T.astype(bf16)
    q2 = (qkv[rows, 3 * LANES : 4 * LANES].astype(f32) * score_scale).T.astype(bf16)[:DH]
    ones = (lax.broadcasted_iota(jnp.int32, (DH, quarter), 0) == 0).astype(f32).astype(bf16)
    zeros = jnp.zeros((DH, quarter), bf16)
    queries = (
        jnp.concatenate([q01[:DH], zeros, ones, zeros], axis=0),
        jnp.concatenate([zeros, q01[DH:], ones, zeros], axis=0),
        jnp.concatenate([zeros, zeros, ones, q2], axis=0),
    )
    full_len = kaug.shape[0]
    all_scores = [mm(kaug[...], queries[h]) for h in range(3)]
    for h in range(3):
        scores = all_scores[h]
        top = jnp.max(jnp.max(scores.reshape(8, full_len // 8, quarter), axis=0), axis=0, keepdims=True)
        low = jnp.exp(scores - top).astype(bf16)
        chances[h] = low
        summed = mm(vt[h], low)
        part = 1.0 / summed[DH : DH + 1]
        totals[0, h : h + 1, :] = part
        context[0, h * DH : (h + 1) * DH, :] = (summed[:DH] * part).astype(bf16)
    for j, ref in enumerate(sent):

        @pl.when(step == info[0] ^ j)
        def _():
            ref[...] = context[0]


def attention_forward(info, qkv, kaug, vt, blocks):
    full_len = qkv.shape[0]
    quarter = full_len // blocks
    inner = 3 * DH
    return pl.pallas_call(
        attention_kernel,
        grid=(blocks,),
        in_specs=[scalars(), whole(qkv.shape), whole(kaug.shape), whole(vt.shape)],
        out_specs=[
            pl.BlockSpec((1, inner, quarter), lambda i: (i, 0, 0)),
            pl.BlockSpec((3, full_len, quarter), lambda i: (0, 0, i)),
            pl.BlockSpec((1, 3, quarter), lambda i: (i, 0, 0)),
        ]
        + [whole((inner, quarter))] * blocks,
        out_shape=[
            shape_of((blocks, inner, quarter), bf16),
            shape_of((3, full_len, full_len), bf16),
            shape_of((blocks, 3, quarter), f32),
        ]
        + [shape_of((inner, quarter), bf16)] * blocks,
        compiler_params=params(60),
        cost_estimate=LIGHT,
        name="attend",
    )(info, qkv, kaug, vt)


def turn_kernel(quarter, blocks, info, x0, x1, x2, x3, qkv, context, xt, kt, q2, cn):
    for j, ref in enumerate((x0, x1, x2, x3)):
        xt[info[0] ^ j] = ref[...].T
    for j in range(blocks):
        rows = slice(j * quarter, (j + 1) * quarter)
        third = qkv[rows, 3 * LANES : 4 * LANES].T
        kt[:LANES, rows] = qkv[rows, LANES : 2 * LANES].T
        kt[LANES:, rows] = third[DH:]
        zeros = jnp.zeros((DH, quarter), bf16)
        q2[rows, :] = jnp.concatenate([zeros, third[:DH]], axis=0).T
        cn[rows, :LANES] = context[j, :LANES, :].T
        cn[rows, LANES:] = jnp.concatenate([zeros, context[j, LANES:, :]], axis=0).T


def turn(info, rows, qkv, context):
    quarter, width = rows[0].shape
    blocks = len(rows)
    full_len = quarter * blocks
    shapes = [
        shape_of((blocks, width, quarter), bf16),
        shape_of((3 * DH, full_len), bf16),
        shape_of((full_len, LANES), bf16),
        shape_of((full_len, 2 * LANES), bf16),
    ]
    return pl.pallas_call(
        lambda *refs: turn_kernel(quarter, blocks, *refs),
        in_specs=[scalars()] + [whole((quarter, width))] * 4 + [whole(qkv.shape), whole(context.shape)],
        out_specs=[whole(s.shape) for s in shapes],
        out_shape=shapes,
        compiler_params=params(60),
        cost_estimate=LIGHT,
        name="turn",
    )(info, *rows, qkv, context)


def two_columns(column):
    high = column.astype(bf16).astype(f32)
    lane = lax.broadcasted_iota(jnp.int32, (column.shape[0], LANES), 1)
    return jnp.where(lane == 0, high, jnp.where(lane == 1, column - high, 0.0)).astype(bf16)


def middle_kernel(
    rows, c0, c1, c2, c3, w0, w1, w2, w3, small, place, match, valid, middle, root, chances, gate, slots
):
    gain, router = small[1:2, :], small[2 : 2 + match.shape[1], :]
    total = rows[...]
    for context, weight in zip((c0, c1, c2, c3), (w0, w1, w2, w3)):
        total = total + mm_tn(context[...], weight[...])
    middle[...] = total
    scale = norm_root(total)
    root[...] = scale
    hidden = total * scale * gain
    scores = mm_nt(hidden, router, HIGHEST)
    powers = jnp.exp(scores - jnp.max(scores, axis=-1, keepdims=True))
    share = powers / jnp.sum(powers, axis=-1, keepdims=True)
    chances[...] = share
    own = jnp.sum(share * match[...], axis=-1, keepdims=True)
    gate[...] = own
    width = rows.shape[1]
    slots[:, :width] = mm(place[...], hidden.astype(bf16)).astype(bf16)
    slots[:, width:] = mm(place[...], two_columns(own * valid[...])).astype(bf16)


def middle_part(rows, contexts, out_weights, small, place, match, valid):
    quarter, width = rows.shape
    experts = match.shape[1]
    shapes = [
        shape_of((quarter, width), f32),
        shape_of((quarter, 1), f32),
        shape_of((quarter, experts), f32),
        shape_of((quarter, 1), f32),
        shape_of((place.shape[0], width + LANES), bf16),
    ]
    arrays = (rows, *contexts, *out_weights, small, place, match, valid)
    return pl.pallas_call(
        middle_kernel,
        in_specs=[whole(a.shape) for a in arrays],
        out_specs=[whole(s.shape) for s in shapes],
        out_shape=shapes,
        compiler_params=params(60),
        cost_estimate=LIGHT,
        name="middle",
    )(*arrays)


def expert_kernel(rows, grads, *refs):
    count = (len(refs) - 4) // 2
    early_parts, late_parts = refs[:count], refs[count : 2 * count]
    out, back, held, arrived = refs[2 * count :]
    width = grads.shape[1]
    early = early_parts[0].shape[0]
    ends = (slice(0, early), slice(early, 2 * width))
    copies = [
        [
            pltpu.make_async_copy(ref, held.at[i, end, :], arrived.at[i, k])
            for k, (ref, end) in enumerate(zip(pair, ends))
        ]
        for i, pair in enumerate(zip(early_parts, late_parts))
    ]
    for pair in copies:
        for copy in pair:
            copy.start()
    out_total, back_total = None, None
    for i, pair in enumerate(copies):
        for copy in pair:
            copy.wait()
        grad = mm(grads[...], held[i, width:, :])
        active, slope = gelu_pair(mm(rows[:, :width], held[i, :width, :]))
        part = mm_nt(active.astype(bf16), held[i, width:, :])
        back_part = mm_nt((grad * slope).astype(bf16), held[i, :width, :])
        out_total = part if i == 0 else out_total + part
        back_total = back_part if i == 0 else back_total + back_part
    result = out_total.astype(bf16)
    out[...] = result
    back[:, :width] = back_total.astype(bf16)
    match = jnp.sum(grads[...].astype(f32) * result.astype(f32), axis=-1, keepdims=True)
    back[:, width:] = two_columns(match)


def expert_part(rows, grads, early_parts, late_parts):
    slots, width = grads.shape
    hidden = early_parts[0].shape[1]
    count = len(early_parts)
    shapes = [shape_of((slots, width), bf16), shape_of((slots, width + LANES), bf16)]
    return pl.pallas_call(
        expert_kernel,
        in_specs=[whole(rows.shape), whole(grads.shape)] + [pl.BlockSpec(memory_space=pl.ANY)] * (2 * count),
        out_specs=[whole(s.shape) for s in shapes],
        out_shape=shapes,
        scratch_shapes=[pltpu.VMEM((count, 2 * width, hidden), bf16), pltpu.SemaphoreType.DMA((count, 2))],
        compiler_params=params(60),
        cost_estimate=LIGHT,
        name="experts",
    )(rows, grads, *early_parts, *late_parts)


def expert_grad_kernel(count, *refs):
    rows, grads = refs[:count], refs[count : 2 * count]
    near_in, near_out, out, square, weight, row_all, grad_all, inner_all, active_all, arrived = refs[2 * count :]
    early = near_in.shape[0]
    ends = (slice(0, early), slice(early, weight.shape[0]))
    copies = [
        pltpu.make_async_copy(ref, weight.at[end, :], arrived.at[i])
        for i, (ref, end) in enumerate(zip((near_in, near_out), ends))
    ]
    for copy in copies:
        copy.start()
    for copy in copies:
        copy.wait()
    slots, width = grads[0].shape
    for j in range(count):
        at = slice(j * slots, (j + 1) * slots)
        gate = rows[j][:, width : width + 1].astype(f32) + rows[j][:, width + 1 : width + 2].astype(f32)
        row_all[at, :] = rows[j][:, :width]
        grad_all[at, :] = (grads[j][...].astype(f32) * gate).astype(bf16)
        back = mm(grads[j][...], weight[width:, :])
        active, slope = gelu_pair(mm(rows[j][:, :width], weight[:width, :]))
        inner_all[at, :] = (back * slope * gate).astype(bf16)
        active_all[at, :] = active.astype(bf16)
    first = mm_tn(row_all[...], inner_all[...])
    out[0] = first.astype(bf16)
    second = mm_tn(grad_all[...], active_all[...])
    out[1] = second.astype(bf16)
    square[...] = jnp.sum(first * first + second * second, axis=0, keepdims=True)


def expert_gradient(rows, grads, near_in, near_out):
    count = len(rows)
    slots, width = grads[0].shape
    hidden = near_in.shape[1]
    arrays = (*rows, *grads)
    shapes = [
        shape_of((2, width, hidden), bf16),
        shape_of((1, hidden), f32),
    ]
    return pl.pallas_call(
        lambda *refs: expert_grad_kernel(count, *refs),
        in_specs=[whole(a.shape) for a in arrays] + [pl.BlockSpec(memory_space=pl.ANY)] * 2,
        out_specs=[whole(s.shape) for s in shapes],
        out_shape=shapes,
        scratch_shapes=[pltpu.VMEM((2 * width, hidden), bf16)]
        + [pltpu.VMEM((count * slots, width), bf16)] * 2
        + [pltpu.VMEM((count * slots, hidden), bf16)] * 2
        + [pltpu.SemaphoreType.DMA((2,))],
        compiler_params=params(60),
        cost_estimate=LIGHT,
        name="expert_gradient",
    )(*arrays, near_in, near_out)


def pack_small(small, cut):
    devices = cut.shape[0]
    rows, width = small.shape
    share = width // devices
    groups = rows // 8
    column = lax.broadcasted_iota(jnp.int32, (devices, 1, width), 2)
    owner = column - share * lax.broadcasted_iota(jnp.int32, (devices, 1, width), 0)
    owner = jnp.where((owner >= 0) & (owner < share), 1.0, 0.0)
    lane = lax.broadcasted_iota(jnp.int32, (width, LANES), 1)
    inside = lax.rem(lax.broadcasted_iota(jnp.int32, (width, LANES), 0), share)
    total = None
    for k in range(groups):
        pick = jnp.where(lane == inside + k * share, 1.0, 0.0).astype(bf16)
        spread = (small[8 * k : 8 * k + 8, :][None] * owner).reshape(devices * 8, width)
        part = split_dot(spread, pick, 2)
        total = part if total is None else total + part
    cut[...] = total.reshape(devices, 8, LANES)


def return_kernel(
    back, place, middle, root, chances, gate, match, cotangent, small, w0, w1, w2, w3,
    grad, turned, cut, p0, p1, p2, p3, small_grad,
):
    experts = match.shape[1]
    gain, router = small[1:2, :], small[2 : 2 + experts, :]
    width = middle.shape[1]
    came = mm_tn(place[...], back[...])
    gate_grad = came[:, width : width + 1] + came[:, width + 1 : width + 2]
    own = gate[...]
    score_grad = own * (match[...] - chances[...]) * gate_grad
    scaled = middle[...] * root[...]
    hidden = scaled * gain
    tall = small_grad.shape[0]
    small_grad[1 : 1 + experts, :] = mm_tn(score_grad, hidden, HIGHEST)
    small_grad[1 + experts :, :] = jnp.zeros((tall - 1 - experts, hidden.shape[1]), f32)
    second = own * came[:, :width] + jnp.dot(
        score_grad, router, precision=HIGHEST, preferred_element_type=f32
    )
    small_grad[:1, :] = jnp.sum(second * scaled, axis=0, keepdims=True)
    inner = second * gain
    centre = jnp.mean(inner * scaled, axis=-1, keepdims=True)
    total = cotangent[...] + root[...] * (inner - scaled * centre)
    grad[...] = total
    low = total.astype(bf16)
    turned[...] = low.T
    for ref, weight in zip((p0, p1, p2, p3), (w0, w1, w2, w3)):
        ref[...] = mm_nt(weight[...], low).astype(bf16)
    pack_small(small_grad, cut)


def return_part(back, place, middle, root, chances, gate, match, cotangent, small, out_weights, device_count):
    quarter, width = middle.shape
    experts = match.shape[1]
    inner = out_weights[0].shape[0]
    shapes = [
        shape_of((quarter, width), f32),
        shape_of((width, quarter), bf16),
        shape_of((device_count, 8, LANES), f32),
    ] + [shape_of((inner, quarter), bf16)] * len(out_weights)
    arrays = (back, place, middle, root, chances, gate, match, cotangent, small, *out_weights)
    return pl.pallas_call(
        return_kernel,
        in_specs=[whole(a.shape) for a in arrays],
        out_specs=[whole(s.shape) for s in shapes],
        out_shape=shapes,
        scratch_shapes=[pltpu.VMEM((8 * -(-(1 + experts) // 8), width), f32)],
        compiler_params=params(60),
        cost_estimate=LIGHT,
        name="returned",
    )(*arrays)


def attention_back_kernel(
    blocks, info, g0, g1, g2, g3, context, chances, totals, qkv, kt, q2, packed, grads, vaug, k01, k2, v01, v2
):
    step = pl.program_id(0)
    quarter = grads.shape[2]

    @pl.when(step == 0)
    def _():
        for j, ref in enumerate((g0, g1, g2, g3)):
            grads[info[0] ^ j] = ref[...]
        vaug[:, :LANES] = qkv[:, 2 * LANES : 3 * LANES]
        lane = lax.broadcasted_iota(jnp.int32, (vaug.shape[0], LANES), 1)
        ones = jnp.where(lane < DH + 2, 1.0, 0.0)
        vaug[:, LANES:] = jnp.where(lane < DH, qkv[:, 4 * LANES :].astype(f32), ones).astype(bf16)
        for ref in (k01, k2, v01, v2):
            ref[...] = jnp.zeros(ref.shape, f32)

    rows = pl.ds(pl.multiple_of(step * quarter, quarter), quarter)
    raw = grads[step].astype(f32)
    scale = totals[0]
    scaled = [raw[h * DH : (h + 1) * DH] * scale[h : h + 1] for h in range(3)]
    heads = jnp.concatenate(scaled, axis=0).astype(bf16)
    lane = lax.broadcasted_iota(jnp.int32, (quarter, LANES), 1)
    row = lax.broadcasted_iota(jnp.int32, (DH, quarter), 0)
    zeros = jnp.zeros((DH, quarter), bf16)
    q01 = qkv[rows, :LANES].astype(f32)
    g01 = heads[:LANES].T.astype(f32)
    third = jnp.concatenate([heads[LANES:], zeros], axis=0).T
    query_parts = []
    for h in range(3):
        part = heads[h * DH : (h + 1) * DH]
        centre = -jnp.sum(
            part.astype(f32) * context[0, h * DH : (h + 1) * DH, :].astype(f32), axis=0, keepdims=True
        )
        high = centre.astype(bf16).astype(f32)
        tail = jnp.where(row == 0, high, jnp.where(row == 1, centre - high, 0.0)).astype(bf16)
        pieces = [zeros, zeros, zeros, tail]
        pieces[h] = part
        chance_grad = mm(vaug[...], jnp.concatenate(pieces, axis=0))
        low = chances[h]
        score_grad = (low.astype(f32) * chance_grad).astype(bf16)
        query_parts.append(mm(kt[h * DH : (h + 1) * DH, :], score_grad) * score_scale)
        if h < 2:
            inside = (lane >= h * DH) & (lane < (h + 1) * DH)
            k01[...] += mm(score_grad, jnp.where(inside, q01, 0.0).astype(bf16))
            v01[...] += mm(low, jnp.where(inside, g01, 0.0).astype(bf16))
        else:
            k2[...] += mm(score_grad, q2[rows, :])
            v2[...] += mm(low, third)
    packed[rows, :LANES] = jnp.concatenate(query_parts[:2], axis=0).T.astype(bf16)
    packed[rows, 4 * LANES : 5 * LANES] = (
        jnp.concatenate([query_parts[2], jnp.zeros((DH, quarter), f32)], axis=0).T.astype(bf16)
    )

    @pl.when(step == blocks - 1)
    def _():
        packed[:, LANES : 2 * LANES] = (k01[...] * score_scale).astype(bf16)
        packed[:, 2 * LANES : 3 * LANES] = v01[...].astype(bf16)
        packed[:, 3 * LANES : 4 * LANES] = jnp.zeros(k01.shape, bf16)
        packed[:, 4 * LANES : 5 * LANES] = packed[:, 4 * LANES : 5 * LANES] + (k2[...] * score_scale).astype(bf16)
        packed[:, 5 * LANES :] = v2[...].astype(bf16)


def attention_backward(info, grads, context, chances, totals, qkv, kt, q2):
    blocks, inner, quarter = context.shape
    full_len = quarter * blocks
    block = pl.BlockSpec((1, inner, quarter), lambda i: (i, 0, 0))
    return pl.pallas_call(
        lambda *refs: attention_back_kernel(blocks, *refs),
        grid=(blocks,),
        in_specs=[
            scalars(),
            *[whole((inner, quarter))] * blocks,
            block,
            pl.BlockSpec((3, full_len, quarter), lambda i: (0, 0, i)),
            pl.BlockSpec((1, 3, quarter), lambda i: (i, 0, 0)),
            whole(qkv.shape),
            whole(kt.shape),
            whole(q2.shape),
        ],
        out_specs=whole((full_len, 6 * LANES)),
        out_shape=shape_of((full_len, 6 * LANES), bf16),
        scratch_shapes=[pltpu.VMEM(context.shape, bf16), pltpu.VMEM((full_len, 2 * LANES), bf16)]
        + [pltpu.VMEM((full_len, LANES), f32)] * 4,
        compiler_params=params(60),
        cost_estimate=LIGHT,
        name="attend_back",
    )(info, *grads, context, chances, totals, qkv, kt, q2)


def weight_grad_kernel(blocks, info, xt, packed, g0, g1, g2, g3, cn, weight, gain, out, gain_grad):
    quarter = xt.shape[2]
    total, outer = None, None
    for j, ref in enumerate((g0, g1, g2, g3)):
        rows = slice(j * quarter, (j + 1) * quarter)
        there = pl.ds(pl.multiple_of((info[0] ^ j) * quarter, quarter), quarter)
        part = mm(xt[j], packed[rows, :])
        own = mm(ref[...], cn[there, :])
        total = part if total is None else total + part
        outer = own if outer is None else outer + own
    gain_grad[...] = jnp.sum(total * weight[...].astype(f32), axis=1, keepdims=True)
    total = total * gain[...]
    out[:, : 3 * LANES] = total[:, : 3 * LANES].astype(bf16)
    out[:, 3 * LANES : 4 * LANES] = outer[:, :LANES].astype(bf16)
    out[:, 4 * LANES : 5 * LANES] = total[:, 4 * LANES : 5 * LANES].astype(bf16)
    out[:, 5 * LANES :] = (total[:, 5 * LANES :] + outer[:, LANES:]).astype(bf16)


def weight_gradient(info, xt, packed, grads, cn, weight, gain):
    blocks, width, quarter = xt.shape
    tall = 256
    full_len = quarter * blocks
    return pl.pallas_call(
        lambda *refs: weight_grad_kernel(blocks, *refs),
        grid=(width // tall,),
        in_specs=[
            scalars(),
            pl.BlockSpec((blocks, tall, quarter), lambda i: (0, i, 0)),
            whole(packed.shape),
            *[pl.BlockSpec((tall, quarter), lambda i: (i, 0))] * blocks,
            whole(cn.shape),
            pl.BlockSpec((tall, 6 * LANES), lambda i: (i, 0)),
            pl.BlockSpec((tall, 1), lambda i: (i, 0)),
        ],
        out_specs=[pl.BlockSpec((tall, 6 * LANES), lambda i: (i, 0)), pl.BlockSpec((tall, 1), lambda i: (i, 0))],
        out_shape=[shape_of((width, 6 * LANES), bf16), shape_of((width, 1), f32)],
        compiler_params=params(60),
        cost_estimate=LIGHT,
        name="weight_gradient",
    )(info, xt, packed, *grads, cn, weight, gain)


def input_grad_kernel(quarter, info, packed, weight, *parts):
    for j, ref in enumerate(parts):
        rows = pl.ds(pl.multiple_of((info[0] ^ j) * quarter, quarter), quarter)
        ref[...] = mm_nt(packed[rows, :], weight[...]).astype(bf16)


def input_gradient(info, packed, weight, blocks):
    quarter = packed.shape[0] // blocks
    shapes = [shape_of((quarter, weight.shape[0]), bf16)] * blocks
    return pl.pallas_call(
        lambda *refs: input_grad_kernel(quarter, *refs),
        in_specs=[scalars(), whole(packed.shape), whole(weight.shape)],
        out_specs=[whole(s.shape) for s in shapes],
        out_shape=shapes,
        compiler_params=params(60),
        cost_estimate=LIGHT,
        name="input_gradient",
    )(info, packed, weight)


def sums_kernel(came, squares, small, gain_grad, gradient, payload, small_sum):
    count = came.shape[0]
    total = came[0].astype(f32)
    for i in range(1, count):
        total = total + came[i].astype(f32)
    gradient[...] = total
    own = jnp.sum(small[...], axis=0)
    square = (
        jnp.sum(total * total, keepdims=True)
        + jnp.sum(squares[...], keepdims=True)
        + jnp.sum(own * own, keepdims=True)
    )
    small_sum[...] = own
    rows = gain_grad.shape[0]
    row = lax.broadcasted_iota(jnp.int32, (8, LANES), 0)
    gain = jnp.concatenate([gain_grad[...], jnp.zeros((8 - rows, LANES), f32)], axis=0)
    payload[...] = jnp.broadcast_to(jnp.where(row < rows, gain, square)[None], payload.shape)


def sums_part(came, squares, small, gain_grad, device_count):
    shapes = [
        shape_of(came.shape[1:], f32),
        shape_of((device_count, 8, LANES), f32),
        shape_of((8, LANES), f32),
    ]
    arrays = (came, squares, small, gain_grad)
    return pl.pallas_call(
        sums_kernel,
        in_specs=[whole(a.shape) for a in arrays],
        out_specs=[whole(s.shape) for s in shapes],
        out_shape=shapes,
        compiler_params=params(60),
        cost_estimate=LIGHT,
        name="sums",
    )(*arrays)


def adam_kernel(lanes, share, expert_rates, info, last, small_sum, *refs):
    held, outs, factor = refs[:14], refs[14:27], refs[27]
    dense, dense_grad, gains, router = held[:3], held[3], held[4:7], held[7:10]
    weight, first, second, gradient = held[10:14]
    norm_out, outs = outs[0], outs[1:]
    dense_out, gains_out, router_out, expert_out = outs[:3], outs[3:6], outs[6:9], outs[9:12]
    matrix, part = pl.program_id(0), pl.program_id(1)
    experts = router[0].shape[0]

    @pl.when((matrix == 0) & (part == 0))
    def _():
        total = jnp.sum(last[...], axis=0)
        row = lax.broadcasted_iota(jnp.int32, (8, LANES), 0)
        squares = jnp.sum(jnp.where(row < lanes, total * total, 0.0), keepdims=True)
        norm = jnp.sqrt(squares + total[7:8, :1])
        scale = jnp.minimum(1.0, clip_limit / (norm + norm_epsilon))
        norm_out[...] = norm
        factor[...] = jnp.broadcast_to(scale, (8, LANES))
        rates = (0.71 / math.sqrt(D), 0.71 / math.sqrt(D), 0.83 / math.sqrt(D), 0.79 / math.sqrt(H * DH))
        for i, rate in enumerate(rates):
            grad = jnp.concatenate(
                [
                    dense_grad[:, i * LANES : (i + 1) * LANES],
                    dense_grad[:, 4 * LANES + i * DH : 4 * LANES + (i + 1) * DH],
                ],
                axis=1,
            )
            result = adam_update(*[ref[i] for ref in dense], grad * scale, rate)
            for ref, value in zip(dense_out, result):
                ref[i] = value
        column = lax.broadcasted_iota(jnp.int32, (LANES, LANES), 1)
        place = lax.broadcasted_iota(jnp.int32, (LANES, LANES), 0) - info[3] * share
        own = jnp.zeros((8, LANES), f32)
        for i in range(lanes):
            pick = jnp.where((column == place + i * LANES) & (column < share), 1.0, 0.0)
            own = own + jnp.dot(
                jnp.broadcast_to(total[i : i + 1], (8, LANES)), pick, precision=HIGHEST, preferred_element_type=f32
            )
        groups = -(-(1 + experts) // 8)
        table = small_sum[...]
        table = jnp.concatenate([table[:, k * share : (k + 1) * share] for k in range(groups)], axis=0)
        grad = jnp.concatenate([own[:1, :share], table[:1]], axis=0)
        for ref, value in zip(gains_out, adam_update(*[ref[...] for ref in gains], grad * scale, 0.5)):
            ref[...] = value
        grad = table[1 : 1 + experts]
        result = adam_update(*[ref[...] for ref in router], grad * scale, 0.24 / math.sqrt(D))
        for ref, value in zip(router_out, result):
            ref[...] = value

    rate = jnp.where(matrix == 0, expert_rates[0], expert_rates[1])
    grad = gradient[...].astype(f32) * factor[:1, :1]
    result = adam_update(weight[...], first[...], second[...], grad, rate)
    for ref, value in zip(expert_out, result):
        ref[...] = value


def adam(info, last, small_sum, dense, dense_grad, gains, router, expert, expert_grad, rates):
    _, tall, wide = expert_grad.shape
    parts = 4
    block = pl.BlockSpec((1, tall // parts, wide), lambda i, j: (i, j, 0))
    small = [*dense, *gains, *router]
    shapes = [shape_of((1, 1), f32)] + [shape_of(a.shape, f32) for a in small]
    ins = (last, small_sum, *dense, dense_grad, *gains, *router)
    return pl.pallas_call(
        lambda *refs: adam_kernel(tall // LANES, gains[0].shape[1], rates, *refs),
        grid=(2, parts),
        in_specs=[scalars()] + [whole(a.shape) for a in ins] + [block] * 4,
        out_specs=[whole(a.shape) for a in shapes] + [block] * 3,
        out_shape=shapes + [shape_of(expert_grad.shape, f32)] * 3,
        scratch_shapes=[pltpu.VMEM((8, LANES), f32)],
        compiler_params=params(60),
        cost_estimate=LIGHT,
        name="adam",
    )(info, *ins, *expert, expert_grad)


def tie(*values):
    return lax.optimization_barrier(values)


def on_device(
    inputs,
    cotangent,
    lengths,
    routes,
    attention_weight,
    attention_mean,
    attention_square,
    expert_weight,
    expert_mean,
    expert_square,
    router_matrix,
    router_mean,
    router_square,
    norm_gains,
    gains_mean,
    gains_square,
):
    quarter, width = inputs.shape[1:]
    dp_count, tensor_count = lax.axis_size(DP), lax.axis_size(TENSOR)
    device_count = dp_count * tensor_count
    expert_count = router_matrix.shape[1]
    capacity = max(2, (5 * quarter + 4 * expert_count - 1) // (4 * expert_count))
    own_dp, own_tensor = lax.axis_index(DP), lax.axis_index(TENSOR)
    share = router_matrix.shape[0]
    rows, grad_rows, length = inputs[0], cotangent[0], lengths[0]
    info = jnp.stack([own_tensor, length, own_dp, lax.axis_index(EVERYONE)]).astype(jnp.int32)

    scaled_one, root_one, weight_own, payload = prologue(
        rows, attention_weight, norm_gains, router_matrix.T, device_count
    )
    block_two = swap(scaled_one, TENSOR, 2)
    small_came = lax.all_to_all(payload, EVERYONE, 0, 0, tiled=True)
    expert_flat = expert_weight[0].reshape(2 * width, -1)
    early_own, late_own = expert_flat[:EARLY].astype(bf16), expert_flat[EARLY:].astype(bf16)
    place, match, valid_scale, grad_slots = slots_part(info, routes[0], grad_rows, expert_count, capacity)
    if dp_count == 8:
        w4, w2, w1 = [swap(weight_own, DP, mask) for mask in (4, 2, 1)]
        w4, w2, w1, small_came, block_two, early_own = tie(w4, w2, w1, small_came, block_two, early_own)
        w6, w5, w3 = swap(w4, DP, 2), swap(w4, DP, 1), swap(w2, DP, 1)
        w6, w5, w3, scaled_one = tie(w6, w5, w3, scaled_one)
        w7, grad_slots = tie(swap(w6, DP, 1), grad_slots)
        shards = [weight_own, w1, w2, w3, w4, w5, w6, w7]
    else:
        weight_own, grad_slots, small_came, block_two, early_own = tie(
            weight_own, grad_slots, small_came, block_two, early_own
        )
        shards = [lax.all_gather(weight_own, DP, axis=0, tiled=True)]
    early_far = swap(early_own, TENSOR, 2)
    row_blocks = [scaled_one, swap(scaled_one, TENSOR, 1), block_two, swap(block_two, TENSOR, 1)]

    slot_count = expert_count * capacity

    def trade(values):
        blocks = values.reshape(expert_count, capacity, values.shape[1])
        return lax.all_to_all(blocks, DP, 0, 0, tiled=True).reshape(values.shape)

    expert_grads = trade(grad_slots)
    small, gain_column, weight, out_weight, qkv, keys_wide, values_turned = project(
        info, small_came, row_blocks, shards, share, expert_count
    )
    out_weight, early_own = tie(out_weight, early_own)
    out_near, out_far = swap(out_weight, TENSOR, 1), swap(out_weight, TENSOR, 2)
    early_near = swap(early_own, TENSOR, 1)
    context, chances, totals, *sent = attention_forward(info, qkv, keys_wide, values_turned, tensor_count)
    expert_grads, early_far, out_near, out_far, *sent = tie(expert_grads, early_far, out_near, out_far, *sent)
    contexts = [sent[0]] + [swap(sent[j], TENSOR, j) for j in range(1, tensor_count)]
    out_weights = [out_weight, out_near, out_far, swap(out_far, TENSOR, 1)]
    late_own, early_far, *contexts = tie(late_own, early_far, *contexts)
    late_far = swap(late_own, TENSOR, 2)

    middle, root_two, shares, gate, slots = middle_part(
        rows, contexts, out_weights, small, place, match, valid_scale
    )
    qkv, slots, late_own = tie(qkv, slots, late_own)
    expert_rows = trade(slots)
    turned_rows, keys_turned, third_query, context_rows = turn(info, row_blocks, qkv, context)
    early_parts = [early_own, early_far, early_near, swap(early_far, TENSOR, 1)]
    turned_rows, late_far = tie(turned_rows, late_far)
    late_parts = [late_own, late_far, swap(late_own, TENSOR, 1), swap(late_far, TENSOR, 1)]
    expert_rows, turned_rows = tie(expert_rows, turned_rows)
    expert_outs, expert_back = expert_part(expert_rows, expert_grads, early_parts, late_parts)
    expert_rows, expert_back = tie(expert_rows, expert_back)
    rows_near, rows_far = swap(expert_rows, TENSOR, 1), swap(expert_rows, TENSOR, 2)
    rows_far, expert_grads = tie(rows_far, expert_grads)
    rows_all = [expert_rows, rows_near, rows_far, swap(rows_far, TENSOR, 1)]
    grads_near, grads_far = swap(expert_grads, TENSOR, 1), swap(expert_grads, TENSOR, 2)
    expert_back, rows_all = tie(trade(expert_back), rows_all)

    middle_grad, middle_turned, small_cut, *parts = return_part(
        expert_back, place, middle, root_two, shares, gate, match, grad_rows, small, out_weights, device_count
    )
    expert_outs, middle_turned, *parts = tie(expert_outs, middle_turned, *parts)
    context_grads = [parts[0]] + [swap(parts[j], TENSOR, j) for j in range(1, tensor_count)]
    expert_outs = trade(expert_outs)
    middle_turned, *context_grads = tie(middle_turned, *context_grads)
    middle_near, middle_far = swap(middle_turned, TENSOR, 1), swap(middle_turned, TENSOR, 2)

    packed = attention_backward(info, context_grads, context, chances, totals, qkv, keys_turned, third_query)
    packed, middle_far, grads_far, small_cut, expert_outs = tie(packed, middle_far, grads_far, small_cut, expert_outs)
    middle_all = [middle_turned, middle_near, middle_far, swap(middle_far, TENSOR, 1)]
    grads_all = [expert_grads, grads_near, grads_far, swap(grads_far, TENSOR, 1)]
    small_grads = lax.all_to_all(small_cut, EVERYONE, 0, 0, tiled=True)
    weight_grad, gain_one_grad = weight_gradient(
        info, turned_rows, packed, middle_all, context_rows, weight, gain_column
    )
    weight_grad, early_own, small_grads = tie(weight_grad, early_own, small_grads)
    weight_came = lax.all_to_all(weight_grad.reshape(dp_count, -1, width), DP, 0, 0, tiled=True)
    expert_grad, expert_squares = expert_gradient(rows_all, grads_all, early_own, late_own)
    expert_squares, packed = tie(expert_squares, packed)

    input_parts = input_gradient(info, packed, weight, tensor_count)
    first_half = input_parts[0].astype(f32) + swap(input_parts[1], TENSOR, 1).astype(f32)
    second_half = (input_parts[2].astype(f32) + swap(input_parts[3], TENSOR, 1).astype(f32)).astype(bf16)

    second_came = swap(second_half, TENSOR, 2)
    dense_grad, last, small_sum = sums_part(
        weight_came, expert_squares, small_grads, gain_one_grad.reshape(-1, LANES), device_count
    )
    last, expert_outs, middle_grad, rows_late = tie(last, expert_outs, middle_grad, rows)
    last_all = lax.all_to_all(last, EVERYONE, 0, 0, tiled=True)
    input_grad = middle_grad + norm_backward(
        rows_late, root_one, small[:1], first_half + second_came.astype(f32)
    )
    picked = mm_tn(place, expert_outs)
    branch = gate * valid_scale * picked
    block_output = middle + branch
    last_all, input_grad, block_output, branch = tie(last_all, input_grad, block_output, branch)

    rates = (0.4 * math.sqrt(expert_count / D), 1.38 * math.sqrt(expert_count / FF))
    norm, *updated = adam(
        info,
        last_all,
        small_sum,
        (attention_weight, attention_mean, attention_square),
        dense_grad,
        (norm_gains, gains_mean, gains_square),
        (router_matrix.T, router_mean.T, router_square.T),
        (expert_weight[0], expert_mean[0], expert_square[0]),
        expert_grad,
        rates,
    )
    attention_new, gains_new, router_new, expert_new = updated[:3], updated[3:6], updated[6:9], updated[9:]
    router_new = [part.T for part in router_new]
    grad_norm = norm.reshape(())
    return (
        block_output[None],
        input_grad[None],
        grad_norm,
        *attention_new,
        *[part[None] for part in expert_new],
        *router_new,
        *gains_new,
        branch[None],
    )


def solution(mesh):
    names = mesh.axis_names
    dp_count, tensor_count = mesh.shape[names[0]], mesh.shape[names[1]]
    cut = jax.sharding.Mesh(mesh.devices.reshape(dp_count // 2, 2, tensor_count // 2, 2), EVERYONE)
    rows = P(DP, TENSOR, None)
    attention = P(None, DP, TENSOR)
    expert = P(DP, None, None, TENSOR)
    router = P(EVERYONE, None)
    gains = P(None, EVERYONE)
    weights = (attention,) * 3 + (expert,) * 3 + (router,) * 3 + (gains,) * 3
    return jax.shard_map(
        on_device,
        mesh=cut,
        in_specs=(rows, rows, P(DP), rows) + weights,
        out_specs=(rows, rows, P()) + weights + (rows,),
        check_vma=False,
    )
```

```python
import math

import jax
import jax.numpy as jnp
from jax import lax
from jax.experimental import pallas as pl
from jax.experimental.pallas import tpu as pltpu
from jax.sharding import PartitionSpec as P

D = 768
H = 12
DH = 64
FF = 3072
STEP = 10

HIGHEST = lax.Precision.HIGHEST
norm_epsilon = 1e-06
beta_first = 0.9
beta_second = 0.999
adam_epsilon = 1e-08
decay_factor = 0.01
clip_limit = 1.0
masked_score = -1e30
score_scale = 1.0 / math.sqrt(DH)
bf16 = jnp.bfloat16
f32 = jnp.float32
MIB = 1 << 20
LANES = 128
EARLY = 944


DP = ("dh", "dl")
TENSOR = ("th", "tl")
EVERYONE = DP + TENSOR


def swap(values, axis, mask):
    count = lax.axis_size(axis)
    return lax.ppermute(values, axis, [(i, i ^ mask) for i in range(count)])


def bits_of(count):
    return [1 << b for b in range(count.bit_length() - 1)]


def gather_relative(block, axis, order):
    held = {0: block}
    for mask in order:
        for j in list(held):
            held[j ^ mask] = swap(held[j], axis, mask)
    return [held[j] for j in range(len(held))]


def mm(a, b):
    return jnp.dot(a, b, preferred_element_type=f32)


def mm_nt(a, b, precision=None):
    return lax.dot_general(
        a, b, (((1,), (1,)), ((), ())), preferred_element_type=f32, precision=precision
    )


def mm_tn(a, b, precision=None):
    return lax.dot_general(
        a, b, (((0,), (0,)), ((), ())), preferred_element_type=f32, precision=precision
    )


def norm_root(values):
    return lax.rsqrt(jnp.mean(values * values, axis=-1, keepdims=True) + norm_epsilon)


def norm_backward(values, root, gain_row, grad):
    scaled = values * root
    inner = grad * gain_row
    centre = jnp.mean(inner * scaled, axis=-1, keepdims=True)
    return root * (inner - scaled * centre)


def gelu_pair(values):
    c = math.sqrt(2.0 / math.pi)
    square = values * values
    th = jnp.tanh(c * values * (1.0 + 0.044715 * square))
    half = 0.5 * (1.0 + th)
    slope = half + 0.5 * values * (1.0 - th * th) * c * (1.0 + 3.0 * 0.044715 * square)
    return values * half, slope


def adam_update(weight, moment_one, moment_two, gradient, step_rate):
    moment_one_next = beta_first * moment_one + (1.0 - beta_first) * gradient
    moment_two_next = beta_second * moment_two + (1.0 - beta_second) * gradient * gradient
    corrected_one = moment_one_next / (1.0 - beta_first**STEP)
    corrected_two = moment_two_next / (1.0 - beta_second**STEP)
    weight_next = weight - step_rate * (
        corrected_one / (jnp.sqrt(corrected_two) + adam_epsilon) + decay_factor * weight
    )
    return (weight_next, moment_one_next, moment_two_next)


def shape_of(shape, dtype):
    return jax.ShapeDtypeStruct(shape, dtype)


def whole(shape):
    return pl.BlockSpec(shape, lambda *_: (0,) * len(shape))


def scalars():
    return pl.BlockSpec(memory_space=pltpu.SMEM)


LIGHT = pl.CostEstimate(flops=1, bytes_accessed=1, transcendentals=0)


def params(limit):
    return pltpu.CompilerParams(vmem_limit_bytes=limit * MIB)


def split_dot(values, picks, parts):
    total, left = None, values
    for _ in range(parts):
        high = left.astype(bf16)
        part = mm(high, picks)
        total = part if total is None else total + part
        left = left - high.astype(f32)
    return total


def prologue_kernel(inputs, attention, gains, router, scaled, root, packed, payload):
    values = inputs[...]
    scale = norm_root(values)
    root[...] = scale
    scaled[...] = (values * scale).astype(bf16)
    parts = [attention[i].astype(bf16) for i in range(4)]
    packed[...] = jnp.concatenate(
        [part[:, :LANES] for part in parts] + [part[:, LANES:] for part in parts], axis=1
    )
    experts, share = router.shape
    groups = -(-(2 + experts) // 8)
    wide = jnp.concatenate([gains[...], router[...]], axis=0)
    wide = jnp.pad(wide, ((0, 8 * groups - 2 - experts), (0, 0)))
    row = jnp.concatenate([wide[8 * k : 8 * k + 8] for k in range(groups)], axis=1)
    row = jnp.pad(row, ((0, 0), (0, LANES - groups * share)))
    payload[...] = jnp.broadcast_to(row[None], payload.shape)


def prologue(inputs, attention, gains, router, device_count):
    quarter, width = inputs.shape
    tall = attention.shape[1]
    shapes = [
        shape_of((quarter, width), bf16),
        shape_of((quarter, 1), f32),
        shape_of((tall, 6 * LANES), bf16),
        shape_of((device_count, 8, LANES), f32),
    ]
    arrays = (inputs, attention, gains, router)
    return pl.pallas_call(
        prologue_kernel,
        in_specs=[whole(a.shape) for a in arrays],
        out_specs=[whole(s.shape) for s in shapes],
        out_shape=shapes,
        compiler_params=params(60),
        cost_estimate=LIGHT,
        name="prologue",
    )(*arrays)


def slots_kernel(capacity, info, routes, grads, place, match, valid, slots):
    quarter = routes.shape[0]
    experts = match.shape[1]
    row = lax.broadcasted_iota(jnp.int32, (quarter, 1), 0) + info[0] * quarter
    inside = jnp.where(row < info[1], 1.0, 0.0)
    valid[...] = inside
    column = lax.broadcasted_iota(jnp.int32, (quarter, experts), 1)
    named = jnp.where(routes[...] == column, 1.0, 0.0)
    match[...] = named
    at = lax.broadcasted_iota(jnp.int32, (quarter, quarter), 0)
    before = lax.broadcasted_iota(jnp.int32, (quarter, quarter), 1)
    lower = jnp.where(at >= before, 1.0, 0.0).astype(bf16)
    rank = jnp.sum(mm(lower, (named * inside).astype(bf16)) * named, axis=1, keepdims=True) - 1.0
    slot = jnp.where(inside > 0.0, routes[...].astype(f32) * capacity + rank, -1.0)
    slot = jnp.broadcast_to(slot, (quarter, LANES)).T[:1]
    number = lax.broadcasted_iota(jnp.int32, place.shape, 0).astype(f32)
    chosen = jnp.where(number == slot, 1.0, 0.0).astype(bf16)
    place[...] = chosen
    slots[...] = mm(chosen, grads[...].astype(bf16)).astype(bf16)


def slots_part(info, routes, grads, experts, capacity):
    quarter, width = grads.shape
    shapes = [
        shape_of((experts * capacity, quarter), bf16),
        shape_of((quarter, experts), f32),
        shape_of((quarter, 1), f32),
        shape_of((experts * capacity, width), bf16),
    ]
    return pl.pallas_call(
        lambda *refs: slots_kernel(capacity, *refs),
        in_specs=[scalars(), whole(routes.shape), whole(grads.shape)],
        out_specs=[whole(s.shape) for s in shapes],
        out_shape=shapes,
        compiler_params=params(60),
        cost_estimate=LIGHT,
        name="slots",
    )(info, routes, grads)


def project_kernel(quarter, blocks, count, share, info, came, x0, x1, x2, x3, *refs):
    shards, (small, column_gain, weight, out_weight, qkv, kaug, vt) = refs[:count], refs[count:]
    tall = shards[0].shape[0]
    width = weight.shape[0]
    for j, ref in enumerate(shards):
        start = pl.multiple_of((info[2] ^ j) * tall, tall) if count > 1 else 0
        weight[pl.ds(start, tall), :] = ref[...]
    out_weight[:LANES, :] = weight[:, 3 * LANES : 4 * LANES].T
    out_weight[LANES:, :] = weight[:, 5 * LANES :].T[DH:]
    groups = small.shape[0] // 8
    devices = came.shape[0]
    flat = came[...].reshape(devices * 8, LANES)
    lane = lax.broadcasted_iota(jnp.int32, (LANES, width), 0)
    column = lax.broadcasted_iota(jnp.int32, (LANES, width), 1)
    inside = lax.rem(column, share)
    owner = lax.broadcasted_iota(jnp.int32, (devices, 1, width), 2) - share * lax.broadcasted_iota(
        jnp.int32, (devices, 1, width), 0
    )
    owner = jnp.where((owner >= 0) & (owner < share), 1.0, 0.0)
    for k in range(groups):
        pick = jnp.where(lane == inside + k * share, 1.0, 0.0).astype(bf16)
        spread = split_dot(flat, pick, 3)
        small[8 * k : 8 * k + 8, :] = jnp.sum(spread.reshape(devices, 8, width) * owner, axis=0)
    gain = small[:1, :]
    column_gain[...] = jnp.broadcast_to(gain, (LANES, width)).T[:, :1]
    for j, ref in enumerate((x0, x1, x2, x3)):
        start = pl.multiple_of((info[0] ^ j) * quarter, quarter)
        rows = pl.ds(start, quarter)
        scaled = (ref[...].astype(f32) * gain).astype(bf16)
        first = mm(scaled, weight[:, : 3 * LANES]).astype(bf16)
        second = mm(scaled, weight[:, 4 * LANES :]).astype(bf16)
        qkv[rows, : 3 * LANES] = first
        qkv[rows, 3 * LANES :] = second
        kaug[rows, :LANES] = first[:, LANES : 2 * LANES]
        lane = lax.broadcasted_iota(jnp.int32, (quarter, LANES), 1)
        row = lax.broadcasted_iota(jnp.int32, (quarter, LANES), 0) + start
        hidden = jnp.where((lane == 0) & (row >= info[1]), masked_score, 0.0)
        kaug[rows, LANES:] = jnp.where(lane < DH, hidden, second[:, :LANES].astype(f32)).astype(bf16)
        values = first[:, 2 * LANES :].T
        vt[0, :DH, rows] = values[:DH]
        vt[1, :DH, rows] = values[DH:]
        vt[2, :DH, rows] = second[:, LANES:].T[:DH]
    full_len = quarter * blocks
    tail = (lax.broadcasted_iota(jnp.int32, (16, full_len), 0) == 0).astype(f32).astype(bf16)
    for h in range(3):
        vt[h, DH:, :] = tail


def project(info, came, rows, shards, share, experts):
    quarter, width = rows[0].shape
    blocks = len(rows)
    full_len = quarter * blocks
    shapes = [
        shape_of((8 * -(-(2 + experts) // 8), width), f32),
        shape_of((width, 1), f32),
        shape_of((width, 6 * LANES), bf16),
        shape_of((3 * DH, width), bf16),
        shape_of((full_len, 5 * LANES), bf16),
        shape_of((full_len, 2 * LANES), bf16),
        shape_of((3, DH + 16, full_len), bf16),
    ]
    arrays = (came, *rows, *shards)
    return pl.pallas_call(
        lambda *refs: project_kernel(quarter, blocks, len(shards), share, *refs),
        in_specs=[scalars()] + [whole(a.shape) for a in arrays],
        out_specs=[whole(s.shape) for s in shapes],
        out_shape=shapes,
        compiler_params=params(60),
        cost_estimate=LIGHT,
        name="project",
    )(info, *arrays)


def attention_kernel(info, qkv, kaug, vt, context, chances, totals, *sent):
    quarter = context.shape[2]
    step = pl.program_id(0)
    rows = pl.ds(pl.multiple_of(step * quarter, quarter), quarter)
    q01 = (qkv[rows, :LANES].astype(f32) * score_scale).T.astype(bf16)
    q2 = (qkv[rows, 3 * LANES : 4 * LANES].astype(f32) * score_scale).T.astype(bf16)[:DH]
    ones = (lax.broadcasted_iota(jnp.int32, (DH, quarter), 0) == 0).astype(f32).astype(bf16)
    zeros = jnp.zeros((DH, quarter), bf16)
    queries = (
        jnp.concatenate([q01[:DH], zeros, ones, zeros], axis=0),
        jnp.concatenate([zeros, q01[DH:], ones, zeros], axis=0),
        jnp.concatenate([zeros, zeros, ones, q2], axis=0),
    )
    full_len = kaug.shape[0]
    all_scores = [mm(kaug[...], queries[h]) for h in range(3)]
    for h in range(3):
        scores = all_scores[h]
        top = jnp.max(jnp.max(scores.reshape(8, full_len // 8, quarter), axis=0), axis=0, keepdims=True)
        low = jnp.exp(scores - top).astype(bf16)
        chances[h] = low
        summed = mm(vt[h], low)
        part = 1.0 / summed[DH : DH + 1]
        totals[0, h : h + 1, :] = part
        context[0, h * DH : (h + 1) * DH, :] = (summed[:DH] * part).astype(bf16)
    for j, ref in enumerate(sent):

        @pl.when(step == info[0] ^ j)
        def _():
            ref[...] = context[0]


def attention_forward(info, qkv, kaug, vt, blocks):
    full_len = qkv.shape[0]
    quarter = full_len // blocks
    inner = 3 * DH
    return pl.pallas_call(
        attention_kernel,
        grid=(blocks,),
        in_specs=[scalars(), whole(qkv.shape), whole(kaug.shape), whole(vt.shape)],
        out_specs=[
            pl.BlockSpec((1, inner, quarter), lambda i: (i, 0, 0)),
            pl.BlockSpec((3, full_len, quarter), lambda i: (0, 0, i)),
            pl.BlockSpec((1, 3, quarter), lambda i: (i, 0, 0)),
        ]
        + [whole((inner, quarter))] * blocks,
        out_shape=[
            shape_of((blocks, inner, quarter), bf16),
            shape_of((3, full_len, full_len), bf16),
            shape_of((blocks, 3, quarter), f32),
        ]
        + [shape_of((inner, quarter), bf16)] * blocks,
        compiler_params=params(60),
        cost_estimate=LIGHT,
        name="attend",
    )(info, qkv, kaug, vt)


def turn_kernel(quarter, blocks, info, x0, x1, x2, x3, qkv, context, xt, kt, q2, cn):
    for j, ref in enumerate((x0, x1, x2, x3)):
        xt[info[0] ^ j] = ref[...].T
    for j in range(blocks):
        rows = slice(j * quarter, (j + 1) * quarter)
        third = qkv[rows, 3 * LANES : 4 * LANES].T
        kt[:LANES, rows] = qkv[rows, LANES : 2 * LANES].T
        kt[LANES:, rows] = third[DH:]
        zeros = jnp.zeros((DH, quarter), bf16)
        q2[rows, :] = jnp.concatenate([zeros, third[:DH]], axis=0).T
        cn[rows, :LANES] = context[j, :LANES, :].T
        cn[rows, LANES:] = jnp.concatenate([zeros, context[j, LANES:, :]], axis=0).T


def turn(info, rows, qkv, context):
    quarter, width = rows[0].shape
    blocks = len(rows)
    full_len = quarter * blocks
    shapes = [
        shape_of((blocks, width, quarter), bf16),
        shape_of((3 * DH, full_len), bf16),
        shape_of((full_len, LANES), bf16),
        shape_of((full_len, 2 * LANES), bf16),
    ]
    return pl.pallas_call(
        lambda *refs: turn_kernel(quarter, blocks, *refs),
        in_specs=[scalars()] + [whole((quarter, width))] * 4 + [whole(qkv.shape), whole(context.shape)],
        out_specs=[whole(s.shape) for s in shapes],
        out_shape=shapes,
        compiler_params=params(60),
        cost_estimate=LIGHT,
        name="turn",
    )(info, *rows, qkv, context)


def two_columns(column):
    high = column.astype(bf16).astype(f32)
    lane = lax.broadcasted_iota(jnp.int32, (column.shape[0], LANES), 1)
    return jnp.where(lane == 0, high, jnp.where(lane == 1, column - high, 0.0)).astype(bf16)


def middle_kernel(
    rows, c0, c1, c2, c3, w0, w1, w2, w3, small, place, match, valid, middle, root, chances, gate, slots
):
    gain, router = small[1:2, :], small[2 : 2 + match.shape[1], :]
    total = rows[...]
    for context, weight in zip((c0, c1, c2, c3), (w0, w1, w2, w3)):
        total = total + mm_tn(context[...], weight[...])
    middle[...] = total
    scale = norm_root(total)
    root[...] = scale
    hidden = total * scale * gain
    scores = mm_nt(hidden, router, HIGHEST)
    powers = jnp.exp(scores - jnp.max(scores, axis=-1, keepdims=True))
    share = powers / jnp.sum(powers, axis=-1, keepdims=True)
    chances[...] = share
    own = jnp.sum(share * match[...], axis=-1, keepdims=True)
    gate[...] = own
    width = rows.shape[1]
    slots[:, :width] = mm(place[...], hidden.astype(bf16)).astype(bf16)
    slots[:, width:] = mm(place[...], two_columns(own * valid[...])).astype(bf16)


def middle_part(rows, contexts, out_weights, small, place, match, valid):
    quarter, width = rows.shape
    experts = match.shape[1]
    shapes = [
        shape_of((quarter, width), f32),
        shape_of((quarter, 1), f32),
        shape_of((quarter, experts), f32),
        shape_of((quarter, 1), f32),
        shape_of((place.shape[0], width + LANES), bf16),
    ]
    arrays = (rows, *contexts, *out_weights, small, place, match, valid)
    return pl.pallas_call(
        middle_kernel,
        in_specs=[whole(a.shape) for a in arrays],
        out_specs=[whole(s.shape) for s in shapes],
        out_shape=shapes,
        compiler_params=params(60),
        cost_estimate=LIGHT,
        name="middle",
    )(*arrays)


def expert_kernel(rows, grads, *refs):
    count = (len(refs) - 4) // 2
    early_parts, late_parts = refs[:count], refs[count : 2 * count]
    out, back, held, arrived = refs[2 * count :]
    width = grads.shape[1]
    early = early_parts[0].shape[0]
    ends = (slice(0, early), slice(early, 2 * width))
    copies = [
        [
            pltpu.make_async_copy(ref, held.at[i, end, :], arrived.at[i, k])
            for k, (ref, end) in enumerate(zip(pair, ends))
        ]
        for i, pair in enumerate(zip(early_parts, late_parts))
    ]
    for pair in copies:
        for copy in pair:
            copy.start()
    out_total, back_total = None, None
    for i, pair in enumerate(copies):
        for copy in pair:
            copy.wait()
        grad = mm(grads[...], held[i, width:, :])
        active, slope = gelu_pair(mm(rows[:, :width], held[i, :width, :]))
        part = mm_nt(active.astype(bf16), held[i, width:, :])
        back_part = mm_nt((grad * slope).astype(bf16), held[i, :width, :])
        out_total = part if i == 0 else out_total + part
        back_total = back_part if i == 0 else back_total + back_part
    result = out_total.astype(bf16)
    out[...] = result
    back[:, :width] = back_total.astype(bf16)
    match = jnp.sum(grads[...].astype(f32) * result.astype(f32), axis=-1, keepdims=True)
    back[:, width:] = two_columns(match)


def expert_part(rows, grads, early_parts, late_parts):
    slots, width = grads.shape
    hidden = early_parts[0].shape[1]
    count = len(early_parts)
    shapes = [shape_of((slots, width), bf16), shape_of((slots, width + LANES), bf16)]
    return pl.pallas_call(
        expert_kernel,
        in_specs=[whole(rows.shape), whole(grads.shape)] + [pl.BlockSpec(memory_space=pl.ANY)] * (2 * count),
        out_specs=[whole(s.shape) for s in shapes],
        out_shape=shapes,
        scratch_shapes=[pltpu.VMEM((count, 2 * width, hidden), bf16), pltpu.SemaphoreType.DMA((count, 2))],
        compiler_params=params(60),
        cost_estimate=LIGHT,
        name="experts",
    )(rows, grads, *early_parts, *late_parts)


def expert_grad_kernel(count, *refs):
    rows, grads = refs[:count], refs[count : 2 * count]
    near_in, near_out, out, square, weight, row_all, grad_all, inner_all, active_all, arrived = refs[2 * count :]
    early = near_in.shape[0]
    ends = (slice(0, early), slice(early, weight.shape[0]))
    copies = [
        pltpu.make_async_copy(ref, weight.at[end, :], arrived.at[i])
        for i, (ref, end) in enumerate(zip((near_in, near_out), ends))
    ]
    for copy in copies:
        copy.start()
    for copy in copies:
        copy.wait()
    slots, width = grads[0].shape
    for j in range(count):
        at = slice(j * slots, (j + 1) * slots)
        gate = rows[j][:, width : width + 1].astype(f32) + rows[j][:, width + 1 : width + 2].astype(f32)
        row_all[at, :] = rows[j][:, :width]
        grad_all[at, :] = (grads[j][...].astype(f32) * gate).astype(bf16)
        back = mm(grads[j][...], weight[width:, :])
        active, slope = gelu_pair(mm(rows[j][:, :width], weight[:width, :]))
        inner_all[at, :] = (back * slope * gate).astype(bf16)
        active_all[at, :] = active.astype(bf16)
    first = mm_tn(row_all[...], inner_all[...])
    out[0] = first.astype(bf16)
    second = mm_tn(grad_all[...], active_all[...])
    out[1] = second.astype(bf16)
    square[...] = jnp.sum(first * first + second * second, axis=0, keepdims=True)


def expert_gradient(rows, grads, near_in, near_out):
    count = len(rows)
    slots, width = grads[0].shape
    hidden = near_in.shape[1]
    arrays = (*rows, *grads)
    shapes = [
        shape_of((2, width, hidden), bf16),
        shape_of((1, hidden), f32),
    ]
    return pl.pallas_call(
        lambda *refs: expert_grad_kernel(count, *refs),
        in_specs=[whole(a.shape) for a in arrays] + [pl.BlockSpec(memory_space=pl.ANY)] * 2,
        out_specs=[whole(s.shape) for s in shapes],
        out_shape=shapes,
        scratch_shapes=[pltpu.VMEM((2 * width, hidden), bf16)]
        + [pltpu.VMEM((count * slots, width), bf16)] * 2
        + [pltpu.VMEM((count * slots, hidden), bf16)] * 2
        + [pltpu.SemaphoreType.DMA((2,))],
        compiler_params=params(60),
        cost_estimate=LIGHT,
        name="expert_gradient",
    )(*arrays, near_in, near_out)


def pack_small(small, cut):
    devices = cut.shape[0]
    rows, width = small.shape
    share = width // devices
    groups = rows // 8
    column = lax.broadcasted_iota(jnp.int32, (devices, 1, width), 2)
    owner = column - share * lax.broadcasted_iota(jnp.int32, (devices, 1, width), 0)
    owner = jnp.where((owner >= 0) & (owner < share), 1.0, 0.0)
    lane = lax.broadcasted_iota(jnp.int32, (width, LANES), 1)
    inside = lax.rem(lax.broadcasted_iota(jnp.int32, (width, LANES), 0), share)
    total = None
    for k in range(groups):
        pick = jnp.where(lane == inside + k * share, 1.0, 0.0).astype(bf16)
        spread = (small[8 * k : 8 * k + 8, :][None] * owner).reshape(devices * 8, width)
        part = split_dot(spread, pick, 2)
        total = part if total is None else total + part
    cut[...] = total.reshape(devices, 8, LANES)


def return_kernel(
    back, place, middle, root, chances, gate, match, cotangent, small, w0, w1, w2, w3,
    grad, turned, cut, p0, p1, p2, p3, small_grad,
):
    experts = match.shape[1]
    gain, router = small[1:2, :], small[2 : 2 + experts, :]
    width = middle.shape[1]
    came = mm_tn(place[...], back[...])
    gate_grad = came[:, width : width + 1] + came[:, width + 1 : width + 2]
    own = gate[...]
    score_grad = own * (match[...] - chances[...]) * gate_grad
    scaled = middle[...] * root[...]
    hidden = scaled * gain
    tall = small_grad.shape[0]
    small_grad[1 : 1 + experts, :] = mm_tn(score_grad, hidden, HIGHEST)
    small_grad[1 + experts :, :] = jnp.zeros((tall - 1 - experts, hidden.shape[1]), f32)
    second = own * came[:, :width] + jnp.dot(
        score_grad, router, precision=HIGHEST, preferred_element_type=f32
    )
    small_grad[:1, :] = jnp.sum(second * scaled, axis=0, keepdims=True)
    inner = second * gain
    centre = jnp.mean(inner * scaled, axis=-1, keepdims=True)
    total = cotangent[...] + root[...] * (inner - scaled * centre)
    grad[...] = total
    low = total.astype(bf16)
    turned[...] = low.T
    for ref, weight in zip((p0, p1, p2, p3), (w0, w1, w2, w3)):
        ref[...] = mm_nt(weight[...], low).astype(bf16)
    pack_small(small_grad, cut)


def return_part(back, place, middle, root, chances, gate, match, cotangent, small, out_weights, device_count):
    quarter, width = middle.shape
    experts = match.shape[1]
    inner = out_weights[0].shape[0]
    shapes = [
        shape_of((quarter, width), f32),
        shape_of((width, quarter), bf16),
        shape_of((device_count, 8, LANES), f32),
    ] + [shape_of((inner, quarter), bf16)] * len(out_weights)
    arrays = (back, place, middle, root, chances, gate, match, cotangent, small, *out_weights)
    return pl.pallas_call(
        return_kernel,
        in_specs=[whole(a.shape) for a in arrays],
        out_specs=[whole(s.shape) for s in shapes],
        out_shape=shapes,
        scratch_shapes=[pltpu.VMEM((8 * -(-(1 + experts) // 8), width), f32)],
        compiler_params=params(60),
        cost_estimate=LIGHT,
        name="returned",
    )(*arrays)


def attention_back_kernel(
    blocks, info, g0, g1, g2, g3, context, chances, totals, qkv, kt, q2, packed, grads, vaug, k01, k2, v01, v2
):
    step = pl.program_id(0)
    quarter = grads.shape[2]

    @pl.when(step == 0)
    def _():
        for j, ref in enumerate((g0, g1, g2, g3)):
            grads[info[0] ^ j] = ref[...]
        vaug[:, :LANES] = qkv[:, 2 * LANES : 3 * LANES]
        lane = lax.broadcasted_iota(jnp.int32, (vaug.shape[0], LANES), 1)
        ones = jnp.where(lane < DH + 2, 1.0, 0.0)
        vaug[:, LANES:] = jnp.where(lane < DH, qkv[:, 4 * LANES :].astype(f32), ones).astype(bf16)
        for ref in (k01, k2, v01, v2):
            ref[...] = jnp.zeros(ref.shape, f32)

    rows = pl.ds(pl.multiple_of(step * quarter, quarter), quarter)
    raw = grads[step].astype(f32)
    scale = totals[0]
    scaled = [raw[h * DH : (h + 1) * DH] * scale[h : h + 1] for h in range(3)]
    heads = jnp.concatenate(scaled, axis=0).astype(bf16)
    lane = lax.broadcasted_iota(jnp.int32, (quarter, LANES), 1)
    row = lax.broadcasted_iota(jnp.int32, (DH, quarter), 0)
    zeros = jnp.zeros((DH, quarter), bf16)
    q01 = qkv[rows, :LANES].astype(f32)
    g01 = heads[:LANES].T.astype(f32)
    third = jnp.concatenate([heads[LANES:], zeros], axis=0).T
    query_parts = []
    for h in range(3):
        part = heads[h * DH : (h + 1) * DH]
        centre = -jnp.sum(
            part.astype(f32) * context[0, h * DH : (h + 1) * DH, :].astype(f32), axis=0, keepdims=True
        )
        high = centre.astype(bf16).astype(f32)
        tail = jnp.where(row == 0, high, jnp.where(row == 1, centre - high, 0.0)).astype(bf16)
        pieces = [zeros, zeros, zeros, tail]
        pieces[h] = part
        chance_grad = mm(vaug[...], jnp.concatenate(pieces, axis=0))
        low = chances[h]
        score_grad = (low.astype(f32) * chance_grad).astype(bf16)
        query_parts.append(mm(kt[h * DH : (h + 1) * DH, :], score_grad) * score_scale)
        if h < 2:
            inside = (lane >= h * DH) & (lane < (h + 1) * DH)
            k01[...] += mm(score_grad, jnp.where(inside, q01, 0.0).astype(bf16))
            v01[...] += mm(low, jnp.where(inside, g01, 0.0).astype(bf16))
        else:
            k2[...] += mm(score_grad, q2[rows, :])
            v2[...] += mm(low, third)
    packed[rows, :LANES] = jnp.concatenate(query_parts[:2], axis=0).T.astype(bf16)
    packed[rows, 4 * LANES : 5 * LANES] = (
        jnp.concatenate([query_parts[2], jnp.zeros((DH, quarter), f32)], axis=0).T.astype(bf16)
    )

    @pl.when(step == blocks - 1)
    def _():
        packed[:, LANES : 2 * LANES] = (k01[...] * score_scale).astype(bf16)
        packed[:, 2 * LANES : 3 * LANES] = v01[...].astype(bf16)
        packed[:, 3 * LANES : 4 * LANES] = jnp.zeros(k01.shape, bf16)
        packed[:, 4 * LANES : 5 * LANES] = packed[:, 4 * LANES : 5 * LANES] + (k2[...] * score_scale).astype(bf16)
        packed[:, 5 * LANES :] = v2[...].astype(bf16)


def attention_backward(info, grads, context, chances, totals, qkv, kt, q2):
    blocks, inner, quarter = context.shape
    full_len = quarter * blocks
    block = pl.BlockSpec((1, inner, quarter), lambda i: (i, 0, 0))
    return pl.pallas_call(
        lambda *refs: attention_back_kernel(blocks, *refs),
        grid=(blocks,),
        in_specs=[
            scalars(),
            *[whole((inner, quarter))] * blocks,
            block,
            pl.BlockSpec((3, full_len, quarter), lambda i: (0, 0, i)),
            pl.BlockSpec((1, 3, quarter), lambda i: (i, 0, 0)),
            whole(qkv.shape),
            whole(kt.shape),
            whole(q2.shape),
        ],
        out_specs=whole((full_len, 6 * LANES)),
        out_shape=shape_of((full_len, 6 * LANES), bf16),
        scratch_shapes=[pltpu.VMEM(context.shape, bf16), pltpu.VMEM((full_len, 2 * LANES), bf16)]
        + [pltpu.VMEM((full_len, LANES), f32)] * 4,
        compiler_params=params(60),
        cost_estimate=LIGHT,
        name="attend_back",
    )(info, *grads, context, chances, totals, qkv, kt, q2)


def weight_grad_kernel(blocks, info, xt, packed, g0, g1, g2, g3, cn, weight, gain, out, gain_grad):
    quarter = xt.shape[2]
    total, outer = None, None
    for j, ref in enumerate((g0, g1, g2, g3)):
        rows = slice(j * quarter, (j + 1) * quarter)
        there = pl.ds(pl.multiple_of((info[0] ^ j) * quarter, quarter), quarter)
        part = mm(xt[j], packed[rows, :])
        own = mm(ref[...], cn[there, :])
        total = part if total is None else total + part
        outer = own if outer is None else outer + own
    gain_grad[...] = jnp.sum(total * weight[...].astype(f32), axis=1, keepdims=True)
    total = total * gain[...]
    out[:, : 3 * LANES] = total[:, : 3 * LANES].astype(bf16)
    out[:, 3 * LANES : 4 * LANES] = outer[:, :LANES].astype(bf16)
    out[:, 4 * LANES : 5 * LANES] = total[:, 4 * LANES : 5 * LANES].astype(bf16)
    out[:, 5 * LANES :] = (total[:, 5 * LANES :] + outer[:, LANES:]).astype(bf16)


def weight_gradient(info, xt, packed, grads, cn, weight, gain):
    blocks, width, quarter = xt.shape
    tall = 256
    full_len = quarter * blocks
    return pl.pallas_call(
        lambda *refs: weight_grad_kernel(blocks, *refs),
        grid=(width // tall,),
        in_specs=[
            scalars(),
            pl.BlockSpec((blocks, tall, quarter), lambda i: (0, i, 0)),
            whole(packed.shape),
            *[pl.BlockSpec((tall, quarter), lambda i: (i, 0))] * blocks,
            whole(cn.shape),
            pl.BlockSpec((tall, 6 * LANES), lambda i: (i, 0)),
            pl.BlockSpec((tall, 1), lambda i: (i, 0)),
        ],
        out_specs=[pl.BlockSpec((tall, 6 * LANES), lambda i: (i, 0)), pl.BlockSpec((tall, 1), lambda i: (i, 0))],
        out_shape=[shape_of((width, 6 * LANES), bf16), shape_of((width, 1), f32)],
        compiler_params=params(60),
        cost_estimate=LIGHT,
        name="weight_gradient",
    )(info, xt, packed, *grads, cn, weight, gain)


def input_grad_kernel(quarter, info, packed, weight, *parts):
    for j, ref in enumerate(parts):
        rows = pl.ds(pl.multiple_of((info[0] ^ j) * quarter, quarter), quarter)
        ref[...] = mm_nt(packed[rows, :], weight[...]).astype(bf16)


def input_gradient(info, packed, weight, blocks):
    quarter = packed.shape[0] // blocks
    shapes = [shape_of((quarter, weight.shape[0]), bf16)] * blocks
    return pl.pallas_call(
        lambda *refs: input_grad_kernel(quarter, *refs),
        in_specs=[scalars(), whole(packed.shape), whole(weight.shape)],
        out_specs=[whole(s.shape) for s in shapes],
        out_shape=shapes,
        compiler_params=params(60),
        cost_estimate=LIGHT,
        name="input_gradient",
    )(info, packed, weight)


def sums_kernel(came, squares, small, gain_grad, gradient, payload, small_sum):
    count = came.shape[0]
    total = came[0].astype(f32)
    for i in range(1, count):
        total = total + came[i].astype(f32)
    gradient[...] = total
    own = jnp.sum(small[...], axis=0)
    square = (
        jnp.sum(total * total, keepdims=True)
        + jnp.sum(squares[...], keepdims=True)
        + jnp.sum(own * own, keepdims=True)
    )
    small_sum[...] = own
    rows = gain_grad.shape[0]
    row = lax.broadcasted_iota(jnp.int32, (8, LANES), 0)
    gain = jnp.concatenate([gain_grad[...], jnp.zeros((8 - rows, LANES), f32)], axis=0)
    payload[...] = jnp.broadcast_to(jnp.where(row < rows, gain, square)[None], payload.shape)


def sums_part(came, squares, small, gain_grad, device_count):
    shapes = [
        shape_of(came.shape[1:], f32),
        shape_of((device_count, 8, LANES), f32),
        shape_of((8, LANES), f32),
    ]
    arrays = (came, squares, small, gain_grad)
    return pl.pallas_call(
        sums_kernel,
        in_specs=[whole(a.shape) for a in arrays],
        out_specs=[whole(s.shape) for s in shapes],
        out_shape=shapes,
        compiler_params=params(60),
        cost_estimate=LIGHT,
        name="sums",
    )(*arrays)


def adam_kernel(lanes, share, expert_rates, info, last, small_sum, *refs):
    held, outs, factor = refs[:14], refs[14:27], refs[27]
    dense, dense_grad, gains, router = held[:3], held[3], held[4:7], held[7:10]
    weight, first, second, gradient = held[10:14]
    norm_out, outs = outs[0], outs[1:]
    dense_out, gains_out, router_out, expert_out = outs[:3], outs[3:6], outs[6:9], outs[9:12]
    matrix, part = pl.program_id(0), pl.program_id(1)
    experts = router[0].shape[0]

    @pl.when((matrix == 0) & (part == 0))
    def _():
        total = jnp.sum(last[...], axis=0)
        row = lax.broadcasted_iota(jnp.int32, (8, LANES), 0)
        squares = jnp.sum(jnp.where(row < lanes, total * total, 0.0), keepdims=True)
        norm = jnp.sqrt(squares + total[7:8, :1])
        scale = jnp.minimum(1.0, clip_limit / (norm + norm_epsilon))
        norm_out[...] = norm
        factor[...] = jnp.broadcast_to(scale, (8, LANES))
        rates = (0.71 / math.sqrt(D), 0.71 / math.sqrt(D), 0.83 / math.sqrt(D), 0.79 / math.sqrt(H * DH))
        for i, rate in enumerate(rates):
            grad = jnp.concatenate(
                [
                    dense_grad[:, i * LANES : (i + 1) * LANES],
                    dense_grad[:, 4 * LANES + i * DH : 4 * LANES + (i + 1) * DH],
                ],
                axis=1,
            )
            result = adam_update(*[ref[i] for ref in dense], grad * scale, rate)
            for ref, value in zip(dense_out, result):
                ref[i] = value
        column = lax.broadcasted_iota(jnp.int32, (LANES, LANES), 1)
        place = lax.broadcasted_iota(jnp.int32, (LANES, LANES), 0) - info[3] * share
        own = jnp.zeros((8, LANES), f32)
        for i in range(lanes):
            pick = jnp.where((column == place + i * LANES) & (column < share), 1.0, 0.0)
            own = own + jnp.dot(
                jnp.broadcast_to(total[i : i + 1], (8, LANES)), pick, precision=HIGHEST, preferred_element_type=f32
            )
        groups = -(-(1 + experts) // 8)
        table = small_sum[...]
        table = jnp.concatenate([table[:, k * share : (k + 1) * share] for k in range(groups)], axis=0)
        grad = jnp.concatenate([own[:1, :share], table[:1]], axis=0)
        for ref, value in zip(gains_out, adam_update(*[ref[...] for ref in gains], grad * scale, 0.5)):
            ref[...] = value
        grad = table[1 : 1 + experts]
        result = adam_update(*[ref[...] for ref in router], grad * scale, 0.24 / math.sqrt(D))
        for ref, value in zip(router_out, result):
            ref[...] = value

    rate = jnp.where(matrix == 0, expert_rates[0], expert_rates[1])
    grad = gradient[...].astype(f32) * factor[:1, :1]
    result = adam_update(weight[...], first[...], second[...], grad, rate)
    for ref, value in zip(expert_out, result):
        ref[...] = value


def adam(info, last, small_sum, dense, dense_grad, gains, router, expert, expert_grad, rates):
    _, tall, wide = expert_grad.shape
    parts = 4
    block = pl.BlockSpec((1, tall // parts, wide), lambda i, j: (i, j, 0))
    small = [*dense, *gains, *router]
    shapes = [shape_of((1, 1), f32)] + [shape_of(a.shape, f32) for a in small]
    ins = (last, small_sum, *dense, dense_grad, *gains, *router)
    return pl.pallas_call(
        lambda *refs: adam_kernel(tall // LANES, gains[0].shape[1], rates, *refs),
        grid=(2, parts),
        in_specs=[scalars()] + [whole(a.shape) for a in ins] + [block] * 4,
        out_specs=[whole(a.shape) for a in shapes] + [block] * 3,
        out_shape=shapes + [shape_of(expert_grad.shape, f32)] * 3,
        scratch_shapes=[pltpu.VMEM((8, LANES), f32)],
        compiler_params=params(60),
        cost_estimate=LIGHT,
        name="adam",
    )(info, *ins, *expert, expert_grad)


def tie(*values):
    return lax.optimization_barrier(values)


def on_device(
    inputs,
    cotangent,
    lengths,
    routes,
    attention_weight,
    attention_mean,
    attention_square,
    expert_weight,
    expert_mean,
    expert_square,
    router_matrix,
    router_mean,
    router_square,
    norm_gains,
    gains_mean,
    gains_square,
):
    quarter, width = inputs.shape[1:]
    dp_count, tensor_count = lax.axis_size(DP), lax.axis_size(TENSOR)
    device_count = dp_count * tensor_count
    expert_count = router_matrix.shape[1]
    capacity = max(2, (5 * quarter + 4 * expert_count - 1) // (4 * expert_count))
    own_dp, own_tensor = lax.axis_index(DP), lax.axis_index(TENSOR)
    share = router_matrix.shape[0]
    rows, grad_rows, length = inputs[0], cotangent[0], lengths[0]
    info = jnp.stack([own_tensor, length, own_dp, lax.axis_index(EVERYONE)]).astype(jnp.int32)

    scaled_one, root_one, weight_own, payload = prologue(
        rows, attention_weight, norm_gains, router_matrix.T, device_count
    )
    block_two = swap(scaled_one, TENSOR, 2)
    small_came = lax.all_to_all(payload, EVERYONE, 0, 0, tiled=True)
    expert_flat = expert_weight[0].reshape(2 * width, -1)
    early_own, late_own = expert_flat[:EARLY].astype(bf16), expert_flat[EARLY:].astype(bf16)
    place, match, valid_scale, grad_slots = slots_part(info, routes[0], grad_rows, expert_count, capacity)
    if dp_count == 8:
        w4, w2, w1 = [swap(weight_own, DP, mask) for mask in (4, 2, 1)]
        w4, w2, w1, small_came, block_two, early_own = tie(w4, w2, w1, small_came, block_two, early_own)
        w6, w5, w3 = swap(w4, DP, 2), swap(w4, DP, 1), swap(w2, DP, 1)
        w6, w5, w3, scaled_one = tie(w6, w5, w3, scaled_one)
        w7, grad_slots = tie(swap(w6, DP, 1), grad_slots)
        shards = [weight_own, w1, w2, w3, w4, w5, w6, w7]
    else:
        weight_own, grad_slots, small_came, block_two, early_own = tie(
            weight_own, grad_slots, small_came, block_two, early_own
        )
        shards = [lax.all_gather(weight_own, DP, axis=0, tiled=True)]
    early_far = swap(early_own, TENSOR, 2)
    row_blocks = [scaled_one, swap(scaled_one, TENSOR, 1), block_two, swap(block_two, TENSOR, 1)]

    slot_count = expert_count * capacity

    def trade(values):
        blocks = values.reshape(expert_count, capacity, values.shape[1])
        return lax.all_to_all(blocks, DP, 0, 0, tiled=True).reshape(values.shape)

    expert_grads = trade(grad_slots)
    small, gain_column, weight, out_weight, qkv, keys_wide, values_turned = project(
        info, small_came, row_blocks, shards, share, expert_count
    )
    out_weight, early_own = tie(out_weight, early_own)
    out_near, out_far = swap(out_weight, TENSOR, 1), swap(out_weight, TENSOR, 2)
    early_near = swap(early_own, TENSOR, 1)
    context, chances, totals, *sent = attention_forward(info, qkv, keys_wide, values_turned, tensor_count)
    expert_grads, early_far, out_near, out_far, *sent = tie(expert_grads, early_far, out_near, out_far, *sent)
    contexts = [sent[0]] + [swap(sent[j], TENSOR, j) for j in range(1, tensor_count)]
    out_weights = [out_weight, out_near, out_far, swap(out_far, TENSOR, 1)]
    late_own, early_far, *contexts = tie(late_own, early_far, *contexts)
    late_far = swap(late_own, TENSOR, 2)

    middle, root_two, shares, gate, slots = middle_part(
        rows, contexts, out_weights, small, place, match, valid_scale
    )
    slots, late_own = tie(slots, late_own)
    expert_rows = trade(slots)
    early_parts = [early_own, early_far, early_near, swap(early_far, TENSOR, 1)]
    expert_rows, late_far = tie(expert_rows, late_far)
    late_parts = [late_own, late_far, swap(late_own, TENSOR, 1), swap(late_far, TENSOR, 1)]
    expert_outs, expert_back = expert_part(expert_rows, expert_grads, early_parts, late_parts)
    expert_rows, expert_back, qkv = tie(expert_rows, expert_back, qkv)
    turned_rows, keys_turned, third_query, context_rows = turn(info, row_blocks, qkv, context)
    rows_near, rows_far = swap(expert_rows, TENSOR, 1), swap(expert_rows, TENSOR, 2)
    rows_far, expert_grads = tie(rows_far, expert_grads)
    rows_all = [expert_rows, rows_near, rows_far, swap(rows_far, TENSOR, 1)]
    grads_near, grads_far = swap(expert_grads, TENSOR, 1), swap(expert_grads, TENSOR, 2)
    expert_back, rows_all, turned_rows = tie(trade(expert_back), rows_all, turned_rows)

    middle_grad, middle_turned, small_cut, *parts = return_part(
        expert_back, place, middle, root_two, shares, gate, match, grad_rows, small, out_weights, device_count
    )
    expert_outs, middle_turned, *parts = tie(expert_outs, middle_turned, *parts)
    context_grads = [parts[0]] + [swap(parts[j], TENSOR, j) for j in range(1, tensor_count)]
    expert_outs = trade(expert_outs)
    middle_turned, *context_grads = tie(middle_turned, *context_grads)
    middle_near, middle_far = swap(middle_turned, TENSOR, 1), swap(middle_turned, TENSOR, 2)

    packed = attention_backward(info, context_grads, context, chances, totals, qkv, keys_turned, third_query)
    packed, middle_far, grads_far, small_cut, expert_outs = tie(packed, middle_far, grads_far, small_cut, expert_outs)
    middle_all = [middle_turned, middle_near, middle_far, swap(middle_far, TENSOR, 1)]
    grads_all = [expert_grads, grads_near, grads_far, swap(grads_far, TENSOR, 1)]
    small_grads = lax.all_to_all(small_cut, EVERYONE, 0, 0, tiled=True)
    weight_grad, gain_one_grad = weight_gradient(
        info, turned_rows, packed, middle_all, context_rows, weight, gain_column
    )
    weight_grad, early_own, small_grads = tie(weight_grad, early_own, small_grads)
    weight_came = lax.all_to_all(weight_grad.reshape(dp_count, -1, width), DP, 0, 0, tiled=True)
    expert_grad, expert_squares = expert_gradient(rows_all, grads_all, early_own, late_own)
    expert_squares, packed = tie(expert_squares, packed)

    input_parts = input_gradient(info, packed, weight, tensor_count)
    first_half = input_parts[0].astype(f32) + swap(input_parts[1], TENSOR, 1).astype(f32)
    second_half = (input_parts[2].astype(f32) + swap(input_parts[3], TENSOR, 1).astype(f32)).astype(bf16)

    second_came = swap(second_half, TENSOR, 2)
    dense_grad, last, small_sum = sums_part(
        weight_came, expert_squares, small_grads, gain_one_grad.reshape(-1, LANES), device_count
    )
    last, expert_outs, middle_grad, rows_late = tie(last, expert_outs, middle_grad, rows)
    last_all = lax.all_to_all(last, EVERYONE, 0, 0, tiled=True)
    input_grad = middle_grad + norm_backward(
        rows_late, root_one, small[:1], first_half + second_came.astype(f32)
    )
    picked = mm_tn(place, expert_outs)
    branch = gate * valid_scale * picked
    block_output = middle + branch
    last_all, input_grad, block_output, branch = tie(last_all, input_grad, block_output, branch)

    rates = (0.4 * math.sqrt(expert_count / D), 1.38 * math.sqrt(expert_count / FF))
    norm, *updated = adam(
        info,
        last_all,
        small_sum,
        (attention_weight, attention_mean, attention_square),
        dense_grad,
        (norm_gains, gains_mean, gains_square),
        (router_matrix.T, router_mean.T, router_square.T),
        (expert_weight[0], expert_mean[0], expert_square[0]),
        expert_grad,
        rates,
    )
    attention_new, gains_new, router_new, expert_new = updated[:3], updated[3:6], updated[6:9], updated[9:]
    router_new = [part.T for part in router_new]
    grad_norm = norm.reshape(())
    return (
        block_output[None],
        input_grad[None],
        grad_norm,
        *attention_new,
        *[part[None] for part in expert_new],
        *router_new,
        *gains_new,
        branch[None],
    )


def solution(mesh):
    names = mesh.axis_names
    dp_count, tensor_count = mesh.shape[names[0]], mesh.shape[names[1]]
    cut = jax.sharding.Mesh(mesh.devices.reshape(dp_count // 2, 2, tensor_count // 2, 2), EVERYONE)
    rows = P(DP, TENSOR, None)
    attention = P(None, DP, TENSOR)
    expert = P(DP, None, None, TENSOR)
    router = P(EVERYONE, None)
    gains = P(None, EVERYONE)
    weights = (attention,) * 3 + (expert,) * 3 + (router,) * 3 + (gains,) * 3
    return jax.shard_map(
        on_device,
        mesh=cut,
        in_specs=(rows, rows, P(DP), rows) + weights,
        out_specs=(rows, rows, P()) + weights + (rows,),
        check_vma=False,
    )
```

```python
import math

import jax
import jax.numpy as jnp
from jax import lax
from jax.experimental import pallas as pl
from jax.experimental.pallas import tpu as pltpu
from jax.sharding import PartitionSpec as P

D = 768
H = 12
DH = 64
FF = 3072
STEP = 10

HIGHEST = lax.Precision.HIGHEST
norm_epsilon = 1e-06
beta_first = 0.9
beta_second = 0.999
adam_epsilon = 1e-08
decay_factor = 0.01
clip_limit = 1.0
masked_score = -1e30
score_scale = 1.0 / math.sqrt(DH)
bf16 = jnp.bfloat16
f32 = jnp.float32
MIB = 1 << 20
LANES = 128
CUTS = (944, 1136)


DP = ("dh", "dl")
TENSOR = ("th", "tl")
EVERYONE = DP + TENSOR


def swap(values, axis, mask):
    count = lax.axis_size(axis)
    return lax.ppermute(values, axis, [(i, i ^ mask) for i in range(count)])


def bits_of(count):
    return [1 << b for b in range(count.bit_length() - 1)]


def gather_relative(block, axis, order):
    held = {0: block}
    for mask in order:
        for j in list(held):
            held[j ^ mask] = swap(held[j], axis, mask)
    return [held[j] for j in range(len(held))]


def mm(a, b):
    return jnp.dot(a, b, preferred_element_type=f32)


def mm_nt(a, b, precision=None):
    return lax.dot_general(
        a, b, (((1,), (1,)), ((), ())), preferred_element_type=f32, precision=precision
    )


def mm_tn(a, b, precision=None):
    return lax.dot_general(
        a, b, (((0,), (0,)), ((), ())), preferred_element_type=f32, precision=precision
    )


def norm_root(values):
    return lax.rsqrt(jnp.mean(values * values, axis=-1, keepdims=True) + norm_epsilon)


def norm_backward(values, root, gain_row, grad):
    scaled = values * root
    inner = grad * gain_row
    centre = jnp.mean(inner * scaled, axis=-1, keepdims=True)
    return root * (inner - scaled * centre)


def gelu_pair(values):
    c = math.sqrt(2.0 / math.pi)
    square = values * values
    th = jnp.tanh(c * values * (1.0 + 0.044715 * square))
    half = 0.5 * (1.0 + th)
    slope = half + 0.5 * values * (1.0 - th * th) * c * (1.0 + 3.0 * 0.044715 * square)
    return values * half, slope


def adam_update(weight, moment_one, moment_two, gradient, step_rate):
    moment_one_next = beta_first * moment_one + (1.0 - beta_first) * gradient
    moment_two_next = beta_second * moment_two + (1.0 - beta_second) * gradient * gradient
    corrected_one = moment_one_next / (1.0 - beta_first**STEP)
    corrected_two = moment_two_next / (1.0 - beta_second**STEP)
    weight_next = weight - step_rate * (
        corrected_one / (jnp.sqrt(corrected_two) + adam_epsilon) + decay_factor * weight
    )
    return (weight_next, moment_one_next, moment_two_next)


def shape_of(shape, dtype):
    return jax.ShapeDtypeStruct(shape, dtype)


def whole(shape):
    return pl.BlockSpec(shape, lambda *_: (0,) * len(shape))


def scalars():
    return pl.BlockSpec(memory_space=pltpu.SMEM)


LIGHT = pl.CostEstimate(flops=1, bytes_accessed=1, transcendentals=0)


def params(limit):
    return pltpu.CompilerParams(vmem_limit_bytes=limit * MIB)


def split_dot(values, picks, parts):
    total, left = None, values
    for _ in range(parts):
        high = left.astype(bf16)
        part = mm(high, picks)
        total = part if total is None else total + part
        left = left - high.astype(f32)
    return total


def prologue_kernel(inputs, attention, gains, router, scaled, root, packed, payload):
    values = inputs[...]
    scale = norm_root(values)
    root[...] = scale
    scaled[...] = (values * scale).astype(bf16)
    parts = [attention[i].astype(bf16) for i in range(4)]
    packed[...] = jnp.concatenate(
        [part[:, :LANES] for part in parts] + [part[:, LANES:] for part in parts], axis=1
    )
    experts, share = router.shape
    groups = -(-(2 + experts) // 8)
    wide = jnp.concatenate([gains[...], router[...]], axis=0)
    wide = jnp.pad(wide, ((0, 8 * groups - 2 - experts), (0, 0)))
    row = jnp.concatenate([wide[8 * k : 8 * k + 8] for k in range(groups)], axis=1)
    row = jnp.pad(row, ((0, 0), (0, LANES - groups * share)))
    payload[...] = jnp.broadcast_to(row[None], payload.shape)


def prologue(inputs, attention, gains, router, device_count):
    quarter, width = inputs.shape
    tall = attention.shape[1]
    shapes = [
        shape_of((quarter, width), bf16),
        shape_of((quarter, 1), f32),
        shape_of((tall, 6 * LANES), bf16),
        shape_of((device_count, 8, LANES), f32),
    ]
    arrays = (inputs, attention, gains, router)
    return pl.pallas_call(
        prologue_kernel,
        in_specs=[whole(a.shape) for a in arrays],
        out_specs=[whole(s.shape) for s in shapes],
        out_shape=shapes,
        compiler_params=params(60),
        cost_estimate=LIGHT,
        name="prologue",
    )(*arrays)


def slots_kernel(capacity, info, routes, grads, place, match, valid, slots):
    quarter = routes.shape[0]
    experts = match.shape[1]
    row = lax.broadcasted_iota(jnp.int32, (quarter, 1), 0) + info[0] * quarter
    inside = jnp.where(row < info[1], 1.0, 0.0)
    valid[...] = inside
    column = lax.broadcasted_iota(jnp.int32, (quarter, experts), 1)
    named = jnp.where(routes[...] == column, 1.0, 0.0)
    match[...] = named
    at = lax.broadcasted_iota(jnp.int32, (quarter, quarter), 0)
    before = lax.broadcasted_iota(jnp.int32, (quarter, quarter), 1)
    lower = jnp.where(at >= before, 1.0, 0.0).astype(bf16)
    rank = jnp.sum(mm(lower, (named * inside).astype(bf16)) * named, axis=1, keepdims=True) - 1.0
    slot = jnp.where(inside > 0.0, routes[...].astype(f32) * capacity + rank, -1.0)
    slot = jnp.broadcast_to(slot, (quarter, LANES)).T[:1]
    number = lax.broadcasted_iota(jnp.int32, place.shape, 0).astype(f32)
    chosen = jnp.where(number == slot, 1.0, 0.0).astype(bf16)
    place[...] = chosen
    slots[...] = mm(chosen, grads[...].astype(bf16)).astype(bf16)


def slots_part(info, routes, grads, experts, capacity):
    quarter, width = grads.shape
    shapes = [
        shape_of((experts * capacity, quarter), bf16),
        shape_of((quarter, experts), f32),
        shape_of((quarter, 1), f32),
        shape_of((experts * capacity, width), bf16),
    ]
    return pl.pallas_call(
        lambda *refs: slots_kernel(capacity, *refs),
        in_specs=[scalars(), whole(routes.shape), whole(grads.shape)],
        out_specs=[whole(s.shape) for s in shapes],
        out_shape=shapes,
        compiler_params=params(60),
        cost_estimate=LIGHT,
        name="slots",
    )(info, routes, grads)


def project_kernel(quarter, blocks, count, share, info, came, x0, x1, x2, x3, *refs):
    shards, (small, column_gain, weight, out_weight, qkv, kaug, vt) = refs[:count], refs[count:]
    tall = shards[0].shape[0]
    width = weight.shape[0]
    for j, ref in enumerate(shards):
        start = pl.multiple_of((info[2] ^ j) * tall, tall) if count > 1 else 0
        weight[pl.ds(start, tall), :] = ref[...]
    out_weight[:LANES, :] = weight[:, 3 * LANES : 4 * LANES].T
    out_weight[LANES:, :] = weight[:, 5 * LANES :].T[DH:]
    groups = small.shape[0] // 8
    devices = came.shape[0]
    flat = came[...].reshape(devices * 8, LANES)
    lane = lax.broadcasted_iota(jnp.int32, (LANES, width), 0)
    column = lax.broadcasted_iota(jnp.int32, (LANES, width), 1)
    inside = lax.rem(column, share)
    owner = lax.broadcasted_iota(jnp.int32, (devices, 1, width), 2) - share * lax.broadcasted_iota(
        jnp.int32, (devices, 1, width), 0
    )
    owner = jnp.where((owner >= 0) & (owner < share), 1.0, 0.0)
    for k in range(groups):
        pick = jnp.where(lane == inside + k * share, 1.0, 0.0).astype(bf16)
        spread = split_dot(flat, pick, 3)
        small[8 * k : 8 * k + 8, :] = jnp.sum(spread.reshape(devices, 8, width) * owner, axis=0)
    gain = small[:1, :]
    column_gain[...] = jnp.broadcast_to(gain, (LANES, width)).T[:, :1]
    for j, ref in enumerate((x0, x1, x2, x3)):
        start = pl.multiple_of((info[0] ^ j) * quarter, quarter)
        rows = pl.ds(start, quarter)
        scaled = (ref[...].astype(f32) * gain).astype(bf16)
        first = mm(scaled, weight[:, : 3 * LANES]).astype(bf16)
        second = mm(scaled, weight[:, 4 * LANES :]).astype(bf16)
        qkv[rows, : 3 * LANES] = first
        qkv[rows, 3 * LANES :] = second
        kaug[rows, :LANES] = first[:, LANES : 2 * LANES]
        lane = lax.broadcasted_iota(jnp.int32, (quarter, LANES), 1)
        row = lax.broadcasted_iota(jnp.int32, (quarter, LANES), 0) + start
        hidden = jnp.where((lane == 0) & (row >= info[1]), masked_score, 0.0)
        kaug[rows, LANES:] = jnp.where(lane < DH, hidden, second[:, :LANES].astype(f32)).astype(bf16)
        values = first[:, 2 * LANES :].T
        vt[0, :DH, rows] = values[:DH]
        vt[1, :DH, rows] = values[DH:]
        vt[2, :DH, rows] = second[:, LANES:].T[:DH]
    full_len = quarter * blocks
    tail = (lax.broadcasted_iota(jnp.int32, (16, full_len), 0) == 0).astype(f32).astype(bf16)
    for h in range(3):
        vt[h, DH:, :] = tail


def project(info, came, rows, shards, share, experts):
    quarter, width = rows[0].shape
    blocks = len(rows)
    full_len = quarter * blocks
    shapes = [
        shape_of((8 * -(-(2 + experts) // 8), width), f32),
        shape_of((width, 1), f32),
        shape_of((width, 6 * LANES), bf16),
        shape_of((3 * DH, width), bf16),
        shape_of((full_len, 5 * LANES), bf16),
        shape_of((full_len, 2 * LANES), bf16),
        shape_of((3, DH + 16, full_len), bf16),
    ]
    arrays = (came, *rows, *shards)
    return pl.pallas_call(
        lambda *refs: project_kernel(quarter, blocks, len(shards), share, *refs),
        in_specs=[scalars()] + [whole(a.shape) for a in arrays],
        out_specs=[whole(s.shape) for s in shapes],
        out_shape=shapes,
        compiler_params=params(60),
        cost_estimate=LIGHT,
        name="project",
    )(info, *arrays)


def attention_kernel(info, qkv, kaug, vt, context, chances, totals, *sent):
    quarter = context.shape[2]
    step = pl.program_id(0)
    rows = pl.ds(pl.multiple_of(step * quarter, quarter), quarter)
    q01 = (qkv[rows, :LANES].astype(f32) * score_scale).T.astype(bf16)
    q2 = (qkv[rows, 3 * LANES : 4 * LANES].astype(f32) * score_scale).T.astype(bf16)[:DH]
    ones = (lax.broadcasted_iota(jnp.int32, (DH, quarter), 0) == 0).astype(f32).astype(bf16)
    zeros = jnp.zeros((DH, quarter), bf16)
    queries = (
        jnp.concatenate([q01[:DH], zeros, ones, zeros], axis=0),
        jnp.concatenate([zeros, q01[DH:], ones, zeros], axis=0),
        jnp.concatenate([zeros, zeros, ones, q2], axis=0),
    )
    full_len = kaug.shape[0]
    all_scores = [mm(kaug[...], queries[h]) for h in range(3)]
    for h in range(3):
        scores = all_scores[h]
        top = jnp.max(jnp.max(scores.reshape(8, full_len // 8, quarter), axis=0), axis=0, keepdims=True)
        low = jnp.exp(scores - top).astype(bf16)
        chances[h] = low
        summed = mm(vt[h], low)
        part = 1.0 / summed[DH : DH + 1]
        totals[0, h : h + 1, :] = part
        context[0, h * DH : (h + 1) * DH, :] = (summed[:DH] * part).astype(bf16)
    for j, ref in enumerate(sent):

        @pl.when(step == info[0] ^ j)
        def _():
            ref[...] = context[0]


def attention_forward(info, qkv, kaug, vt, blocks):
    full_len = qkv.shape[0]
    quarter = full_len // blocks
    inner = 3 * DH
    return pl.pallas_call(
        attention_kernel,
        grid=(blocks,),
        in_specs=[scalars(), whole(qkv.shape), whole(kaug.shape), whole(vt.shape)],
        out_specs=[
            pl.BlockSpec((1, inner, quarter), lambda i: (i, 0, 0)),
            pl.BlockSpec((3, full_len, quarter), lambda i: (0, 0, i)),
            pl.BlockSpec((1, 3, quarter), lambda i: (i, 0, 0)),
        ]
        + [whole((inner, quarter))] * blocks,
        out_shape=[
            shape_of((blocks, inner, quarter), bf16),
            shape_of((3, full_len, full_len), bf16),
            shape_of((blocks, 3, quarter), f32),
        ]
        + [shape_of((inner, quarter), bf16)] * blocks,
        compiler_params=params(60),
        cost_estimate=LIGHT,
        name="attend",
    )(info, qkv, kaug, vt)


def turn_kernel(quarter, blocks, info, x0, x1, x2, x3, qkv, context, xt, kt, q2, cn):
    for j, ref in enumerate((x0, x1, x2, x3)):
        xt[info[0] ^ j] = ref[...].T
    for j in range(blocks):
        rows = slice(j * quarter, (j + 1) * quarter)
        third = qkv[rows, 3 * LANES : 4 * LANES].T
        kt[:LANES, rows] = qkv[rows, LANES : 2 * LANES].T
        kt[LANES:, rows] = third[DH:]
        zeros = jnp.zeros((DH, quarter), bf16)
        q2[rows, :] = jnp.concatenate([zeros, third[:DH]], axis=0).T
        cn[rows, :LANES] = context[j, :LANES, :].T
        cn[rows, LANES:] = jnp.concatenate([zeros, context[j, LANES:, :]], axis=0).T


def turn(info, rows, qkv, context):
    quarter, width = rows[0].shape
    blocks = len(rows)
    full_len = quarter * blocks
    shapes = [
        shape_of((blocks, width, quarter), bf16),
        shape_of((3 * DH, full_len), bf16),
        shape_of((full_len, LANES), bf16),
        shape_of((full_len, 2 * LANES), bf16),
    ]
    return pl.pallas_call(
        lambda *refs: turn_kernel(quarter, blocks, *refs),
        in_specs=[scalars()] + [whole((quarter, width))] * 4 + [whole(qkv.shape), whole(context.shape)],
        out_specs=[whole(s.shape) for s in shapes],
        out_shape=shapes,
        compiler_params=params(60),
        cost_estimate=LIGHT,
        name="turn",
    )(info, *rows, qkv, context)


def two_columns(column):
    high = column.astype(bf16).astype(f32)
    lane = lax.broadcasted_iota(jnp.int32, (column.shape[0], LANES), 1)
    return jnp.where(lane == 0, high, jnp.where(lane == 1, column - high, 0.0)).astype(bf16)


def middle_kernel(
    rows, c0, c1, c2, c3, w0, w1, w2, w3, small, place, match, valid, middle, root, chances, gate, slots
):
    gain, router = small[1:2, :], small[2 : 2 + match.shape[1], :]
    total = rows[...]
    for context, weight in zip((c0, c1, c2, c3), (w0, w1, w2, w3)):
        total = total + mm_tn(context[...], weight[...])
    middle[...] = total
    scale = norm_root(total)
    root[...] = scale
    hidden = total * scale * gain
    scores = mm_nt(hidden, router, HIGHEST)
    powers = jnp.exp(scores - jnp.max(scores, axis=-1, keepdims=True))
    share = powers / jnp.sum(powers, axis=-1, keepdims=True)
    chances[...] = share
    own = jnp.sum(share * match[...], axis=-1, keepdims=True)
    gate[...] = own
    width = rows.shape[1]
    slots[:, :width] = mm(place[...], hidden.astype(bf16)).astype(bf16)
    slots[:, width:] = mm(place[...], two_columns(own * valid[...])).astype(bf16)


def middle_part(rows, contexts, out_weights, small, place, match, valid):
    quarter, width = rows.shape
    experts = match.shape[1]
    shapes = [
        shape_of((quarter, width), f32),
        shape_of((quarter, 1), f32),
        shape_of((quarter, experts), f32),
        shape_of((quarter, 1), f32),
        shape_of((place.shape[0], width + LANES), bf16),
    ]
    arrays = (rows, *contexts, *out_weights, small, place, match, valid)
    return pl.pallas_call(
        middle_kernel,
        in_specs=[whole(a.shape) for a in arrays],
        out_specs=[whole(s.shape) for s in shapes],
        out_shape=shapes,
        compiler_params=params(60),
        cost_estimate=LIGHT,
        name="middle",
    )(*arrays)


def expert_kernel(rows, grads, *refs):
    out, back, held, arrived = refs[-4:]
    count = held.shape[0]
    width = grads.shape[1]
    parts = [refs[k : k + count] for k in range(0, len(refs) - 4, count)]
    starts = [sum(part[0].shape[0] for part in parts[:k]) for k in range(len(parts))]
    copies = [
        [
            pltpu.make_async_copy(
                part[i], held.at[i, slice(start, start + part[i].shape[0]), :], arrived.at[i, k]
            )
            for k, (part, start) in enumerate(zip(parts, starts))
        ]
        for i in range(count)
    ]
    for pair in copies:
        for copy in pair:
            copy.start()
    out_total, back_total = None, None
    for i, pair in enumerate(copies):
        for copy in pair:
            copy.wait()
        grad = mm(grads[...], held[i, width:, :])
        active, slope = gelu_pair(mm(rows[:, :width], held[i, :width, :]))
        part = mm_nt(active.astype(bf16), held[i, width:, :])
        back_part = mm_nt((grad * slope).astype(bf16), held[i, :width, :])
        out_total = part if i == 0 else out_total + part
        back_total = back_part if i == 0 else back_total + back_part
    result = out_total.astype(bf16)
    out[...] = result
    back[:, :width] = back_total.astype(bf16)
    match = jnp.sum(grads[...].astype(f32) * result.astype(f32), axis=-1, keepdims=True)
    back[:, width:] = two_columns(match)


def expert_part(rows, grads, *parts):
    slots, width = grads.shape
    hidden = parts[0][0].shape[1]
    count, pieces = len(parts[0]), len(parts)
    flat = [piece for part in parts for piece in part]
    shapes = [shape_of((slots, width), bf16), shape_of((slots, width + LANES), bf16)]
    return pl.pallas_call(
        expert_kernel,
        in_specs=[whole(rows.shape), whole(grads.shape)] + [pl.BlockSpec(memory_space=pl.ANY)] * len(flat),
        out_specs=[whole(s.shape) for s in shapes],
        out_shape=shapes,
        scratch_shapes=[pltpu.VMEM((count, 2 * width, hidden), bf16), pltpu.SemaphoreType.DMA((count, pieces))],
        compiler_params=params(60),
        cost_estimate=LIGHT,
        name="experts",
    )(rows, grads, *flat)


def expert_grad_kernel(count, *refs):
    rows, grads = refs[:count], refs[count : 2 * count]
    near_in, near_mid, near_out, out, square, weight, row_all, grad_all, inner_all, active_all, arrived = refs[2 * count :]
    early, late = near_in.shape[0], near_in.shape[0] + near_mid.shape[0]
    ends = (slice(0, early), slice(early, late), slice(late, weight.shape[0]))
    copies = [
        pltpu.make_async_copy(ref, weight.at[end, :], arrived.at[i])
        for i, (ref, end) in enumerate(zip((near_in, near_mid, near_out), ends))
    ]
    for copy in copies:
        copy.start()
    for copy in copies:
        copy.wait()
    slots, width = grads[0].shape
    for j in range(count):
        at = slice(j * slots, (j + 1) * slots)
        gate = rows[j][:, width : width + 1].astype(f32) + rows[j][:, width + 1 : width + 2].astype(f32)
        row_all[at, :] = rows[j][:, :width]
        grad_all[at, :] = (grads[j][...].astype(f32) * gate).astype(bf16)
        back = mm(grads[j][...], weight[width:, :])
        active, slope = gelu_pair(mm(rows[j][:, :width], weight[:width, :]))
        inner_all[at, :] = (back * slope * gate).astype(bf16)
        active_all[at, :] = active.astype(bf16)
    first = mm_tn(row_all[...], inner_all[...])
    out[0] = first.astype(bf16)
    second = mm_tn(grad_all[...], active_all[...])
    out[1] = second.astype(bf16)
    square[...] = jnp.sum(first * first + second * second, axis=0, keepdims=True)


def expert_gradient(rows, grads, near_in, near_mid, near_out):
    count = len(rows)
    slots, width = grads[0].shape
    hidden = near_in.shape[1]
    arrays = (*rows, *grads)
    shapes = [
        shape_of((2, width, hidden), bf16),
        shape_of((1, hidden), f32),
    ]
    return pl.pallas_call(
        lambda *refs: expert_grad_kernel(count, *refs),
        in_specs=[whole(a.shape) for a in arrays] + [pl.BlockSpec(memory_space=pl.ANY)] * 3,
        out_specs=[whole(s.shape) for s in shapes],
        out_shape=shapes,
        scratch_shapes=[pltpu.VMEM((2 * width, hidden), bf16)]
        + [pltpu.VMEM((count * slots, width), bf16)] * 2
        + [pltpu.VMEM((count * slots, hidden), bf16)] * 2
        + [pltpu.SemaphoreType.DMA((3,))],
        compiler_params=params(60),
        cost_estimate=LIGHT,
        name="expert_gradient",
    )(*arrays, near_in, near_mid, near_out)


def pack_small(small, cut):
    devices = cut.shape[0]
    rows, width = small.shape
    share = width // devices
    groups = rows // 8
    column = lax.broadcasted_iota(jnp.int32, (devices, 1, width), 2)
    owner = column - share * lax.broadcasted_iota(jnp.int32, (devices, 1, width), 0)
    owner = jnp.where((owner >= 0) & (owner < share), 1.0, 0.0)
    lane = lax.broadcasted_iota(jnp.int32, (width, LANES), 1)
    inside = lax.rem(lax.broadcasted_iota(jnp.int32, (width, LANES), 0), share)
    total = None
    for k in range(groups):
        pick = jnp.where(lane == inside + k * share, 1.0, 0.0).astype(bf16)
        spread = (small[8 * k : 8 * k + 8, :][None] * owner).reshape(devices * 8, width)
        part = split_dot(spread, pick, 2)
        total = part if total is None else total + part
    cut[...] = total.reshape(devices, 8, LANES)


def return_kernel(
    back, place, middle, root, chances, gate, match, cotangent, small, w0, w1, w2, w3,
    grad, turned, cut, p0, p1, p2, p3, small_grad,
):
    experts = match.shape[1]
    gain, router = small[1:2, :], small[2 : 2 + experts, :]
    width = middle.shape[1]
    came = mm_tn(place[...], back[...])
    gate_grad = came[:, width : width + 1] + came[:, width + 1 : width + 2]
    own = gate[...]
    score_grad = own * (match[...] - chances[...]) * gate_grad
    scaled = middle[...] * root[...]
    hidden = scaled * gain
    tall = small_grad.shape[0]
    small_grad[1 : 1 + experts, :] = mm_tn(score_grad, hidden, HIGHEST)
    small_grad[1 + experts :, :] = jnp.zeros((tall - 1 - experts, hidden.shape[1]), f32)
    second = own * came[:, :width] + jnp.dot(
        score_grad, router, precision=HIGHEST, preferred_element_type=f32
    )
    small_grad[:1, :] = jnp.sum(second * scaled, axis=0, keepdims=True)
    inner = second * gain
    centre = jnp.mean(inner * scaled, axis=-1, keepdims=True)
    total = cotangent[...] + root[...] * (inner - scaled * centre)
    grad[...] = total
    low = total.astype(bf16)
    turned[...] = low.T
    for ref, weight in zip((p0, p1, p2, p3), (w0, w1, w2, w3)):
        ref[...] = mm_nt(weight[...], low).astype(bf16)
    pack_small(small_grad, cut)


def return_part(back, place, middle, root, chances, gate, match, cotangent, small, out_weights, device_count):
    quarter, width = middle.shape
    experts = match.shape[1]
    inner = out_weights[0].shape[0]
    shapes = [
        shape_of((quarter, width), f32),
        shape_of((width, quarter), bf16),
        shape_of((device_count, 8, LANES), f32),
    ] + [shape_of((inner, quarter), bf16)] * len(out_weights)
    arrays = (back, place, middle, root, chances, gate, match, cotangent, small, *out_weights)
    return pl.pallas_call(
        return_kernel,
        in_specs=[whole(a.shape) for a in arrays],
        out_specs=[whole(s.shape) for s in shapes],
        out_shape=shapes,
        scratch_shapes=[pltpu.VMEM((8 * -(-(1 + experts) // 8), width), f32)],
        compiler_params=params(60),
        cost_estimate=LIGHT,
        name="returned",
    )(*arrays)


def attention_back_kernel(
    blocks, info, g0, g1, g2, g3, context, chances, totals, qkv, kt, q2, packed, grads, vaug, k01, k2, v01, v2
):
    step = pl.program_id(0)
    quarter = grads.shape[2]

    @pl.when(step == 0)
    def _():
        for j, ref in enumerate((g0, g1, g2, g3)):
            grads[info[0] ^ j] = ref[...]
        vaug[:, :LANES] = qkv[:, 2 * LANES : 3 * LANES]
        lane = lax.broadcasted_iota(jnp.int32, (vaug.shape[0], LANES), 1)
        ones = jnp.where(lane < DH + 2, 1.0, 0.0)
        vaug[:, LANES:] = jnp.where(lane < DH, qkv[:, 4 * LANES :].astype(f32), ones).astype(bf16)
        for ref in (k01, k2, v01, v2):
            ref[...] = jnp.zeros(ref.shape, f32)

    rows = pl.ds(pl.multiple_of(step * quarter, quarter), quarter)
    raw = grads[step].astype(f32)
    scale = totals[0]
    scaled = [raw[h * DH : (h + 1) * DH] * scale[h : h + 1] for h in range(3)]
    heads = jnp.concatenate(scaled, axis=0).astype(bf16)
    lane = lax.broadcasted_iota(jnp.int32, (quarter, LANES), 1)
    row = lax.broadcasted_iota(jnp.int32, (DH, quarter), 0)
    zeros = jnp.zeros((DH, quarter), bf16)
    q01 = qkv[rows, :LANES].astype(f32)
    g01 = heads[:LANES].T.astype(f32)
    third = jnp.concatenate([heads[LANES:], zeros], axis=0).T
    query_parts = []
    for h in range(3):
        part = heads[h * DH : (h + 1) * DH]
        centre = -jnp.sum(
            part.astype(f32) * context[0, h * DH : (h + 1) * DH, :].astype(f32), axis=0, keepdims=True
        )
        high = centre.astype(bf16).astype(f32)
        tail = jnp.where(row == 0, high, jnp.where(row == 1, centre - high, 0.0)).astype(bf16)
        pieces = [zeros, zeros, zeros, tail]
        pieces[h] = part
        chance_grad = mm(vaug[...], jnp.concatenate(pieces, axis=0))
        low = chances[h]
        score_grad = (low.astype(f32) * chance_grad).astype(bf16)
        query_parts.append(mm(kt[h * DH : (h + 1) * DH, :], score_grad) * score_scale)
        if h < 2:
            inside = (lane >= h * DH) & (lane < (h + 1) * DH)
            k01[...] += mm(score_grad, jnp.where(inside, q01, 0.0).astype(bf16))
            v01[...] += mm(low, jnp.where(inside, g01, 0.0).astype(bf16))
        else:
            k2[...] += mm(score_grad, q2[rows, :])
            v2[...] += mm(low, third)
    packed[rows, :LANES] = jnp.concatenate(query_parts[:2], axis=0).T.astype(bf16)
    packed[rows, 4 * LANES : 5 * LANES] = (
        jnp.concatenate([query_parts[2], jnp.zeros((DH, quarter), f32)], axis=0).T.astype(bf16)
    )

    @pl.when(step == blocks - 1)
    def _():
        packed[:, LANES : 2 * LANES] = (k01[...] * score_scale).astype(bf16)
        packed[:, 2 * LANES : 3 * LANES] = v01[...].astype(bf16)
        packed[:, 3 * LANES : 4 * LANES] = jnp.zeros(k01.shape, bf16)
        packed[:, 4 * LANES : 5 * LANES] = packed[:, 4 * LANES : 5 * LANES] + (k2[...] * score_scale).astype(bf16)
        packed[:, 5 * LANES :] = v2[...].astype(bf16)


def attention_backward(info, grads, context, chances, totals, qkv, kt, q2):
    blocks, inner, quarter = context.shape
    full_len = quarter * blocks
    block = pl.BlockSpec((1, inner, quarter), lambda i: (i, 0, 0))
    return pl.pallas_call(
        lambda *refs: attention_back_kernel(blocks, *refs),
        grid=(blocks,),
        in_specs=[
            scalars(),
            *[whole((inner, quarter))] * blocks,
            block,
            pl.BlockSpec((3, full_len, quarter), lambda i: (0, 0, i)),
            pl.BlockSpec((1, 3, quarter), lambda i: (i, 0, 0)),
            whole(qkv.shape),
            whole(kt.shape),
            whole(q2.shape),
        ],
        out_specs=whole((full_len, 6 * LANES)),
        out_shape=shape_of((full_len, 6 * LANES), bf16),
        scratch_shapes=[pltpu.VMEM(context.shape, bf16), pltpu.VMEM((full_len, 2 * LANES), bf16)]
        + [pltpu.VMEM((full_len, LANES), f32)] * 4,
        compiler_params=params(60),
        cost_estimate=LIGHT,
        name="attend_back",
    )(info, *grads, context, chances, totals, qkv, kt, q2)


def weight_grad_kernel(blocks, info, xt, packed, g0, g1, g2, g3, cn, weight, gain, out, gain_grad):
    quarter = xt.shape[2]
    total, outer = None, None
    for j, ref in enumerate((g0, g1, g2, g3)):
        rows = slice(j * quarter, (j + 1) * quarter)
        there = pl.ds(pl.multiple_of((info[0] ^ j) * quarter, quarter), quarter)
        part = mm(xt[j], packed[rows, :])
        own = mm(ref[...], cn[there, :])
        total = part if total is None else total + part
        outer = own if outer is None else outer + own
    gain_grad[...] = jnp.sum(total * weight[...].astype(f32), axis=1, keepdims=True)
    total = total * gain[...]
    out[:, : 3 * LANES] = total[:, : 3 * LANES].astype(bf16)
    out[:, 3 * LANES : 4 * LANES] = outer[:, :LANES].astype(bf16)
    out[:, 4 * LANES : 5 * LANES] = total[:, 4 * LANES : 5 * LANES].astype(bf16)
    out[:, 5 * LANES :] = (total[:, 5 * LANES :] + outer[:, LANES:]).astype(bf16)


def weight_gradient(info, xt, packed, grads, cn, weight, gain):
    blocks, width, quarter = xt.shape
    tall = 256
    full_len = quarter * blocks
    return pl.pallas_call(
        lambda *refs: weight_grad_kernel(blocks, *refs),
        grid=(width // tall,),
        in_specs=[
            scalars(),
            pl.BlockSpec((blocks, tall, quarter), lambda i: (0, i, 0)),
            whole(packed.shape),
            *[pl.BlockSpec((tall, quarter), lambda i: (i, 0))] * blocks,
            whole(cn.shape),
            pl.BlockSpec((tall, 6 * LANES), lambda i: (i, 0)),
            pl.BlockSpec((tall, 1), lambda i: (i, 0)),
        ],
        out_specs=[pl.BlockSpec((tall, 6 * LANES), lambda i: (i, 0)), pl.BlockSpec((tall, 1), lambda i: (i, 0))],
        out_shape=[shape_of((width, 6 * LANES), bf16), shape_of((width, 1), f32)],
        compiler_params=params(60),
        cost_estimate=LIGHT,
        name="weight_gradient",
    )(info, xt, packed, *grads, cn, weight, gain)


def input_grad_kernel(quarter, info, packed, weight, *parts):
    for j, ref in enumerate(parts):
        rows = pl.ds(pl.multiple_of((info[0] ^ j) * quarter, quarter), quarter)
        ref[...] = mm_nt(packed[rows, :], weight[...]).astype(bf16)


def input_gradient(info, packed, weight, blocks):
    quarter = packed.shape[0] // blocks
    shapes = [shape_of((quarter, weight.shape[0]), bf16)] * blocks
    return pl.pallas_call(
        lambda *refs: input_grad_kernel(quarter, *refs),
        in_specs=[scalars(), whole(packed.shape), whole(weight.shape)],
        out_specs=[whole(s.shape) for s in shapes],
        out_shape=shapes,
        compiler_params=params(60),
        cost_estimate=LIGHT,
        name="input_gradient",
    )(info, packed, weight)


def sums_kernel(came, squares, small, gain_grad, gradient, payload, small_sum):
    count = came.shape[0]
    total = came[0].astype(f32)
    for i in range(1, count):
        total = total + came[i].astype(f32)
    gradient[...] = total
    own = jnp.sum(small[...], axis=0)
    square = (
        jnp.sum(total * total, keepdims=True)
        + jnp.sum(squares[...], keepdims=True)
        + jnp.sum(own * own, keepdims=True)
    )
    small_sum[...] = own
    rows = gain_grad.shape[0]
    row = lax.broadcasted_iota(jnp.int32, (8, LANES), 0)
    gain = jnp.concatenate([gain_grad[...], jnp.zeros((8 - rows, LANES), f32)], axis=0)
    payload[...] = jnp.broadcast_to(jnp.where(row < rows, gain, square)[None], payload.shape)


def sums_part(came, squares, small, gain_grad, device_count):
    shapes = [
        shape_of(came.shape[1:], f32),
        shape_of((device_count, 8, LANES), f32),
        shape_of((8, LANES), f32),
    ]
    arrays = (came, squares, small, gain_grad)
    return pl.pallas_call(
        sums_kernel,
        in_specs=[whole(a.shape) for a in arrays],
        out_specs=[whole(s.shape) for s in shapes],
        out_shape=shapes,
        compiler_params=params(60),
        cost_estimate=LIGHT,
        name="sums",
    )(*arrays)


def adam_kernel(lanes, share, expert_rates, info, last, small_sum, *refs):
    held, outs, factor = refs[:14], refs[14:27], refs[27]
    dense, dense_grad, gains, router = held[:3], held[3], held[4:7], held[7:10]
    weight, first, second, gradient = held[10:14]
    norm_out, outs = outs[0], outs[1:]
    dense_out, gains_out, router_out, expert_out = outs[:3], outs[3:6], outs[6:9], outs[9:12]
    matrix, part = pl.program_id(0), pl.program_id(1)
    experts = router[0].shape[0]

    @pl.when((matrix == 0) & (part == 0))
    def _():
        total = jnp.sum(last[...], axis=0)
        row = lax.broadcasted_iota(jnp.int32, (8, LANES), 0)
        squares = jnp.sum(jnp.where(row < lanes, total * total, 0.0), keepdims=True)
        norm = jnp.sqrt(squares + total[7:8, :1])
        scale = jnp.minimum(1.0, clip_limit / (norm + norm_epsilon))
        norm_out[...] = norm
        factor[...] = jnp.broadcast_to(scale, (8, LANES))
        rates = (0.71 / math.sqrt(D), 0.71 / math.sqrt(D), 0.83 / math.sqrt(D), 0.79 / math.sqrt(H * DH))
        for i, rate in enumerate(rates):
            grad = jnp.concatenate(
                [
                    dense_grad[:, i * LANES : (i + 1) * LANES],
                    dense_grad[:, 4 * LANES + i * DH : 4 * LANES + (i + 1) * DH],
                ],
                axis=1,
            )
            result = adam_update(*[ref[i] for ref in dense], grad * scale, rate)
            for ref, value in zip(dense_out, result):
                ref[i] = value
        column = lax.broadcasted_iota(jnp.int32, (LANES, LANES), 1)
        place = lax.broadcasted_iota(jnp.int32, (LANES, LANES), 0) - info[3] * share
        own = jnp.zeros((8, LANES), f32)
        for i in range(lanes):
            pick = jnp.where((column == place + i * LANES) & (column < share), 1.0, 0.0)
            own = own + jnp.dot(
                jnp.broadcast_to(total[i : i + 1], (8, LANES)), pick, precision=HIGHEST, preferred_element_type=f32
            )
        groups = -(-(1 + experts) // 8)
        table = small_sum[...]
        table = jnp.concatenate([table[:, k * share : (k + 1) * share] for k in range(groups)], axis=0)
        grad = jnp.concatenate([own[:1, :share], table[:1]], axis=0)
        for ref, value in zip(gains_out, adam_update(*[ref[...] for ref in gains], grad * scale, 0.5)):
            ref[...] = value
        grad = table[1 : 1 + experts]
        result = adam_update(*[ref[...] for ref in router], grad * scale, 0.24 / math.sqrt(D))
        for ref, value in zip(router_out, result):
            ref[...] = value

    rate = jnp.where(matrix == 0, expert_rates[0], expert_rates[1])
    grad = gradient[...].astype(f32) * factor[:1, :1]
    result = adam_update(weight[...], first[...], second[...], grad, rate)
    for ref, value in zip(expert_out, result):
        ref[...] = value


def adam(info, last, small_sum, dense, dense_grad, gains, router, expert, expert_grad, rates):
    _, tall, wide = expert_grad.shape
    parts = 8
    block = pl.BlockSpec((1, tall // parts, wide), lambda i, j: (i, j, 0))
    small = [*dense, *gains, *router]
    shapes = [shape_of((1, 1), f32)] + [shape_of(a.shape, f32) for a in small]
    ins = (last, small_sum, *dense, dense_grad, *gains, *router)
    return pl.pallas_call(
        lambda *refs: adam_kernel(tall // LANES, gains[0].shape[1], rates, *refs),
        grid=(2, parts),
        in_specs=[scalars()] + [whole(a.shape) for a in ins] + [block] * 4,
        out_specs=[whole(a.shape) for a in shapes] + [block] * 3,
        out_shape=shapes + [shape_of(expert_grad.shape, f32)] * 3,
        scratch_shapes=[pltpu.VMEM((8, LANES), f32)],
        compiler_params=params(60),
        cost_estimate=LIGHT,
        name="adam",
    )(info, *ins, *expert, expert_grad)


def tie(*values):
    return lax.optimization_barrier(values)


def on_device(
    inputs,
    cotangent,
    lengths,
    routes,
    attention_weight,
    attention_mean,
    attention_square,
    expert_weight,
    expert_mean,
    expert_square,
    router_matrix,
    router_mean,
    router_square,
    norm_gains,
    gains_mean,
    gains_square,
):
    quarter, width = inputs.shape[1:]
    dp_count, tensor_count = lax.axis_size(DP), lax.axis_size(TENSOR)
    device_count = dp_count * tensor_count
    expert_count = router_matrix.shape[1]
    capacity = max(2, (5 * quarter + 4 * expert_count - 1) // (4 * expert_count))
    own_dp, own_tensor = lax.axis_index(DP), lax.axis_index(TENSOR)
    share = router_matrix.shape[0]
    rows, grad_rows, length = inputs[0], cotangent[0], lengths[0]
    info = jnp.stack([own_tensor, length, own_dp, lax.axis_index(EVERYONE)]).astype(jnp.int32)

    scaled_one, root_one, weight_own, payload = prologue(
        rows, attention_weight, norm_gains, router_matrix.T, device_count
    )
    block_two = swap(scaled_one, TENSOR, 2)
    small_came = lax.all_to_all(payload, EVERYONE, 0, 0, tiled=True)
    expert_flat = expert_weight[0].reshape(2 * width, -1)
    early_own, mid_own, late_own = [part.astype(bf16) for part in jnp.split(expert_flat, CUTS)]
    place, match, valid_scale, grad_slots = slots_part(info, routes[0], grad_rows, expert_count, capacity)
    if dp_count == 8:
        w4, w2, w1 = [swap(weight_own, DP, mask) for mask in (4, 2, 1)]
        w4, w2, w1, small_came, block_two, early_own = tie(w4, w2, w1, small_came, block_two, early_own)
        w6, w5, w3 = swap(w4, DP, 2), swap(w4, DP, 1), swap(w2, DP, 1)
        w6, w5, w3, scaled_one = tie(w6, w5, w3, scaled_one)
        w7, grad_slots = tie(swap(w6, DP, 1), grad_slots)
        shards = [weight_own, w1, w2, w3, w4, w5, w6, w7]
    else:
        weight_own, grad_slots, small_came, block_two, early_own = tie(
            weight_own, grad_slots, small_came, block_two, early_own
        )
        shards = [lax.all_gather(weight_own, DP, axis=0, tiled=True)]
    early_far = swap(early_own, TENSOR, 2)
    row_blocks = [scaled_one, swap(scaled_one, TENSOR, 1), block_two, swap(block_two, TENSOR, 1)]

    slot_count = expert_count * capacity

    def trade(values):
        blocks = values.reshape(expert_count, capacity, values.shape[1])
        return lax.all_to_all(blocks, DP, 0, 0, tiled=True).reshape(values.shape)

    expert_grads = trade(grad_slots)
    small, gain_column, weight, out_weight, qkv, keys_wide, values_turned = project(
        info, small_came, row_blocks, shards, share, expert_count
    )
    out_weight, early_own = tie(out_weight, early_own)
    out_near, out_far = swap(out_weight, TENSOR, 1), swap(out_weight, TENSOR, 2)
    early_near = swap(early_own, TENSOR, 1)
    context, chances, totals, *sent = attention_forward(info, qkv, keys_wide, values_turned, tensor_count)
    expert_grads, early_far, out_near, out_far, *sent = tie(expert_grads, early_far, out_near, out_far, *sent)
    contexts = [sent[0]] + [swap(sent[j], TENSOR, j) for j in range(1, tensor_count)]
    out_weights = [out_weight, out_near, out_far, swap(out_far, TENSOR, 1)]
    late_own, mid_own, early_far, *contexts = tie(late_own, mid_own, early_far, *contexts)
    mid_far = swap(mid_own, TENSOR, 2)

    middle, root_two, shares, gate, slots = middle_part(
        rows, contexts, out_weights, small, place, match, valid_scale
    )
    slots, late_own, mid_own, mid_far = tie(slots, late_own, mid_own, mid_far)
    late_far = swap(late_own, TENSOR, 2)
    expert_rows = trade(slots)
    early_parts = [early_own, early_far, early_near, swap(early_far, TENSOR, 1)]
    mid_parts = [mid_own, mid_far, swap(mid_own, TENSOR, 1), swap(mid_far, TENSOR, 1)]
    expert_rows, late_far = tie(expert_rows, late_far)
    late_parts = [late_own, late_far, swap(late_own, TENSOR, 1), swap(late_far, TENSOR, 1)]
    expert_outs, expert_back = expert_part(expert_rows, expert_grads, early_parts, mid_parts, late_parts)
    expert_rows, expert_back, qkv = tie(expert_rows, expert_back, qkv)
    turned_rows, keys_turned, third_query, context_rows = turn(info, row_blocks, qkv, context)
    rows_near, rows_far = swap(expert_rows, TENSOR, 1), swap(expert_rows, TENSOR, 2)
    rows_far, expert_grads = tie(rows_far, expert_grads)
    rows_all = [expert_rows, rows_near, rows_far, swap(rows_far, TENSOR, 1)]
    grads_near, grads_far = swap(expert_grads, TENSOR, 1), swap(expert_grads, TENSOR, 2)
    expert_back, rows_all, turned_rows = tie(trade(expert_back), rows_all, turned_rows)

    middle_grad, middle_turned, small_cut, *parts = return_part(
        expert_back, place, middle, root_two, shares, gate, match, grad_rows, small, out_weights, device_count
    )
    expert_outs, middle_turned, *parts = tie(expert_outs, middle_turned, *parts)
    context_grads = [parts[0]] + [swap(parts[j], TENSOR, j) for j in range(1, tensor_count)]
    expert_outs = trade(expert_outs)
    middle_turned, *context_grads = tie(middle_turned, *context_grads)
    middle_near, middle_far = swap(middle_turned, TENSOR, 1), swap(middle_turned, TENSOR, 2)

    packed = attention_backward(info, context_grads, context, chances, totals, qkv, keys_turned, third_query)
    packed, middle_far, grads_far, small_cut, expert_outs = tie(packed, middle_far, grads_far, small_cut, expert_outs)
    middle_all = [middle_turned, middle_near, middle_far, swap(middle_far, TENSOR, 1)]
    grads_all = [expert_grads, grads_near, grads_far, swap(grads_far, TENSOR, 1)]
    small_grads = lax.all_to_all(small_cut, EVERYONE, 0, 0, tiled=True)
    weight_grad, gain_one_grad = weight_gradient(
        info, turned_rows, packed, middle_all, context_rows, weight, gain_column
    )
    weight_grad, early_own, small_grads = tie(weight_grad, early_own, small_grads)
    weight_came = lax.all_to_all(weight_grad.reshape(dp_count, -1, width), DP, 0, 0, tiled=True)
    expert_grad, expert_squares = expert_gradient(rows_all, grads_all, early_own, mid_own, late_own)
    expert_squares, packed = tie(expert_squares, packed)

    input_parts = input_gradient(info, packed, weight, tensor_count)
    first_half = input_parts[0].astype(f32) + swap(input_parts[1], TENSOR, 1).astype(f32)
    second_half = (input_parts[2].astype(f32) + swap(input_parts[3], TENSOR, 1).astype(f32)).astype(bf16)

    second_came = swap(second_half, TENSOR, 2)
    dense_grad, last, small_sum = sums_part(
        weight_came, expert_squares, small_grads, gain_one_grad.reshape(-1, LANES), device_count
    )
    last, expert_outs, middle_grad, rows_late = tie(last, expert_outs, middle_grad, rows)
    last_all = lax.all_to_all(last, EVERYONE, 0, 0, tiled=True)
    input_grad = middle_grad + norm_backward(
        rows_late, root_one, small[:1], first_half + second_came.astype(f32)
    )
    picked = mm_tn(place, expert_outs)
    branch = gate * valid_scale * picked
    block_output = middle + branch
    last_all, input_grad, block_output, branch = tie(last_all, input_grad, block_output, branch)

    rates = (0.4 * math.sqrt(expert_count / D), 1.38 * math.sqrt(expert_count / FF))
    norm, *updated = adam(
        info,
        last_all,
        small_sum,
        (attention_weight, attention_mean, attention_square),
        dense_grad,
        (norm_gains, gains_mean, gains_square),
        (router_matrix.T, router_mean.T, router_square.T),
        (expert_weight[0], expert_mean[0], expert_square[0]),
        expert_grad,
        rates,
    )
    attention_new, gains_new, router_new, expert_new = updated[:3], updated[3:6], updated[6:9], updated[9:]
    router_new = [part.T for part in router_new]
    grad_norm = norm.reshape(())
    return (
        block_output[None],
        input_grad[None],
        grad_norm,
        *attention_new,
        *[part[None] for part in expert_new],
        *router_new,
        *gains_new,
        branch[None],
    )


def solution(mesh):
    names = mesh.axis_names
    dp_count, tensor_count = mesh.shape[names[0]], mesh.shape[names[1]]
    cut = jax.sharding.Mesh(mesh.devices.reshape(dp_count // 2, 2, tensor_count // 2, 2), EVERYONE)
    rows = P(DP, TENSOR, None)
    attention = P(None, DP, TENSOR)
    expert = P(DP, None, None, TENSOR)
    router = P(EVERYONE, None)
    gains = P(None, EVERYONE)
    weights = (attention,) * 3 + (expert,) * 3 + (router,) * 3 + (gains,) * 3
    return jax.shard_map(
        on_device,
        mesh=cut,
        in_specs=(rows, rows, P(DP), rows) + weights,
        out_specs=(rows, rows, P()) + weights + (rows,),
        check_vma=False,
    )
```
